32 devices in a mesh: member: 4 (over y, core), space: 8 (over z, x).
Axes of the slice: x: 2, y: 2, z: 4, core: 2. Of those that a mesh axis runs over, the one named last changes fastest.
Arguments:
- ensemble: float32 [96, 4, 64, 4, 256], P('member', None, 'space'), may hold values from 0 to 2
- diffusivity: float32 [64, 4, 256], P('space'), may hold values from 0.03 to 0.16
- binding: float32 [64, 4, 256], P('space'), may hold values from 0.02 to 0.2
- source: float32 [64, 4, 256], P('space'), may hold values from 0.005 to 0.05
- obs_index: int32 [4, 2048], replicated, may hold values from 0 to 8191
- owner: int32 [4], replicated, may hold values from 0 to 7
- observed: float32 [4, 2048], replicated, may hold values from -6 to 6
- obs_var: float32 [4, 2048], replicated, may hold values from 0.5 to 2
Outputs:
- analysis: float32 [96, 4, 64, 4, 256], P('member', None, 'space')
The draws below stay inside these ranges and needn't reach their ends.
Inputs may be any that keep to these rules, and one draw needn't show every extreme that they name: owner holds space indices of devices.
All inputs are finite; a program needn't handle non-finite values.
Results may differ from the reference program's by a relative error of at most 0.0003.
Values sent between devices are 32-bit elements; how exact they have to be, the bound alone decides.
No kernel may reach another device: no remote copies, remote signals or barrier semaphores. Data moves between devices by JAX's collectives and lax.ppermute only.
A program may use at most 64 MiB of HBM per device.

```python
import math
import jax
import jax.numpy as jnp
from jax import lax

ENSEMBLE_SIZE = 96
CX = 8
NY = 256
NZ = 4
SUBSTEPS = 6
BATCHES = 4
NOBS = 2048
NEWTON = 16
NX = 64
N_SPACE = 8


def place_ends(entries, stream_key, low, high):
    extent = entries.shape
    spot = [jax.random.randint(jax.random.fold_in(stream_key, axis), (), 0, extent[axis]) for axis in range(len(extent))]
    entries = entries.at[tuple(spot)].set(low)
    longest = extent.index(max(extent))
    spot[longest] = (spot[longest] + 1) % extent[longest]
    return entries.at[tuple(spot)].set(high)


def steps_of(key, dims, cuts, smallest, top_value):
    level, own = 1.0, jax.random.fold_in(key, 6)
    for dim, blocks in cuts:
        draws = jnp.exp(jax.random.uniform(jax.random.fold_in(own, dim), (blocks,), jnp.float32, smallest / len(cuts), top_value / len(cuts)))
        level = level * jnp.repeat(draws, dims[dim] // blocks).reshape([-1 if axis == dim else 1 for axis in range(len(dims))])
    return level


def centred(own_key, dims, deviation, reach, held_as=jnp.bfloat16):
    values = deviation * jax.random.normal(own_key, dims, jnp.float32)
    return jnp.clip(values, min=-reach, max=reach).astype(held_as)


def setup_inputs(seed: int = 0) -> dict:
    key_list = jax.random.split(jax.random.key(seed), 9)
    return {
        "ensemble": jnp.clip(2.0 * jax.random.uniform(key_list[0], (ENSEMBLE_SIZE, 4, NX, NZ, NY), jnp.float32) ** steps_of(key_list[0], (ENSEMBLE_SIZE, 4, NX, NZ, NY), ((0, 4), (2, 8)), -0.2, 0.2), 0.0, 2.0),
        "diffusivity": jnp.clip(jnp.exp(math.log(0.16) - 1.6739764 * jax.random.uniform(key_list[1], (NX, NZ, NY), jnp.float32) ** steps_of(key_list[1], (NX, NZ, NY), ((0, 8),), -0.2, 0.2)), 0.03, 0.16),
        "binding": jnp.clip(jnp.exp(math.log(0.2) - 2.3025851 * jax.random.uniform(key_list[2], (NX, NZ, NY), jnp.float32) ** steps_of(key_list[2], (NX, NZ, NY), ((0, 8),), -0.2, 0.2)), 0.02, 0.2),
        "source": jnp.clip(jnp.exp(math.log(0.05) - 2.3025851 * jax.random.uniform(key_list[3], (NX, NZ, NY), jnp.float32) ** steps_of(key_list[3], (NX, NZ, NY), ((0, 8),), -0.2, 0.2)), 0.005, 0.05),
        "obs_index": place_ends(jax.random.randint(key_list[4], (BATCHES, NOBS), 0, CX * NZ * NY), jax.random.fold_in(key_list[4], 1), 0, (CX * NZ * NY) - 1).astype(jnp.int32),
        "owner": place_ends(jax.random.randint(key_list[5], (BATCHES,), 0, N_SPACE), jax.random.fold_in(key_list[5], 1), 0, N_SPACE - 1).astype(jnp.int32),
        "observed": centred(key_list[6], (BATCHES, NOBS), 1.0, 6.0, jnp.float32),
        "obs_var": jnp.clip(jnp.exp(jax.random.uniform(key_list[7], (BATCHES, NOBS), jnp.float32, math.log(0.5), math.log(2.0))), 0.5, 2.0),
    }


unbind_rate = 0.05
uptake_rate = 0.1
recycle_rate = 0.02
highest = lax.Precision.HIGHEST

def react(free, receptor, complexed, internal, neighbours, diffusivity, binding, source):
    binding_flux = binding * free * receptor
    updated_unbound = free + diffusivity * (neighbours - 6.0 * free) - binding_flux + unbind_rate * complexed + source
    new_receptor = receptor - binding_flux + unbind_rate * complexed + recycle_rate * internal
    updated_bound_complex = complexed + binding_flux - (unbind_rate + uptake_rate) * complexed
    new_internal = internal + uptake_rate * complexed - recycle_rate * internal
    return jnp.stack([updated_unbound, new_receptor, updated_bound_complex, new_internal], axis=-4)

def transform(priors, observed, obs_var):
    members = priors.shape[1]
    identity_k = jnp.eye(members, dtype=priors.dtype)
    mean_prior = lax.optimization_barrier(jnp.mean(priors, axis=1))
    spread = priors - mean_prior[:, None]
    weight_applied = spread / obs_var[:, None]
    system = identity_k + jnp.dot(spread.T, weight_applied, precision=highest) / (members - 1)
    frobenius = jnp.sqrt(jnp.sum(system * system))

    def newton(iteration, iterates):
        scaled_root, inverse_root = iterates
        factor = 1.5 * identity_k - 0.5 * jnp.dot(inverse_root, scaled_root, precision=highest)
        return (jnp.dot(scaled_root, factor, precision=highest), jnp.dot(factor, inverse_root, precision=highest))
    scaled_root, inverse_root = lax.fori_loop(0, NEWTON, newton, (system / frobenius, identity_k))
    root_inv = inverse_root / jnp.sqrt(frobenius)
    innovation = jnp.dot(observed - mean_prior, weight_applied, precision=highest) / (members - 1)
    mean_weight = jnp.dot(root_inv, jnp.dot(root_inv, innovation, precision=highest), precision=highest)
    average = jnp.full((members, members), 1.0 / members, dtype=priors.dtype)
    return jnp.dot(identity_k - average, root_inv + mean_weight[:, None], precision=highest) + average

def predicted_member_state(fields_per_member, diffusivity, binding, source):
    for substep in range(SUBSTEPS):
        free = fields_per_member[0]
        padded = jnp.pad(free, 1)
        neighbours = padded[2:, 1:-1, 1:-1] + padded[:-2, 1:-1, 1:-1]
        neighbours = neighbours + padded[1:-1, 2:, 1:-1] + padded[1:-1, :-2, 1:-1]
        neighbours = neighbours + padded[1:-1, 1:-1, 2:] + padded[1:-1, 1:-1, :-2]
        fields_per_member = react(free, fields_per_member[1], fields_per_member[2], fields_per_member[3], neighbours, diffusivity, binding, source)
    return fields_per_member

def reference(ensemble, diffusivity, binding, source, obs_index, owner, observed, obs_var):
    present_fields = lax.map(lambda fields_per_member: predicted_member_state(fields_per_member, diffusivity, binding, source), ensemble)
    members = present_fields.shape[0]
    slab_cells = CX * NZ * NY
    for which_batch in range(BATCHES):
        totals = (present_fields[:, 2] + present_fields[:, 3]).reshape(members, -1)
        voxels = (owner[which_batch] * slab_cells + obs_index[which_batch]).astype(jnp.int32)
        priors = jnp.take(totals, voxels, axis=1).T
        mixing_matrix = transform(priors, observed[which_batch], obs_var[which_batch])
        present_fields = jnp.einsum('jk,jsxzy->ksxzy', mixing_matrix, present_fields, precision=highest)
    return present_fields
```

```python
import functools

import jax
import jax.numpy as jnp
from jax import lax
from jax.experimental import pallas as pl
from jax.experimental.pallas import tpu as pltpu
from jax.sharding import PartitionSpec as P

SUBSTEPS = 6
NEWTON = 16
LANES = 128

unbind_rate = 0.05
uptake_rate = 0.1
recycle_rate = 0.02

VMEM = pl.BlockSpec(memory_space=pltpu.VMEM)
SMEM = pl.BlockSpec(memory_space=pltpu.SMEM)
bf16 = jnp.bfloat16
f32 = jnp.float32


def split(x):
    high = x.astype(bf16)
    return high, (x - high.astype(f32)).astype(bf16)


def dot_parts(a, b, dims):
    a_high, a_low = a
    b_high, b_low = b
    mul = functools.partial(
        lax.dot_general, dimension_numbers=(dims, ((), ())), preferred_element_type=f32
    )
    return mul(a_high, b_high) + (mul(a_high, b_low) + mul(a_low, b_high))


def wide_left(x):
    return jnp.concatenate(split(x), axis=1)


def wide_right(x):
    both = jnp.concatenate(split(x), axis=1)
    return jnp.concatenate([both, both], axis=0)


def square_dot(left, right):
    out = jnp.dot(left, right, preferred_element_type=f32)
    side = out.shape[0]
    return out[:, :side] + out[:, side:]


NN = ((1,), (0,))
NT = ((1,), (1,))


def substep_kernel(
    a, r, c, i, low, high, diffusivity, binding, source, out_a, out_r, out_c, out_i, *edges, final
):
    nx, nz, members, ny = a.shape
    lane = lax.broadcasted_iota(jnp.int32, (members, ny), 1)
    at_left, at_right = lane == 0, lane == ny - 1

    def cell(x, z):
        free = a[x, z]
        neighbours = (low[z] if x == 0 else a[x - 1, z]) + (
            high[z] if x == nx - 1 else a[x + 1, z]
        )
        if z + 1 < nz:
            neighbours += a[x, z + 1]
        if z > 0:
            neighbours += a[x, z - 1]
        neighbours += jnp.where(at_right, 0.0, pltpu.roll(free, ny - 1, 1))
        neighbours += jnp.where(at_left, 0.0, pltpu.roll(free, 1, 1))
        receptor, complexed, internal = r[x, z], c[x, z], i[x, z]
        row = pl.ds(z, 1)
        flux = binding[x, row, :] * free * receptor
        back = unbind_rate * complexed - flux
        new_free = (
            free
            + diffusivity[x, row, :] * (neighbours - 6.0 * free)
            + back
            + source[x, row, :]
        )
        new_internal = internal + uptake_rate * complexed - recycle_rate * internal
        new_complexed = complexed + flux - (unbind_rate + uptake_rate) * complexed
        out_a[x, z] = new_free
        out_r[x, z] = receptor + back + recycle_rate * internal
        out_c[x, z] = new_complexed + new_internal if final else new_complexed
        out_i[x, z] = new_internal
        if not final and x == 0:
            edges[0][z] = new_free
        if not final and x == nx - 1:
            edges[1][z] = new_free

    for x in range(nx):
        for z in range(nz):
            cell(x, z)


def substep(fields, low, high, diffusivity, binding, source, final):
    nx, nz, members, ny = fields[0].shape
    whole = jax.ShapeDtypeStruct((nx, nz, members, ny), f32)
    plane = jax.ShapeDtypeStruct((nz, members, ny), f32)
    cells = nx * nz * members * ny
    return pl.pallas_call(
        functools.partial(substep_kernel, final=final),
        out_shape=[whole] * 4 + ([] if final else [plane] * 2),
        in_specs=[VMEM] * 9,
        out_specs=[VMEM] * (4 if final else 6),
        compiler_params=pltpu.CompilerParams(vmem_limit_bytes=48 * 2**20),
        cost_estimate=pl.CostEstimate(
            flops=30 * cells, bytes_accessed=32 * cells, transcendentals=0
        ),
        name="substep",
    )(*fields, low, high, diffusivity, binding, source)


def weights_kernel(place, owner, obs_index, observed, obs_var, omega, eta):
    count, rows, ny = omega.shape
    batch_size = obs_index.shape[1]
    for k in range(count):
        batch = place[0] * count + k
        mine = owner[batch] == place[1]
        line = pl.ds(batch, 1)
        voxel = obs_index[line, :]
        scale = jnp.where(mine, 1.0, 0.0) / obs_var[line, :]
        shift = ny.bit_length() - 1
        row = lax.shift_right_logical(voxel, shift)
        column = jnp.bitwise_and(voxel, ny - 1)
        at_row = lax.broadcasted_iota(jnp.int32, (rows, batch_size), 0) == row
        at_column = lax.broadcasted_iota(jnp.int32, (ny, batch_size), 0) == column
        both = jnp.concatenate(
            [jnp.where(at_row, scale, 0.0), jnp.where(at_row, scale * observed[line, :], 0.0)],
            axis=0,
        )
        one = both.astype(bf16)
        rest = both - one.astype(f32)
        two = rest.astype(bf16)
        three = (rest - two.astype(f32)).astype(bf16)
        columns = jnp.where(at_column, 1.0, 0.0).astype(bf16)
        sums = lax.dot_general(
            jnp.concatenate([one, two, three], axis=0),
            columns,
            (NT, ((), ())),
            preferred_element_type=f32,
        )
        sums = sums[: 2 * rows] + sums[2 * rows : 4 * rows] + sums[4 * rows :]
        omega[k] = sums[:rows]
        eta[k] = sums[rows:]


def voxel_weights(place, owner, obs_index, observed, obs_var, count, rows, ny):
    out = jax.ShapeDtypeStruct((count, rows, ny), f32)
    return pl.pallas_call(
        weights_kernel,
        out_shape=[out, out],
        in_specs=[SMEM, SMEM, VMEM, VMEM, VMEM],
        out_specs=[VMEM, VMEM],
        compiler_params=pltpu.CompilerParams(vmem_limit_bytes=32 * 2**20),
        name="voxel_weights",
    )(place, owner, obs_index, observed, obs_var)


def gram_kernel(place, owner, omega, eta, *refs, offsets):
    *sources, out, members_at = refs
    count = out.shape[0]
    nx, nz, rows, ny = sources[0].shape
    members = members_at.shape[0]
    for k in range(count):
        out[k] = jnp.zeros(out.shape[1:], f32)

        @pl.when(owner[place[0] * count + k] == place[1])
        def _(k=k):
            def tile(t, total):
                x, z = t // nz, t % nz
                for j, source in enumerate(sources):
                    start = pl.multiple_of(offsets(place[2], j), 8)
                    members_at[pl.ds(start, rows), :] = source[x, z]
                values = members_at[...]
                mean = jnp.sum(values, axis=0, keepdims=True) * (1.0 / members)
                spread = values - mean
                weight = omega[k, pl.ds(t, 1), :]
                shift = eta[k, pl.ds(t, 1), :] - weight * mean
                tail = lax.broadcasted_iota(jnp.int32, (LANES - members, ny), 0)
                weighted = jnp.concatenate(
                    [spread * weight, jnp.where(tail == 0, shift, 0.0)], axis=0
                )
                return total + dot_parts(split(spread), split(weighted), NT)

            out[k] = lax.fori_loop(0, nx * nz, tile, jnp.zeros(out.shape[1:], f32), unroll=4)


def gram(place, owner, omega, eta, sources, offsets):
    nx, nz, rows, ny = sources[0].shape
    members = rows * len(sources)
    count = omega.shape[0]
    return pl.pallas_call(
        functools.partial(gram_kernel, offsets=offsets),
        out_shape=jax.ShapeDtypeStruct((count, members, LANES), f32),
        in_specs=[SMEM, SMEM, VMEM, VMEM] + [VMEM] * len(sources),
        out_specs=VMEM,
        scratch_shapes=[pltpu.VMEM((members, ny), f32)],
        compiler_params=pltpu.CompilerParams(vmem_limit_bytes=32 * 2**20),
        name="gram",
    )(place, owner, omega, eta, *sources)


def batch_transform(extended, total, members):
    side = extended.shape[0]
    row = lax.broadcasted_iota(jnp.int32, (side, side), 0)
    column = lax.broadcasted_iota(jnp.int32, (side, side), 1)
    in_column = column < members
    inside = in_column & (row < members)
    last = column == members
    identity = jnp.where((row == column) & inside, 1.0, 0.0)
    matrix = jnp.where(in_column, extended, 0.0)

    mean = jnp.sum(total, axis=1, keepdims=True) * (1.0 / members)
    centred = jnp.where(in_column, total - mean, 0.0)
    product = square_dot(wide_left(matrix), wide_right(jnp.where(last, mean, centred)))
    product = jnp.where(last, extended - product, product)
    product = square_dot(wide_left(centred.T), wide_right(product)) * (1.0 / (members - 1))
    innovation = jnp.sum(jnp.where(last, product, 0.0), axis=1, keepdims=True)
    system = identity + jnp.where(in_column, product, 0.0)
    frobenius = jnp.sqrt(jnp.sum(jnp.sum(system * system, axis=1, keepdims=True), axis=0, keepdims=True))

    scaled_root = system / frobenius
    factor = 1.5 * identity - 0.5 * scaled_root
    scaled_root = square_dot(wide_left(scaled_root), wide_right(factor))
    inverse_root = factor

    def newton(iteration, iterates):
        scaled_root, inverse_root = iterates
        factor = 1.5 * identity - 0.5 * square_dot(
            wide_left(inverse_root), wide_right(scaled_root)
        )
        return (
            square_dot(wide_left(scaled_root), wide_right(factor)),
            square_dot(wide_left(factor), wide_right(inverse_root)),
        )

    scaled_root, inverse_root = lax.fori_loop(1, NEWTON, newton, (scaled_root, inverse_root))
    root_inv = inverse_root / jnp.sqrt(frobenius)
    mean_weight = jnp.sum(root_inv * innovation, axis=0, keepdims=True)
    mean_weight = jnp.sum(root_inv * mean_weight, axis=1, keepdims=True)
    mixing = jnp.where(inside, root_inv + mean_weight, 0.0)
    mixing = mixing - jnp.sum(mixing, axis=0, keepdims=True) * (1.0 / members)
    mixing = jnp.where(inside, mixing + 1.0 / members, 0.0)
    return square_dot(wide_left(total), wide_right(mixing))


def transform_kernel(place, mine, other, out, ordered, work, *, offsets, blocks, rows):
    count, members = mine.shape[0], mine.shape[1]
    half = place[0]
    for k in range(count):
        ordered[half * count + k] = mine[k]
        ordered[(1 - half) * count + k] = other[k]
    row = lax.broadcasted_iota(jnp.int32, (LANES, LANES), 0)
    column = lax.broadcasted_iota(jnp.int32, (LANES, LANES), 1)
    total = jnp.where((row == column) & (row < members), 1.0, 0.0)
    for batch in range(2 * count):
        extended = jnp.concatenate(
            [ordered[batch], jnp.zeros((LANES - members, LANES), f32)], axis=0
        )
        total = batch_transform(extended, total, members)
    work[...] = total
    if blocks == 1:
        out[...] = total.T
        return
    parts = [
        work[pl.ds(pl.multiple_of(offsets(place[2], j), 8), rows), :] for j in range(blocks)
    ]
    parts.append(jnp.zeros((LANES - members, LANES), f32))
    work[...] = jnp.concatenate(parts, axis=0).T
    out[...] = work[pl.ds(pl.multiple_of(offsets(place[2], 0), 8), rows), :]


def transforms(place, mine, other, offsets, blocks, rows):
    count, members, _ = mine.shape
    shape = (LANES, LANES) if blocks == 1 else (rows, LANES)
    return pl.pallas_call(
        functools.partial(transform_kernel, offsets=offsets, blocks=blocks, rows=rows),
        out_shape=jax.ShapeDtypeStruct(shape, f32),
        in_specs=[SMEM, VMEM, VMEM],
        out_specs=VMEM,
        scratch_shapes=[
            pltpu.VMEM((2 * count, members, LANES), f32),
            pltpu.VMEM((LANES, LANES), f32),
        ],
        compiler_params=pltpu.CompilerParams(vmem_limit_bytes=32 * 2**20),
        cost_estimate=pl.CostEstimate(
            flops=10**10, bytes_accessed=10**6, transcendentals=0
        ),
        name="transforms",
    )(place, mine, other)


def mix_kernel(weights, *refs, blocks):
    *sources, out = refs
    rows, species, _, nz, ny = out.shape
    members = blocks * sources[0].shape[2]
    high, low = split(weights[:, :members])
    both = jnp.concatenate([high.astype(f32), low.astype(f32)], axis=0).astype(bf16)
    mul = functools.partial(
        lax.dot_general, dimension_numbers=(NN, ((), ())), preferred_element_type=f32
    )
    for z in range(nz):
        mixed = []
        for kind in range(species):
            parts = [sources[kind * blocks + j][0, z] for j in range(blocks)]
            values = parts[0] if blocks == 1 else jnp.concatenate(parts, axis=0)
            value_high, value_low = split(values)
            upper = mul(both, value_high)
            mixed.append(upper[:rows] + (upper[rows:] + mul(high, value_low)))
        mixed[2] = mixed[2] - mixed[3]
        for kind in range(species):
            out[:, kind, 0, z, :] = mixed[kind]


def mix(weights, sources, blocks, rows):
    nx, nz, held, ny = sources[0].shape
    species = len(sources) // blocks
    block = pl.BlockSpec((1, nz, held, ny), lambda x: (x, 0, 0, 0))
    return pl.pallas_call(
        functools.partial(mix_kernel, blocks=blocks),
        grid=(nx,),
        out_shape=jax.ShapeDtypeStruct((rows, species, nx, nz, ny), f32),
        in_specs=[pl.BlockSpec(weights.shape, lambda x: (0, 0))] + [block] * len(sources),
        out_specs=pl.BlockSpec((rows, species, 1, nz, ny), lambda x: (0, 0, x, 0, 0)),
        compiler_params=pltpu.CompilerParams(vmem_limit_bytes=32 * 2**20),
        name="mix",
    )(weights, *sources)


def swap(x, axis, bit):
    count = lax.axis_size(axis)
    return lax.ppermute(x, axis, [(k, k ^ bit) for k in range(count)])


def local(ensemble, diffusivity, binding, source, obs_index, owner, observed, obs_var):
    rows, species, nx, nz, ny = ensemble.shape
    devices = lax.axis_size("member")
    spaces = lax.axis_size("space")
    members = rows * devices
    batches = owner.shape[0]
    member = lax.axis_index("member")
    place = jnp.stack([member & 1, lax.axis_index("space"), member]).astype(jnp.int32)

    forward = [(k, k + 1) for k in range(spaces - 1)]
    backward = [(k + 1, k) for k in range(spaces - 1)]
    fields = [jnp.transpose(ensemble[:, k], (1, 2, 0, 3)) for k in range(species)]
    first, last = fields[0][0], fields[0][-1]
    omega, eta = voxel_weights(
        place, owner, obs_index, observed, obs_var, batches // 2, nx * nz, ny
    )
    for step in range(SUBSTEPS):
        low = lax.ppermute(last, "space", forward)
        high = lax.ppermute(first, "space", backward)
        final = step == SUBSTEPS - 1
        *fields, = substep(fields, low, high, diffusivity, binding, source, final)
        if not final:
            first, last = fields[4:]
            fields = fields[:4]
    free, receptor, tracer, internal = fields

    if devices == 4 and rows % 8 == 0:
        blocks = devices

        def offsets(position, j):
            return jnp.bitwise_xor(position, j) * rows

        def collect(x):
            across = swap(x, "member", 2)
            return [x, swap(x, "member", 1), across, swap(across, "member", 1)]
    else:
        blocks = 1

        def offsets(position, j):
            return 0

        def collect(x):
            return [lax.all_gather(x, "member", axis=2, tiled=True)]

    tracers = collect(tracer)
    half = gram(place, owner, omega, eta, tracers, offsets)
    half = jnp.sum(lax.all_gather(half, "space", axis=0), axis=0)
    weights = transforms(place, half, swap(half, "member", 1), offsets, blocks, rows)
    if blocks == 1:
        weights = lax.dynamic_slice(weights, (member * rows, 0), (rows, LANES))
    sources = collect(free) + collect(receptor) + tracers + collect(internal)
    return mix(weights, sources, blocks, rows)


def solution(mesh):
    in_specs = (
        P("member", None, "space", None, None),
        P("space", None, None),
        P("space", None, None),
        P("space", None, None),
        P(),
        P(),
        P(),
        P(),
    )
    out_specs = P("member", None, "space", None, None)
    return jax.shard_map(local, mesh=mesh, in_specs=in_specs, out_specs=out_specs, check_vma=False)
```

```python
import functools

import jax
import jax.numpy as jnp
from jax import lax
from jax.experimental import pallas as pl
from jax.experimental.pallas import tpu as pltpu
from jax.sharding import PartitionSpec as P

SUBSTEPS = 6
NEWTON = 16
LANES = 128
SCOPED = 8 * 2**20

unbind_rate = 0.05
uptake_rate = 0.1
recycle_rate = 0.02

VMEM = pl.BlockSpec(memory_space=pltpu.VMEM)
SMEM = pl.BlockSpec(memory_space=pltpu.SMEM)
bf16 = jnp.bfloat16
f32 = jnp.float32


def split(x):
    high = x.astype(bf16)
    return high, (x - high.astype(f32)).astype(bf16)


def dot_parts(a, b, dims):
    a_high, a_low = a
    b_high, b_low = b
    mul = functools.partial(
        lax.dot_general, dimension_numbers=(dims, ((), ())), preferred_element_type=f32
    )
    return mul(a_high, b_high) + (mul(a_high, b_low) + mul(a_low, b_high))


def wide_left(x):
    return jnp.concatenate(split(x), axis=1)


def wide_right(x):
    both = jnp.concatenate(split(x), axis=1)
    return jnp.concatenate([both, both], axis=0)


def square_dot(left, right):
    out = jnp.dot(left, right, preferred_element_type=f32)
    side = out.shape[0]
    return out[:, :side] + out[:, side:]


NN = ((1,), (0,))
NT = ((1,), (1,))


def neighbour_sum(a, low, high, x, z, at_left, at_right):
    nx, nz, members, ny = a.shape
    free = a[x, z]
    total = (low[z] if x == 0 else a[x - 1, z]) + (high[z] if x == nx - 1 else a[x + 1, z])
    if z + 1 < nz:
        total += a[x, z + 1]
    if z > 0:
        total += a[x, z - 1]
    total += jnp.where(at_right, 0.0, pltpu.roll(free, ny - 1, 1))
    return total + jnp.where(at_left, 0.0, pltpu.roll(free, 1, 1))


def ends(a):
    _, _, members, ny = a.shape
    lane = lax.broadcasted_iota(jnp.int32, (members, ny), 1)
    return lane == 0, lane == ny - 1


def free_part(a, low, high, diffusivity, x, z, at):
    free = a[x, z]
    neighbours = neighbour_sum(a, low, high, x, z, *at)
    return free + diffusivity[x, pl.ds(z, 1), :] * (neighbours - 6.0 * free)


def react(free, receptor, complexed, internal, binding):
    flux = binding * free * receptor
    back = unbind_rate * complexed - flux
    return (
        back,
        receptor + back + recycle_rate * internal,
        complexed + flux - (unbind_rate + uptake_rate) * complexed,
        internal + uptake_rate * complexed - recycle_rate * internal,
    )


def edges_kernel(a, r, c, low, high, diffusivity, binding, source, first, last):
    nx, nz, _, _ = a.shape
    at = ends(a)
    for x, out in ((0, first), (nx - 1, last)):
        for z in range(nz):
            row = pl.ds(z, 1)
            flux = binding[x, row, :] * a[x, z] * r[x, z]
            out[z] = (
                free_part(a, low, high, diffusivity, x, z, at)
                + (unbind_rate * c[x, z] - flux)
                + source[x, row, :]
            )


def substep_kernel(
    a, r, c, i, low, high, diffusivity, binding, source, out_a, out_r, out_c, out_i
):
    nx, nz, _, _ = a.shape
    at = ends(a)
    for x in range(nx):
        for z in range(nz):
            row = pl.ds(z, 1)
            back, out_r[x, z], out_c[x, z], out_i[x, z] = react(
                a[x, z], r[x, z], c[x, z], i[x, z], binding[x, row, :]
            )
            out_a[x, z] = (
                free_part(a, low, high, diffusivity, x, z, at) + back + source[x, row, :]
            )


def last_but_one_kernel(
    a, r, c, i, low, high, diffusivity, binding, source, out_a, out_add, out_tracer, out_i
):
    nx, nz, _, _ = a.shape
    at = ends(a)
    for x in range(nx):
        for z in range(nz):
            row = pl.ds(z, 1)
            bind = binding[x, row, :]
            back, receptor, complexed, internal = react(
                a[x, z], r[x, z], c[x, z], i[x, z], bind
            )
            free = free_part(a, low, high, diffusivity, x, z, at) + back + source[x, row, :]
            back, _, complexed, internal = react(free, receptor, complexed, internal, bind)
            out_a[x, z] = free
            out_add[x, z] = back + source[x, row, :]
            out_tracer[x, z] = complexed + internal
            out_i[x, z] = internal


def last_free_kernel(a, add, low, high, diffusivity, out_a):
    nx, nz, _, _ = a.shape
    at = ends(a)
    for x in range(nx):
        for z in range(nz):
            out_a[x, z] = free_part(a, low, high, diffusivity, x, z, at) + add[x, z]


def forecast_call(kernel, inputs, outputs, share=1.0, ready=()):
    nx, nz, members, ny = inputs[0].shape
    cells = int(nx * nz * members * ny * share)

    def body(*refs):
        kernel(*refs[: len(inputs)], *refs[len(inputs) + len(ready) :])

    return pl.pallas_call(
        body,
        out_shape=[jax.ShapeDtypeStruct(shape, f32) for shape in outputs],
        in_specs=[VMEM] * len(inputs) + [pl.BlockSpec(memory_space=pl.ANY)] * len(ready),
        out_specs=[VMEM] * len(outputs),
        compiler_params=pltpu.CompilerParams(vmem_limit_bytes=SCOPED),
        cost_estimate=pl.CostEstimate(
            flops=30 * cells, bytes_accessed=32 * cells, transcendentals=0
        ),
        name=kernel.__name__.removesuffix("_kernel"),
    )(*inputs, *ready)


def weights_kernel(place, owner, obs_index, observed, obs_var, omega, eta):
    count, rows, ny = omega.shape
    batch_size = obs_index.shape[1]
    for k in range(count):
        batch = place[0] * count + k
        mine = owner[batch] == place[1]
        line = pl.ds(batch, 1)
        voxel = obs_index[line, :]
        scale = jnp.where(mine, 1.0, 0.0) / obs_var[line, :]
        shift = ny.bit_length() - 1
        row = lax.shift_right_logical(voxel, shift)
        column = jnp.bitwise_and(voxel, ny - 1)
        at_row = lax.broadcasted_iota(jnp.int32, (rows, batch_size), 0) == row
        at_column = lax.broadcasted_iota(jnp.int32, (ny, batch_size), 0) == column
        both = jnp.concatenate(
            [jnp.where(at_row, scale, 0.0), jnp.where(at_row, scale * observed[line, :], 0.0)],
            axis=0,
        )
        one = both.astype(bf16)
        rest = both - one.astype(f32)
        two = rest.astype(bf16)
        three = (rest - two.astype(f32)).astype(bf16)
        columns = jnp.where(at_column, 1.0, 0.0).astype(bf16)
        sums = lax.dot_general(
            jnp.concatenate([one, two, three], axis=0),
            columns,
            (NT, ((), ())),
            preferred_element_type=f32,
        )
        sums = sums[: 2 * rows] + sums[2 * rows : 4 * rows] + sums[4 * rows :]
        omega[k] = sums[:rows]
        eta[k] = sums[rows:]


def voxel_weights(place, owner, obs_index, observed, obs_var, count, rows, ny):
    out = jax.ShapeDtypeStruct((count, rows, ny), f32)
    return pl.pallas_call(
        weights_kernel,
        out_shape=[out, out],
        in_specs=[SMEM, SMEM, VMEM, VMEM, VMEM],
        out_specs=[VMEM, VMEM],
        compiler_params=pltpu.CompilerParams(vmem_limit_bytes=SCOPED),
        name="voxel_weights",
    )(place, owner, obs_index, observed, obs_var)


def gram_kernel(place, owner, omega, eta, *refs, offsets):
    *sources, packed, out, members_at = refs
    count = out.shape[0]
    nx, nz, rows, ny = sources[0].shape
    members = members_at.shape[0]
    for k in range(count):
        out[k] = jnp.zeros(out.shape[1:], f32)

        @pl.when(owner[place[0] * count + k] == place[1])
        def _(k=k):
            def tile(t, total):
                x, z = t // nz, t % nz
                for j, source in enumerate(sources):
                    start = pl.multiple_of(offsets(place[2], j), 8)
                    members_at[pl.ds(start, rows), :] = source[x, z]
                values = members_at[...]
                mean = jnp.sum(values, axis=0, keepdims=True) * (1.0 / members)
                spread = values - mean
                weight = omega[k, pl.ds(t, 1), :]
                shift = eta[k, pl.ds(t, 1), :] - weight * mean
                tail = lax.broadcasted_iota(jnp.int32, (LANES - members, ny), 0)
                weighted = jnp.concatenate(
                    [spread * weight, jnp.where(tail == 0, shift, 0.0)], axis=0
                )
                return total + dot_parts(split(spread), split(weighted), NT)

            out[k] = lax.fori_loop(0, nx * nz, tile, jnp.zeros(out.shape[1:], f32), unroll=4)

    row = lax.broadcasted_iota(jnp.int32, (members, LANES), 0)
    column = lax.broadcasted_iota(jnp.int32, (members, LANES), 1)
    above, below = out[0], out[1]

    def pick(where, x):
        return jnp.sum(jnp.where(where, x, 0.0), axis=1, keepdims=True)

    both = jnp.where(column >= row, above, below)
    both = jnp.where(column == members, pick(column == row, below), both)
    both = jnp.where(column == members + 1, pick(column == members, above), both)
    packed[...] = jnp.where(column == members + 2, pick(column == members, below), both)


def gram(place, owner, omega, eta, sources, offsets):
    nx, nz, rows, ny = sources[0].shape
    members = rows * len(sources)
    count = omega.shape[0]
    return pl.pallas_call(
        functools.partial(gram_kernel, offsets=offsets),
        out_shape=jax.ShapeDtypeStruct((members, LANES), f32),
        in_specs=[SMEM, SMEM, VMEM, VMEM] + [VMEM] * len(sources),
        out_specs=VMEM,
        scratch_shapes=[pltpu.VMEM((count, members, LANES), f32), pltpu.VMEM((members, ny), f32)],
        compiler_params=pltpu.CompilerParams(vmem_limit_bytes=SCOPED),
        name="gram",
    )(place, owner, omega, eta, *sources)


def batch_transform(extended, total, members):
    side = extended.shape[0]
    row = lax.broadcasted_iota(jnp.int32, (side, side), 0)
    column = lax.broadcasted_iota(jnp.int32, (side, side), 1)
    in_column = column < members
    inside = in_column & (row < members)
    last = column == members
    identity = jnp.where((row == column) & inside, 1.0, 0.0)
    matrix = jnp.where(in_column, extended, 0.0)

    mean = jnp.sum(total, axis=1, keepdims=True) * (1.0 / members)
    centred = jnp.where(in_column, total - mean, 0.0)
    product = square_dot(wide_left(matrix), wide_right(jnp.where(last, mean, centred)))
    product = jnp.where(last, extended - product, product)
    product = square_dot(wide_left(centred.T), wide_right(product)) * (1.0 / (members - 1))
    innovation = jnp.sum(jnp.where(last, product, 0.0), axis=1, keepdims=True)
    system = identity + jnp.where(in_column, product, 0.0)
    frobenius = jnp.sqrt(jnp.sum(jnp.sum(system * system, axis=1, keepdims=True), axis=0, keepdims=True))

    scaled_root = system / frobenius
    factor = 1.5 * identity - 0.5 * scaled_root
    scaled_root = square_dot(wide_left(scaled_root), wide_right(factor))
    inverse_root = factor

    def newton(iteration, iterates):
        scaled_root, inverse_root = iterates
        factor = 1.5 * identity - 0.5 * square_dot(
            wide_left(inverse_root), wide_right(scaled_root)
        )
        return (
            square_dot(wide_left(scaled_root), wide_right(factor)),
            square_dot(wide_left(factor), wide_right(inverse_root)),
        )

    scaled_root, inverse_root = lax.fori_loop(1, NEWTON, newton, (scaled_root, inverse_root))
    root_inv = inverse_root / jnp.sqrt(frobenius)
    mean_weight = jnp.sum(root_inv * innovation, axis=0, keepdims=True)
    mean_weight = jnp.sum(root_inv * mean_weight, axis=1, keepdims=True)
    mixing = jnp.where(inside, root_inv + mean_weight, 0.0)
    mixing = mixing - jnp.sum(mixing, axis=0, keepdims=True) * (1.0 / members)
    mixing = jnp.where(inside, mixing + 1.0 / members, 0.0)
    return square_dot(wide_left(total), wide_right(mixing))


def transform_kernel(place, mine, other, out, ordered, work, *, offsets, blocks, rows):
    members = mine.shape[0]
    row = lax.broadcasted_iota(jnp.int32, (LANES, LANES), 0)
    column = lax.broadcasted_iota(jnp.int32, (LANES, LANES), 1)
    rest = jnp.zeros((LANES - members, LANES), f32)

    def pick(where, x):
        return jnp.sum(jnp.where(where, x, 0.0), axis=1, keepdims=True)

    for half, shared in ((place[0], mine), (1 - place[0], other)):
        packed = jnp.concatenate([shared[...], rest], axis=0)
        inside = column < members
        above = jnp.where(inside & (column > row), packed, 0.0)
        below = jnp.where(inside & (column < row), packed, 0.0)
        middle = jnp.where(inside & (column == row), packed, 0.0)
        side = jnp.where(column == members, pick(column == members + 1, packed), 0.0)
        ordered[2 * half] = above + above.T + (middle + side)
        middle = jnp.where(inside & (column == row), pick(column == members, packed), 0.0)
        side = jnp.where(column == members, pick(column == members + 2, packed), 0.0)
        ordered[2 * half + 1] = below + below.T + (middle + side)
    total = jnp.where((row == column) & (row < members), 1.0, 0.0)
    for batch in range(ordered.shape[0]):
        total = batch_transform(ordered[batch], total, members)
    work[...] = total
    if blocks == 1:
        out[...] = total.T
        return
    parts = [
        work[pl.ds(pl.multiple_of(offsets(place[2], j), 8), rows), :] for j in range(blocks)
    ]
    parts.append(jnp.zeros((LANES - members, LANES), f32))
    work[...] = jnp.concatenate(parts, axis=0).T
    out[...] = work[pl.ds(pl.multiple_of(offsets(place[2], 0), 8), rows), :]


def transforms(place, mine, other, offsets, blocks, rows):
    members = mine.shape[0]
    shape = (LANES, LANES) if blocks == 1 else (rows, LANES)
    return pl.pallas_call(
        functools.partial(transform_kernel, offsets=offsets, blocks=blocks, rows=rows),
        out_shape=jax.ShapeDtypeStruct(shape, f32),
        in_specs=[SMEM, VMEM, VMEM],
        out_specs=VMEM,
        scratch_shapes=[
            pltpu.VMEM((4, LANES, LANES), f32),
            pltpu.VMEM((LANES, LANES), f32),
        ],
        compiler_params=pltpu.CompilerParams(vmem_limit_bytes=SCOPED),
        cost_estimate=pl.CostEstimate(
            flops=10**10, bytes_accessed=10**6, transcendentals=0
        ),
        name="transforms",
    )(place, mine, other)


def mix_kernel(weights, *refs, blocks):
    *sources, out = refs
    rows, species, _, nz, ny = out.shape
    x = pl.program_id(0)
    members = blocks * sources[0].shape[2]
    high, low = split(weights[:, :members])
    both = jnp.concatenate([high.astype(f32), low.astype(f32)], axis=0).astype(bf16)
    mul = functools.partial(
        lax.dot_general, dimension_numbers=(NN, ((), ())), preferred_element_type=f32
    )
    for z in range(nz):
        mixed = []
        for kind in range(species):
            parts = [sources[kind * blocks + j][x, z] for j in range(blocks)]
            values = parts[0] if blocks == 1 else jnp.concatenate(parts, axis=0)
            value_high, value_low = split(values)
            upper = mul(both, value_high)
            mixed.append(upper[:rows] + (upper[rows:] + mul(high, value_low)))
        mixed[1] = mixed[1] - mixed[2]
        mixed[2] = mixed[2] - mixed[3]
        for kind in range(species):
            out[:, kind, 0, z, :] = mixed[kind]


def mix(weights, sources, blocks, rows):
    nx, nz, held, ny = sources[0].shape
    species = len(sources) // blocks
    return pl.pallas_call(
        functools.partial(mix_kernel, blocks=blocks),
        grid=(nx,),
        out_shape=jax.ShapeDtypeStruct((rows, species, nx, nz, ny), f32),
        in_specs=[VMEM] * (1 + len(sources)),
        out_specs=pl.BlockSpec((rows, species, 1, nz, ny), lambda x: (0, 0, x, 0, 0)),
        compiler_params=pltpu.CompilerParams(vmem_limit_bytes=SCOPED),
        name="mix",
    )(weights, *sources)


def swap(x, axis, bit):
    count = lax.axis_size(axis)
    return lax.ppermute(x, axis, [(k, k ^ bit) for k in range(count)])


def total_over(x, axis):
    bit = 1
    while bit < lax.axis_size(axis):
        x = x + swap(x, axis, bit)
        bit *= 2
    return x


def local(ensemble, diffusivity, binding, source, obs_index, owner, observed, obs_var):
    rows, species, nx, nz, ny = ensemble.shape
    devices = lax.axis_size("member")
    spaces = lax.axis_size("space")
    members = rows * devices
    batches = owner.shape[0]
    member = lax.axis_index("member")
    place = jnp.stack([member & 1, lax.axis_index("space"), member]).astype(jnp.int32)

    forward = [(k, k + 1) for k in range(spaces - 1)]
    backward = [(k + 1, k) for k in range(spaces - 1)]

    def halos(first, last):
        return lax.ppermute(last, "space", forward), lax.ppermute(first, "space", backward)

    if devices == 4 and rows % 8 == 0:
        blocks = devices

        def offsets(position, j):
            return jnp.bitwise_xor(position, j) * rows

        def collect(x):
            return [x, swap(x, "member", 1), swap(x, "member", 2)]

        def complete(held, *after):
            return [*held, swap(lax.optimization_barrier((held[2], *after))[0], "member", 1)]
    else:
        blocks = 1

        def offsets(position, j):
            return 0

        def collect(x):
            return [lax.all_gather(x, "member", axis=2, tiled=True)]

        def complete(held, *after):
            return held

    whole, plane = (nx, nz, rows, ny), (nz, rows, ny)
    coefficients = (diffusivity, binding, source)
    around = halos(
        jnp.transpose(ensemble[:, 0, 0], (1, 0, 2)), jnp.transpose(ensemble[:, 0, -1], (1, 0, 2))
    )
    fields = [jnp.transpose(ensemble[:, k], (1, 2, 0, 3)) for k in range(species)]
    conserved = fields[1] + fields[2] + fields[3]
    omega, eta = voxel_weights(
        place, owner, obs_index, observed, obs_var, batches // 2, nx * nz, ny
    )
    for step in range(SUBSTEPS - 2):
        if step == 1:
            conserved = collect(lax.optimization_barrier((conserved, fields[0]))[0])
            ready = (omega, eta)
        elif step == 3:
            ready = conserved[1:]
        else:
            ready = ()
        next_edges = forecast_call(
            edges_kernel, [*fields[:3], *around, *coefficients], [plane] * 2, 2 / nx
        )
        fields_now, around_now = fields, around
        around = halos(*next_edges)
        fields = forecast_call(
            substep_kernel,
            [*fields_now, *around_now, *coefficients],
            [whole] * 4,
            ready=ready,
        )
    conserved = complete(conserved, fields[0])
    free, add, tracer, internal = forecast_call(
        last_but_one_kernel, [*fields, *around, *coefficients], [whole] * 4
    )
    around = halos(free[0], free[-1])
    (free,) = forecast_call(last_free_kernel, [free, add, *around, diffusivity], [whole])

    tracer = complete(collect(tracer))
    internal = collect(internal)
    free = collect(free)
    half = total_over(gram(place, owner, omega, eta, tracer, offsets), "space")
    weights = transforms(place, half, swap(half, "member", 1), offsets, blocks, rows)
    internal = complete(internal, weights)
    free = complete(free, weights)
    if blocks == 1:
        weights = lax.dynamic_slice(weights, (member * rows, 0), (rows, LANES))
    return mix(weights, free + conserved + tracer + internal, blocks, rows)


def solution(mesh):
    in_specs = (
        P("member", None, "space", None, None),
        P("space", None, None),
        P("space", None, None),
        P("space", None, None),
        P(),
        P(),
        P(),
        P(),
    )
    out_specs = P("member", None, "space", None, None)
    return jax.shard_map(local, mesh=mesh, in_specs=in_specs, out_specs=out_specs, check_vma=False)
```

```python
import functools

import jax
import jax.numpy as jnp
from jax import lax
from jax.experimental import pallas as pl
from jax.experimental.pallas import tpu as pltpu
from jax.sharding import PartitionSpec as P

SUBSTEPS = 6
NEWTON = 16
LANES = 128
SCOPED = 10 * 2**20

unbind_rate = 0.05
uptake_rate = 0.1
recycle_rate = 0.02

VMEM = pl.BlockSpec(memory_space=pltpu.VMEM)
SMEM = pl.BlockSpec(memory_space=pltpu.SMEM)
bf16 = jnp.bfloat16
f32 = jnp.float32


def split(x):
    high = x.astype(bf16)
    return high, (x - high.astype(f32)).astype(bf16)


def dot_parts(a, b, dims):
    a_high, a_low = a
    b_high, b_low = b
    mul = functools.partial(
        lax.dot_general, dimension_numbers=(dims, ((), ())), preferred_element_type=f32
    )
    return mul(a_high, b_high) + (mul(a_high, b_low) + mul(a_low, b_high))


def wide_left(x):
    return jnp.concatenate(split(x), axis=1)


def wide_right(x):
    both = jnp.concatenate(split(x), axis=1)
    return jnp.concatenate([both, both], axis=0)


def square_dot(left, right):
    out = jnp.dot(left, right, preferred_element_type=f32)
    side = out.shape[0]
    return out[:, :side] + out[:, side:]


NN = ((1,), (0,))
NT = ((1,), (1,))


def react(free, receptor, complexed, internal, binding):
    flux = binding * free * receptor
    back = unbind_rate * complexed - flux
    return (
        back,
        receptor + back + recycle_rate * internal,
        complexed + flux - (unbind_rate + uptake_rate) * complexed,
        internal + uptake_rate * complexed - recycle_rate * internal,
    )


def spread_free(free, planes, neighbours, diffusivity):
    lane = lax.broadcasted_iota(jnp.int32, free.shape, 1)
    last = free.shape[1] - 1
    for plane in planes:
        neighbours = plane if neighbours is None else neighbours + plane
    neighbours += jnp.where(lane == last, 0.0, pltpu.roll(free, last, 1))
    neighbours += jnp.where(lane == 0, 0.0, pltpu.roll(free, 1, 1))
    return free + diffusivity * (neighbours - 6.0 * free)


def beside(read, x, z, nx, nz, low, high):
    around = [low if x == 0 else read(x - 1, z), high if x == nx - 1 else read(x + 1, z)]
    around += [read(x, other) for other in (z + 1, z - 1) if 0 <= other < nz]
    return [value for value in around if value is not None]


def edge_free(read, rest, x, nz, nx, z, diffusivity):
    return spread_free(read(x, z), beside(read, x, z, nx, nz, None, None), None, diffusivity) + rest


def first_edges_kernel(below, above, diffusivity, binding, source, first, last):
    _, _, nz, members, _ = below.shape
    nx = diffusivity.shape[0]
    for x, ends, out in ((0, below, first), (nx - 1, above, last)):
        shift = 0 if x == 0 else nx - 2

        def read(at, z, ends=ends, shift=shift):
            return ends[0, at - shift, z]

        for z in range(nz):
            row = pl.ds(z, 1)
            free = read(x, z)
            flux = binding[x, row, :] * free * ends[1, x - shift, z]
            rest = unbind_rate * ends[2, x - shift, z] - flux + source[x, row, :]
            spread = diffusivity[x, row, :]
            out[z, :members, :] = free
            out[z, members : 2 * members, :] = edge_free(read, rest, x, nz, nx, z, spread)
            out[z, 2 * members :, :] = jnp.broadcast_to(spread, (8, spread.shape[1]))


def two_substeps_kernel(
    a, r, c, i, low, high, low_first, high_first, diffusivity, binding, source, *refs, final
):
    out_a, out_r, out_c, out_i = refs[:4]
    middle = refs[-1]
    nx, nz, members, _ = a.shape

    def outside(x, z, later):
        part = slice(members, 2 * members) if later else slice(0, members)
        values = []
        for end, halo, origin in ((0, low, low_first), (nx - 1, high, high_first)):
            value = halo[z, part, :] if x == end else None
            if x == end and later:
                value += origin[z, 2 * members : 2 * members + 1, :] * a[x, z]
            values.append(value)
        return values

    for x in range(nx):
        for z in range(nz):
            row = pl.ds(z, 1)
            back, out_r[x, z], out_c[x, z], out_i[x, z] = react(
                a[x, z], r[x, z], c[x, z], i[x, z], binding[x, row, :]
            )
            around = beside(lambda x, z: a[x, z], x, z, nx, nz, *outside(x, z, False))
            middle[x, z] = (
                spread_free(a[x, z], around, None, diffusivity[x, row, :])
                + back
                + source[x, row, :]
            )
    for x in range(nx):
        for z in range(nz):
            row = pl.ds(z, 1)
            back, receptor, complexed, internal = react(
                middle[x, z], out_r[x, z], out_c[x, z], out_i[x, z], binding[x, row, :]
            )
            around = beside(lambda x, z: middle[x, z], x, z, nx, nz, *outside(x, z, True))
            out_a[x, z] = (
                spread_free(middle[x, z], around, None, diffusivity[x, row, :])
                + back
                + source[x, row, :]
            )
            if not final:
                out_r[x, z] = receptor
            out_c[x, z] = complexed + internal if final else complexed
            out_i[x, z] = internal
    if final:
        return
    for x, out in ((0, refs[4]), (nx - 1, refs[5])):
        for z in range(nz):
            row = pl.ds(z, 1)
            free = out_a[x, z]
            flux = binding[x, row, :] * free * out_r[x, z]
            rest = unbind_rate * out_c[x, z] - flux + source[x, row, :]
            out[z, :members, :] = free
            out[z, members:, :] = edge_free(
                lambda x, z: out_a[x, z], rest, x, nz, nx, z, diffusivity[x, row, :]
            )


def forecast_call(kernel, name, inputs, outputs, cells, scratch=(), ready=()):
    def body(*refs):
        kernel(*refs[: len(inputs)], *refs[len(inputs) + len(ready) :])

    return pl.pallas_call(
        body,
        out_shape=[jax.ShapeDtypeStruct(shape, f32) for shape in outputs],
        in_specs=[VMEM] * len(inputs) + [pl.BlockSpec(memory_space=pl.ANY)] * len(ready),
        out_specs=[VMEM] * len(outputs),
        scratch_shapes=[pltpu.VMEM(shape, f32) for shape in scratch],
        compiler_params=pltpu.CompilerParams(vmem_limit_bytes=SCOPED),
        cost_estimate=pl.CostEstimate(
            flops=30 * cells, bytes_accessed=32 * cells, transcendentals=0
        ),
        name=name,
    )(*inputs, *ready)


def weights_kernel(place, owner, obs_index, observed, obs_var, omega, eta):
    count, rows, ny = omega.shape
    batch_size = obs_index.shape[1]
    for k in range(count):
        batch = place[0] * count + k
        mine = owner[batch] == place[1]
        line = pl.ds(batch, 1)
        voxel = obs_index[line, :]
        scale = jnp.where(mine, 1.0, 0.0) / obs_var[line, :]
        shift = ny.bit_length() - 1
        row = lax.shift_right_logical(voxel, shift)
        column = jnp.bitwise_and(voxel, ny - 1)
        at_row = lax.broadcasted_iota(jnp.int32, (rows, batch_size), 0) == row
        at_column = lax.broadcasted_iota(jnp.int32, (ny, batch_size), 0) == column
        both = jnp.concatenate(
            [jnp.where(at_row, scale, 0.0), jnp.where(at_row, scale * observed[line, :], 0.0)],
            axis=0,
        )
        one = both.astype(bf16)
        rest = both - one.astype(f32)
        two = rest.astype(bf16)
        three = (rest - two.astype(f32)).astype(bf16)
        columns = jnp.where(at_column, 1.0, 0.0).astype(bf16)
        sums = lax.dot_general(
            jnp.concatenate([one, two, three], axis=0),
            columns,
            (NT, ((), ())),
            preferred_element_type=f32,
        )
        sums = sums[: 2 * rows] + sums[2 * rows : 4 * rows] + sums[4 * rows :]
        omega[k] = sums[:rows]
        eta[k] = sums[rows:]


def voxel_weights(place, owner, obs_index, observed, obs_var, count, rows, ny):
    out = jax.ShapeDtypeStruct((count, rows, ny), f32)
    return pl.pallas_call(
        weights_kernel,
        out_shape=[out, out],
        in_specs=[SMEM, SMEM, VMEM, VMEM, VMEM],
        out_specs=[VMEM, VMEM],
        compiler_params=pltpu.CompilerParams(vmem_limit_bytes=SCOPED),
        name="voxel_weights",
    )(place, owner, obs_index, observed, obs_var)


def gram_kernel(place, owner, omega, eta, *refs, offsets):
    *sources, packed, out, members_at = refs
    count = out.shape[0]
    nx, nz, rows, ny = sources[0].shape
    members = members_at.shape[0]
    for k in range(count):
        out[k] = jnp.zeros(out.shape[1:], f32)

        @pl.when(owner[place[0] * count + k] == place[1])
        def _(k=k):
            def tile(t, total):
                x, z = t // nz, t % nz
                for j, source in enumerate(sources):
                    start = pl.multiple_of(offsets(place[2], j), 8)
                    members_at[pl.ds(start, rows), :] = source[x, z]
                values = members_at[...]
                mean = jnp.sum(values, axis=0, keepdims=True) * (1.0 / members)
                spread = values - mean
                weight = omega[k, pl.ds(t, 1), :]
                shift = eta[k, pl.ds(t, 1), :] - weight * mean
                tail = lax.broadcasted_iota(jnp.int32, (LANES - members, ny), 0)
                weighted = jnp.concatenate(
                    [spread * weight, jnp.where(tail == 0, shift, 0.0)], axis=0
                )
                return total + dot_parts(split(spread), split(weighted), NT)

            out[k] = lax.fori_loop(0, nx * nz, tile, jnp.zeros(out.shape[1:], f32), unroll=4)

    row = lax.broadcasted_iota(jnp.int32, (members, LANES), 0)
    column = lax.broadcasted_iota(jnp.int32, (members, LANES), 1)
    above, below = out[0], out[1]

    def pick(where, x):
        return jnp.sum(jnp.where(where, x, 0.0), axis=1, keepdims=True)

    both = jnp.where(column >= row, above, below)
    both = jnp.where(column == members, pick(column == row, below), both)
    both = jnp.where(column == members + 1, pick(column == members, above), both)
    packed[...] = jnp.where(column == members + 2, pick(column == members, below), both)


def gram(place, owner, omega, eta, sources, offsets):
    nx, nz, rows, ny = sources[0].shape
    members = rows * len(sources)
    count = omega.shape[0]
    return pl.pallas_call(
        functools.partial(gram_kernel, offsets=offsets),
        out_shape=jax.ShapeDtypeStruct((members, LANES), f32),
        in_specs=[SMEM, SMEM, VMEM, VMEM] + [VMEM] * len(sources),
        out_specs=VMEM,
        scratch_shapes=[pltpu.VMEM((count, members, LANES), f32), pltpu.VMEM((members, ny), f32)],
        compiler_params=pltpu.CompilerParams(vmem_limit_bytes=SCOPED),
        name="gram",
    )(place, owner, omega, eta, *sources)


def batch_transform(extended, total, members):
    side = extended.shape[0]
    row = lax.broadcasted_iota(jnp.int32, (side, side), 0)
    column = lax.broadcasted_iota(jnp.int32, (side, side), 1)
    in_column = column < members
    inside = in_column & (row < members)
    last = column == members
    identity = jnp.where((row == column) & inside, 1.0, 0.0)
    matrix = jnp.where(in_column, extended, 0.0)

    mean = jnp.sum(total, axis=1, keepdims=True) * (1.0 / members)
    centred = jnp.where(in_column, total - mean, 0.0)
    product = square_dot(wide_left(matrix), wide_right(jnp.where(last, mean, centred)))
    product = jnp.where(last, extended - product, product)
    product = square_dot(wide_left(centred.T), wide_right(product)) * (1.0 / (members - 1))
    innovation = jnp.sum(jnp.where(last, product, 0.0), axis=1, keepdims=True)
    system = identity + jnp.where(in_column, product, 0.0)
    frobenius = jnp.sqrt(jnp.sum(jnp.sum(system * system, axis=1, keepdims=True), axis=0, keepdims=True))

    scaled_root = system / frobenius
    factor = 1.5 * identity - 0.5 * scaled_root
    scaled_root = square_dot(wide_left(scaled_root), wide_right(factor))
    inverse_root = factor

    def newton(iteration, iterates):
        scaled_root, inverse_root = iterates
        factor = 1.5 * identity - 0.5 * square_dot(
            wide_left(inverse_root), wide_right(scaled_root)
        )
        return (
            square_dot(wide_left(scaled_root), wide_right(factor)),
            square_dot(wide_left(factor), wide_right(inverse_root)),
        )

    scaled_root, inverse_root = lax.fori_loop(1, NEWTON, newton, (scaled_root, inverse_root))
    root_inv = inverse_root / jnp.sqrt(frobenius)
    mean_weight = jnp.sum(root_inv * innovation, axis=0, keepdims=True)
    mean_weight = jnp.sum(root_inv * mean_weight, axis=1, keepdims=True)
    mixing = jnp.where(inside, root_inv + mean_weight, 0.0)
    mixing = mixing - jnp.sum(mixing, axis=0, keepdims=True) * (1.0 / members)
    mixing = jnp.where(inside, mixing + 1.0 / members, 0.0)
    return square_dot(wide_left(total), wide_right(mixing))


def transform_kernel(place, mine, other, out, ordered, work, *, offsets, blocks, rows):
    members = mine.shape[0]
    row = lax.broadcasted_iota(jnp.int32, (LANES, LANES), 0)
    column = lax.broadcasted_iota(jnp.int32, (LANES, LANES), 1)
    rest = jnp.zeros((LANES - members, LANES), f32)

    def pick(where, x):
        return jnp.sum(jnp.where(where, x, 0.0), axis=1, keepdims=True)

    for half, shared in ((place[0], mine), (1 - place[0], other)):
        packed = jnp.concatenate([shared[...], rest], axis=0)
        inside = column < members
        above = jnp.where(inside & (column > row), packed, 0.0)
        below = jnp.where(inside & (column < row), packed, 0.0)
        middle = jnp.where(inside & (column == row), packed, 0.0)
        side = jnp.where(column == members, pick(column == members + 1, packed), 0.0)
        ordered[2 * half] = above + above.T + (middle + side)
        middle = jnp.where(inside & (column == row), pick(column == members, packed), 0.0)
        side = jnp.where(column == members, pick(column == members + 2, packed), 0.0)
        ordered[2 * half + 1] = below + below.T + (middle + side)
    total = jnp.where((row == column) & (row < members), 1.0, 0.0)
    for batch in range(ordered.shape[0]):
        total = batch_transform(ordered[batch], total, members)
    work[...] = total
    if blocks == 1:
        out[...] = total.T
        return
    parts = [
        work[pl.ds(pl.multiple_of(offsets(place[2], j), 8), rows), :] for j in range(blocks)
    ]
    parts.append(jnp.zeros((LANES - members, LANES), f32))
    work[...] = jnp.concatenate(parts, axis=0).T
    out[...] = work[pl.ds(pl.multiple_of(offsets(place[2], 0), 8), rows), :]


def transforms(place, mine, other, offsets, blocks, rows):
    members = mine.shape[0]
    shape = (LANES, LANES) if blocks == 1 else (rows, LANES)
    return pl.pallas_call(
        functools.partial(transform_kernel, offsets=offsets, blocks=blocks, rows=rows),
        out_shape=jax.ShapeDtypeStruct(shape, f32),
        in_specs=[SMEM, VMEM, VMEM],
        out_specs=VMEM,
        scratch_shapes=[
            pltpu.VMEM((4, LANES, LANES), f32),
            pltpu.VMEM((LANES, LANES), f32),
        ],
        compiler_params=pltpu.CompilerParams(vmem_limit_bytes=SCOPED),
        cost_estimate=pl.CostEstimate(
            flops=10**8, bytes_accessed=10**6, transcendentals=0
        ),
        name="transforms",
    )(place, mine, other)


def mix_kernel(weights, *refs, blocks):
    *sources, out = refs
    rows, species, _, nz, ny = out.shape
    x = pl.program_id(0)
    members = blocks * sources[0].shape[2]
    high, low = split(weights[:, :members])
    both = jnp.concatenate([high.astype(f32), low.astype(f32)], axis=0).astype(bf16)
    mul = functools.partial(
        lax.dot_general, dimension_numbers=(NN, ((), ())), preferred_element_type=f32
    )
    for z in range(nz):
        mixed = []
        for kind in range(species):
            parts = [sources[kind * blocks + j][x, z] for j in range(blocks)]
            values = parts[0] if blocks == 1 else jnp.concatenate(parts, axis=0)
            value_high, value_low = split(values)
            upper = mul(both, value_high)
            mixed.append(upper[:rows] + (upper[rows:] + mul(high, value_low)))
        mixed[1] = mixed[1] - mixed[2]
        mixed[2] = mixed[2] - mixed[3]
        for kind in range(species):
            out[:, kind, 0, z, :] = mixed[kind]


def mix(weights, sources, blocks, rows):
    nx, nz, held, ny = sources[0].shape
    species = len(sources) // blocks
    return pl.pallas_call(
        functools.partial(mix_kernel, blocks=blocks),
        grid=(nx,),
        out_shape=jax.ShapeDtypeStruct((rows, species, nx, nz, ny), f32),
        in_specs=[VMEM] * (1 + len(sources)),
        out_specs=pl.BlockSpec((rows, species, 1, nz, ny), lambda x: (0, 0, x, 0, 0)),
        compiler_params=pltpu.CompilerParams(vmem_limit_bytes=SCOPED),
        name="mix",
    )(weights, *sources)


def swap(x, axis, bit):
    count = lax.axis_size(axis)
    return lax.ppermute(x, axis, [(k, k ^ bit) for k in range(count)])


def total_over(x, axis):
    bit = 1
    while bit < lax.axis_size(axis):
        x = x + swap(x, axis, bit)
        bit *= 2
    return x


def local(ensemble, diffusivity, binding, source, obs_index, owner, observed, obs_var):
    rows, species, nx, nz, ny = ensemble.shape
    devices = lax.axis_size("member")
    spaces = lax.axis_size("space")
    members = rows * devices
    batches = owner.shape[0]
    member = lax.axis_index("member")
    place = jnp.stack([member & 1, lax.axis_index("space"), member]).astype(jnp.int32)

    forward = [(k, k + 1) for k in range(spaces - 1)]
    backward = [(k + 1, k) for k in range(spaces - 1)]

    def halos(first, last):
        return lax.ppermute(last, "space", forward), lax.ppermute(first, "space", backward)

    if devices == 4 and rows % 8 == 0:
        blocks = devices

        def offsets(position, j):
            return jnp.bitwise_xor(position, j) * rows

        def collect(x):
            return [x, swap(x, "member", 1), swap(x, "member", 2)]

        def complete(held, *after):
            return [*held, swap(lax.optimization_barrier((held[2], *after))[0], "member", 1)]
    else:
        blocks = 1

        def offsets(position, j):
            return 0

        def collect(x):
            return [lax.all_gather(x, "member", axis=2, tiled=True)]

        def complete(held, *after):
            return held

    def across(held):
        return held[min(2, blocks - 1)]

    whole = (nx, nz, rows, ny)
    coefficients = (diffusivity, binding, source)
    cells = nx * nz * rows * ny
    ends = [
        jnp.transpose(ensemble[:, :3, part], (1, 2, 3, 0, 4))
        for part in (slice(0, 2), slice(nx - 2, nx))
    ]
    edges = forecast_call(
        first_edges_kernel,
        "first_edges",
        [*ends, *coefficients],
        [(nz, 2 * rows + 8, ny)] * 2,
        2 * cells // nx,
    )
    fields = [jnp.transpose(ensemble[:, k], (1, 2, 0, 3)) for k in range(species)]
    conserved = fields[1] + fields[2] + fields[3]
    omega, eta = voxel_weights(
        place, owner, obs_index, observed, obs_var, batches // 2, nx * nz, ny
    )
    around = origin = halos(*edges)
    steps = SUBSTEPS // 2
    for step in range(steps):
        final = step == steps - 1
        ready = ()
        if step == 1:
            conserved = collect(lax.optimization_barrier((conserved, fields[0]))[0])
            ready = (omega, eta)
        elif step == 2:
            ready = conserved[1:]
        *fields, = forecast_call(
            functools.partial(two_substeps_kernel, final=final),
            "two_substeps",
            [*fields, *around, *origin, *coefficients],
            [whole] * 4 + ([] if final else [(nz, 2 * rows, ny)] * 2),
            2 * cells,
            scratch=[whole],
            ready=ready,
        )
        if not final:
            around = halos(*fields[4:])
            fields = fields[:4]
    free, _, tracer, internal = fields

    tracer = complete(collect(tracer))
    conserved = complete(conserved, across(tracer))
    internal = collect(lax.optimization_barrier((internal, across(tracer)))[0])
    half = total_over(gram(place, owner, omega, eta, tracer, offsets), "space")
    half, free, _ = lax.optimization_barrier((half, free, across(internal)))
    free = collect(free)
    internal = complete(internal, half)
    weights = transforms(place, half, swap(half, "member", 1), offsets, blocks, rows)
    free = complete(free, weights)
    if blocks == 1:
        weights = lax.dynamic_slice(weights, (member * rows, 0), (rows, LANES))
    return mix(weights, free + conserved + tracer + internal, blocks, rows)


def solution(mesh):
    in_specs = (
        P("member", None, "space", None, None),
        P("space", None, None),
        P("space", None, None),
        P("space", None, None),
        P(),
        P(),
        P(),
        P(),
    )
    out_specs = P("member", None, "space", None, None)
    return jax.shard_map(local, mesh=mesh, in_specs=in_specs, out_specs=out_specs, check_vma=False)
```

```python
import functools

import jax
import jax.numpy as jnp
from jax import lax
from jax.experimental import pallas as pl
from jax.experimental.pallas import tpu as pltpu
from jax.sharding import PartitionSpec as P

SUBSTEPS = 6
NEWTON = 16
UNROLL = 5
LANES = 128
SCOPED = 10 * 2**20

unbind_rate = 0.05
uptake_rate = 0.1
recycle_rate = 0.02

VMEM = pl.BlockSpec(memory_space=pltpu.VMEM)
SMEM = pl.BlockSpec(memory_space=pltpu.SMEM)
bf16 = jnp.bfloat16
f32 = jnp.float32


def split(x):
    high = x.astype(bf16)
    return high, (x - high.astype(f32)).astype(bf16)


def dot_parts(a, b, dims):
    a_high, a_low = a
    b_high, b_low = b
    mul = functools.partial(
        lax.dot_general, dimension_numbers=(dims, ((), ())), preferred_element_type=f32
    )
    return mul(a_high, b_high) + (mul(a_high, b_low) + mul(a_low, b_high))


def wide_left(x):
    return jnp.concatenate(split(x), axis=1)


def wide_right(x):
    both = jnp.concatenate(split(x), axis=1)
    rows, lanes = both.shape
    if rows < lanes // 2:
        both = jnp.concatenate([both, jnp.zeros((lanes // 2 - rows, lanes), bf16)], axis=0)
    return jnp.concatenate([both, both], axis=0)


def wide_dot(left, right):
    out = jnp.dot(left, right, preferred_element_type=f32)
    side = out.shape[1] // 2
    return out[:, :side] + out[:, side:]


NN = ((1,), (0,))
NT = ((1,), (1,))


def react(free, receptor, complexed, internal, binding):
    flux = binding * free * receptor
    back = unbind_rate * complexed - flux
    return (
        back,
        receptor + back + recycle_rate * internal,
        complexed + flux - (unbind_rate + uptake_rate) * complexed,
        internal + uptake_rate * complexed - recycle_rate * internal,
    )


def spread_free(free, planes, neighbours, diffusivity):
    lane = lax.broadcasted_iota(jnp.int32, free.shape, 1)
    last = free.shape[1] - 1
    for plane in planes:
        neighbours = plane if neighbours is None else neighbours + plane
    neighbours += jnp.where(lane == last, 0.0, pltpu.roll(free, last, 1))
    neighbours += jnp.where(lane == 0, 0.0, pltpu.roll(free, 1, 1))
    return free + diffusivity * (neighbours - 6.0 * free)


def beside(read, x, z, nx, nz, low, high):
    around = [low if x == 0 else read(x - 1, z), high if x == nx - 1 else read(x + 1, z)]
    around += [read(x, other) for other in (z + 1, z - 1) if 0 <= other < nz]
    return [value for value in around if value is not None]


def edge_free(read, rest, x, nz, nx, z, diffusivity):
    return spread_free(read(x, z), beside(read, x, z, nx, nz, None, None), None, diffusivity) + rest


def first_edges_kernel(below, above, diffusivity, binding, source, first, last):
    _, _, nz, members, _ = below.shape
    nx = diffusivity.shape[0]
    for x, ends, out in ((0, below, first), (nx - 1, above, last)):
        shift = 0 if x == 0 else nx - 2

        def read(at, z, ends=ends, shift=shift):
            return ends[0, at - shift, z]

        for z in range(nz):
            row = pl.ds(z, 1)
            free = read(x, z)
            flux = binding[x, row, :] * free * ends[1, x - shift, z]
            rest = unbind_rate * ends[2, x - shift, z] - flux + source[x, row, :]
            spread = diffusivity[x, row, :]
            out[z, :members, :] = free
            out[z, members : 2 * members, :] = edge_free(read, rest, x, nz, nx, z, spread)
            out[z, 2 * members :, :] = jnp.broadcast_to(spread, (8, spread.shape[1]))


def two_substeps_kernel(
    a, r, c, i, low, high, low_first, high_first, diffusivity, binding, source, *refs, final
):
    out_a, out_r, out_c, out_i = refs[:4]
    middle = refs[-1]
    nx, nz, members, _ = a.shape

    def outside(x, z, later):
        part = slice(members, 2 * members) if later else slice(0, members)
        values = []
        for end, halo, origin in ((0, low, low_first), (nx - 1, high, high_first)):
            value = halo[z, part, :] if x == end else None
            if x == end and later:
                value += origin[z, 2 * members : 2 * members + 1, :] * a[x, z]
            values.append(value)
        return values

    for x in range(nx):
        for z in range(nz):
            row = pl.ds(z, 1)
            back, out_r[x, z], out_c[x, z], out_i[x, z] = react(
                a[x, z], r[x, z], c[x, z], i[x, z], binding[x, row, :]
            )
            around = beside(lambda x, z: a[x, z], x, z, nx, nz, *outside(x, z, False))
            middle[x, z] = (
                spread_free(a[x, z], around, None, diffusivity[x, row, :])
                + back
                + source[x, row, :]
            )
    for x in range(nx):
        for z in range(nz):
            row = pl.ds(z, 1)
            back, receptor, complexed, internal = react(
                middle[x, z], out_r[x, z], out_c[x, z], out_i[x, z], binding[x, row, :]
            )
            around = beside(lambda x, z: middle[x, z], x, z, nx, nz, *outside(x, z, True))
            out_a[x, z] = (
                spread_free(middle[x, z], around, None, diffusivity[x, row, :])
                + back
                + source[x, row, :]
            )
            if not final:
                out_r[x, z] = receptor
            out_c[x, z] = complexed + internal if final else complexed
            out_i[x, z] = internal
    if final:
        return
    for x, out in ((0, refs[4]), (nx - 1, refs[5])):
        for z in range(nz):
            row = pl.ds(z, 1)
            free = out_a[x, z]
            flux = binding[x, row, :] * free * out_r[x, z]
            rest = unbind_rate * out_c[x, z] - flux + source[x, row, :]
            out[z, :members, :] = free
            out[z, members:, :] = edge_free(
                lambda x, z: out_a[x, z], rest, x, nz, nx, z, diffusivity[x, row, :]
            )


def forecast_call(kernel, name, inputs, outputs, cells, scratch=(), ready=()):
    def body(*refs):
        kernel(*refs[: len(inputs)], *refs[len(inputs) + len(ready) :])

    return pl.pallas_call(
        body,
        out_shape=[jax.ShapeDtypeStruct(shape, f32) for shape in outputs],
        in_specs=[VMEM] * len(inputs) + [pl.BlockSpec(memory_space=pl.ANY)] * len(ready),
        out_specs=[VMEM] * len(outputs),
        scratch_shapes=[pltpu.VMEM(shape, f32) for shape in scratch],
        compiler_params=pltpu.CompilerParams(vmem_limit_bytes=SCOPED),
        cost_estimate=pl.CostEstimate(
            flops=30 * cells, bytes_accessed=32 * cells, transcendentals=0
        ),
        name=name,
    )(*inputs, *ready)


def weights_kernel(place, owner, obs_index, observed, obs_var, omega, eta):
    count, rows, ny = omega.shape
    batch_size = obs_index.shape[1]
    for k in range(count):
        batch = place[0] * count + k
        mine = owner[batch] == place[1]
        line = pl.ds(batch, 1)
        voxel = obs_index[line, :]
        scale = jnp.where(mine, 1.0, 0.0) / obs_var[line, :]
        shift = ny.bit_length() - 1
        row = lax.shift_right_logical(voxel, shift)
        column = jnp.bitwise_and(voxel, ny - 1)
        at_row = lax.broadcasted_iota(jnp.int32, (rows, batch_size), 0) == row
        at_column = lax.broadcasted_iota(jnp.int32, (ny, batch_size), 0) == column
        both = jnp.concatenate(
            [jnp.where(at_row, scale, 0.0), jnp.where(at_row, scale * observed[line, :], 0.0)],
            axis=0,
        )
        one = both.astype(bf16)
        rest = both - one.astype(f32)
        two = rest.astype(bf16)
        three = (rest - two.astype(f32)).astype(bf16)
        columns = jnp.where(at_column, 1.0, 0.0).astype(bf16)
        sums = lax.dot_general(
            jnp.concatenate([one, two, three], axis=0),
            columns,
            (NT, ((), ())),
            preferred_element_type=f32,
        )
        sums = sums[: 2 * rows] + sums[2 * rows : 4 * rows] + sums[4 * rows :]
        omega[k] = sums[:rows]
        eta[k] = sums[rows:]


def voxel_weights(place, owner, obs_index, observed, obs_var, count, rows, ny):
    out = jax.ShapeDtypeStruct((count, rows, ny), f32)
    return pl.pallas_call(
        weights_kernel,
        out_shape=[out, out],
        in_specs=[SMEM, SMEM, VMEM, VMEM, VMEM],
        out_specs=[VMEM, VMEM],
        compiler_params=pltpu.CompilerParams(vmem_limit_bytes=SCOPED),
        name="voxel_weights",
    )(place, owner, obs_index, observed, obs_var)


def gram_kernel(place, owner, omega, eta, *refs, offsets):
    *sources, packed, out, members_at = refs
    count = out.shape[0]
    nx, nz, rows, ny = sources[0].shape
    members = members_at.shape[0]
    for k in range(count):
        out[k] = jnp.zeros(out.shape[1:], f32)

        @pl.when(owner[place[0] * count + k] == place[1])
        def _(k=k):
            def tile(t, total):
                x, z = t // nz, t % nz
                for j, source in enumerate(sources):
                    start = pl.multiple_of(offsets(place[2], j), 8)
                    members_at[pl.ds(start, rows), :] = source[x, z]
                values = members_at[...]
                mean = jnp.sum(values, axis=0, keepdims=True) * (1.0 / members)
                spread = values - mean
                weight = omega[k, pl.ds(t, 1), :]
                shift = eta[k, pl.ds(t, 1), :] - weight * mean
                tail = lax.broadcasted_iota(jnp.int32, (LANES - members, ny), 0)
                weighted = jnp.concatenate(
                    [spread * weight, jnp.where(tail == 0, shift, 0.0)], axis=0
                )
                return total + dot_parts(split(spread), split(weighted), NT)

            out[k] = lax.fori_loop(0, nx * nz, tile, jnp.zeros(out.shape[1:], f32), unroll=4)

    row = lax.broadcasted_iota(jnp.int32, (members, LANES), 0)
    column = lax.broadcasted_iota(jnp.int32, (members, LANES), 1)
    above, below = out[0], out[1]

    def pick(where, x):
        return jnp.sum(jnp.where(where, x, 0.0), axis=1, keepdims=True)

    both = jnp.where(column >= row, above, below)
    both = jnp.where(column == members, pick(column == row, below), both)
    both = jnp.where(column == members + 1, pick(column == members, above), both)
    packed[...] = jnp.where(column == members + 2, pick(column == members, below), both)


def gram(place, owner, omega, eta, sources, offsets):
    nx, nz, rows, ny = sources[0].shape
    members = rows * len(sources)
    count = omega.shape[0]
    return pl.pallas_call(
        functools.partial(gram_kernel, offsets=offsets),
        out_shape=jax.ShapeDtypeStruct((members, LANES), f32),
        in_specs=[SMEM, SMEM, VMEM, VMEM] + [VMEM] * len(sources),
        out_specs=VMEM,
        scratch_shapes=[pltpu.VMEM((count, members, LANES), f32), pltpu.VMEM((members, ny), f32)],
        compiler_params=pltpu.CompilerParams(vmem_limit_bytes=SCOPED),
        name="gram",
    )(place, owner, omega, eta, *sources)


def turned(x):
    rows = x.shape[0]
    whole = jnp.concatenate([x, jnp.zeros((LANES - rows, LANES), f32)], axis=0)
    return whole.T[:rows]


def batch_transform(extended, total, members):
    row = lax.broadcasted_iota(jnp.int32, extended.shape, 0)
    column = lax.broadcasted_iota(jnp.int32, extended.shape, 1)
    inside = column < members
    last = column == members
    identity = jnp.where(row == column, 1.0, 0.0)
    matrix = jnp.where(inside, extended, 0.0)

    mean = jnp.sum(total, axis=1, keepdims=True) * (1.0 / members)
    centred = jnp.where(inside, total - mean, 0.0)
    product = wide_dot(wide_left(matrix), wide_right(jnp.where(last, mean, centred)))
    product = jnp.where(last, extended - product, product)
    product = wide_dot(wide_left(turned(centred)), wide_right(product)) * (1.0 / (members - 1))
    innovation = jnp.sum(jnp.where(last, product, 0.0), axis=1, keepdims=True)
    system = identity + jnp.where(inside, product, 0.0)
    frobenius = jnp.sqrt(jnp.sum(jnp.sum(system * system, axis=1, keepdims=True), axis=0, keepdims=True))

    scaled_root = system / frobenius
    factor = 1.5 * identity - 0.5 * scaled_root
    scaled_root = wide_dot(wide_left(scaled_root), wide_right(factor))
    inverse_root = factor

    def newton(iteration, iterates):
        scaled_root, inverse_root = iterates
        factor = 1.5 * identity - 0.5 * wide_dot(
            wide_left(inverse_root), wide_right(scaled_root)
        )
        return (
            wide_dot(wide_left(scaled_root), wide_right(factor)),
            wide_dot(wide_left(factor), wide_right(inverse_root)),
        )

    scaled_root, inverse_root = lax.fori_loop(1, NEWTON, newton, (scaled_root, inverse_root), unroll=UNROLL)
    root_inv = inverse_root / jnp.sqrt(frobenius)
    mean_weight = jnp.sum(root_inv * innovation, axis=0, keepdims=True)
    mean_weight = jnp.sum(root_inv * mean_weight, axis=1, keepdims=True)
    mixing = jnp.where(inside, root_inv + mean_weight, 0.0)
    mixing = mixing - jnp.sum(mixing, axis=0, keepdims=True) * (1.0 / members)
    mixing = jnp.where(inside, mixing + 1.0 / members, 0.0)
    return wide_dot(wide_left(total), wide_right(mixing))


def transform_kernel(place, mine, other, out, ordered, work, *, offsets, blocks, rows):
    members = mine.shape[0]
    row = lax.broadcasted_iota(jnp.int32, (members, LANES), 0)
    column = lax.broadcasted_iota(jnp.int32, (members, LANES), 1)
    inside = column < members

    def pick(where, x):
        return jnp.sum(jnp.where(where, x, 0.0), axis=1, keepdims=True)

    for half, shared in ((place[0], mine), (1 - place[0], other)):
        packed = shared[...]
        above = jnp.where(inside & (column > row), packed, 0.0)
        below = jnp.where(inside & (column < row), packed, 0.0)
        middle = jnp.where(column == row, packed, 0.0)
        side = jnp.where(column == members, pick(column == members + 1, packed), 0.0)
        ordered[2 * half] = above + turned(above) + (middle + side)
        middle = jnp.where(column == row, pick(column == members, packed), 0.0)
        side = jnp.where(column == members, pick(column == members + 2, packed), 0.0)
        ordered[2 * half + 1] = below + turned(below) + (middle + side)
    total = jnp.where(row == column, 1.0, 0.0)
    for batch in range(ordered.shape[0]):
        total = batch_transform(ordered[batch], total, members)
    total = jnp.concatenate([total, jnp.zeros((LANES - members, LANES), f32)], axis=0)
    work[...] = total
    if blocks == 1:
        out[...] = total.T
        return
    parts = [
        work[pl.ds(pl.multiple_of(offsets(place[2], j), 8), rows), :] for j in range(blocks)
    ]
    parts.append(jnp.zeros((LANES - members, LANES), f32))
    work[...] = jnp.concatenate(parts, axis=0).T
    out[...] = work[pl.ds(pl.multiple_of(offsets(place[2], 0), 8), rows), :]


def transforms(place, mine, other, offsets, blocks, rows):
    members = mine.shape[0]
    shape = (LANES, LANES) if blocks == 1 else (rows, LANES)
    return pl.pallas_call(
        functools.partial(transform_kernel, offsets=offsets, blocks=blocks, rows=rows),
        out_shape=jax.ShapeDtypeStruct(shape, f32),
        in_specs=[SMEM, VMEM, VMEM],
        out_specs=VMEM,
        scratch_shapes=[
            pltpu.VMEM((4, members, LANES), f32),
            pltpu.VMEM((LANES, LANES), f32),
        ],
        compiler_params=pltpu.CompilerParams(vmem_limit_bytes=SCOPED),
        cost_estimate=pl.CostEstimate(
            flops=10**8, bytes_accessed=10**6, transcendentals=0
        ),
        name="transforms",
    )(place, mine, other)


def mix_kernel(weights, *refs, blocks, kinds, begin):
    *sources, out = refs
    rows, _, _, nz, _ = out.shape
    x = pl.program_id(0)
    members = blocks * sources[0].shape[2]
    high, low = split(weights[:, :members])
    both = jnp.concatenate([high.astype(f32), low.astype(f32)], axis=0).astype(bf16)
    mul = functools.partial(
        lax.dot_general, dimension_numbers=(NN, ((), ())), preferred_element_type=f32
    )
    for z in range(nz):
        mixed = []
        for kind in range(kinds):
            parts = [sources[kind * blocks + j][x, z] for j in range(blocks)]
            values = parts[0] if blocks == 1 else jnp.concatenate(parts, axis=0)
            value_high, value_low = split(values)
            upper = mul(both, value_high)
            mixed.append(upper[:rows] + (upper[rows:] + mul(high, value_low)))
        for kind in range(kinds - 1):
            mixed[kind] = mixed[kind] - mixed[kind + 1]
        for kind in range(kinds):
            out[:, begin + kind, 0, z, :] = mixed[kind]


def mix(weights, sources, blocks, shape, kinds, begin, result=None):
    rows, _, nx, nz, ny = shape
    count = len(sources)
    before = [] if result is None else [result]
    cells = nx * nz * ny * rows * kinds

    def body(*refs):
        mix_kernel(*refs[: 1 + count], refs[-1], blocks=blocks, kinds=kinds, begin=begin)

    return pl.pallas_call(
        body,
        grid=(nx,),
        out_shape=jax.ShapeDtypeStruct(shape, f32),
        in_specs=[VMEM] * (1 + count) + [pl.BlockSpec(memory_space=pl.ANY)] * len(before),
        out_specs=pl.BlockSpec((rows, begin + kinds, 1, nz, ny), lambda x: (0, 0, x, 0, 0)),
        input_output_aliases={} if result is None else {1 + count: 0},
        compiler_params=pltpu.CompilerParams(vmem_limit_bytes=SCOPED),
        cost_estimate=pl.CostEstimate(
            flops=1000 * cells, bytes_accessed=4 * cells, transcendentals=0
        ),
        name="mix",
    )(weights, *sources, *before)


def swap(x, axis, bit):
    count = lax.axis_size(axis)
    return lax.ppermute(x, axis, [(k, k ^ bit) for k in range(count)])


def total_over(x, axis):
    bit = 1
    while bit < lax.axis_size(axis):
        x = x + swap(x, axis, bit)
        bit *= 2
    return x


def local(ensemble, diffusivity, binding, source, obs_index, owner, observed, obs_var):
    rows, species, nx, nz, ny = ensemble.shape
    devices = lax.axis_size("member")
    spaces = lax.axis_size("space")
    members = rows * devices
    batches = owner.shape[0]
    member = lax.axis_index("member")
    place = jnp.stack([member & 1, lax.axis_index("space"), member]).astype(jnp.int32)

    forward = [(k, k + 1) for k in range(spaces - 1)]
    backward = [(k + 1, k) for k in range(spaces - 1)]

    def halos(first, last):
        return lax.ppermute(last, "space", forward), lax.ppermute(first, "space", backward)

    if devices == 4 and rows % 8 == 0:
        blocks = devices

        def offsets(position, j):
            return jnp.bitwise_xor(position, j) * rows

        def collect(x):
            return [x, swap(x, "member", 1), swap(x, "member", 2)]

        def complete(held, *after):
            return [*held, swap(lax.optimization_barrier((held[2], *after))[0], "member", 1)]
    else:
        blocks = 1

        def offsets(position, j):
            return 0

        def collect(x):
            return [lax.all_gather(x, "member", axis=2, tiled=True)]

        def complete(held, *after):
            return held

    def across(held):
        return held[min(2, blocks - 1)]

    whole = (nx, nz, rows, ny)
    coefficients = (diffusivity, binding, source)
    cells = nx * nz * rows * ny
    ends = [
        jnp.transpose(ensemble[:, :3, part], (1, 2, 3, 0, 4))
        for part in (slice(0, 2), slice(nx - 2, nx))
    ]
    edges = forecast_call(
        first_edges_kernel,
        "first_edges",
        [*ends, *coefficients],
        [(nz, 2 * rows + 8, ny)] * 2,
        2 * cells // nx,
    )
    fields = [jnp.transpose(ensemble[:, k], (1, 2, 0, 3)) for k in range(species)]
    conserved = fields[1] + fields[2] + fields[3]
    omega, eta = voxel_weights(
        place, owner, obs_index, observed, obs_var, batches // 2, nx * nz, ny
    )
    around = origin = halos(*edges)
    steps = SUBSTEPS // 2
    for step in range(steps):
        final = step == steps - 1
        ready = ()
        if step == 0:
            ready = (omega, eta)
        elif step == 1:
            conserved = collect(lax.optimization_barrier((conserved, fields[0]))[0])
        elif step == 2:
            ready = conserved[1:]
        *fields, = forecast_call(
            functools.partial(two_substeps_kernel, final=final),
            "two_substeps",
            [*fields, *around, *origin, *coefficients],
            [whole] * 4 + ([] if final else [(nz, 2 * rows, ny)] * 2),
            2 * cells,
            scratch=[whole],
            ready=ready,
        )
        if not final:
            around = halos(*fields[4:])
            fields = fields[:4]
    free, _, tracer, internal = fields

    tracer = complete(collect(tracer))
    conserved = complete(conserved, across(tracer))
    internal = collect(lax.optimization_barrier((internal, across(tracer)))[0])
    half = total_over(gram(place, owner, omega, eta, tracer, offsets), "space")
    half, free, _ = lax.optimization_barrier((half, free, across(internal)))
    free = collect(free)
    internal = complete(internal, half)
    weights = transforms(place, half, swap(half, "member", 1), offsets, blocks, rows)
    free = complete(free, weights)
    if blocks == 1:
        weights = lax.dynamic_slice(weights, (member * rows, 0), (rows, LANES))
    bound = conserved + tracer + internal
    result = mix(weights, bound, blocks, ensemble.shape, species - 1, 1)
    return mix(weights, free, blocks, ensemble.shape, 1, 0, result)


def solution(mesh):
    in_specs = (
        P("member", None, "space", None, None),
        P("space", None, None),
        P("space", None, None),
        P("space", None, None),
        P(),
        P(),
        P(),
        P(),
    )
    out_specs = P("member", None, "space", None, None)
    return jax.shard_map(local, mesh=mesh, in_specs=in_specs, out_specs=out_specs, check_vma=False)
```

```python
import functools

import jax
import jax.numpy as jnp
from jax import lax
from jax.experimental import pallas as pl
from jax.experimental.pallas import tpu as pltpu
from jax.sharding import PartitionSpec as P

SUBSTEPS = 6
NEWTON = 16
UNROLL = 5
LANES = 128
SCOPED = 10 * 2**20

unbind_rate = 0.05
uptake_rate = 0.1
recycle_rate = 0.02

VMEM = pl.BlockSpec(memory_space=pltpu.VMEM)
SMEM = pl.BlockSpec(memory_space=pltpu.SMEM)
bf16 = jnp.bfloat16
f32 = jnp.float32


def split(x):
    high = x.astype(bf16)
    return high, (x - high.astype(f32)).astype(bf16)


def dot_parts(a, b, dims):
    a_high, a_low = a
    b_high, b_low = b
    mul = functools.partial(
        lax.dot_general, dimension_numbers=(dims, ((), ())), preferred_element_type=f32
    )
    return mul(a_high, b_high) + (mul(a_high, b_low) + mul(a_low, b_high))


def wide_left(x):
    return jnp.concatenate(split(x), axis=1)


def wide_right(x):
    both = jnp.concatenate(split(x), axis=1)
    rows, lanes = both.shape
    if rows < lanes // 2:
        both = jnp.concatenate([both, jnp.zeros((lanes // 2 - rows, lanes), bf16)], axis=0)
    return jnp.concatenate([both, both], axis=0)


def wide_dot(left, right):
    out = jnp.dot(left, right, preferred_element_type=f32)
    side = out.shape[1] // 2
    return out[:, :side] + out[:, side:]


NN = ((1,), (0,))
NT = ((1,), (1,))


def react(free, receptor, complexed, internal, binding):
    flux = binding * free * receptor
    back = unbind_rate * complexed - flux
    return (
        back,
        receptor + back + recycle_rate * internal,
        complexed + flux - (unbind_rate + uptake_rate) * complexed,
        internal + uptake_rate * complexed - recycle_rate * internal,
    )


def spread_free(free, planes, neighbours, diffusivity):
    lane = lax.broadcasted_iota(jnp.int32, free.shape, 1)
    last = free.shape[1] - 1
    for plane in planes:
        neighbours = plane if neighbours is None else neighbours + plane
    neighbours += jnp.where(lane == last, 0.0, pltpu.roll(free, last, 1))
    neighbours += jnp.where(lane == 0, 0.0, pltpu.roll(free, 1, 1))
    return free + diffusivity * (neighbours - 6.0 * free)


def beside(read, x, z, nx, nz, low, high):
    around = [low if x == 0 else read(x - 1, z), high if x == nx - 1 else read(x + 1, z)]
    around += [read(x, other) for other in (z + 1, z - 1) if 0 <= other < nz]
    return [value for value in around if value is not None]


def edge_free(read, rest, x, nz, nx, z, diffusivity):
    return spread_free(read(x, z), beside(read, x, z, nx, nz, None, None), None, diffusivity) + rest


def first_edges_kernel(below, above, diffusivity, binding, source, first, last):
    _, _, nz, members, _ = below.shape
    nx = diffusivity.shape[0]
    for x, ends, out in ((0, below, first), (nx - 1, above, last)):
        shift = 0 if x == 0 else nx - 2

        def read(at, z, ends=ends, shift=shift):
            return ends[0, at - shift, z]

        for z in range(nz):
            row = pl.ds(z, 1)
            free = read(x, z)
            flux = binding[x, row, :] * free * ends[1, x - shift, z]
            rest = unbind_rate * ends[2, x - shift, z] - flux + source[x, row, :]
            spread = diffusivity[x, row, :]
            out[z, :members, :] = free
            out[z, members : 2 * members, :] = edge_free(read, rest, x, nz, nx, z, spread)
            out[z, 2 * members :, :] = jnp.broadcast_to(spread, (8, spread.shape[1]))


def first_substep(
    a, r, c, i, low, high, diffusivity, binding, source, out_a, out_r, out_c, out_i
):
    nx, nz, _, _ = a.shape
    for x in range(nx):
        for z in range(nz):
            row = pl.ds(z, 1)
            back, out_r[x, z], out_c[x, z], out_i[x, z] = react(
                a[x, z], r[x, z], c[x, z], i[x, z], binding[x, row, :]
            )
            around = beside(lambda x, z: a[x, z], x, z, nx, nz, low(z), high(z))
            out_a[x, z] = (
                spread_free(a[x, z], around, None, diffusivity[x, row, :])
                + back
                + source[x, row, :]
            )


def two_substeps_kernel(
    a, r, c, i, low, high, low_first, high_first, diffusivity, binding, source, *refs, lean
):
    out_a, out_r, out_c, out_i, first, last, middle = refs
    nx, nz, members, _ = a.shape
    first_substep(
        a,
        r,
        c,
        i,
        lambda z: low[z, :members, :],
        lambda z: high[z, :members, :],
        diffusivity,
        binding,
        source,
        middle,
        out_r,
        out_c,
        out_i,
    )

    def outside(halo, origin, x, z):
        later = halo[z, members : 2 * members, :]
        return later + origin[z, 2 * members : 2 * members + 1, :] * a[x, z]

    for x in range(nx):
        for z in range(nz):
            row = pl.ds(z, 1)
            back, out_r[x, z], out_c[x, z], out_i[x, z] = react(
                middle[x, z], out_r[x, z], out_c[x, z], out_i[x, z], binding[x, row, :]
            )
            around = beside(
                lambda x, z: middle[x, z],
                x,
                z,
                nx,
                nz,
                outside(low, low_first, x, z) if x == 0 else None,
                outside(high, high_first, x, z) if x == nx - 1 else None,
            )
            out_a[x, z] = (
                spread_free(middle[x, z], around, None, diffusivity[x, row, :])
                + back
                + source[x, row, :]
            )
    for x, out in ((0, first), (nx - 1, last)):
        for z in range(nz):
            row = pl.ds(z, 1)
            free = out_a[x, z]
            out[z, :members, :] = free
            if lean:
                continue
            flux = binding[x, row, :] * free * out_r[x, z]
            rest = unbind_rate * out_c[x, z] - flux + source[x, row, :]
            out[z, members:, :] = edge_free(
                lambda x, z: out_a[x, z], rest, x, nz, nx, z, diffusivity[x, row, :]
            )


def last_but_one_kernel(
    place, a, r, c, i, low, high, diffusivity, binding, source, *refs, halves
):
    *tracers, out_i, out_a, out_add, first, last, mid_r, mid_c, mid_i = refs
    nx, nz, _, _ = a.shape
    first_substep(
        a,
        r,
        c,
        i,
        lambda z: low[z],
        lambda z: high[z],
        diffusivity,
        binding,
        source,
        out_a,
        mid_r,
        mid_c,
        mid_i,
    )
    span = nx // halves
    for part, tracer in enumerate(tracers):
        begin = jnp.bitwise_xor(part, lax.shift_right_logical(place[2], 1)) * span
        for j in range(span):
            x = j if halves == 1 else begin + j
            for z in range(nz):
                row = pl.ds(z, 1)
                back, _, complexed, internal = react(
                    out_a[x, z], mid_r[x, z], mid_c[x, z], mid_i[x, z], binding[x, row, :]
                )
                tracer[j, z] = complexed + internal
                out_i[x, z] = internal
                out_add[x, z] = back + source[x, row, :]
    for x, out in ((0, first), (nx - 1, last)):
        for z in range(nz):
            out[z] = out_a[x, z]


def last_free_kernel(a, add, low, high, diffusivity, out_a):
    nx, nz, _, _ = a.shape
    for x in range(nx):
        for z in range(nz):
            around = beside(lambda x, z: a[x, z], x, z, nx, nz, low[z], high[z])
            out_a[x, z] = (
                spread_free(a[x, z], around, None, diffusivity[x, pl.ds(z, 1), :]) + add[x, z]
            )


def forecast_call(kernel, name, inputs, outputs, cells, scratch=(), ready=(), scalars=()):
    def body(*refs):
        count = len(scalars) + len(inputs)
        kernel(*refs[:count], *refs[count + len(ready) :])

    return pl.pallas_call(
        body,
        out_shape=[jax.ShapeDtypeStruct(shape, f32) for shape in outputs],
        in_specs=[SMEM] * len(scalars)
        + [VMEM] * len(inputs)
        + [pl.BlockSpec(memory_space=pl.ANY)] * len(ready),
        out_specs=[VMEM] * len(outputs),
        scratch_shapes=[pltpu.VMEM(shape, f32) for shape in scratch],
        compiler_params=pltpu.CompilerParams(vmem_limit_bytes=SCOPED),
        cost_estimate=pl.CostEstimate(
            flops=30 * cells, bytes_accessed=32 * cells, transcendentals=0
        ),
        name=name,
    )(*scalars, *inputs, *ready)


def weights_kernel(place, owner, obs_index, observed, obs_var, omega, eta):
    count, rows, ny = omega.shape
    batch_size = obs_index.shape[1]
    for k in range(count):
        batch = place[0] * count + k
        mine = owner[batch] == place[1]
        line = pl.ds(batch, 1)
        voxel = obs_index[line, :]
        scale = jnp.where(mine, 1.0, 0.0) / obs_var[line, :]
        shift = ny.bit_length() - 1
        row = lax.shift_right_logical(voxel, shift)
        column = jnp.bitwise_and(voxel, ny - 1)
        at_row = lax.broadcasted_iota(jnp.int32, (rows, batch_size), 0) == row
        at_column = lax.broadcasted_iota(jnp.int32, (ny, batch_size), 0) == column
        both = jnp.concatenate(
            [jnp.where(at_row, scale, 0.0), jnp.where(at_row, scale * observed[line, :], 0.0)],
            axis=0,
        )
        one = both.astype(bf16)
        rest = both - one.astype(f32)
        two = rest.astype(bf16)
        three = (rest - two.astype(f32)).astype(bf16)
        columns = jnp.where(at_column, 1.0, 0.0).astype(bf16)
        sums = lax.dot_general(
            jnp.concatenate([one, two, three], axis=0),
            columns,
            (NT, ((), ())),
            preferred_element_type=f32,
        )
        sums = sums[: 2 * rows] + sums[2 * rows : 4 * rows] + sums[4 * rows :]
        omega[k] = sums[:rows]
        eta[k] = sums[rows:]


def voxel_weights(place, owner, obs_index, observed, obs_var, count, rows, ny):
    out = jax.ShapeDtypeStruct((count, rows, ny), f32)
    return pl.pallas_call(
        weights_kernel,
        out_shape=[out, out],
        in_specs=[SMEM, SMEM, VMEM, VMEM, VMEM],
        out_specs=[VMEM, VMEM],
        compiler_params=pltpu.CompilerParams(vmem_limit_bytes=SCOPED),
        name="voxel_weights",
    )(place, owner, obs_index, observed, obs_var)


def gram_kernel(place, owner, omega, eta, *refs, offsets, halves):
    *sources, packed, out, members_at = refs
    count = out.shape[0]
    span, nz, rows, ny = sources[0].shape
    members = members_at.shape[0]
    begin = 0 if halves == 1 else lax.shift_right_logical(place[2], 1) * (span * nz)
    for k in range(count):
        out[k] = jnp.zeros(out.shape[1:], f32)

        @pl.when(owner[place[0] * count + k] == place[1])
        def _(k=k):
            def tile(t, total):
                x, z = t // nz, t % nz
                for j, source in enumerate(sources):
                    start = pl.multiple_of(offsets(place[2], j), 8)
                    members_at[pl.ds(start, rows), :] = source[x, z]
                values = members_at[...]
                mean = jnp.sum(values, axis=0, keepdims=True) * (1.0 / members)
                spread = values - mean
                weight = omega[k, pl.ds(begin + t, 1), :]
                shift = eta[k, pl.ds(begin + t, 1), :] - weight * mean
                tail = lax.broadcasted_iota(jnp.int32, (LANES - members, ny), 0)
                weighted = jnp.concatenate(
                    [spread * weight, jnp.where(tail == 0, shift, 0.0)], axis=0
                )
                return total + dot_parts(split(spread), split(weighted), NT)

            out[k] = lax.fori_loop(0, span * nz, tile, jnp.zeros(out.shape[1:], f32), unroll=4)

    row = lax.broadcasted_iota(jnp.int32, (members, LANES), 0)
    column = lax.broadcasted_iota(jnp.int32, (members, LANES), 1)
    above, below = out[0], out[1]

    def pick(where, x):
        return jnp.sum(jnp.where(where, x, 0.0), axis=1, keepdims=True)

    both = jnp.where(column >= row, above, below)
    both = jnp.where(column == members, pick(column == row, below), both)
    both = jnp.where(column == members + 1, pick(column == members, above), both)
    packed[...] = jnp.where(column == members + 2, pick(column == members, below), both)


def gram(place, owner, omega, eta, sources, offsets, halves, ready):
    _, _, rows, ny = sources[0].shape
    members = rows * len(sources)
    count = omega.shape[0]

    def body(*refs):
        inputs = 4 + len(sources)
        gram_kernel(
            *refs[:inputs], *refs[inputs + len(ready) :], offsets=offsets, halves=halves
        )

    return pl.pallas_call(
        body,
        out_shape=jax.ShapeDtypeStruct((members, LANES), f32),
        in_specs=[SMEM, SMEM, VMEM, VMEM]
        + [VMEM] * len(sources)
        + [pl.BlockSpec(memory_space=pl.ANY)] * len(ready),
        out_specs=VMEM,
        scratch_shapes=[pltpu.VMEM((count, members, LANES), f32), pltpu.VMEM((members, ny), f32)],
        compiler_params=pltpu.CompilerParams(vmem_limit_bytes=SCOPED),
        name="gram",
    )(place, owner, omega, eta, *sources, *ready)


def turned(x):
    rows = x.shape[0]
    whole = jnp.concatenate([x, jnp.zeros((LANES - rows, LANES), f32)], axis=0)
    return whole.T[:rows]


def batch_transform(extended, total, members):
    row = lax.broadcasted_iota(jnp.int32, extended.shape, 0)
    column = lax.broadcasted_iota(jnp.int32, extended.shape, 1)
    inside = column < members
    last = column == members
    identity = jnp.where(row == column, 1.0, 0.0)
    matrix = jnp.where(inside, extended, 0.0)

    mean = jnp.sum(total, axis=1, keepdims=True) * (1.0 / members)
    centred = jnp.where(inside, total - mean, 0.0)
    product = wide_dot(wide_left(matrix), wide_right(jnp.where(last, mean, centred)))
    product = jnp.where(last, extended - product, product)
    product = wide_dot(wide_left(turned(centred)), wide_right(product)) * (1.0 / (members - 1))
    innovation = jnp.sum(jnp.where(last, product, 0.0), axis=1, keepdims=True)
    system = identity + jnp.where(inside, product, 0.0)
    frobenius = jnp.sqrt(jnp.sum(jnp.sum(system * system, axis=1, keepdims=True), axis=0, keepdims=True))

    scaled_root = system / frobenius
    factor = 1.5 * identity - 0.5 * scaled_root
    scaled_root = wide_dot(wide_left(scaled_root), wide_right(factor))
    inverse_root = factor

    def newton(iteration, iterates):
        scaled_root, inverse_root = iterates
        factor = 1.5 * identity - 0.5 * wide_dot(
            wide_left(inverse_root), wide_right(scaled_root)
        )
        return (
            wide_dot(wide_left(scaled_root), wide_right(factor)),
            wide_dot(wide_left(factor), wide_right(inverse_root)),
        )

    scaled_root, inverse_root = lax.fori_loop(1, NEWTON, newton, (scaled_root, inverse_root), unroll=UNROLL)
    root_inv = inverse_root / jnp.sqrt(frobenius)
    mean_weight = jnp.sum(root_inv * innovation, axis=0, keepdims=True)
    mean_weight = jnp.sum(root_inv * mean_weight, axis=1, keepdims=True)
    mixing = jnp.where(inside, root_inv + mean_weight, 0.0)
    mixing = mixing - jnp.sum(mixing, axis=0, keepdims=True) * (1.0 / members)
    mixing = jnp.where(inside, mixing + 1.0 / members, 0.0)
    return wide_dot(wide_left(total), wide_right(mixing))


def unpack(place, shares, groups, ordered):
    members = ordered.shape[1]
    row = lax.broadcasted_iota(jnp.int32, (members, LANES), 0)
    column = lax.broadcasted_iota(jnp.int32, (members, LANES), 1)
    inside = column < members

    def pick(where, x):
        return jnp.sum(jnp.where(where, x, 0.0), axis=1, keepdims=True)

    for half, group in zip((place[0], 1 - place[0]), groups(place[2])):
        packed = sum(shares[k] for k in group)
        above = jnp.where(inside & (column > row), packed, 0.0)
        below = jnp.where(inside & (column < row), packed, 0.0)
        middle = jnp.where(column == row, packed, 0.0)
        side = jnp.where(column == members, pick(column == members + 1, packed), 0.0)
        ordered[2 * half] = above + turned(above) + (middle + side)
        middle = jnp.where(column == row, pick(column == members, packed), 0.0)
        side = jnp.where(column == members, pick(column == members + 2, packed), 0.0)
        ordered[2 * half + 1] = below + turned(below) + (middle + side)


def early_kernel(place, shares, total, last, ordered, *, groups):
    unpack(place, shares, groups, ordered)
    batches, members, _ = ordered.shape
    row = lax.broadcasted_iota(jnp.int32, (members, LANES), 0)
    column = lax.broadcasted_iota(jnp.int32, (members, LANES), 1)
    product = jnp.where(row == column, 1.0, 0.0)
    for batch in range(batches - 1):
        product = batch_transform(ordered[batch], product, members)
    total[...] = product
    last[...] = ordered[batches - 1]


def late_kernel(place, total, last, out, work, *, offsets, blocks, rows):
    members = total.shape[0]
    product = batch_transform(last[...], total[...], members)
    rest = jnp.zeros((LANES - members, LANES), f32)
    work[...] = jnp.concatenate([product, rest], axis=0)
    if blocks == 1:
        out[...] = work[...].T
        return
    parts = [
        work[pl.ds(pl.multiple_of(offsets(place[2], j), 8), rows), :] for j in range(blocks)
    ]
    work[...] = jnp.concatenate([*parts, rest], axis=0).T
    out[...] = work[pl.ds(pl.multiple_of(offsets(place[2], 0), 8), rows), :]


def transform_call(kernel, name, out_shape, scratch, inputs):
    many = isinstance(out_shape, list)
    return pl.pallas_call(
        kernel,
        out_shape=out_shape,
        in_specs=[SMEM] + [VMEM] * (len(inputs) - 1),
        out_specs=[VMEM] * len(out_shape) if many else VMEM,
        scratch_shapes=[pltpu.VMEM(shape, f32) for shape in scratch],
        compiler_params=pltpu.CompilerParams(vmem_limit_bytes=SCOPED),
        cost_estimate=pl.CostEstimate(
            flops=10**8, bytes_accessed=10**6, transcendentals=0
        ),
        name=name,
    )(*inputs)


def mix_kernel(place, weights, *refs, blocks, halves):
    *sources, out = refs
    rows, species, _, nz, _ = out.shape
    step = pl.program_id(0)
    span = pl.num_programs(0) // halves
    free, conserved, internal, *tracers = [
        sources[k : k + blocks] for k in range(0, len(sources), blocks)
    ]
    members = blocks * free[0].shape[2]
    high, low = split(weights[:, :members])
    both = jnp.concatenate([high.astype(f32), low.astype(f32)], axis=0).astype(bf16)
    mul = functools.partial(
        lax.dot_general, dimension_numbers=(NN, ((), ())), preferred_element_type=f32
    )

    def mixed(held, x, z):
        parts = [array[x, z] for array in held]
        values = parts[0] if blocks == 1 else jnp.concatenate(parts, axis=0)
        value_high, value_low = split(values)
        upper = mul(both, value_high)
        return upper[:rows] + (upper[rows:] + mul(high, value_low))

    for part in range(halves):

        @pl.when(step // span == part)
        def _(part=part):
            at = step % span
            x = at if halves == 1 else half_begin(place, part, span) + at
            for z in range(nz):
                tracer = mixed(tracers[part], at, z)
                inside = mixed(internal, x, z)
                out[:, 0, 0, z, :] = mixed(free, x, z)
                out[:, 1, 0, z, :] = mixed(conserved, x, z) - tracer
                out[:, 2, 0, z, :] = tracer - inside
                out[:, 3, 0, z, :] = inside


def half_begin(place, part, span):
    return jnp.bitwise_xor(part, lax.shift_right_logical(place[2], 1)) * span


def mix(place, weights, sources, blocks, halves, shape):
    rows, species, nx, nz, ny = shape
    span = nx // halves

    def at(step, place):
        if halves == 1:
            return (0, 0, step, 0, 0)
        return (0, 0, half_begin(place, step // span, span) + step % span, 0, 0)

    return pl.pallas_call(
        functools.partial(mix_kernel, blocks=blocks, halves=halves),
        grid_spec=pltpu.PrefetchScalarGridSpec(
            num_scalar_prefetch=1,
            grid=(nx,),
            in_specs=[VMEM] * (1 + len(sources)),
            out_specs=pl.BlockSpec((rows, species, 1, nz, ny), at),
        ),
        out_shape=jax.ShapeDtypeStruct(shape, f32),
        compiler_params=pltpu.CompilerParams(vmem_limit_bytes=SCOPED),
        name="mix",
    )(place, weights, *sources)


def swap(x, axis, bit):
    count = lax.axis_size(axis)
    return lax.ppermute(x, axis, [(k, k ^ bit) for k in range(count)])


def total_over(x, axis):
    bit = 1
    while bit < lax.axis_size(axis):
        x = x + swap(x, axis, bit)
        bit *= 2
    return x


def local(ensemble, diffusivity, binding, source, obs_index, owner, observed, obs_var):
    rows, species, nx, nz, ny = ensemble.shape
    devices = lax.axis_size("member")
    spaces = lax.axis_size("space")
    members = rows * devices
    batches = owner.shape[0]
    member = lax.axis_index("member")
    place = jnp.stack([member & 1, lax.axis_index("space"), member]).astype(jnp.int32)

    forward = [(k, k + 1) for k in range(spaces - 1)]
    backward = [(k + 1, k) for k in range(spaces - 1)]

    def halos(first, last):
        return lax.ppermute(last, "space", forward), lax.ppermute(first, "space", backward)

    if devices == 4 and rows % 8 == 0 and nx % 2 == 0:
        blocks, halves = devices, 2

        def offsets(position, j):
            return jnp.bitwise_xor(position, j) * rows

        def groups(position):
            flip = functools.partial(jnp.bitwise_xor, position)
            return (position, flip(2)), (flip(1), flip(3))

        def collect(x, sent=None):
            return [x, swap(x, "member", 1), swap(x if sent is None else sent, "member", 2)]

        def complete(held, *after):
            return [*held, swap(lax.optimization_barrier((held[2], *after))[0], "member", 1)]
    else:
        blocks, halves = 1, 1

        def offsets(position, j):
            return 0

        def groups(position):
            return (0,), (1,)

        def collect(x):
            return [lax.all_gather(x, "member", axis=2, tiled=True)]

        def complete(held, *after):
            return held

    def across(held):
        return held[min(2, blocks - 1)]

    def tie(x, *after):
        return lax.optimization_barrier((x, *after))[0]

    whole, plane = (nx, nz, rows, ny), (nz, rows, ny)
    coefficients = (diffusivity, binding, source)
    cells = nx * nz * rows * ny
    ends = [
        jnp.transpose(ensemble[:, :3, part], (1, 2, 3, 0, 4))
        for part in (slice(0, 2), slice(nx - 2, nx))
    ]
    edges = forecast_call(
        first_edges_kernel,
        "first_edges",
        [*ends, *coefficients],
        [(nz, 2 * rows + 8, ny)] * 2,
        2 * cells // nx,
    )
    fields = [jnp.transpose(ensemble[:, k], (1, 2, 0, 3)) for k in range(species)]
    conserved = fields[1] + fields[2] + fields[3]
    omega, eta = voxel_weights(
        place, owner, obs_index, observed, obs_var, batches // 2, nx * nz, ny
    )
    around = origin = halos(*edges)
    steps = SUBSTEPS // 2 - 1
    for step in range(steps):
        lean = step == steps - 1
        *fields, first, last = forecast_call(
            functools.partial(two_substeps_kernel, lean=lean),
            "two_substeps",
            [*fields, *around, *origin, *coefficients],
            [whole] * 4 + [plane if lean else (nz, 2 * rows, ny)] * 2,
            2 * cells,
            scratch=[whole],
            ready=(omega, eta) if step == 0 else (),
        )
        around = halos(first, last)
        if step == 0:
            conserved = collect(tie(conserved, fields[0]))
    *tracers, internal, free, add, first, last = forecast_call(
        functools.partial(last_but_one_kernel, halves=halves),
        "last_but_one",
        [*fields, *around, *coefficients],
        [(nx // halves, nz, rows, ny)] * halves + [whole] * 3 + [plane] * 2,
        2 * cells,
        scratch=[whole] * 3,
        ready=conserved[1:],
        scalars=[place],
    )
    if halves == 2:
        near, far = tracers
        near = complete(collect(near, far))
    else:
        near = collect(tracers[0])
    (free,) = forecast_call(
        last_free_kernel,
        "last_free",
        [free, add, *halos(first, last), diffusivity],
        [whole],
        cells,
    )
    conserved = complete(conserved, across(near), free)
    internal = collect(tie(internal, across(near), free))
    half = total_over(gram(place, owner, omega, eta, near, offsets, halves, [free]), "space")
    if halves == 2:
        half = tie(half, across(internal))
        shares = lax.all_to_all(
            jnp.broadcast_to(half, (devices, *half.shape)), "member", 0, 0
        )
        far = collect(tie(far, shares), tie(tracers[0], shares))
        free = collect(tie(free, shares))
    else:
        free = collect(free)
        shares = jnp.stack([half, swap(half, "member", 1)])
    internal = complete(internal, half)
    square = jax.ShapeDtypeStruct((members, LANES), f32)
    total, extended = transform_call(
        functools.partial(early_kernel, groups=groups),
        "transforms_early",
        [square, square],
        [(batches, members, LANES)],
        [place, shares],
    )
    if halves == 2:
        far = complete(far, total)
    free = complete(free, total)
    weights = transform_call(
        functools.partial(late_kernel, offsets=offsets, blocks=blocks, rows=rows),
        "transforms_late",
        jax.ShapeDtypeStruct((LANES, LANES) if blocks == 1 else (rows, LANES), f32),
        [(LANES, LANES)],
        [place, total, extended],
    )
    if blocks == 1:
        weights = lax.dynamic_slice(weights, (member * rows, 0), (rows, LANES))
    sources = free + conserved + internal + near + (far if halves == 2 else [])
    return mix(place, weights, sources, blocks, halves, ensemble.shape)


def solution(mesh):
    in_specs = (
        P("member", None, "space", None, None),
        P("space", None, None),
        P("space", None, None),
        P("space", None, None),
        P(),
        P(),
        P(),
        P(),
    )
    out_specs = P("member", None, "space", None, None)
    return jax.shard_map(local, mesh=mesh, in_specs=in_specs, out_specs=out_specs, check_vma=False)
```

```python
import functools

import jax
import jax.numpy as jnp
from jax import lax
from jax.experimental import pallas as pl
from jax.experimental.pallas import tpu as pltpu
from jax.sharding import PartitionSpec as P

SUBSTEPS = 6
NEWTON = 16
UNROLL = 15
LANES = 128
SCOPED = 5 * 2**20

unbind_rate = 0.05
uptake_rate = 0.1
recycle_rate = 0.02

VMEM = pl.BlockSpec(memory_space=pltpu.VMEM)
SMEM = pl.BlockSpec(memory_space=pltpu.SMEM)
bf16 = jnp.bfloat16
f32 = jnp.float32


def split(x):
    high = x.astype(bf16)
    return high, (x - high.astype(f32)).astype(bf16)


def dot_parts(a, b, dims):
    a_high, a_low = a
    b_high, b_low = b
    mul = functools.partial(
        lax.dot_general, dimension_numbers=(dims, ((), ())), preferred_element_type=f32
    )
    return mul(a_high, b_high) + (mul(a_high, b_low) + mul(a_low, b_high))


def wide_left(x):
    return jnp.concatenate(split(x), axis=1)


def wide_right(x):
    both = jnp.concatenate(split(x), axis=1)
    rows, lanes = both.shape
    if rows < lanes // 2:
        both = jnp.concatenate([both, jnp.zeros((lanes // 2 - rows, lanes), bf16)], axis=0)
    return jnp.concatenate([both, both], axis=0)


def wide_dot(left, right):
    out = jnp.dot(left, right, preferred_element_type=f32)
    side = out.shape[1] // 2
    return out[:, :side] + out[:, side:]


NN = ((1,), (0,))
NT = ((1,), (1,))


def react(free, receptor, complexed, internal, binding):
    flux = binding * free * receptor
    back = unbind_rate * complexed - flux
    return (
        back,
        receptor + back + recycle_rate * internal,
        complexed + flux - (unbind_rate + uptake_rate) * complexed,
        internal + uptake_rate * complexed - recycle_rate * internal,
    )


def spread_free(free, planes, neighbours, diffusivity):
    lane = lax.broadcasted_iota(jnp.int32, free.shape, 1)
    last = free.shape[1] - 1
    for plane in planes:
        neighbours = plane if neighbours is None else neighbours + plane
    neighbours += jnp.where(lane == last, 0.0, pltpu.roll(free, last, 1))
    neighbours += jnp.where(lane == 0, 0.0, pltpu.roll(free, 1, 1))
    return free + diffusivity * (neighbours - 6.0 * free)


def beside(read, x, z, nx, nz, low, high):
    around = [low if x == 0 else read(x - 1, z), high if x == nx - 1 else read(x + 1, z)]
    around += [read(x, other) for other in (z + 1, z - 1) if 0 <= other < nz]
    return [value for value in around if value is not None]


def edge_free(read, rest, x, nz, nx, z, diffusivity):
    return spread_free(read(x, z), beside(read, x, z, nx, nz, None, None), None, diffusivity) + rest


def first_edges_kernel(below, above, diffusivity, binding, source, first, last):
    _, _, nz, members, _ = below.shape
    nx = diffusivity.shape[0]
    for x, ends, out in ((0, below, first), (nx - 1, above, last)):
        shift = 0 if x == 0 else nx - 2

        def read(at, z, ends=ends, shift=shift):
            return ends[0, at - shift, z]

        for z in range(nz):
            row = pl.ds(z, 1)
            free = read(x, z)
            flux = binding[x, row, :] * free * ends[1, x - shift, z]
            rest = unbind_rate * ends[2, x - shift, z] - flux + source[x, row, :]
            spread = diffusivity[x, row, :]
            out[z, :members, :] = free
            out[z, members : 2 * members, :] = edge_free(read, rest, x, nz, nx, z, spread)
            out[z, 2 * members :, :] = jnp.broadcast_to(spread, (8, spread.shape[1]))


def first_substep(
    a, r, c, i, low, high, diffusivity, binding, source, out_a, out_r, out_c, out_i
):
    nx, nz, _, _ = a.shape
    for x in range(nx):
        for z in range(nz):
            row = pl.ds(z, 1)
            back, out_r[x, z], out_c[x, z], out_i[x, z] = react(
                a[x, z], r[x, z], c[x, z], i[x, z], binding[x, row, :]
            )
            around = beside(lambda x, z: a[x, z], x, z, nx, nz, low(z), high(z))
            out_a[x, z] = (
                spread_free(a[x, z], around, None, diffusivity[x, row, :])
                + back
                + source[x, row, :]
            )


def two_substeps_kernel(
    place, a, r, c, i, low, high, low_first, high_first, diffusivity, binding, source, *refs, halves
):
    if halves is None:
        out_a, out_r, out_c, out_i, first, last, middle = refs
        mid_r, mid_c, mid_i = out_r, out_c, out_i
    else:
        *tracers, out_i, out_a, middle, mid_r, mid_c, mid_i = refs
    nx, nz, members, _ = a.shape
    first_substep(
        a,
        r,
        c,
        i,
        lambda z: low[z, :members, :],
        lambda z: high[z, :members, :],
        diffusivity,
        binding,
        source,
        middle,
        mid_r,
        mid_c,
        mid_i,
    )
    if halves is not None:
        span = nx // halves
        for part, tracer in enumerate(tracers):
            begin = half_begin(place, part, span)
            for j in range(span):
                x = j if halves == 1 else begin + j
                for z in range(nz):
                    _, _, complexed, internal = react(
                        middle[x, z], mid_r[x, z], mid_c[x, z], mid_i[x, z], binding[x, pl.ds(z, 1), :]
                    )
                    tracer[j, z] = complexed + internal
                    out_i[x, z] = internal

    def outside(halo, origin, x, z):
        later = halo[z, members : 2 * members, :]
        return later + origin[z, 2 * members : 2 * members + 1, :] * a[x, z]

    for x in range(nx):
        for z in range(nz):
            row = pl.ds(z, 1)
            if halves is None:
                back, out_r[x, z], out_c[x, z], out_i[x, z] = react(
                    middle[x, z], out_r[x, z], out_c[x, z], out_i[x, z], binding[x, row, :]
                )
            else:
                back = react(middle[x, z], mid_r[x, z], mid_c[x, z], 0.0, binding[x, row, :])[0]
            around = beside(
                lambda x, z: middle[x, z],
                x,
                z,
                nx,
                nz,
                outside(low, low_first, x, z) if x == 0 else None,
                outside(high, high_first, x, z) if x == nx - 1 else None,
            )
            out_a[x, z] = (
                spread_free(middle[x, z], around, None, diffusivity[x, row, :])
                + back
                + source[x, row, :]
            )
    if halves is not None:
        return
    for x, out in ((0, first), (nx - 1, last)):
        for z in range(nz):
            row = pl.ds(z, 1)
            free = out_a[x, z]
            flux = binding[x, row, :] * free * out_r[x, z]
            rest = unbind_rate * out_c[x, z] - flux + source[x, row, :]
            out[z, :members, :] = free
            out[z, members:, :] = edge_free(
                lambda x, z: out_a[x, z], rest, x, nz, nx, z, diffusivity[x, row, :]
            )


def half_begin(place, part, span):
    return jnp.bitwise_xor(part, lax.shift_right_logical(place[2], 1)) * span


def forecast_call(kernel, name, inputs, outputs, cells, scratch=(), ready=(), scalars=()):
    def body(*refs):
        count = len(scalars) + len(inputs)
        kernel(*refs[:count], *refs[count + len(ready) :])

    return pl.pallas_call(
        body,
        out_shape=[jax.ShapeDtypeStruct(shape, f32) for shape in outputs],
        in_specs=[SMEM] * len(scalars)
        + [VMEM] * len(inputs)
        + [pl.BlockSpec(memory_space=pl.ANY)] * len(ready),
        out_specs=[VMEM] * len(outputs),
        scratch_shapes=[pltpu.VMEM(shape, f32) for shape in scratch],
        compiler_params=pltpu.CompilerParams(vmem_limit_bytes=SCOPED),
        cost_estimate=pl.CostEstimate(
            flops=30 * cells, bytes_accessed=32 * cells, transcendentals=0
        ),
        name=name,
    )(*scalars, *inputs, *ready)


def weights_kernel(place, owner, obs_index, observed, obs_var, omega, eta):
    count, rows, ny = omega.shape
    batch_size = obs_index.shape[1]
    for k in range(count):
        batch = place[0] * count + k
        mine = owner[batch] == place[1]
        line = pl.ds(batch, 1)
        voxel = obs_index[line, :]
        scale = jnp.where(mine, 1.0, 0.0) / obs_var[line, :]
        shift = ny.bit_length() - 1
        row = lax.shift_right_logical(voxel, shift)
        column = jnp.bitwise_and(voxel, ny - 1)
        at_row = lax.broadcasted_iota(jnp.int32, (rows, batch_size), 0) == row
        at_column = lax.broadcasted_iota(jnp.int32, (ny, batch_size), 0) == column
        both = jnp.concatenate(
            [jnp.where(at_row, scale, 0.0), jnp.where(at_row, scale * observed[line, :], 0.0)],
            axis=0,
        )
        one = both.astype(bf16)
        rest = both - one.astype(f32)
        two = rest.astype(bf16)
        three = (rest - two.astype(f32)).astype(bf16)
        columns = jnp.where(at_column, 1.0, 0.0).astype(bf16)
        sums = lax.dot_general(
            jnp.concatenate([one, two, three], axis=0),
            columns,
            (NT, ((), ())),
            preferred_element_type=f32,
        )
        sums = sums[: 2 * rows] + sums[2 * rows : 4 * rows] + sums[4 * rows :]
        omega[k] = sums[:rows]
        eta[k] = sums[rows:]


def voxel_weights(place, owner, obs_index, observed, obs_var, count, rows, ny):
    out = jax.ShapeDtypeStruct((count, rows, ny), f32)
    return pl.pallas_call(
        weights_kernel,
        out_shape=[out, out],
        in_specs=[SMEM, SMEM, VMEM, VMEM, VMEM],
        out_specs=[VMEM, VMEM],
        compiler_params=pltpu.CompilerParams(vmem_limit_bytes=SCOPED),
        name="voxel_weights",
    )(place, owner, obs_index, observed, obs_var)


def gram_kernel(place, owner, omega, eta, *refs, offsets, halves):
    *sources, packed, out, members_at = refs
    count = out.shape[0]
    span, nz, rows, ny = sources[0].shape
    members = members_at.shape[0]
    begin = 0 if halves == 1 else lax.shift_right_logical(place[2], 1) * (span * nz)
    for k in range(count):
        out[k] = jnp.zeros(out.shape[1:], f32)

        @pl.when(owner[place[0] * count + k] == place[1])
        def _(k=k):
            def tile(t, total):
                x, z = t // nz, t % nz
                for j, source in enumerate(sources):
                    start = pl.multiple_of(offsets(place[2], j), 8)
                    members_at[pl.ds(start, rows), :] = source[x, z]
                values = members_at[...]
                mean = jnp.sum(values, axis=0, keepdims=True) * (1.0 / members)
                spread = values - mean
                weight = omega[k, pl.ds(begin + t, 1), :]
                shift = eta[k, pl.ds(begin + t, 1), :] - weight * mean
                tail = lax.broadcasted_iota(jnp.int32, (LANES - members, ny), 0)
                weighted = jnp.concatenate(
                    [spread * weight, jnp.where(tail == 0, shift, 0.0)], axis=0
                )
                return total + dot_parts(split(spread), split(weighted), NT)

            out[k] = lax.fori_loop(0, span * nz, tile, jnp.zeros(out.shape[1:], f32), unroll=4)

    row = lax.broadcasted_iota(jnp.int32, (members, LANES), 0)
    column = lax.broadcasted_iota(jnp.int32, (members, LANES), 1)
    above, below = out[0], out[1]

    def pick(where, x):
        return jnp.sum(jnp.where(where, x, 0.0), axis=1, keepdims=True)

    both = jnp.where(column >= row, above, below)
    both = jnp.where(column == members, pick(column == row, below), both)
    both = jnp.where(column == members + 1, pick(column == members, above), both)
    packed[...] = jnp.where(column == members + 2, pick(column == members, below), both)


def gram(place, owner, omega, eta, sources, offsets, halves, ready):
    _, _, rows, ny = sources[0].shape
    members = rows * len(sources)
    count = omega.shape[0]

    def body(*refs):
        inputs = 4 + len(sources)
        gram_kernel(
            *refs[:inputs], *refs[inputs + len(ready) :], offsets=offsets, halves=halves
        )

    return pl.pallas_call(
        body,
        out_shape=jax.ShapeDtypeStruct((members, LANES), f32),
        in_specs=[SMEM, SMEM, VMEM, VMEM]
        + [VMEM] * len(sources)
        + [pl.BlockSpec(memory_space=pl.ANY)] * len(ready),
        out_specs=VMEM,
        scratch_shapes=[pltpu.VMEM((count, members, LANES), f32), pltpu.VMEM((members, ny), f32)],
        compiler_params=pltpu.CompilerParams(vmem_limit_bytes=SCOPED),
        name="gram",
    )(place, owner, omega, eta, *sources, *ready)


def turned(x):
    rows = x.shape[0]
    whole = jnp.concatenate([x, jnp.zeros((LANES - rows, LANES), f32)], axis=0)
    return whole.T[:rows]


def batch_transform(extended, total, members):
    row = lax.broadcasted_iota(jnp.int32, extended.shape, 0)
    column = lax.broadcasted_iota(jnp.int32, extended.shape, 1)
    inside = column < members
    last = column == members
    identity = jnp.where(row == column, 1.0, 0.0)
    matrix = jnp.where(inside, extended, 0.0)

    mean = jnp.sum(total, axis=1, keepdims=True) * (1.0 / members)
    centred = jnp.where(inside, total - mean, 0.0)
    product = wide_dot(wide_left(matrix), wide_right(jnp.where(last, mean, centred)))
    product = jnp.where(last, extended - product, product)
    product = wide_dot(wide_left(turned(centred)), wide_right(product)) * (1.0 / (members - 1))
    innovation = jnp.sum(jnp.where(last, product, 0.0), axis=1, keepdims=True)
    system = identity + jnp.where(inside, product, 0.0)
    frobenius = jnp.sqrt(jnp.sum(jnp.sum(system * system, axis=1, keepdims=True), axis=0, keepdims=True))

    scaled_root = system / frobenius
    factor = 1.5 * identity - 0.5 * scaled_root
    scaled_root = wide_dot(wide_left(scaled_root), wide_right(factor))
    inverse_root = factor

    def newton(iteration, iterates):
        scaled_root, inverse_root = iterates
        factor = 1.5 * identity - 0.5 * wide_dot(
            wide_left(inverse_root), wide_right(scaled_root)
        )
        return (
            wide_dot(wide_left(scaled_root), wide_right(factor)),
            wide_dot(wide_left(factor), wide_right(inverse_root)),
        )

    scaled_root, inverse_root = lax.fori_loop(1, NEWTON, newton, (scaled_root, inverse_root), unroll=UNROLL)
    root_inv = inverse_root / jnp.sqrt(frobenius)
    mean_weight = jnp.sum(root_inv * innovation, axis=0, keepdims=True)
    mean_weight = jnp.sum(root_inv * mean_weight, axis=1, keepdims=True)
    mixing = jnp.where(inside, root_inv + mean_weight, 0.0)
    mixing = mixing - jnp.sum(mixing, axis=0, keepdims=True) * (1.0 / members)
    mixing = jnp.where(inside, mixing + 1.0 / members, 0.0)
    return wide_dot(wide_left(total), wide_right(mixing))


def transform_kernel(place, mine, other, out, ordered, work, *, offsets, blocks, rows):
    members = mine.shape[0]
    row = lax.broadcasted_iota(jnp.int32, (members, LANES), 0)
    column = lax.broadcasted_iota(jnp.int32, (members, LANES), 1)
    inside = column < members

    def pick(where, x):
        return jnp.sum(jnp.where(where, x, 0.0), axis=1, keepdims=True)

    for half, shared in ((place[0], mine), (1 - place[0], other)):
        packed = shared[...]
        above = jnp.where(inside & (column > row), packed, 0.0)
        below = jnp.where(inside & (column < row), packed, 0.0)
        middle = jnp.where(column == row, packed, 0.0)
        side = jnp.where(column == members, pick(column == members + 1, packed), 0.0)
        ordered[2 * half] = above + turned(above) + (middle + side)
        middle = jnp.where(column == row, pick(column == members, packed), 0.0)
        side = jnp.where(column == members, pick(column == members + 2, packed), 0.0)
        ordered[2 * half + 1] = below + turned(below) + (middle + side)
    total = jnp.where(row == column, 1.0, 0.0)
    for batch in range(ordered.shape[0]):
        total = batch_transform(ordered[batch], total, members)
    rest = jnp.zeros((LANES - members, LANES), f32)
    work[...] = jnp.concatenate([total, rest], axis=0)
    if blocks == 1:
        out[...] = work[...].T
        return
    parts = [
        work[pl.ds(pl.multiple_of(offsets(place[2], j), 8), rows), :] for j in range(blocks)
    ]
    work[...] = jnp.concatenate([*parts, rest], axis=0).T
    out[...] = work[pl.ds(pl.multiple_of(offsets(place[2], 0), 8), rows), :]


def transforms(place, mine, other, offsets, blocks, rows):
    members = mine.shape[0]
    shape = (LANES, LANES) if blocks == 1 else (rows, LANES)
    return pl.pallas_call(
        functools.partial(transform_kernel, offsets=offsets, blocks=blocks, rows=rows),
        out_shape=jax.ShapeDtypeStruct(shape, f32),
        in_specs=[SMEM, VMEM, VMEM],
        out_specs=VMEM,
        scratch_shapes=[
            pltpu.VMEM((4, members, LANES), f32),
            pltpu.VMEM((LANES, LANES), f32),
        ],
        compiler_params=pltpu.CompilerParams(vmem_limit_bytes=SCOPED),
        cost_estimate=pl.CostEstimate(
            flops=10**8, bytes_accessed=10**6, transcendentals=0
        ),
        name="transforms",
    )(place, mine, other)


def mix_kernel(place, weights, *refs, blocks, halves):
    *sources, out = refs
    rows, species, _, nz, _ = out.shape
    step = pl.program_id(0)
    span = pl.num_programs(0) // halves
    free, conserved, internal, *tracers = [
        sources[k : k + blocks] for k in range(0, len(sources), blocks)
    ]
    members = blocks * free[0].shape[2]
    high, low = split(weights[:, :members])
    both = jnp.concatenate([high.astype(f32), low.astype(f32)], axis=0).astype(bf16)
    mul = functools.partial(
        lax.dot_general, dimension_numbers=(NN, ((), ())), preferred_element_type=f32
    )

    def mixed(held, x, z):
        parts = [array[x, z] for array in held]
        values = parts[0] if blocks == 1 else jnp.concatenate(parts, axis=0)
        value_high, value_low = split(values)
        upper = mul(both, value_high)
        return upper[:rows] + (upper[rows:] + mul(high, value_low))

    for part in range(halves):

        @pl.when(step // span == part)
        def _(part=part):
            at = step % span
            x = at if halves == 1 else half_begin(place, part, span) + at
            for z in range(nz):
                tracer = mixed(tracers[part], at, z)
                inside = mixed(internal, x, z)
                out[:, 0, 0, z, :] = mixed(free, x, z)
                out[:, 1, 0, z, :] = mixed(conserved, x, z) - tracer
                out[:, 2, 0, z, :] = tracer - inside
                out[:, 3, 0, z, :] = inside


def mix(place, weights, sources, blocks, halves, shape):
    rows, species, nx, nz, ny = shape
    span = nx // halves

    def at(step, place):
        if halves == 1:
            return (0, 0, step, 0, 0)
        return (0, 0, half_begin(place, step // span, span) + step % span, 0, 0)

    return pl.pallas_call(
        functools.partial(mix_kernel, blocks=blocks, halves=halves),
        grid_spec=pltpu.PrefetchScalarGridSpec(
            num_scalar_prefetch=1,
            grid=(nx,),
            in_specs=[VMEM] * (1 + len(sources)),
            out_specs=pl.BlockSpec((rows, species, 1, nz, ny), at),
        ),
        out_shape=jax.ShapeDtypeStruct(shape, f32),
        compiler_params=pltpu.CompilerParams(vmem_limit_bytes=SCOPED),
        name="mix",
    )(place, weights, *sources)


def swap(x, axis, bit):
    count = lax.axis_size(axis)
    return lax.ppermute(x, axis, [(k, k ^ bit) for k in range(count)])


def total_over(x, axis):
    bit = 1
    while bit < lax.axis_size(axis):
        x = x + swap(x, axis, bit)
        bit *= 2
    return x


def local(ensemble, diffusivity, binding, source, obs_index, owner, observed, obs_var):
    rows, species, nx, nz, ny = ensemble.shape
    devices = lax.axis_size("member")
    spaces = lax.axis_size("space")
    members = rows * devices
    batches = owner.shape[0]
    member = lax.axis_index("member")
    place = jnp.stack([member & 1, lax.axis_index("space"), member]).astype(jnp.int32)

    forward = [(k, k + 1) for k in range(spaces - 1)]
    backward = [(k + 1, k) for k in range(spaces - 1)]

    def halos(first, last):
        return lax.ppermute(last, "space", forward), lax.ppermute(first, "space", backward)

    if devices == 4 and rows % 8 == 0 and nx % 2 == 0:
        blocks, halves = devices, 2

        def offsets(position, j):
            return jnp.bitwise_xor(position, j) * rows

        def collect(x, sent=None):
            return [x, swap(x, "member", 1), swap(x if sent is None else sent, "member", 2)]

        def complete(held, *after):
            return [*held, swap(lax.optimization_barrier((held[2], *after))[0], "member", 1)]
    else:
        blocks, halves = 1, 1

        def offsets(position, j):
            return 0

        def collect(x):
            return [lax.all_gather(x, "member", axis=2, tiled=True)]

        def complete(held, *after):
            return held

    def across(held):
        return held[min(2, blocks - 1)]

    def tie(x, *after):
        return lax.optimization_barrier((x, *after))[0]

    whole = (nx, nz, rows, ny)
    coefficients = (diffusivity, binding, source)
    cells = nx * nz * rows * ny
    ends = [
        jnp.transpose(ensemble[:, :3, part], (1, 2, 3, 0, 4))
        for part in (slice(0, 2), slice(nx - 2, nx))
    ]
    edges = forecast_call(
        first_edges_kernel,
        "first_edges",
        [*ends, *coefficients],
        [(nz, 2 * rows + 8, ny)] * 2,
        2 * cells // nx,
    )
    fields = [jnp.transpose(ensemble[:, k], (1, 2, 0, 3)) for k in range(species)]
    conserved = fields[1] + fields[2] + fields[3]
    omega, eta = voxel_weights(
        place, owner, obs_index, observed, obs_var, batches // 2, nx * nz, ny
    )
    around = origin = halos(*edges)
    steps = SUBSTEPS // 2
    for step in range(steps):
        final = step == steps - 1
        outputs = [whole] * 4 + [(nz, 2 * rows, ny)] * 2
        if final:
            outputs = [(nx // halves, nz, rows, ny)] * halves + [whole] * 2
        *fields, = forecast_call(
            functools.partial(two_substeps_kernel, halves=halves if final else None),
            "two_substeps",
            [*fields, *around, *origin, *coefficients],
            outputs,
            2 * cells,
            scratch=[whole] * (4 if final else 1),
            ready=(omega, eta) if step == 0 else conserved[1:] if final else (),
            scalars=[place],
        )
        if not final:
            around = halos(*fields[4:])
            fields = fields[:4]
        if step == 0:
            conserved = collect(tie(conserved, fields[0]))
    *tracers, internal, free = fields
    near = complete(collect(*tracers))
    conserved = complete(conserved, across(near))
    internal = collect(tie(internal, across(near)))
    half = total_over(gram(place, owner, omega, eta, near, offsets, halves, ()), "space")
    half = tie(half, across(internal))
    if halves == 2:
        half = half + swap(half, "member", 2)
        far = collect(tie(tracers[1], half), tie(tracers[0], half))
    free = collect(tie(free, half))
    internal = complete(internal, half)
    weights = transforms(place, half, swap(half, "member", 1), offsets, blocks, rows)
    free = complete(free, weights)
    if halves == 2:
        far = complete(far, weights)
    if blocks == 1:
        weights = lax.dynamic_slice(weights, (member * rows, 0), (rows, LANES))
    sources = free + conserved + internal + near + (far if halves == 2 else [])
    return mix(place, weights, sources, blocks, halves, ensemble.shape)


def solution(mesh):
    in_specs = (
        P("member", None, "space", None, None),
        P("space", None, None),
        P("space", None, None),
        P("space", None, None),
        P(),
        P(),
        P(),
        P(),
    )
    out_specs = P("member", None, "space", None, None)
    return jax.shard_map(local, mesh=mesh, in_specs=in_specs, out_specs=out_specs, check_vma=False)
```

```python
import functools

import jax
import jax.numpy as jnp
from jax import lax
from jax.experimental import pallas as pl
from jax.experimental.pallas import tpu as pltpu
from jax.sharding import PartitionSpec as P

SUBSTEPS = 6
NEWTON = 16
UNROLL = 5
LANES = 128
SCOPED = 10 * 2**20

unbind_rate = 0.05
uptake_rate = 0.1
recycle_rate = 0.02

VMEM = pl.BlockSpec(memory_space=pltpu.VMEM)
SMEM = pl.BlockSpec(memory_space=pltpu.SMEM)
bf16 = jnp.bfloat16
f32 = jnp.float32


def split(x):
    high = x.astype(bf16)
    return high, (x - high.astype(f32)).astype(bf16)


def dot_parts(a, b, dims):
    a_high, a_low = a
    b_high, b_low = b
    mul = functools.partial(
        lax.dot_general, dimension_numbers=(dims, ((), ())), preferred_element_type=f32
    )
    return mul(a_high, b_high) + (mul(a_high, b_low) + mul(a_low, b_high))


def wide_left(x):
    return jnp.concatenate(split(x), axis=1)


def wide_right(x):
    both = jnp.concatenate(split(x), axis=1)
    rows, lanes = both.shape
    if rows < lanes // 2:
        both = jnp.concatenate([both, jnp.zeros((lanes // 2 - rows, lanes), bf16)], axis=0)
    return jnp.concatenate([both, both], axis=0)


def wide_dot(left, right):
    out = jnp.dot(left, right, preferred_element_type=f32)
    side = out.shape[1] // 2
    return out[:, :side] + out[:, side:]


NN = ((1,), (0,))
NT = ((1,), (1,))


def react(free, receptor, complexed, internal, binding):
    flux = binding * free * receptor
    back = unbind_rate * complexed - flux
    return (
        back,
        receptor + back + recycle_rate * internal,
        complexed + flux - (unbind_rate + uptake_rate) * complexed,
        internal + uptake_rate * complexed - recycle_rate * internal,
    )


def spread_free(free, planes, neighbours, diffusivity):
    lane = lax.broadcasted_iota(jnp.int32, free.shape, 1)
    last = free.shape[1] - 1
    for plane in planes:
        neighbours = plane if neighbours is None else neighbours + plane
    neighbours += jnp.where(lane == last, 0.0, pltpu.roll(free, last, 1))
    neighbours += jnp.where(lane == 0, 0.0, pltpu.roll(free, 1, 1))
    return free + diffusivity * (neighbours - 6.0 * free)


def beside(read, x, z, nx, nz, low, high):
    around = [low if x == 0 else read(x - 1, z), high if x == nx - 1 else read(x + 1, z)]
    around += [read(x, other) for other in (z + 1, z - 1) if 0 <= other < nz]
    return [value for value in around if value is not None]


def edge_free(read, rest, x, nz, nx, z, diffusivity):
    return spread_free(read(x, z), beside(read, x, z, nx, nz, None, None), None, diffusivity) + rest


def first_edges_kernel(below, above, diffusivity, binding, source, first, last):
    _, _, nz, members, _ = below.shape
    nx = diffusivity.shape[0]
    for x, ends, out in ((0, below, first), (nx - 1, above, last)):
        shift = 0 if x == 0 else nx - 2

        def read(at, z, ends=ends, shift=shift):
            return ends[0, at - shift, z]

        for z in range(nz):
            row = pl.ds(z, 1)
            free = read(x, z)
            flux = binding[x, row, :] * free * ends[1, x - shift, z]
            rest = unbind_rate * ends[2, x - shift, z] - flux + source[x, row, :]
            spread = diffusivity[x, row, :]
            out[z, :members, :] = free
            out[z, members : 2 * members, :] = edge_free(read, rest, x, nz, nx, z, spread)
            out[z, 2 * members :, :] = jnp.broadcast_to(spread, (8, spread.shape[1]))


def step_planes(planes, a, r, c, i, outside, diffusivity, binding, source, out_a, outs, keep):
    nx, nz, _, _ = a.shape
    for x in planes:
        for z in range(nz):
            row = pl.ds(z, 1)
            back, *others = react(a[x, z], r[x, z], c[x, z], i[x, z], binding[x, row, :])
            around = beside(lambda x, z: a[x, z], x, z, nx, nz, *outside(x, z))
            out_a[x, z] = (
                spread_free(a[x, z], around, None, diffusivity[x, row, :])
                + back
                + source[x, row, :]
            )
            if x in keep:
                for out, value in zip(outs, others):
                    out[x, z] = value


def before_last(a, low, high):
    nx, _, members, _ = a.shape

    def outside(x, z):
        return (
            low[z, :members, :] if x == 0 else None,
            high[z, :members, :] if x == nx - 1 else None,
        )

    return outside


def after_first(a, low, high, low_first, high_first):
    nx, _, members, _ = a.shape

    def completed(halo, origin, x, z):
        later = halo[z, members : 2 * members, :]
        return later + origin[z, 2 * members : 2 * members + 1, :] * a[x, z]

    def outside(x, z):
        return (
            completed(low, low_first, x, z) if x == 0 else None,
            completed(high, high_first, x, z) if x == nx - 1 else None,
        )

    return outside


def next_edges_kernel(
    a, r, c, i, low, high, low_first, high_first, diffusivity, binding, source, *refs
):
    first, last, *kept = refs
    middle, later = kept[:4], kept[4:]
    nx, nz, members, _ = a.shape
    coefficients = (diffusivity, binding, source)

    def near(depth):
        return [x for x in range(nx) if min(x, nx - 1 - x) < depth]

    step_planes(
        near(3), a, r, c, i, before_last(a, low, high), *coefficients, middle[0], middle[1:], near(2)
    )
    step_planes(
        near(2),
        *middle,
        after_first(a, low, high, low_first, high_first),
        *coefficients,
        later[0],
        later[1:],
        near(1),
    )
    free, receptor, complexed = later[:3]
    for x, out in ((0, first), (nx - 1, last)):
        for z in range(nz):
            row = pl.ds(z, 1)
            flux = binding[x, row, :] * free[x, z] * receptor[x, z]
            rest = unbind_rate * complexed[x, z] - flux + source[x, row, :]
            out[z, :members, :] = free[x, z]
            out[z, members:, :] = edge_free(
                lambda x, z: free[x, z], rest, x, nz, nx, z, diffusivity[x, row, :]
            )


def two_substeps_kernel(
    a, r, c, i, low, high, low_first, high_first, diffusivity, binding, source, *refs
):
    outs, middle = refs[:4], refs[4:]
    everywhere = range(a.shape[0])
    coefficients = (diffusivity, binding, source)
    step_planes(
        everywhere,
        a,
        r,
        c,
        i,
        before_last(a, low, high),
        *coefficients,
        middle[0],
        middle[1:],
        everywhere,
    )
    step_planes(
        everywhere,
        *middle,
        after_first(a, low, high, low_first, high_first),
        *coefficients,
        outs[0],
        outs[1:],
        everywhere,
    )


def last_but_one_kernel(
    place, a, r, c, i, low, high, diffusivity, binding, source, *refs, halves
):
    *tracers, out_i, out_a, out_add, mid_r, mid_c, mid_i = refs
    nx, nz, _, _ = a.shape
    step_planes(
        range(nx),
        a,
        r,
        c,
        i,
        before_last(a, low, high),
        diffusivity,
        binding,
        source,
        out_a,
        (mid_r, mid_c, mid_i),
        range(nx),
    )
    span = nx // halves
    for part, tracer in enumerate(tracers):
        begin = half_begin(place, part, span)
        for j in range(span):
            x = j if halves == 1 else begin + j
            for z in range(nz):
                row = pl.ds(z, 1)
                back, _, complexed, internal = react(
                    out_a[x, z], mid_r[x, z], mid_c[x, z], mid_i[x, z], binding[x, row, :]
                )
                tracer[j, z] = complexed + internal
                out_i[x, z] = internal
                out_add[x, z] = back + source[x, row, :]


def last_free_kernel(
    before, a, add, low, high, low_first, high_first, diffusivity, out_a
):
    nx, nz, _, _ = a.shape
    outside = after_first(before, low, high, low_first, high_first)
    for x in range(nx):
        for z in range(nz):
            around = beside(lambda x, z: a[x, z], x, z, nx, nz, *outside(x, z))
            out_a[x, z] = (
                spread_free(a[x, z], around, None, diffusivity[x, pl.ds(z, 1), :]) + add[x, z]
            )


def half_begin(place, part, span):
    return jnp.bitwise_xor(part, lax.shift_right_logical(place[2], 1)) * span


def forecast_call(kernel, name, inputs, outputs, cells, scratch=(), ready=(), scalars=()):
    def body(*refs):
        count = len(scalars) + len(inputs)
        kernel(*refs[:count], *refs[count + len(ready) :])

    return pl.pallas_call(
        body,
        out_shape=[jax.ShapeDtypeStruct(shape, f32) for shape in outputs],
        in_specs=[SMEM] * len(scalars)
        + [VMEM] * len(inputs)
        + [pl.BlockSpec(memory_space=pl.ANY)] * len(ready),
        out_specs=[VMEM] * len(outputs),
        scratch_shapes=[pltpu.VMEM(shape, f32) for shape in scratch],
        compiler_params=pltpu.CompilerParams(vmem_limit_bytes=SCOPED),
        cost_estimate=pl.CostEstimate(
            flops=30 * cells, bytes_accessed=32 * cells, transcendentals=0
        ),
        name=name,
    )(*scalars, *inputs, *ready)


def weights_kernel(place, owner, obs_index, observed, obs_var, omega, eta):
    count, rows, ny = omega.shape
    batch_size = obs_index.shape[1]
    for k in range(count):
        batch = place[0] * count + k
        mine = owner[batch] == place[1]
        line = pl.ds(batch, 1)
        voxel = obs_index[line, :]
        scale = jnp.where(mine, 1.0, 0.0) / obs_var[line, :]
        shift = ny.bit_length() - 1
        row = lax.shift_right_logical(voxel, shift)
        column = jnp.bitwise_and(voxel, ny - 1)
        at_row = lax.broadcasted_iota(jnp.int32, (rows, batch_size), 0) == row
        at_column = lax.broadcasted_iota(jnp.int32, (ny, batch_size), 0) == column
        both = jnp.concatenate(
            [jnp.where(at_row, scale, 0.0), jnp.where(at_row, scale * observed[line, :], 0.0)],
            axis=0,
        )
        one = both.astype(bf16)
        rest = both - one.astype(f32)
        two = rest.astype(bf16)
        three = (rest - two.astype(f32)).astype(bf16)
        columns = jnp.where(at_column, 1.0, 0.0).astype(bf16)
        sums = lax.dot_general(
            jnp.concatenate([one, two, three], axis=0),
            columns,
            (NT, ((), ())),
            preferred_element_type=f32,
        )
        sums = sums[: 2 * rows] + sums[2 * rows : 4 * rows] + sums[4 * rows :]
        omega[k] = sums[:rows]
        eta[k] = sums[rows:]


def voxel_weights(place, owner, obs_index, observed, obs_var, count, rows, ny):
    out = jax.ShapeDtypeStruct((count, rows, ny), f32)
    return pl.pallas_call(
        weights_kernel,
        out_shape=[out, out],
        in_specs=[SMEM, SMEM, VMEM, VMEM, VMEM],
        out_specs=[VMEM, VMEM],
        compiler_params=pltpu.CompilerParams(vmem_limit_bytes=SCOPED),
        name="voxel_weights",
    )(place, owner, obs_index, observed, obs_var)


def gram_kernel(place, owner, omega, eta, *refs, offsets, halves):
    *sources, packed, out, members_at = refs
    count = out.shape[0]
    span, nz, rows, ny = sources[0].shape
    members = members_at.shape[0]
    begin = 0 if halves == 1 else lax.shift_right_logical(place[2], 1) * (span * nz)
    for k in range(count):
        out[k] = jnp.zeros(out.shape[1:], f32)

        @pl.when(owner[place[0] * count + k] == place[1])
        def _(k=k):
            def tile(t, total):
                x, z = t // nz, t % nz
                for j, source in enumerate(sources):
                    start = pl.multiple_of(offsets(place[2], j), 8)
                    members_at[pl.ds(start, rows), :] = source[x, z]
                values = members_at[...]
                mean = jnp.sum(values, axis=0, keepdims=True) * (1.0 / members)
                spread = values - mean
                weight = omega[k, pl.ds(begin + t, 1), :]
                shift = eta[k, pl.ds(begin + t, 1), :] - weight * mean
                tail = lax.broadcasted_iota(jnp.int32, (LANES - members, ny), 0)
                weighted = jnp.concatenate(
                    [spread * weight, jnp.where(tail == 0, shift, 0.0)], axis=0
                )
                return total + dot_parts(split(spread), split(weighted), NT)

            out[k] = lax.fori_loop(0, span * nz, tile, jnp.zeros(out.shape[1:], f32), unroll=4)

    row = lax.broadcasted_iota(jnp.int32, (members, LANES), 0)
    column = lax.broadcasted_iota(jnp.int32, (members, LANES), 1)
    above, below = out[0], out[1]

    def pick(where, x):
        return jnp.sum(jnp.where(where, x, 0.0), axis=1, keepdims=True)

    both = jnp.where(column >= row, above, below)
    both = jnp.where(column == members, pick(column == row, below), both)
    both = jnp.where(column == members + 1, pick(column == members, above), both)
    packed[...] = jnp.where(column == members + 2, pick(column == members, below), both)


def gram(place, owner, omega, eta, sources, offsets, halves, ready):
    _, _, rows, ny = sources[0].shape
    members = rows * len(sources)
    count = omega.shape[0]

    def body(*refs):
        inputs = 4 + len(sources)
        gram_kernel(
            *refs[:inputs], *refs[inputs + len(ready) :], offsets=offsets, halves=halves
        )

    return pl.pallas_call(
        body,
        out_shape=jax.ShapeDtypeStruct((members, LANES), f32),
        in_specs=[SMEM, SMEM, VMEM, VMEM]
        + [VMEM] * len(sources)
        + [pl.BlockSpec(memory_space=pl.ANY)] * len(ready),
        out_specs=VMEM,
        scratch_shapes=[pltpu.VMEM((count, members, LANES), f32), pltpu.VMEM((members, ny), f32)],
        compiler_params=pltpu.CompilerParams(vmem_limit_bytes=SCOPED),
        name="gram",
    )(place, owner, omega, eta, *sources, *ready)


def turned(x):
    rows = x.shape[0]
    whole = jnp.concatenate([x, jnp.zeros((LANES - rows, LANES), f32)], axis=0)
    return whole.T[:rows]


def batch_transform(extended, total, members):
    row = lax.broadcasted_iota(jnp.int32, extended.shape, 0)
    column = lax.broadcasted_iota(jnp.int32, extended.shape, 1)
    inside = column < members
    last = column == members
    identity = jnp.where(row == column, 1.0, 0.0)
    matrix = jnp.where(inside, extended, 0.0)

    mean = jnp.sum(total, axis=1, keepdims=True) * (1.0 / members)
    centred = jnp.where(inside, total - mean, 0.0)
    product = wide_dot(wide_left(matrix), wide_right(jnp.where(last, mean, centred)))
    product = jnp.where(last, extended - product, product)
    product = wide_dot(wide_left(turned(centred)), wide_right(product)) * (1.0 / (members - 1))
    innovation = jnp.sum(jnp.where(last, product, 0.0), axis=1, keepdims=True)
    system = identity + jnp.where(inside, product, 0.0)
    frobenius = jnp.sqrt(jnp.sum(jnp.sum(system * system, axis=1, keepdims=True), axis=0, keepdims=True))

    scaled_root = system / frobenius
    factor = 1.5 * identity - 0.5 * scaled_root
    scaled_root = wide_dot(wide_left(scaled_root), wide_right(factor))
    inverse_root = factor

    def newton(iteration, iterates):
        scaled_root, inverse_root = iterates
        factor = 1.5 * identity - 0.5 * wide_dot(
            wide_left(inverse_root), wide_right(scaled_root)
        )
        return (
            wide_dot(wide_left(scaled_root), wide_right(factor)),
            wide_dot(wide_left(factor), wide_right(inverse_root)),
        )

    scaled_root, inverse_root = lax.fori_loop(1, NEWTON, newton, (scaled_root, inverse_root), unroll=UNROLL)
    root_inv = inverse_root / jnp.sqrt(frobenius)
    mean_weight = jnp.sum(root_inv * innovation, axis=0, keepdims=True)
    mean_weight = jnp.sum(root_inv * mean_weight, axis=1, keepdims=True)
    mixing = jnp.where(inside, root_inv + mean_weight, 0.0)
    mixing = mixing - jnp.sum(mixing, axis=0, keepdims=True) * (1.0 / members)
    mixing = jnp.where(inside, mixing + 1.0 / members, 0.0)
    return wide_dot(wide_left(total), wide_right(mixing))


def early_kernel(place, mine, other, total, last, ordered):
    members = mine.shape[0]
    row = lax.broadcasted_iota(jnp.int32, (members, LANES), 0)
    column = lax.broadcasted_iota(jnp.int32, (members, LANES), 1)
    inside = column < members

    def pick(where, x):
        return jnp.sum(jnp.where(where, x, 0.0), axis=1, keepdims=True)

    for half, shared in ((place[0], mine), (1 - place[0], other)):
        packed = shared[...]
        above = jnp.where(inside & (column > row), packed, 0.0)
        below = jnp.where(inside & (column < row), packed, 0.0)
        middle = jnp.where(column == row, packed, 0.0)
        side = jnp.where(column == members, pick(column == members + 1, packed), 0.0)
        ordered[2 * half] = above + turned(above) + (middle + side)
        middle = jnp.where(column == row, pick(column == members, packed), 0.0)
        side = jnp.where(column == members, pick(column == members + 2, packed), 0.0)
        ordered[2 * half + 1] = below + turned(below) + (middle + side)
    batches = ordered.shape[0]
    product = jnp.where(row == column, 1.0, 0.0)
    for batch in range(batches - 1):
        product = batch_transform(ordered[batch], product, members)
    total[...] = product
    last[...] = ordered[batches - 1]


def late_kernel(place, total, last, out, work, *, offsets, blocks, rows):
    members = total.shape[0]
    product = batch_transform(last[...], total[...], members)
    rest = jnp.zeros((LANES - members, LANES), f32)
    work[...] = jnp.concatenate([product, rest], axis=0)
    if blocks == 1:
        out[...] = work[...].T
        return
    parts = [
        work[pl.ds(pl.multiple_of(offsets(place[2], j), 8), rows), :] for j in range(blocks)
    ]
    work[...] = jnp.concatenate([*parts, rest], axis=0).T
    out[...] = work[pl.ds(pl.multiple_of(offsets(place[2], 0), 8), rows), :]


def transform_call(kernel, name, outputs, scratch, inputs):
    return pl.pallas_call(
        kernel,
        out_shape=[jax.ShapeDtypeStruct(shape, f32) for shape in outputs],
        in_specs=[SMEM] + [VMEM] * (len(inputs) - 1),
        out_specs=[VMEM] * len(outputs),
        scratch_shapes=[pltpu.VMEM(shape, f32) for shape in scratch],
        compiler_params=pltpu.CompilerParams(vmem_limit_bytes=SCOPED),
        cost_estimate=pl.CostEstimate(
            flops=10**8, bytes_accessed=10**6, transcendentals=0
        ),
        name=name,
    )(*inputs)


def mix_kernel(place, weights, *refs, blocks, halves):
    *sources, out = refs
    rows, species, _, nz, _ = out.shape
    step = pl.program_id(0)
    span = pl.num_programs(0) // halves
    free, conserved, internal, *tracers = [
        sources[k : k + blocks] for k in range(0, len(sources), blocks)
    ]
    members = blocks * free[0].shape[2]
    high, low = split(weights[:, :members])
    both = jnp.concatenate([high.astype(f32), low.astype(f32)], axis=0).astype(bf16)
    mul = functools.partial(
        lax.dot_general, dimension_numbers=(NN, ((), ())), preferred_element_type=f32
    )

    def mixed(held, x, z):
        parts = [array[x, z] for array in held]
        values = parts[0] if blocks == 1 else jnp.concatenate(parts, axis=0)
        value_high, value_low = split(values)
        upper = mul(both, value_high)
        return upper[:rows] + (upper[rows:] + mul(high, value_low))

    for part in range(halves):

        @pl.when(step // span == part)
        def _(part=part):
            at = step % span
            x = at if halves == 1 else half_begin(place, part, span) + at
            for z in range(nz):
                tracer = mixed(tracers[part], at, z)
                inside = mixed(internal, x, z)
                out[:, 0, 0, z, :] = mixed(free, x, z)
                out[:, 1, 0, z, :] = mixed(conserved, x, z) - tracer
                out[:, 2, 0, z, :] = tracer - inside
                out[:, 3, 0, z, :] = inside


def mix(place, weights, sources, blocks, halves, shape):
    rows, species, nx, nz, ny = shape
    span = nx // halves

    def at(step, place):
        if halves == 1:
            return (0, 0, step, 0, 0)
        return (0, 0, half_begin(place, step // span, span) + step % span, 0, 0)

    return pl.pallas_call(
        functools.partial(mix_kernel, blocks=blocks, halves=halves),
        grid_spec=pltpu.PrefetchScalarGridSpec(
            num_scalar_prefetch=1,
            grid=(nx,),
            in_specs=[VMEM] * (1 + len(sources)),
            out_specs=pl.BlockSpec((rows, species, 1, nz, ny), at),
        ),
        out_shape=jax.ShapeDtypeStruct(shape, f32),
        compiler_params=pltpu.CompilerParams(vmem_limit_bytes=SCOPED),
        name="mix",
    )(place, weights, *sources)


def swap(x, axis, bit):
    count = lax.axis_size(axis)
    return lax.ppermute(x, axis, [(k, k ^ bit) for k in range(count)])


def total_over(x, axis):
    bit = 1
    while bit < lax.axis_size(axis):
        x = x + swap(x, axis, bit)
        bit *= 2
    return x


def local(ensemble, diffusivity, binding, source, obs_index, owner, observed, obs_var):
    rows, species, nx, nz, ny = ensemble.shape
    devices = lax.axis_size("member")
    spaces = lax.axis_size("space")
    members = rows * devices
    batches = owner.shape[0]
    member = lax.axis_index("member")
    place = jnp.stack([member & 1, lax.axis_index("space"), member]).astype(jnp.int32)

    forward = [(k, k + 1) for k in range(spaces - 1)]
    backward = [(k + 1, k) for k in range(spaces - 1)]

    def halos(first, last):
        return lax.ppermute(last, "space", forward), lax.ppermute(first, "space", backward)

    if devices == 4 and rows % 8 == 0 and nx % 2 == 0:
        blocks, halves = devices, 2

        def offsets(position, j):
            return jnp.bitwise_xor(position, j) * rows

        def collect(x, sent=None):
            return [x, swap(x, "member", 1), swap(x if sent is None else sent, "member", 2)]

        def complete(held, *after):
            return [*held, swap(lax.optimization_barrier((held[2], *after))[0], "member", 1)]
    else:
        blocks, halves = 1, 1

        def offsets(position, j):
            return 0

        def collect(x, sent=None):
            return [lax.all_gather(x, "member", axis=2, tiled=True)]

        def complete(held, *after):
            return held

    def across(held):
        return held[min(2, blocks - 1)]

    def tie(x, *after):
        return lax.optimization_barrier((x, *after))[0]

    whole = (nx, nz, rows, ny)
    coefficients = (diffusivity, binding, source)
    cells = nx * nz * rows * ny
    ends = [
        jnp.transpose(ensemble[:, :3, part], (1, 2, 3, 0, 4))
        for part in (slice(0, 2), slice(nx - 2, nx))
    ]
    edges = forecast_call(
        first_edges_kernel,
        "first_edges",
        [*ends, *coefficients],
        [(nz, 2 * rows + 8, ny)] * 2,
        2 * cells // nx,
    )
    fields = [jnp.transpose(ensemble[:, k], (1, 2, 0, 3)) for k in range(species)]
    conserved = fields[1] + fields[2] + fields[3]
    around = origin = halos(*edges)
    for step in range(SUBSTEPS // 2 - 1):
        inputs = [*fields, *around, *origin, *coefficients]
        if step == 1:
            conserved = collect(tie(conserved, fields[0]))
        around = halos(
            *forecast_call(
                next_edges_kernel,
                "next_edges",
                inputs,
                [(nz, 2 * rows, ny)] * 2,
                cells,
                scratch=[whole] * 8,
            )
        )
        fields = forecast_call(
            two_substeps_kernel, "two_substeps", inputs, [whole] * 4, 2 * cells, scratch=[whole] * 4
        )
    omega, eta = voxel_weights(
        place, owner, obs_index, observed, obs_var, batches // 2, nx * nz, ny
    )
    *tracers, internal, middle, add = forecast_call(
        functools.partial(last_but_one_kernel, halves=halves),
        "last_but_one",
        [*fields, *around, *coefficients],
        [(nx // halves, nz, rows, ny)] * halves + [whole] * 3,
        2 * cells,
        scratch=[whole] * 3,
        ready=[*conserved[1:], omega, eta],
        scalars=[place],
    )
    (free,) = forecast_call(
        last_free_kernel,
        "last_free",
        [fields[0], middle, add, *around, *origin, diffusivity],
        [whole],
        cells,
    )
    near = collect(*tracers)
    conserved = complete(conserved, tracers[0])
    near = complete(near)
    far = collect(tracers[1], tie(tracers[0], across(near))) if halves == 2 else []
    half = gram(place, owner, omega, eta, near, offsets, halves, [*conserved[3:], *far[1:2]])
    if halves == 2:
        half = tie(half + swap(half, "member", 2), across(far))
        far = complete(far, half)
    internal = collect(internal, tie(internal, half))
    free = collect(free, tie(free, half))
    half = total_over(half, "space")
    other = swap(half, "member", 1)
    internal = complete(internal, half)
    square = (members, LANES)
    total, extended = transform_call(
        early_kernel,
        "transforms_early",
        [square, square],
        [(batches, members, LANES)],
        [place, half, other],
    )
    free = complete(free, total)
    (weights,) = transform_call(
        functools.partial(late_kernel, offsets=offsets, blocks=blocks, rows=rows),
        "transforms_late",
        [(LANES, LANES) if blocks == 1 else (rows, LANES)],
        [(LANES, LANES)],
        [place, total, extended],
    )
    if blocks == 1:
        weights = lax.dynamic_slice(weights, (member * rows, 0), (rows, LANES))
    sources = free + conserved + internal + near + (far if halves == 2 else [])
    return mix(place, weights, sources, blocks, halves, ensemble.shape)


def solution(mesh):
    in_specs = (
        P("member", None, "space", None, None),
        P("space", None, None),
        P("space", None, None),
        P("space", None, None),
        P(),
        P(),
        P(),
        P(),
    )
    out_specs = P("member", None, "space", None, None)
    return jax.shard_map(local, mesh=mesh, in_specs=in_specs, out_specs=out_specs, check_vma=False)
```

```python
import functools

import jax
import jax.numpy as jnp
from jax import lax
from jax.experimental import pallas as pl
from jax.experimental.pallas import tpu as pltpu
from jax.sharding import PartitionSpec as P

SUBSTEPS = 6
NEWTON = 16
UNROLL = 5
LANES = 128
SCOPED = 10 * 2**20

unbind_rate = 0.05
uptake_rate = 0.1
recycle_rate = 0.02

VMEM = pl.BlockSpec(memory_space=pltpu.VMEM)
SMEM = pl.BlockSpec(memory_space=pltpu.SMEM)
bf16 = jnp.bfloat16
f32 = jnp.float32


def split(x):
    high = x.astype(bf16)
    return high, (x - high.astype(f32)).astype(bf16)


def dot_parts(a, b, dims):
    a_high, a_low = a
    b_high, b_low = b
    mul = functools.partial(
        lax.dot_general, dimension_numbers=(dims, ((), ())), preferred_element_type=f32
    )
    return mul(a_high, b_high) + (mul(a_high, b_low) + mul(a_low, b_high))


def wide_left(x):
    return jnp.concatenate(split(x), axis=1)


def wide_right(x):
    rows, lanes = x.shape
    parts = []
    for part in split(x):
        if rows < lanes:
            part = jnp.concatenate([part, jnp.zeros((lanes - rows, lanes), bf16)], axis=0)
        parts.append(jnp.concatenate([part, part], axis=0))
    return parts


def wide_dot(left, right):
    high, low = [jnp.dot(left, part, preferred_element_type=f32) for part in right]
    return high + low


NN = ((1,), (0,))
NT = ((1,), (1,))


def react(free, receptor, complexed, internal, binding):
    flux = binding * free * receptor
    back = unbind_rate * complexed - flux
    return (
        back,
        receptor + back + recycle_rate * internal,
        complexed + flux - (unbind_rate + uptake_rate) * complexed,
        internal + uptake_rate * complexed - recycle_rate * internal,
    )


def spread_free(free, planes, neighbours, diffusivity):
    lane = lax.broadcasted_iota(jnp.int32, free.shape, 1)
    last = free.shape[1] - 1
    for plane in planes:
        neighbours = plane if neighbours is None else neighbours + plane
    neighbours += jnp.where(lane == last, 0.0, pltpu.roll(free, last, 1))
    neighbours += jnp.where(lane == 0, 0.0, pltpu.roll(free, 1, 1))
    return free + diffusivity * (neighbours - 6.0 * free)


def beside(read, x, z, nx, nz, low, high):
    around = [low if x == 0 else read(x - 1, z), high if x == nx - 1 else read(x + 1, z)]
    around += [read(x, other) for other in (z + 1, z - 1) if 0 <= other < nz]
    return [value for value in around if value is not None]


def edge_free(read, rest, x, nz, nx, z, diffusivity):
    return spread_free(read(x, z), beside(read, x, z, nx, nz, None, None), None, diffusivity) + rest


def first_edges_kernel(below, above, diffusivity, binding, source, first, last):
    _, _, nz, members, _ = below.shape
    nx = diffusivity.shape[0]
    for x, ends, out in ((0, below, first), (nx - 1, above, last)):
        shift = 0 if x == 0 else nx - 2

        def read(at, z, ends=ends, shift=shift):
            return ends[0, at - shift, z]

        for z in range(nz):
            row = pl.ds(z, 1)
            free = read(x, z)
            flux = binding[x, row, :] * free * ends[1, x - shift, z]
            rest = unbind_rate * ends[2, x - shift, z] - flux + source[x, row, :]
            spread = diffusivity[x, row, :]
            out[z, :members, :] = free
            out[z, members : 2 * members, :] = edge_free(read, rest, x, nz, nx, z, spread)
            out[z, 2 * members :, :] = jnp.broadcast_to(spread, (8, spread.shape[1]))


def step_planes(planes, a, r, c, i, outside, diffusivity, binding, source, out_a, outs, keep):
    nx, nz, _, _ = a.shape
    for x in planes:
        for z in range(nz):
            row = pl.ds(z, 1)
            back, *others = react(a[x, z], r[x, z], c[x, z], i[x, z], binding[x, row, :])
            around = beside(lambda x, z: a[x, z], x, z, nx, nz, *outside(x, z))
            out_a[x, z] = (
                spread_free(a[x, z], around, None, diffusivity[x, row, :])
                + back
                + source[x, row, :]
            )
            if x in keep:
                for out, value in zip(outs, others):
                    out[x, z] = value


def before_last(a, low, high):
    nx, _, members, _ = a.shape

    def outside(x, z):
        return (
            low[z, :members, :] if x == 0 else None,
            high[z, :members, :] if x == nx - 1 else None,
        )

    return outside


def after_first(a, low, high, low_first, high_first):
    nx, _, members, _ = a.shape

    def completed(halo, origin, x, z):
        later = halo[z, members : 2 * members, :]
        return later + origin[z, 2 * members : 2 * members + 1, :] * a[x, z]

    def outside(x, z):
        return (
            completed(low, low_first, x, z) if x == 0 else None,
            completed(high, high_first, x, z) if x == nx - 1 else None,
        )

    return outside


def next_edges_kernel(
    a, r, c, i, low, high, low_first, high_first, diffusivity, binding, source, *refs
):
    first, last, *kept = refs
    middle, later = kept[:4], kept[4:]
    nx, nz, members, _ = a.shape
    coefficients = (diffusivity, binding, source)

    def near(depth):
        return [x for x in range(nx) if min(x, nx - 1 - x) < depth]

    step_planes(
        near(3), a, r, c, i, before_last(a, low, high), *coefficients, middle[0], middle[1:], near(2)
    )
    step_planes(
        near(2),
        *middle,
        after_first(a, low, high, low_first, high_first),
        *coefficients,
        later[0],
        later[1:],
        near(1),
    )
    free, receptor, complexed = later[:3]
    for x, out in ((0, first), (nx - 1, last)):
        for z in range(nz):
            row = pl.ds(z, 1)
            flux = binding[x, row, :] * free[x, z] * receptor[x, z]
            rest = unbind_rate * complexed[x, z] - flux + source[x, row, :]
            out[z, :members, :] = free[x, z]
            out[z, members:, :] = edge_free(
                lambda x, z: free[x, z], rest, x, nz, nx, z, diffusivity[x, row, :]
            )


def two_substeps_kernel(*refs, weigh):
    if weigh:
        place, owner, *refs = refs
    a, r, c, i, low, high, low_first, high_first, diffusivity, binding, source, *refs = refs
    if weigh:
        obs_index, observed, obs_var, *refs = refs
        *refs, omega, eta, m0, m1, m2, m3 = refs
        refs = [*refs, m0, m1, m2, m3]
        voxel_weights(place, owner, obs_index, observed, obs_var, omega, eta)
    outs, middle = refs[:4], refs[4:]
    everywhere = range(a.shape[0])
    coefficients = (diffusivity, binding, source)
    step_planes(
        everywhere,
        a,
        r,
        c,
        i,
        before_last(a, low, high),
        *coefficients,
        middle[0],
        middle[1:],
        everywhere,
    )
    step_planes(
        everywhere,
        *middle,
        after_first(a, low, high, low_first, high_first),
        *coefficients,
        outs[0],
        outs[1:],
        everywhere,
    )


def last_but_one_kernel(
    place, a, r, c, i, low, high, diffusivity, binding, source, *refs, halves
):
    *tracers, out_i, out_a, out_add, mid_r, mid_c, mid_i = refs
    nx, nz, _, _ = a.shape
    step_planes(
        range(nx),
        a,
        r,
        c,
        i,
        before_last(a, low, high),
        diffusivity,
        binding,
        source,
        out_a,
        (mid_r, mid_c, mid_i),
        range(nx),
    )
    span = nx // halves
    for part, tracer in enumerate(tracers):
        begin = half_begin(place, part, span)
        for j in range(span):
            x = j if halves == 1 else begin + j
            for z in range(nz):
                row = pl.ds(z, 1)
                back, _, complexed, internal = react(
                    out_a[x, z], mid_r[x, z], mid_c[x, z], mid_i[x, z], binding[x, row, :]
                )
                tracer[j, z] = complexed + internal
                out_i[x, z] = internal
                out_add[x, z] = back + source[x, row, :]


def last_free_kernel(
    before, a, add, low, high, low_first, high_first, diffusivity, out_a
):
    nx, nz, _, _ = a.shape
    outside = after_first(before, low, high, low_first, high_first)
    for x in range(nx):
        for z in range(nz):
            around = beside(lambda x, z: a[x, z], x, z, nx, nz, *outside(x, z))
            out_a[x, z] = (
                spread_free(a[x, z], around, None, diffusivity[x, pl.ds(z, 1), :]) + add[x, z]
            )


def half_begin(place, part, span):
    return jnp.bitwise_xor(part, lax.shift_right_logical(place[2], 1)) * span


def forecast_call(kernel, name, inputs, outputs, cells, scratch=(), ready=(), scalars=()):
    def body(*refs):
        count = len(scalars) + len(inputs)
        kernel(*refs[:count], *refs[count + len(ready) :])

    return pl.pallas_call(
        body,
        out_shape=[jax.ShapeDtypeStruct(shape, f32) for shape in outputs],
        in_specs=[SMEM] * len(scalars)
        + [VMEM] * len(inputs)
        + [pl.BlockSpec(memory_space=pl.ANY)] * len(ready),
        out_specs=[VMEM] * len(outputs),
        scratch_shapes=[pltpu.VMEM(shape, f32) for shape in scratch],
        compiler_params=pltpu.CompilerParams(vmem_limit_bytes=SCOPED),
        cost_estimate=pl.CostEstimate(
            flops=30 * cells, bytes_accessed=32 * cells, transcendentals=0
        ),
        name=name,
    )(*scalars, *inputs, *ready)


def voxel_weights(place, owner, obs_index, observed, obs_var, omega, eta):
    count, rows, ny = omega.shape
    batch_size = obs_index.shape[1]
    for k in range(count):
        batch = place[0] * count + k
        mine = owner[batch] == place[1]
        line = pl.ds(batch, 1)
        voxel = obs_index[line, :]
        scale = jnp.where(mine, 1.0, 0.0) / obs_var[line, :]
        shift = ny.bit_length() - 1
        row = lax.shift_right_logical(voxel, shift)
        column = jnp.bitwise_and(voxel, ny - 1)
        at_row = lax.broadcasted_iota(jnp.int32, (rows, batch_size), 0) == row
        at_column = lax.broadcasted_iota(jnp.int32, (ny, batch_size), 0) == column
        both = jnp.concatenate(
            [jnp.where(at_row, scale, 0.0), jnp.where(at_row, scale * observed[line, :], 0.0)],
            axis=0,
        )
        one = both.astype(bf16)
        rest = both - one.astype(f32)
        two = rest.astype(bf16)
        three = (rest - two.astype(f32)).astype(bf16)
        columns = jnp.where(at_column, 1.0, 0.0).astype(bf16)
        sums = lax.dot_general(
            jnp.concatenate([one, two, three], axis=0),
            columns,
            (NT, ((), ())),
            preferred_element_type=f32,
        )
        sums = sums[: 2 * rows] + sums[2 * rows : 4 * rows] + sums[4 * rows :]
        omega[k] = sums[:rows]
        eta[k] = sums[rows:]


def gram_kernel(place, owner, omega, eta, *refs, offsets, halves):
    *sources, packed, out, members_at = refs
    count = out.shape[0]
    span, nz, rows, ny = sources[0].shape
    members = members_at.shape[0]
    begin = 0 if halves == 1 else lax.shift_right_logical(place[2], 1) * (span * nz)
    for k in range(count):
        out[k] = jnp.zeros(out.shape[1:], f32)

        @pl.when(owner[place[0] * count + k] == place[1])
        def _(k=k):
            def tile(t, total):
                x, z = t // nz, t % nz
                for j, source in enumerate(sources):
                    start = pl.multiple_of(offsets(place[2], j), 8)
                    members_at[pl.ds(start, rows), :] = source[x, z]
                values = members_at[...]
                mean = jnp.sum(values, axis=0, keepdims=True) * (1.0 / members)
                spread = values - mean
                weight = omega[k, pl.ds(begin + t, 1), :]
                shift = eta[k, pl.ds(begin + t, 1), :] - weight * mean
                tail = lax.broadcasted_iota(jnp.int32, (LANES - members, ny), 0)
                weighted = jnp.concatenate(
                    [spread * weight, jnp.where(tail == 0, shift, 0.0)], axis=0
                )
                return total + dot_parts(split(spread), split(weighted), NT)

            out[k] = lax.fori_loop(0, span * nz, tile, jnp.zeros(out.shape[1:], f32), unroll=4)

    row = lax.broadcasted_iota(jnp.int32, (members, LANES), 0)
    column = lax.broadcasted_iota(jnp.int32, (members, LANES), 1)
    above, below = out[0], out[1]

    def pick(where, x):
        return jnp.sum(jnp.where(where, x, 0.0), axis=1, keepdims=True)

    both = jnp.where(column >= row, above, below)
    both = jnp.where(column == members, pick(column == row, below), both)
    both = jnp.where(column == members + 1, pick(column == members, above), both)
    packed[...] = jnp.where(column == members + 2, pick(column == members, below), both)


def gram(place, owner, omega, eta, sources, offsets, halves, ready):
    _, _, rows, ny = sources[0].shape
    members = rows * len(sources)
    count = omega.shape[0]

    def body(*refs):
        inputs = 4 + len(sources)
        gram_kernel(
            *refs[:inputs], *refs[inputs + len(ready) :], offsets=offsets, halves=halves
        )

    return pl.pallas_call(
        body,
        out_shape=jax.ShapeDtypeStruct((members, LANES), f32),
        in_specs=[SMEM, SMEM, VMEM, VMEM]
        + [VMEM] * len(sources)
        + [pl.BlockSpec(memory_space=pl.ANY)] * len(ready),
        out_specs=VMEM,
        scratch_shapes=[pltpu.VMEM((count, members, LANES), f32), pltpu.VMEM((members, ny), f32)],
        compiler_params=pltpu.CompilerParams(vmem_limit_bytes=SCOPED),
        name="gram",
    )(place, owner, omega, eta, *sources, *ready)


def turned(x):
    rows = x.shape[0]
    whole = jnp.concatenate([x, jnp.zeros((LANES - rows, LANES), f32)], axis=0)
    return whole.T[:rows]


def batch_transform(extended, total, members):
    row = lax.broadcasted_iota(jnp.int32, extended.shape, 0)
    column = lax.broadcasted_iota(jnp.int32, extended.shape, 1)
    inside = column < members
    last = column == members
    identity = jnp.where(row == column, 1.0, 0.0)
    matrix = jnp.where(inside, extended, 0.0)

    mean = jnp.sum(total, axis=1, keepdims=True) * (1.0 / members)
    centred = jnp.where(inside, total - mean, 0.0)
    product = wide_dot(wide_left(matrix), wide_right(jnp.where(last, mean, centred)))
    product = jnp.where(last, extended - product, product)
    product = wide_dot(wide_left(turned(centred)), wide_right(product)) * (1.0 / (members - 1))
    innovation = jnp.sum(jnp.where(last, product, 0.0), axis=1, keepdims=True)
    system = identity + jnp.where(inside, product, 0.0)
    frobenius = jnp.sqrt(jnp.sum(jnp.sum(system * system, axis=1, keepdims=True), axis=0, keepdims=True))

    scaled_root = system / frobenius
    factor = 1.5 * identity - 0.5 * scaled_root
    scaled_root = wide_dot(wide_left(scaled_root), wide_right(factor))
    inverse_root = factor

    def newton(iteration, iterates):
        scaled_root, inverse_root = iterates
        factor = 1.5 * identity - 0.5 * wide_dot(
            wide_left(inverse_root), wide_right(scaled_root)
        )
        return (
            wide_dot(wide_left(scaled_root), wide_right(factor)),
            wide_dot(wide_left(factor), wide_right(inverse_root)),
        )

    scaled_root, inverse_root = lax.fori_loop(1, NEWTON, newton, (scaled_root, inverse_root), unroll=UNROLL)
    root_inv = inverse_root / jnp.sqrt(frobenius)
    mean_weight = jnp.sum(root_inv * innovation, axis=0, keepdims=True)
    mean_weight = jnp.sum(root_inv * mean_weight, axis=1, keepdims=True)
    mixing = jnp.where(inside, root_inv + mean_weight, 0.0)
    mixing = mixing - jnp.sum(mixing, axis=0, keepdims=True) * (1.0 / members)
    mixing = jnp.where(inside, mixing + 1.0 / members, 0.0)
    return wide_dot(wide_left(total), wide_right(mixing))


def transform_kernel(place, mine, other, out, ordered, work, *, offsets, blocks, rows):
    members = mine.shape[0]
    row = lax.broadcasted_iota(jnp.int32, (members, LANES), 0)
    column = lax.broadcasted_iota(jnp.int32, (members, LANES), 1)
    inside = column < members

    def pick(where, x):
        return jnp.sum(jnp.where(where, x, 0.0), axis=1, keepdims=True)

    for half, shared in ((place[0], mine), (1 - place[0], other)):
        packed = shared[...]
        above = jnp.where(inside & (column > row), packed, 0.0)
        below = jnp.where(inside & (column < row), packed, 0.0)
        middle = jnp.where(column == row, packed, 0.0)
        side = jnp.where(column == members, pick(column == members + 1, packed), 0.0)
        ordered[2 * half] = above + turned(above) + (middle + side)
        middle = jnp.where(column == row, pick(column == members, packed), 0.0)
        side = jnp.where(column == members, pick(column == members + 2, packed), 0.0)
        ordered[2 * half + 1] = below + turned(below) + (middle + side)
    product = jnp.where(row == column, 1.0, 0.0)
    for batch in range(ordered.shape[0]):
        product = batch_transform(ordered[batch], product, members)
    rest = jnp.zeros((LANES - members, LANES), f32)
    work[...] = jnp.concatenate([product, rest], axis=0)
    if blocks == 1:
        out[...] = work[...].T
        return
    parts = [
        work[pl.ds(pl.multiple_of(offsets(place[2], j), 8), rows), :] for j in range(blocks)
    ]
    work[...] = jnp.concatenate([*parts, rest], axis=0).T
    out[...] = work[pl.ds(pl.multiple_of(offsets(place[2], 0), 8), rows), :]


def transforms(place, mine, other, offsets, blocks, rows):
    members = mine.shape[0]
    shape = (LANES, LANES) if blocks == 1 else (rows, LANES)
    return pl.pallas_call(
        functools.partial(transform_kernel, offsets=offsets, blocks=blocks, rows=rows),
        out_shape=jax.ShapeDtypeStruct(shape, f32),
        in_specs=[SMEM, VMEM, VMEM],
        out_specs=VMEM,
        scratch_shapes=[
            pltpu.VMEM((4, members, LANES), f32),
            pltpu.VMEM((LANES, LANES), f32),
        ],
        compiler_params=pltpu.CompilerParams(vmem_limit_bytes=SCOPED),
        cost_estimate=pl.CostEstimate(
            flops=10**8, bytes_accessed=10**6, transcendentals=0
        ),
        name="transforms",
    )(place, mine, other)


def mix_kernel(place, weights, *refs, blocks, halves):
    *sources, out = refs
    rows, species, _, nz, _ = out.shape
    step = pl.program_id(0)
    span = pl.num_programs(0) // halves
    free, conserved, internal, *tracers = [
        sources[k : k + blocks] for k in range(0, len(sources), blocks)
    ]
    members = blocks * free[0].shape[2]
    high, low = split(weights[:, :members])
    both = jnp.concatenate([high.astype(f32), low.astype(f32)], axis=0).astype(bf16)
    mul = functools.partial(
        lax.dot_general, dimension_numbers=(NN, ((), ())), preferred_element_type=f32
    )

    def mixed(held, x, z):
        parts = [array[x, z] for array in held]
        values = parts[0] if blocks == 1 else jnp.concatenate(parts, axis=0)
        value_high, value_low = split(values)
        upper = mul(both, value_high)
        return upper[:rows] + (upper[rows:] + mul(high, value_low))

    for part in range(halves):

        @pl.when(step // span == part)
        def _(part=part):
            at = step % span
            x = at if halves == 1 else half_begin(place, part, span) + at
            for z in range(nz):
                tracer = mixed(tracers[part], at, z)
                inside = mixed(internal, x, z)
                out[:, 0, 0, z, :] = mixed(free, x, z)
                out[:, 1, 0, z, :] = mixed(conserved, x, z) - tracer
                out[:, 2, 0, z, :] = tracer - inside
                out[:, 3, 0, z, :] = inside


def mix(place, weights, sources, blocks, halves, shape):
    rows, species, nx, nz, ny = shape
    span = nx // halves

    def at(step, place):
        if halves == 1:
            return (0, 0, step, 0, 0)
        return (0, 0, half_begin(place, step // span, span) + step % span, 0, 0)

    return pl.pallas_call(
        functools.partial(mix_kernel, blocks=blocks, halves=halves),
        grid_spec=pltpu.PrefetchScalarGridSpec(
            num_scalar_prefetch=1,
            grid=(nx,),
            in_specs=[VMEM] * (1 + len(sources)),
            out_specs=pl.BlockSpec((rows, species, 1, nz, ny), at),
        ),
        out_shape=jax.ShapeDtypeStruct(shape, f32),
        compiler_params=pltpu.CompilerParams(vmem_limit_bytes=SCOPED),
        name="mix",
    )(place, weights, *sources)


def swap(x, axis, bit):
    count = lax.axis_size(axis)
    return lax.ppermute(x, axis, [(k, k ^ bit) for k in range(count)])


def total_over(x, axis):
    bit = 1
    while bit < lax.axis_size(axis):
        x = x + swap(x, axis, bit)
        bit *= 2
    return x


def local(ensemble, diffusivity, binding, source, obs_index, owner, observed, obs_var):
    rows, species, nx, nz, ny = ensemble.shape
    devices = lax.axis_size("member")
    spaces = lax.axis_size("space")
    members = rows * devices
    batches = owner.shape[0]
    member = lax.axis_index("member")
    place = jnp.stack([member & 1, lax.axis_index("space"), member]).astype(jnp.int32)

    forward = [(k, k + 1) for k in range(spaces - 1)]
    backward = [(k + 1, k) for k in range(spaces - 1)]

    def halos(first, last):
        return lax.ppermute(last, "space", forward), lax.ppermute(first, "space", backward)

    if devices == 4 and rows % 8 == 0 and nx % 2 == 0:
        blocks, halves = devices, 2

        def offsets(position, j):
            return jnp.bitwise_xor(position, j) * rows

        def collect(x, sent=None):
            return [x, swap(x, "member", 1), swap(x if sent is None else sent, "member", 2)]

        def complete(held, *after):
            return [*held, swap(lax.optimization_barrier((held[2], *after))[0], "member", 1)]
    else:
        blocks, halves = 1, 1

        def offsets(position, j):
            return 0

        def collect(x, sent=None):
            return [lax.all_gather(x, "member", axis=2, tiled=True)]

        def complete(held, *after):
            return held

    def across(held):
        return held[min(2, blocks - 1)]

    def tie(x, *after):
        return lax.optimization_barrier((x, *after))[0]

    whole = (nx, nz, rows, ny)
    coefficients = (diffusivity, binding, source)
    cells = nx * nz * rows * ny
    ends = [
        jnp.transpose(ensemble[:, :3, part], (1, 2, 3, 0, 4))
        for part in (slice(0, 2), slice(nx - 2, nx))
    ]
    edges = forecast_call(
        first_edges_kernel,
        "first_edges",
        [*ends, *coefficients],
        [(nz, 2 * rows + 8, ny)] * 2,
        2 * cells // nx,
    )
    fields = [jnp.transpose(ensemble[:, k], (1, 2, 0, 3)) for k in range(species)]
    conserved = fields[1] + fields[2] + fields[3]
    around = origin = halos(*edges)
    for step in range(SUBSTEPS // 2 - 1):
        inputs = [*fields, *around, *origin, *coefficients]
        if step == 1:
            conserved = collect(tie(conserved, fields[0]))
        around = halos(
            *forecast_call(
                next_edges_kernel,
                "next_edges",
                inputs,
                [(nz, 2 * rows, ny)] * 2,
                cells,
                scratch=[whole] * 8,
            )
        )
        weigh = step == 1
        fields = forecast_call(
            functools.partial(two_substeps_kernel, weigh=weigh),
            "two_substeps",
            [*inputs, obs_index, observed, obs_var] if weigh else inputs,
            [whole] * 4 + ([(batches // 2, nx * nz, ny)] * 2 if weigh else []),
            2 * cells,
            scratch=[whole] * 4,
            scalars=[place, owner] if weigh else (),
        )
    *fields, omega, eta = fields
    *tracers, internal, middle, add = forecast_call(
        functools.partial(last_but_one_kernel, halves=halves),
        "last_but_one",
        [*fields, *around, *coefficients],
        [(nx // halves, nz, rows, ny)] * halves + [whole] * 3,
        2 * cells,
        scratch=[whole] * 3,
        ready=conserved[1:],
        scalars=[place],
    )
    (free,) = forecast_call(
        last_free_kernel,
        "last_free",
        [fields[0], middle, add, *around, *origin, diffusivity],
        [whole],
        cells,
    )
    near = collect(*tracers)
    conserved = complete(conserved, tracers[0])
    near = complete(near)
    half = gram(place, owner, omega, eta, near, offsets, halves, conserved[3:])
    if halves == 2:
        half = half + swap(half, "member", 2)
    internal = collect(internal, tie(internal, half))
    free = collect(free, tie(free, half))
    half = total_over(half, "space")
    far = collect(tracers[1], tie(tracers[0], half)) if halves == 2 else []
    other = swap(half, "member", 1)
    weights = transforms(place, half, other, offsets, blocks, rows)
    internal = complete(internal, weights)
    free = complete(free, weights)
    far = complete(far, weights) if halves == 2 else []
    if blocks == 1:
        weights = lax.dynamic_slice(weights, (member * rows, 0), (rows, LANES))
    sources = free + conserved + internal + near + far
    return mix(place, weights, sources, blocks, halves, ensemble.shape)


def solution(mesh):
    in_specs = (
        P("member", None, "space", None, None),
        P("space", None, None),
        P("space", None, None),
        P("space", None, None),
        P(),
        P(),
        P(),
        P(),
    )
    out_specs = P("member", None, "space", None, None)
    return jax.shard_map(local, mesh=mesh, in_specs=in_specs, out_specs=out_specs, check_vma=False)
```

```python
import functools

import jax
import jax.numpy as jnp
from jax import lax
from jax.experimental import pallas as pl
from jax.experimental.pallas import tpu as pltpu
from jax.sharding import PartitionSpec as P

SUBSTEPS = 6
NEWTON = 16
UNROLL = 5
LANES = 128
SCOPED = 10 * 2**20

unbind_rate = 0.05
uptake_rate = 0.1
recycle_rate = 0.02

VMEM = pl.BlockSpec(memory_space=pltpu.VMEM)
SMEM = pl.BlockSpec(memory_space=pltpu.SMEM)
bf16 = jnp.bfloat16
f32 = jnp.float32


def split(x):
    high = x.astype(bf16)
    return high, (x - high.astype(f32)).astype(bf16)


def dot_parts(a, b, dims):
    a_high, a_low = a
    b_high, b_low = b
    mul = functools.partial(
        lax.dot_general, dimension_numbers=(dims, ((), ())), preferred_element_type=f32
    )
    return mul(a_high, b_high) + (mul(a_high, b_low) + mul(a_low, b_high))


def wide_left(x):
    return jnp.concatenate(split(x), axis=1)


def wide_right(x):
    both = jnp.concatenate(split(x), axis=1)
    rows, lanes = both.shape
    if rows < lanes // 2:
        both = jnp.concatenate([both, jnp.zeros((lanes // 2 - rows, lanes), bf16)], axis=0)
    return jnp.concatenate([both, both], axis=0)


def wide_dot(left, right):
    out = jnp.dot(left, right, preferred_element_type=f32)
    side = out.shape[1] // 2
    return out[:, :side] + out[:, side:]


NN = ((1,), (0,))
NT = ((1,), (1,))


def react(free, receptor, complexed, internal, binding):
    flux = binding * free * receptor
    back = unbind_rate * complexed - flux
    return (
        back,
        receptor + back + recycle_rate * internal,
        complexed + flux - (unbind_rate + uptake_rate) * complexed,
        internal + uptake_rate * complexed - recycle_rate * internal,
    )


def spread_free(free, planes, neighbours, diffusivity):
    lane = lax.broadcasted_iota(jnp.int32, free.shape, 1)
    last = free.shape[1] - 1
    for plane in planes:
        neighbours = plane if neighbours is None else neighbours + plane
    neighbours += jnp.where(lane == last, 0.0, pltpu.roll(free, last, 1))
    neighbours += jnp.where(lane == 0, 0.0, pltpu.roll(free, 1, 1))
    return free + diffusivity * (neighbours - 6.0 * free)


def beside(read, x, z, nx, nz, low, high):
    around = [low if x == 0 else read(x - 1, z), high if x == nx - 1 else read(x + 1, z)]
    around += [read(x, other) for other in (z + 1, z - 1) if 0 <= other < nz]
    return [value for value in around if value is not None]


def edge_free(read, rest, x, nz, nx, z, diffusivity):
    return spread_free(read(x, z), beside(read, x, z, nx, nz, None, None), None, diffusivity) + rest


def first_edges_kernel(place, below, above, diffusivity, binding, source, first, last):
    _, _, nz, members, _ = below.shape
    nx = diffusivity.shape[0]
    for x, ends, out in ((0, below, first), (nx - 1, above, last)):
        shift = 0 if x == 0 else nx - 2

        def read(at, z, ends=ends, shift=shift):
            return ends[0, at - shift, z]

        for z in range(nz):
            row = pl.ds(z, 1)
            free = read(x, z)
            flux = binding[x, row, :] * free * ends[1, x - shift, z]
            rest = unbind_rate * ends[2, x - shift, z] - flux + source[x, row, :]
            spread = diffusivity[x, row, :]
            out[z, :members, :] = free
            out[z, members : 2 * members, :] = edge_free(read, rest, x, nz, nx, z, spread)
            out[z, 2 * members :, :] = jnp.broadcast_to(spread, (8, spread.shape[1]))


def step_planes(planes, a, r, c, i, outside, diffusivity, binding, source, out_a, outs, keep):
    nx, nz, _, _ = a.shape
    for x in planes:
        for z in range(nz):
            row = pl.ds(z, 1)
            back, *others = react(a[x, z], r[x, z], c[x, z], i[x, z], binding[x, row, :])
            around = beside(lambda x, z: a[x, z], x, z, nx, nz, *outside(x, z))
            out_a[x, z] = (
                spread_free(a[x, z], around, None, diffusivity[x, row, :])
                + back
                + source[x, row, :]
            )
            if x in keep:
                for out, value in zip(outs, others):
                    out[x, z] = value


def before_last(a, low, high):
    nx, _, members, _ = a.shape

    def outside(x, z):
        return (
            low[z, :members, :] if x == 0 else None,
            high[z, :members, :] if x == nx - 1 else None,
        )

    return outside


def after_first(a, low, high, low_first, high_first):
    nx, _, members, _ = a.shape

    def completed(halo, origin, x, z):
        later = halo[z, members : 2 * members, :]
        return later + origin[z, 2 * members : 2 * members + 1, :] * a[x, z]

    def outside(x, z):
        return (
            completed(low, low_first, x, z) if x == 0 else None,
            completed(high, high_first, x, z) if x == nx - 1 else None,
        )

    return outside


def next_edges_kernel(
    a, r, c, i, low, high, low_first, high_first, diffusivity, binding, source, *refs
):
    first, last, *kept = refs
    middle, later = kept[:4], kept[4:]
    nx, nz, members, _ = a.shape
    coefficients = (diffusivity, binding, source)

    def near(depth):
        return [x for x in range(nx) if min(x, nx - 1 - x) < depth]

    step_planes(
        near(3), a, r, c, i, before_last(a, low, high), *coefficients, middle[0], middle[1:], near(2)
    )
    step_planes(
        near(2),
        *middle,
        after_first(a, low, high, low_first, high_first),
        *coefficients,
        later[0],
        later[1:],
        near(1),
    )
    free, receptor, complexed = later[:3]
    for x, out in ((0, first), (nx - 1, last)):
        for z in range(nz):
            row = pl.ds(z, 1)
            flux = binding[x, row, :] * free[x, z] * receptor[x, z]
            rest = unbind_rate * complexed[x, z] - flux + source[x, row, :]
            out[z, :members, :] = free[x, z]
            out[z, members:, :] = edge_free(
                lambda x, z: free[x, z], rest, x, nz, nx, z, diffusivity[x, row, :]
            )


def two_substeps_kernel(
    a, r, c, i, low, high, low_first, high_first, diffusivity, binding, source, *refs
):
    outs, middle = refs[:4], refs[4:]
    everywhere = range(a.shape[0])
    coefficients = (diffusivity, binding, source)
    step_planes(
        everywhere,
        a,
        r,
        c,
        i,
        before_last(a, low, high),
        *coefficients,
        middle[0],
        middle[1:],
        everywhere,
    )
    step_planes(
        everywhere,
        *middle,
        after_first(a, low, high, low_first, high_first),
        *coefficients,
        outs[0],
        outs[1:],
        everywhere,
    )


def last_steps_kernel(
    a, r, c, i, low, high, low_first, high_first, diffusivity, binding, source, *refs
):
    *outs, m0, m1, m2, m3, later_r, later_c, later_i = refs
    before, first, last, free, tracer, inside, add, ends = outs
    nx, nz, members, _ = a.shape
    coefficients = (diffusivity, binding, source)
    two_substeps_kernel(
        a,
        r,
        c,
        i,
        low,
        high,
        low_first,
        high_first,
        *coefficients,
        before,
        later_r,
        later_c,
        later_i,
        m0,
        m1,
        m2,
        m3,
    )
    step_planes(
        range(nx),
        before,
        later_r,
        later_c,
        later_i,
        lambda x, z: (None, None),
        *coefficients,
        free,
        (m1, m2, m3),
        range(nx),
    )
    for x in range(nx):
        for z in range(nz):
            row = pl.ds(z, 1)
            back, _, complexed, internal = react(
                free[x, z], m1[x, z], m2[x, z], m3[x, z], binding[x, row, :]
            )
            inside[x, z] = internal
            if 0 < x < nx - 1:
                tracer[x - 1, z] = complexed + internal
                add[x - 1, z] = back + source[x, row, :]
                continue
            ends[0, x // (nx - 1), z] = m1[x, z]
            ends[1, x // (nx - 1), z] = m2[x, z]
            ends[2, x // (nx - 1), z] = m3[x, z]
    for x, out in ((0, first), (nx - 1, last)):
        for z in range(nz):
            out[z, :members, :] = before[x, z]
            out[z, members:, :] = free[x, z]


def last_ends_kernel(
    free, ends, low, high, diffusivity, binding, source, tracer, out_free, add
):
    nx, nz, members, _ = free.shape
    for end, (x, halo) in enumerate(((0, low), (nx - 1, high))):
        for z in range(nz):
            row = pl.ds(z, 1)
            value = free[x, z] + diffusivity[x, row, :] * halo[z, :members, :]
            back, _, complexed, internal = react(
                value, ends[0, end, z], ends[1, end, z], ends[2, end, z], binding[x, row, :]
            )
            tracer[end, z] = complexed + internal
            out_free[end, z] = value
            add[end, z] = back + source[x, row, :]


def last_free_kernel(
    before, free, free_ends, add, add_ends, low, high, low_first, high_first, diffusivity, out
):
    nx, nz, _, _ = free.shape
    outside = after_first(before, low, high, low_first, high_first)

    def read(x, z):
        return free[x, z] if 0 < x < nx - 1 else free_ends[x // (nx - 1), z]

    for x in range(nx):
        for z in range(nz):
            around = beside(read, x, z, nx, nz, *outside(x, z))
            rest = add[x - 1, z] if 0 < x < nx - 1 else add_ends[x // (nx - 1), z]
            out[x, z] = (
                spread_free(read(x, z), around, None, diffusivity[x, pl.ds(z, 1), :]) + rest
            )


def forecast_call(kernel, name, inputs, outputs, cells, scratch=(), ready=(), scalars=()):
    def body(*refs):
        count = len(scalars) + len(inputs)
        kernel(*refs[:count], *refs[count + len(ready) :])

    return pl.pallas_call(
        body,
        out_shape=[jax.ShapeDtypeStruct(shape, f32) for shape in outputs],
        in_specs=[SMEM] * len(scalars)
        + [VMEM] * len(inputs)
        + [pl.BlockSpec(memory_space=pl.ANY)] * len(ready),
        out_specs=[VMEM] * len(outputs),
        scratch_shapes=[pltpu.VMEM(shape, f32) for shape in scratch],
        compiler_params=pltpu.CompilerParams(vmem_limit_bytes=SCOPED),
        cost_estimate=pl.CostEstimate(
            flops=30 * cells, bytes_accessed=32 * cells, transcendentals=0
        ),
        name=name,
    )(*scalars, *inputs, *ready)


def weights_kernel(place, owner, obs_index, observed, obs_var, omega, eta):
    count, rows, ny = omega.shape
    batch_size = obs_index.shape[1]
    for k in range(count):
        batch = place[0] * count + k
        mine = owner[batch] == place[1]
        line = pl.ds(batch, 1)
        voxel = obs_index[line, :]
        scale = jnp.where(mine, 1.0, 0.0) / obs_var[line, :]
        shift = ny.bit_length() - 1
        row = lax.shift_right_logical(voxel, shift)
        column = jnp.bitwise_and(voxel, ny - 1)
        at_row = lax.broadcasted_iota(jnp.int32, (rows, batch_size), 0) == row
        at_column = lax.broadcasted_iota(jnp.int32, (ny, batch_size), 0) == column
        both = jnp.concatenate(
            [jnp.where(at_row, scale, 0.0), jnp.where(at_row, scale * observed[line, :], 0.0)],
            axis=0,
        )
        one = both.astype(bf16)
        rest = both - one.astype(f32)
        two = rest.astype(bf16)
        three = (rest - two.astype(f32)).astype(bf16)
        columns = jnp.where(at_column, 1.0, 0.0).astype(bf16)
        sums = lax.dot_general(
            jnp.concatenate([one, two, three], axis=0),
            columns,
            (NT, ((), ())),
            preferred_element_type=f32,
        )
        sums = sums[: 2 * rows] + sums[2 * rows : 4 * rows] + sums[4 * rows :]
        omega[k] = sums[:rows]
        eta[k] = sums[rows:]


def voxel_weights(place, owner, obs_index, observed, obs_var, count, rows, ny):
    out = jax.ShapeDtypeStruct((count, rows, ny), f32)
    return pl.pallas_call(
        weights_kernel,
        out_shape=[out, out],
        in_specs=[SMEM, SMEM, VMEM, VMEM, VMEM],
        out_specs=[VMEM, VMEM],
        compiler_params=pltpu.CompilerParams(vmem_limit_bytes=SCOPED),
        name="voxel_weights",
    )(place, owner, obs_index, observed, obs_var)


def gram_kernel(place, owner, omega, eta, *refs, offsets, planes, first):
    if first:
        *sources, out, members_at = refs
    else:
        begun, *sources, packed, out, members_at = refs
    count = out.shape[0]
    span, nz, rows, ny = sources[0].shape
    members = members_at.shape[0]
    for k in range(count):
        out[k] = jnp.zeros(out.shape[1:], f32) if first else begun[k]

        @pl.when(owner[place[0] * count + k] == place[1])
        def _(k=k):
            def tile(t, total):
                x, z = t // nz, t % nz
                voxels = pl.ds((planes[0] + x * planes[1]) * nz + z, 1)
                for j, source in enumerate(sources):
                    start = pl.multiple_of(offsets(place[2], j), 8)
                    members_at[pl.ds(start, rows), :] = source[x, z]
                values = members_at[...]
                mean = jnp.sum(values, axis=0, keepdims=True) * (1.0 / members)
                spread = values - mean
                weight = omega[k, voxels, :]
                shift = eta[k, voxels, :] - weight * mean
                tail = lax.broadcasted_iota(jnp.int32, (LANES - members, ny), 0)
                weighted = jnp.concatenate(
                    [spread * weight, jnp.where(tail == 0, shift, 0.0)], axis=0
                )
                return total + dot_parts(split(spread), split(weighted), NT)

            out[k] = lax.fori_loop(0, span * nz, tile, out[k], unroll=4)

    if first:
        return
    row = lax.broadcasted_iota(jnp.int32, (members, LANES), 0)
    column = lax.broadcasted_iota(jnp.int32, (members, LANES), 1)
    above, below = out[0], out[1]

    def pick(where, x):
        return jnp.sum(jnp.where(where, x, 0.0), axis=1, keepdims=True)

    both = jnp.where(column >= row, above, below)
    both = jnp.where(column == members, pick(column == row, below), both)
    both = jnp.where(column == members + 1, pick(column == members, above), both)
    packed[...] = jnp.where(column == members + 2, pick(column == members, below), both)


def gram(place, owner, omega, eta, begun, sources, offsets, planes):
    _, _, rows, ny = sources[0].shape
    members = rows * len(sources)
    whole = (omega.shape[0], members, LANES)
    work = pltpu.VMEM((members, ny), f32)
    first = begun is None
    return pl.pallas_call(
        functools.partial(gram_kernel, offsets=offsets, planes=planes, first=first),
        out_shape=jax.ShapeDtypeStruct(whole if first else whole[1:], f32),
        in_specs=[SMEM, SMEM] + [VMEM] * (2 + len(sources) + (not first)),
        out_specs=VMEM,
        scratch_shapes=[work] if first else [pltpu.VMEM(whole, f32), work],
        compiler_params=pltpu.CompilerParams(vmem_limit_bytes=SCOPED),
        name="gram",
    )(place, owner, omega, eta, *([] if first else [begun]), *sources)


def turned(x):
    rows = x.shape[0]
    whole = jnp.concatenate([x, jnp.zeros((LANES - rows, LANES), f32)], axis=0)
    return whole.T[:rows]


def batch_transform(extended, total, members):
    row = lax.broadcasted_iota(jnp.int32, extended.shape, 0)
    column = lax.broadcasted_iota(jnp.int32, extended.shape, 1)
    inside = column < members
    last = column == members
    identity = jnp.where(row == column, 1.0, 0.0)
    matrix = jnp.where(inside, extended, 0.0)

    mean = jnp.sum(total, axis=1, keepdims=True) * (1.0 / members)
    centred = jnp.where(inside, total - mean, 0.0)
    product = wide_dot(wide_left(matrix), wide_right(jnp.where(last, mean, centred)))
    product = jnp.where(last, extended - product, product)
    product = wide_dot(wide_left(turned(centred)), wide_right(product)) * (1.0 / (members - 1))
    innovation = jnp.sum(jnp.where(last, product, 0.0), axis=1, keepdims=True)
    system = identity + jnp.where(inside, product, 0.0)
    frobenius = jnp.sqrt(jnp.sum(jnp.sum(system * system, axis=1, keepdims=True), axis=0, keepdims=True))

    scaled_root = system / frobenius
    factor = 1.5 * identity - 0.5 * scaled_root
    scaled_root = wide_dot(wide_left(scaled_root), wide_right(factor))
    inverse_root = factor

    def newton(iteration, iterates):
        scaled_root, inverse_root = iterates
        factor = 1.5 * identity - 0.5 * wide_dot(
            wide_left(inverse_root), wide_right(scaled_root)
        )
        return (
            wide_dot(wide_left(scaled_root), wide_right(factor)),
            wide_dot(wide_left(factor), wide_right(inverse_root)),
        )

    scaled_root, inverse_root = lax.fori_loop(1, NEWTON, newton, (scaled_root, inverse_root), unroll=UNROLL)
    root_inv = inverse_root / jnp.sqrt(frobenius)
    mean_weight = jnp.sum(root_inv * innovation, axis=0, keepdims=True)
    mean_weight = jnp.sum(root_inv * mean_weight, axis=1, keepdims=True)
    mixing = jnp.where(inside, root_inv + mean_weight, 0.0)
    mixing = mixing - jnp.sum(mixing, axis=0, keepdims=True) * (1.0 / members)
    mixing = jnp.where(inside, mixing + 1.0 / members, 0.0)
    return wide_dot(wide_left(total), wide_right(mixing))


def early_kernel(place, mine, other, total, last, ordered):
    members = mine.shape[0]
    row = lax.broadcasted_iota(jnp.int32, (members, LANES), 0)
    column = lax.broadcasted_iota(jnp.int32, (members, LANES), 1)
    inside = column < members

    def pick(where, x):
        return jnp.sum(jnp.where(where, x, 0.0), axis=1, keepdims=True)

    for half, shared in ((place[0], mine), (1 - place[0], other)):
        packed = shared[...]
        above = jnp.where(inside & (column > row), packed, 0.0)
        below = jnp.where(inside & (column < row), packed, 0.0)
        middle = jnp.where(column == row, packed, 0.0)
        side = jnp.where(column == members, pick(column == members + 1, packed), 0.0)
        ordered[2 * half] = above + turned(above) + (middle + side)
        middle = jnp.where(column == row, pick(column == members, packed), 0.0)
        side = jnp.where(column == members, pick(column == members + 2, packed), 0.0)
        ordered[2 * half + 1] = below + turned(below) + (middle + side)
    batches = ordered.shape[0]
    product = jnp.where(row == column, 1.0, 0.0)
    for batch in range(batches - 1):
        product = batch_transform(ordered[batch], product, members)
    total[...] = product
    last[...] = ordered[batches - 1]


def late_kernel(place, total, last, out, work, *, offsets, blocks, rows):
    members = total.shape[0]
    product = batch_transform(last[...], total[...], members)
    rest = jnp.zeros((LANES - members, LANES), f32)
    work[...] = jnp.concatenate([product, rest], axis=0)
    if blocks == 1:
        out[...] = work[...].T
        return
    parts = [
        work[pl.ds(pl.multiple_of(offsets(place[2], j), 8), rows), :] for j in range(blocks)
    ]
    work[...] = jnp.concatenate([*parts, rest], axis=0).T
    out[...] = work[pl.ds(pl.multiple_of(offsets(place[2], 0), 8), rows), :]


def transform_call(kernel, name, outputs, scratch, inputs):
    return pl.pallas_call(
        kernel,
        out_shape=[jax.ShapeDtypeStruct(shape, f32) for shape in outputs],
        in_specs=[SMEM] + [VMEM] * (len(inputs) - 1),
        out_specs=[VMEM] * len(outputs),
        scratch_shapes=[pltpu.VMEM(shape, f32) for shape in scratch],
        compiler_params=pltpu.CompilerParams(vmem_limit_bytes=SCOPED),
        cost_estimate=pl.CostEstimate(
            flops=10**8, bytes_accessed=10**6, transcendentals=0
        ),
        name=name,
    )(*inputs)


def mix_kernel(weights, *refs, blocks):
    *sources, out = refs
    rows, _, _, nz, _ = out.shape
    x, nx = pl.program_id(0), pl.num_programs(0)
    free, conserved, internal, tracer, tracer_ends = [
        sources[k : k + blocks] for k in range(0, len(sources), blocks)
    ]
    members = blocks * free[0].shape[2]
    high, low = split(weights[:, :members])
    both = jnp.concatenate([high.astype(f32), low.astype(f32)], axis=0).astype(bf16)
    mul = functools.partial(
        lax.dot_general, dimension_numbers=(NN, ((), ())), preferred_element_type=f32
    )

    def mixed(held, x, z):
        parts = [array[x, z] for array in held]
        values = parts[0] if blocks == 1 else jnp.concatenate(parts, axis=0)
        value_high, value_low = split(values)
        upper = mul(both, value_high)
        return upper[:rows] + (upper[rows:] + mul(high, value_low))

    def plane(tracer, at):
        for z in range(nz):
            bound = mixed(tracer, at, z)
            inside = mixed(internal, x, z)
            out[:, 0, 0, z, :] = mixed(free, x, z)
            out[:, 1, 0, z, :] = mixed(conserved, x, z) - bound
            out[:, 2, 0, z, :] = bound - inside
            out[:, 3, 0, z, :] = inside

    at_end = (x == 0) | (x == nx - 1)

    @pl.when(at_end)
    def _():
        plane(tracer_ends, x // (nx - 1))

    @pl.when(jnp.logical_not(at_end))
    def _():
        plane(tracer, x - 1)


def mix(weights, sources, blocks, shape):
    rows, species, nx, nz, ny = shape
    return pl.pallas_call(
        functools.partial(mix_kernel, blocks=blocks),
        grid=(nx,),
        in_specs=[VMEM] * (1 + len(sources)),
        out_specs=pl.BlockSpec((rows, species, 1, nz, ny), lambda x: (0, 0, x, 0, 0)),
        out_shape=jax.ShapeDtypeStruct(shape, f32),
        compiler_params=pltpu.CompilerParams(vmem_limit_bytes=SCOPED),
        name="mix",
    )(weights, *sources)


def swap(x, axis, bit):
    count = lax.axis_size(axis)
    return lax.ppermute(x, axis, [(k, k ^ bit) for k in range(count)])


def total_over(x, axis, *before_last):
    bit, count = 1, lax.axis_size(axis)
    while bit < count:
        if before_last and 2 * bit >= count:
            x = lax.optimization_barrier((x, *before_last))[0]
        x = x + swap(x, axis, bit)
        bit *= 2
    return x


def local(ensemble, diffusivity, binding, source, obs_index, owner, observed, obs_var):
    rows, species, nx, nz, ny = ensemble.shape
    devices = lax.axis_size("member")
    spaces = lax.axis_size("space")
    members = rows * devices
    batches = owner.shape[0]
    member = lax.axis_index("member")
    place = jnp.stack([member & 1, lax.axis_index("space"), member]).astype(jnp.int32)

    forward = [(k, k + 1) for k in range(spaces - 1)]
    backward = [(k + 1, k) for k in range(spaces - 1)]

    def halos(first, last):
        return lax.ppermute(last, "space", forward), lax.ppermute(first, "space", backward)

    def tie(x, *after):
        return lax.optimization_barrier((x, *after))[0]

    if devices == 4 and rows % 8 == 0:
        blocks = devices

        def offsets(position, j):
            return jnp.bitwise_xor(position, j) * rows

        def collect(x, *after):
            return [x, swap(x, "member", 1), swap(tie(x, *after), "member", 2)]

        def complete(held, *after):
            return [*held, swap(lax.optimization_barrier((held[2], *after))[0], "member", 1)]
    else:
        blocks = 1

        def offsets(position, j):
            return 0

        def collect(x, *after):
            return [lax.all_gather(x, "member", axis=2, tiled=True)]

        def complete(held, *after):
            return held

    def across(held):
        return held[min(2, blocks - 1)]

    whole = (nx, nz, rows, ny)
    coefficients = (diffusivity, binding, source)
    cells = nx * nz * rows * ny
    ends = [
        jnp.transpose(ensemble[:, :3, part], (1, 2, 3, 0, 4))
        for part in (slice(0, 2), slice(nx - 2, nx))
    ]
    edges = forecast_call(
        first_edges_kernel,
        "first_edges",
        [*ends, *coefficients],
        [(nz, 2 * rows + 8, ny)] * 2,
        2 * cells // nx,
        scalars=[place],
    )
    fields = [jnp.transpose(ensemble[:, k], (1, 2, 0, 3)) for k in range(species)]
    conserved = fields[1] + fields[2] + fields[3]
    omega, eta = voxel_weights(
        place, owner, obs_index, observed, obs_var, batches // 2, nx * nz, ny
    )
    around = origin = halos(*edges)
    payload = (nz, 2 * rows, ny)
    for step in range(SUBSTEPS // 2 - 2):
        inputs = [*fields, *around, *origin, *coefficients]
        around = halos(
            *forecast_call(
                next_edges_kernel, "next_edges", inputs, [payload] * 2, cells, scratch=[whole] * 8
            )
        )
        fields = forecast_call(
            two_substeps_kernel, "two_substeps", inputs, [whole] * 4, 2 * cells, scratch=[whole] * 4
        )
        if step == 0:
            conserved = collect(conserved, fields[0])
    inner, end = (nx - 2, nz, rows, ny), (2, nz, rows, ny)
    before, first, last, free, tracer, internal, add, ends = forecast_call(
        last_steps_kernel,
        "last_steps",
        [*fields, *around, *origin, *coefficients],
        [whole, payload, payload, whole, inner, whole, inner, (3, *end)],
        4 * cells,
        scratch=[whole] * 7,
        ready=(omega, eta, *conserved[1:]),
    )
    tracer = collect(tracer)
    around = halos(first, last)
    tracer_ends, free_ends, add_ends = forecast_call(
        last_ends_kernel,
        "last_ends",
        [free, ends, *around, *coefficients],
        [end] * 3,
        cells // nx,
    )
    tracer = complete(tracer, tracer_ends)
    tracer_ends = collect(tracer_ends)
    conserved = complete(conserved, tracer_ends[0])
    begun = gram(place, owner, omega, eta, None, tracer, offsets, (1, 1))
    tracer_ends = complete(tracer_ends, begun)
    (free,) = forecast_call(
        last_free_kernel,
        "last_free",
        [before, free, free_ends, add, add_ends, *around, *origin, diffusivity],
        [whole],
        cells,
    )
    internal = collect(internal, across(tracer_ends))
    half = gram(place, owner, omega, eta, begun, tracer_ends, offsets, (0, nx - 1))
    free = collect(free, half)
    half = total_over(half, "space")
    other = swap(half, "member", 1)
    internal = complete(internal, half)
    square = (members, LANES)
    total, extended = transform_call(
        early_kernel,
        "transforms_early",
        [square, square],
        [(batches, members, LANES)],
        [place, half, other],
    )
    free = complete(free, total)
    (weights,) = transform_call(
        functools.partial(late_kernel, offsets=offsets, blocks=blocks, rows=rows),
        "transforms_late",
        [(LANES, LANES) if blocks == 1 else (rows, LANES)],
        [(LANES, LANES)],
        [place, total, extended],
    )
    if blocks == 1:
        weights = lax.dynamic_slice(weights, (member * rows, 0), (rows, LANES))
    held = free + conserved + internal + tracer + tracer_ends
    return mix(weights, held, blocks, ensemble.shape)


def solution(mesh):
    in_specs = (
        P("member", None, "space", None, None),
        P("space", None, None),
        P("space", None, None),
        P("space", None, None),
        P(),
        P(),
        P(),
        P(),
    )
    out_specs = P("member", None, "space", None, None)
    return jax.shard_map(local, mesh=mesh, in_specs=in_specs, out_specs=out_specs, check_vma=False)
```

```python
import functools

import jax
import jax.numpy as jnp
from jax import lax
from jax.experimental import pallas as pl
from jax.experimental.pallas import tpu as pltpu
from jax.sharding import PartitionSpec as P

SUBSTEPS = 6
NEWTON = 16
UNROLL = 5
LANES = 128
SCOPED = 10 * 2**20

unbind_rate = 0.05
uptake_rate = 0.1
recycle_rate = 0.02

VMEM = pl.BlockSpec(memory_space=pltpu.VMEM)
SMEM = pl.BlockSpec(memory_space=pltpu.SMEM)
bf16 = jnp.bfloat16
f32 = jnp.float32


def split(x):
    high = x.astype(bf16)
    return high, (x - high.astype(f32)).astype(bf16)


def dot_parts(a, b, dims):
    a_high, a_low = a
    b_high, b_low = b
    mul = functools.partial(
        lax.dot_general, dimension_numbers=(dims, ((), ())), preferred_element_type=f32
    )
    return mul(a_high, b_high) + (mul(a_high, b_low) + mul(a_low, b_high))


def wide_left(x):
    return jnp.concatenate(split(x), axis=1)


def wide_right(x):
    both = jnp.concatenate(split(x), axis=1)
    rows, lanes = both.shape
    if rows < lanes // 2:
        both = jnp.concatenate([both, jnp.zeros((lanes // 2 - rows, lanes), bf16)], axis=0)
    return jnp.concatenate([both, both], axis=0)


def wide_dot(left, right):
    out = jnp.dot(left, right, preferred_element_type=f32)
    side = out.shape[1] // 2
    return out[:, :side] + out[:, side:]


NN = ((1,), (0,))
NT = ((1,), (1,))


def position():
    member = lax.axis_index("member")
    return member & 1, lax.axis_index("space"), member


def react(free, receptor, complexed, internal, binding):
    flux = binding * free * receptor
    back = unbind_rate * complexed - flux
    return (
        back,
        receptor + back + recycle_rate * internal,
        complexed + flux - (unbind_rate + uptake_rate) * complexed,
        internal + uptake_rate * complexed - recycle_rate * internal,
    )


def spread_free(free, planes, neighbours, diffusivity):
    lane = lax.broadcasted_iota(jnp.int32, free.shape, 1)
    last = free.shape[1] - 1
    for plane in planes:
        neighbours = plane if neighbours is None else neighbours + plane
    neighbours += jnp.where(lane == last, 0.0, pltpu.roll(free, last, 1))
    neighbours += jnp.where(lane == 0, 0.0, pltpu.roll(free, 1, 1))
    return free + diffusivity * (neighbours - 6.0 * free)


def beside(read, x, z, nx, nz, low, high):
    around = [low if x == 0 else read(x - 1, z), high if x == nx - 1 else read(x + 1, z)]
    around += [read(x, other) for other in (z + 1, z - 1) if 0 <= other < nz]
    return [value for value in around if value is not None]


def edge_free(read, rest, x, nz, nx, z, diffusivity):
    return spread_free(read(x, z), beside(read, x, z, nx, nz, None, None), None, diffusivity) + rest


def first_edges_kernel(below, above, diffusivity, binding, source, first, last):
    _, _, nz, members, _ = below.shape
    nx = diffusivity.shape[0]
    for x, ends, out in ((0, below, first), (nx - 1, above, last)):
        shift = 0 if x == 0 else nx - 2

        def read(at, z, ends=ends, shift=shift):
            return ends[0, at - shift, z]

        for z in range(nz):
            row = pl.ds(z, 1)
            free = read(x, z)
            flux = binding[x, row, :] * free * ends[1, x - shift, z]
            rest = unbind_rate * ends[2, x - shift, z] - flux + source[x, row, :]
            spread = diffusivity[x, row, :]
            out[z, :members, :] = free
            out[z, members : 2 * members, :] = edge_free(read, rest, x, nz, nx, z, spread)
            out[z, 2 * members :, :] = jnp.broadcast_to(spread, (8, spread.shape[1]))


def step_planes(planes, a, r, c, i, outside, diffusivity, binding, source, out_a, outs, keep):
    nx, nz, _, _ = a.shape
    for x in planes:
        for z in range(nz):
            row = pl.ds(z, 1)
            back, *others = react(a[x, z], r[x, z], c[x, z], i[x, z], binding[x, row, :])
            around = beside(lambda x, z: a[x, z], x, z, nx, nz, *outside(x, z))
            out_a[x, z] = (
                spread_free(a[x, z], around, None, diffusivity[x, row, :])
                + back
                + source[x, row, :]
            )
            if x in keep:
                for out, value in zip(outs, others):
                    out[x, z] = value


def before_last(a, low, high):
    nx, _, members, _ = a.shape

    def outside(x, z):
        return (
            low[z, :members, :] if x == 0 else None,
            high[z, :members, :] if x == nx - 1 else None,
        )

    return outside


def after_first(a, low, high, low_first, high_first):
    nx, _, members, _ = a.shape

    def completed(halo, origin, x, z):
        later = halo[z, members : 2 * members, :]
        return later + origin[z, 2 * members : 2 * members + 1, :] * a[x, z]

    def outside(x, z):
        return (
            completed(low, low_first, x, z) if x == 0 else None,
            completed(high, high_first, x, z) if x == nx - 1 else None,
        )

    return outside


def next_edges_kernel(
    a, r, c, i, low, high, low_first, high_first, diffusivity, binding, source, *refs
):
    first, last, *kept = refs
    middle, later = kept[:4], kept[4:]
    nx, nz, members, _ = a.shape
    coefficients = (diffusivity, binding, source)

    def near(depth):
        return [x for x in range(nx) if min(x, nx - 1 - x) < depth]

    step_planes(
        near(3), a, r, c, i, before_last(a, low, high), *coefficients, middle[0], middle[1:], near(2)
    )
    step_planes(
        near(2),
        *middle,
        after_first(a, low, high, low_first, high_first),
        *coefficients,
        later[0],
        later[1:],
        near(1),
    )
    free, receptor, complexed = later[:3]
    for x, out in ((0, first), (nx - 1, last)):
        for z in range(nz):
            row = pl.ds(z, 1)
            flux = binding[x, row, :] * free[x, z] * receptor[x, z]
            rest = unbind_rate * complexed[x, z] - flux + source[x, row, :]
            out[z, :members, :] = free[x, z]
            out[z, members:, :] = edge_free(
                lambda x, z: free[x, z], rest, x, nz, nx, z, diffusivity[x, row, :]
            )


def two_substeps_kernel(
    a, r, c, i, low, high, low_first, high_first, diffusivity, binding, source, *refs
):
    outs, middle = refs[:4], refs[4:]
    everywhere = range(a.shape[0])
    coefficients = (diffusivity, binding, source)
    step_planes(
        everywhere,
        a,
        r,
        c,
        i,
        before_last(a, low, high),
        *coefficients,
        middle[0],
        middle[1:],
        everywhere,
    )
    step_planes(
        everywhere,
        *middle,
        after_first(a, low, high, low_first, high_first),
        *coefficients,
        outs[0],
        outs[1:],
        everywhere,
    )


def last_steps_kernel(
    a, r, c, i, low, high, low_first, high_first, diffusivity, binding, source, *refs
):
    *outs, m0, m1, m2, m3, later_r, later_c, later_i = refs
    before, first, last, free, tracer, inside, add, ends = outs
    nx, nz, members, _ = a.shape
    coefficients = (diffusivity, binding, source)
    two_substeps_kernel(
        a,
        r,
        c,
        i,
        low,
        high,
        low_first,
        high_first,
        *coefficients,
        before,
        later_r,
        later_c,
        later_i,
        m0,
        m1,
        m2,
        m3,
    )
    step_planes(
        range(nx),
        before,
        later_r,
        later_c,
        later_i,
        lambda x, z: (None, None),
        *coefficients,
        free,
        (m1, m2, m3),
        range(nx),
    )
    for x in range(nx):
        for z in range(nz):
            row = pl.ds(z, 1)
            back, _, complexed, internal = react(
                free[x, z], m1[x, z], m2[x, z], m3[x, z], binding[x, row, :]
            )
            inside[x, z] = internal
            if 0 < x < nx - 1:
                tracer[x - 1, z] = complexed + internal
                add[x - 1, z] = back + source[x, row, :]
                continue
            ends[0, x // (nx - 1), z] = m1[x, z]
            ends[1, x // (nx - 1), z] = m2[x, z]
            ends[2, x // (nx - 1), z] = m3[x, z]
    for x, out in ((0, first), (nx - 1, last)):
        for z in range(nz):
            out[z, :members, :] = before[x, z]
            out[z, members:, :] = free[x, z]


def last_ends_kernel(
    free, ends, low, high, diffusivity, binding, source, tracer, out_free, add
):
    nx, nz, members, _ = free.shape
    for end, (x, halo) in enumerate(((0, low), (nx - 1, high))):
        for z in range(nz):
            row = pl.ds(z, 1)
            value = free[x, z] + diffusivity[x, row, :] * halo[z, :members, :]
            back, _, complexed, internal = react(
                value, ends[0, end, z], ends[1, end, z], ends[2, end, z], binding[x, row, :]
            )
            tracer[end, z] = complexed + internal
            out_free[end, z] = value
            add[end, z] = back + source[x, row, :]


def last_free_kernel(
    before, free, free_ends, add, add_ends, low, high, low_first, high_first, diffusivity, out
):
    nx, nz, _, _ = free.shape
    outside = after_first(before, low, high, low_first, high_first)

    def read(x, z):
        return free[x, z] if 0 < x < nx - 1 else free_ends[x // (nx - 1), z]

    for x in range(nx):
        for z in range(nz):
            around = beside(read, x, z, nx, nz, *outside(x, z))
            rest = add[x - 1, z] if 0 < x < nx - 1 else add_ends[x // (nx - 1), z]
            out[x, z] = (
                spread_free(read(x, z), around, None, diffusivity[x, pl.ds(z, 1), :]) + rest
            )


def forecast_call(kernel, name, inputs, outputs, cells, scratch=(), ready=()):
    def body(*refs):
        kernel(*refs[: len(inputs)], *refs[len(inputs) + len(ready) :])

    return pl.pallas_call(
        body,
        out_shape=[jax.ShapeDtypeStruct(shape, f32) for shape in outputs],
        in_specs=[VMEM] * len(inputs) + [pl.BlockSpec(memory_space=pl.ANY)] * len(ready),
        out_specs=[VMEM] * len(outputs),
        scratch_shapes=[pltpu.VMEM(shape, f32) for shape in scratch],
        compiler_params=pltpu.CompilerParams(vmem_limit_bytes=SCOPED),
        cost_estimate=pl.CostEstimate(
            flops=30 * cells, bytes_accessed=32 * cells, transcendentals=0
        ),
        name=name,
    )(*inputs, *ready)


def weights_kernel(owner, obs_index, observed, obs_var, omega, eta):
    place = position()
    count, rows, ny = omega.shape
    batch_size = obs_index.shape[1]
    for k in range(count):
        batch = place[0] * count + k
        mine = owner[batch] == place[1]
        line = pl.ds(batch, 1)
        voxel = obs_index[line, :]
        scale = jnp.where(mine, 1.0, 0.0) / obs_var[line, :]
        shift = ny.bit_length() - 1
        row = lax.shift_right_logical(voxel, shift)
        column = jnp.bitwise_and(voxel, ny - 1)
        at_row = lax.broadcasted_iota(jnp.int32, (rows, batch_size), 0) == row
        at_column = lax.broadcasted_iota(jnp.int32, (ny, batch_size), 0) == column
        both = jnp.concatenate(
            [jnp.where(at_row, scale, 0.0), jnp.where(at_row, scale * observed[line, :], 0.0)],
            axis=0,
        )
        one = both.astype(bf16)
        rest = both - one.astype(f32)
        two = rest.astype(bf16)
        three = (rest - two.astype(f32)).astype(bf16)
        columns = jnp.where(at_column, 1.0, 0.0).astype(bf16)
        sums = lax.dot_general(
            jnp.concatenate([one, two, three], axis=0),
            columns,
            (NT, ((), ())),
            preferred_element_type=f32,
        )
        sums = sums[: 2 * rows] + sums[2 * rows : 4 * rows] + sums[4 * rows :]
        omega[k] = sums[:rows]
        eta[k] = sums[rows:]


def voxel_weights(owner, obs_index, observed, obs_var, count, rows, ny):
    out = jax.ShapeDtypeStruct((count, rows, ny), f32)
    return pl.pallas_call(
        weights_kernel,
        out_shape=[out, out],
        in_specs=[SMEM, VMEM, VMEM, VMEM],
        out_specs=[VMEM, VMEM],
        compiler_params=pltpu.CompilerParams(vmem_limit_bytes=SCOPED),
        name="voxel_weights",
    )(owner, obs_index, observed, obs_var)


def gram_kernel(owner, omega, eta, *refs, offsets, planes, first):
    place = position()
    if first:
        *sources, out, members_at = refs
    else:
        begun, *sources, packed, out, members_at = refs
    count = out.shape[0]
    span, nz, rows, ny = sources[0].shape
    members = members_at.shape[0]
    for k in range(count):
        out[k] = jnp.zeros(out.shape[1:], f32) if first else begun[k]

        @pl.when(owner[place[0] * count + k] == place[1])
        def _(k=k):
            def tile(t, total):
                x, z = t // nz, t % nz
                voxels = pl.ds((planes[0] + x * planes[1]) * nz + z, 1)
                for j, source in enumerate(sources):
                    start = pl.multiple_of(offsets(place[2], j), 8)
                    members_at[pl.ds(start, rows), :] = source[x, z]
                values = members_at[...]
                mean = jnp.sum(values, axis=0, keepdims=True) * (1.0 / members)
                spread = values - mean
                weight = omega[k, voxels, :]
                shift = eta[k, voxels, :] - weight * mean
                tail = lax.broadcasted_iota(jnp.int32, (LANES - members, ny), 0)
                weighted = jnp.concatenate(
                    [spread * weight, jnp.where(tail == 0, shift, 0.0)], axis=0
                )
                return total + dot_parts(split(spread), split(weighted), NT)

            out[k] = lax.fori_loop(0, span * nz, tile, out[k], unroll=4)

    if first:
        return
    row = lax.broadcasted_iota(jnp.int32, (members, LANES), 0)
    column = lax.broadcasted_iota(jnp.int32, (members, LANES), 1)
    above, below = out[0], out[1]

    def pick(where, x):
        return jnp.sum(jnp.where(where, x, 0.0), axis=1, keepdims=True)

    both = jnp.where(column >= row, above, below)
    both = jnp.where(column == members, pick(column == row, below), both)
    both = jnp.where(column == members + 1, pick(column == members, above), both)
    packed[...] = jnp.where(column == members + 2, pick(column == members, below), both)


def gram(owner, omega, eta, begun, sources, offsets, planes):
    _, _, rows, ny = sources[0].shape
    members = rows * len(sources)
    whole = (omega.shape[0], members, LANES)
    work = pltpu.VMEM((members, ny), f32)
    first = begun is None
    return pl.pallas_call(
        functools.partial(gram_kernel, offsets=offsets, planes=planes, first=first),
        out_shape=jax.ShapeDtypeStruct(whole if first else whole[1:], f32),
        in_specs=[SMEM] + [VMEM] * (2 + len(sources) + (not first)),
        out_specs=VMEM,
        scratch_shapes=[work] if first else [pltpu.VMEM(whole, f32), work],
        compiler_params=pltpu.CompilerParams(vmem_limit_bytes=SCOPED),
        name="gram",
    )(owner, omega, eta, *([] if first else [begun]), *sources)


def turned(x):
    rows = x.shape[0]
    whole = jnp.concatenate([x, jnp.zeros((LANES - rows, LANES), f32)], axis=0)
    return whole.T[:rows]


def batch_transform(extended, total, members):
    row = lax.broadcasted_iota(jnp.int32, extended.shape, 0)
    column = lax.broadcasted_iota(jnp.int32, extended.shape, 1)
    inside = column < members
    last = column == members
    identity = jnp.where(row == column, 1.0, 0.0)
    matrix = jnp.where(inside, extended, 0.0)

    mean = jnp.sum(total, axis=1, keepdims=True) * (1.0 / members)
    centred = jnp.where(inside, total - mean, 0.0)
    product = wide_dot(wide_left(matrix), wide_right(jnp.where(last, mean, centred)))
    product = jnp.where(last, extended - product, product)
    product = wide_dot(wide_left(turned(centred)), wide_right(product)) * (1.0 / (members - 1))
    innovation = jnp.sum(jnp.where(last, product, 0.0), axis=1, keepdims=True)
    system = identity + jnp.where(inside, product, 0.0)
    frobenius = jnp.sqrt(jnp.sum(jnp.sum(system * system, axis=1, keepdims=True), axis=0, keepdims=True))

    scaled_root = system / frobenius
    factor = 1.5 * identity - 0.5 * scaled_root
    scaled_root = wide_dot(wide_left(scaled_root), wide_right(factor))
    inverse_root = factor

    def newton(iteration, iterates):
        scaled_root, inverse_root = iterates
        factor = 1.5 * identity - 0.5 * wide_dot(
            wide_left(inverse_root), wide_right(scaled_root)
        )
        return (
            wide_dot(wide_left(scaled_root), wide_right(factor)),
            wide_dot(wide_left(factor), wide_right(inverse_root)),
        )

    scaled_root, inverse_root = lax.fori_loop(1, NEWTON, newton, (scaled_root, inverse_root), unroll=UNROLL)
    root_inv = inverse_root / jnp.sqrt(frobenius)
    mean_weight = jnp.sum(root_inv * innovation, axis=0, keepdims=True)
    mean_weight = jnp.sum(root_inv * mean_weight, axis=1, keepdims=True)
    mixing = jnp.where(inside, root_inv + mean_weight, 0.0)
    mixing = mixing - jnp.sum(mixing, axis=0, keepdims=True) * (1.0 / members)
    mixing = jnp.where(inside, mixing + 1.0 / members, 0.0)
    return wide_dot(wide_left(total), wide_right(mixing))


def early_kernel(mine, other, total, last, ordered):
    place = position()
    members = mine.shape[0]
    row = lax.broadcasted_iota(jnp.int32, (members, LANES), 0)
    column = lax.broadcasted_iota(jnp.int32, (members, LANES), 1)
    inside = column < members

    def pick(where, x):
        return jnp.sum(jnp.where(where, x, 0.0), axis=1, keepdims=True)

    for half, shared in ((place[0], mine), (1 - place[0], other)):
        packed = shared[...]
        above = jnp.where(inside & (column > row), packed, 0.0)
        below = jnp.where(inside & (column < row), packed, 0.0)
        middle = jnp.where(column == row, packed, 0.0)
        side = jnp.where(column == members, pick(column == members + 1, packed), 0.0)
        ordered[2 * half] = above + turned(above) + (middle + side)
        middle = jnp.where(column == row, pick(column == members, packed), 0.0)
        side = jnp.where(column == members, pick(column == members + 2, packed), 0.0)
        ordered[2 * half + 1] = below + turned(below) + (middle + side)
    batches = ordered.shape[0]
    product = jnp.where(row == column, 1.0, 0.0)
    for batch in range(batches - 1):
        product = batch_transform(ordered[batch], product, members)
    total[...] = product
    last[...] = ordered[batches - 1]


def late_kernel(total, last, out, work, *, offsets, blocks, rows):
    place = position()
    members = total.shape[0]
    product = batch_transform(last[...], total[...], members)
    rest = jnp.zeros((LANES - members, LANES), f32)
    work[...] = jnp.concatenate([product, rest], axis=0)
    if blocks == 1:
        out[...] = work[...].T
        return
    parts = [
        work[pl.ds(pl.multiple_of(offsets(place[2], j), 8), rows), :] for j in range(blocks)
    ]
    work[...] = jnp.concatenate([*parts, rest], axis=0).T
    out[...] = work[pl.ds(pl.multiple_of(offsets(place[2], 0), 8), rows), :]


def transform_call(kernel, name, outputs, scratch, inputs):
    return pl.pallas_call(
        kernel,
        out_shape=[jax.ShapeDtypeStruct(shape, f32) for shape in outputs],
        in_specs=[VMEM] * len(inputs),
        out_specs=[VMEM] * len(outputs),
        scratch_shapes=[pltpu.VMEM(shape, f32) for shape in scratch],
        compiler_params=pltpu.CompilerParams(vmem_limit_bytes=SCOPED),
        cost_estimate=pl.CostEstimate(
            flops=10**8, bytes_accessed=10**6, transcendentals=0
        ),
        name=name,
    )(*inputs)


def mix_kernel(weights, *refs, blocks):
    *sources, out = refs
    rows, _, _, nz, _ = out.shape
    x, nx = pl.program_id(0), pl.num_programs(0)
    free, conserved, internal, tracer, tracer_ends = [
        sources[k : k + blocks] for k in range(0, len(sources), blocks)
    ]
    members = blocks * free[0].shape[2]
    high, low = split(weights[:, :members])
    high, low = high.astype(f32), low.astype(f32)
    both = jnp.concatenate(
        [
            jnp.concatenate([high, high], axis=1),
            jnp.concatenate([low, jnp.zeros_like(low)], axis=1),
        ],
        axis=0,
    ).astype(bf16)

    def mixed(held, x, z):
        parts = [array[x, z] for array in held]
        values = parts[0] if blocks == 1 else jnp.concatenate(parts, axis=0)
        out = jnp.dot(
            both, jnp.concatenate(split(values), axis=0), preferred_element_type=f32
        )
        return out[:rows] + out[rows:]

    def plane(tracer, at):
        for z in range(nz):
            bound = mixed(tracer, at, z)
            inside = mixed(internal, x, z)
            out[:, 0, 0, z, :] = mixed(free, x, z)
            out[:, 1, 0, z, :] = mixed(conserved, x, z) - bound
            out[:, 2, 0, z, :] = bound - inside
            out[:, 3, 0, z, :] = inside

    at_end = (x == 0) | (x == nx - 1)

    @pl.when(at_end)
    def _():
        plane(tracer_ends, x // (nx - 1))

    @pl.when(jnp.logical_not(at_end))
    def _():
        plane(tracer, x - 1)


def mix(weights, sources, blocks, shape):
    rows, species, nx, nz, ny = shape
    return pl.pallas_call(
        functools.partial(mix_kernel, blocks=blocks),
        grid=(nx,),
        in_specs=[VMEM] * (1 + len(sources)),
        out_specs=pl.BlockSpec((rows, species, 1, nz, ny), lambda x: (0, 0, x, 0, 0)),
        out_shape=jax.ShapeDtypeStruct(shape, f32),
        compiler_params=pltpu.CompilerParams(vmem_limit_bytes=SCOPED),
        name="mix",
    )(weights, *sources)


def swap(x, axis, bit):
    count = lax.axis_size(axis)
    return lax.ppermute(x, axis, [(k, k ^ bit) for k in range(count)])


def total_over(x, axis, bit):
    while bit < lax.axis_size(axis):
        x = x + swap(x, axis, bit)
        bit *= 2
    return x


def local(ensemble, diffusivity, binding, source, obs_index, owner, observed, obs_var):
    rows, species, nx, nz, ny = ensemble.shape
    devices = lax.axis_size("member")
    spaces = lax.axis_size("space")
    members = rows * devices
    batches = owner.shape[0]
    member = lax.axis_index("member")

    forward = [(k, k + 1) for k in range(spaces - 1)]
    backward = [(k + 1, k) for k in range(spaces - 1)]

    def halos(first, last):
        return lax.ppermute(last, "space", forward), lax.ppermute(first, "space", backward)

    def tie(x, *after):
        return lax.optimization_barrier((x, *after))[0]

    if devices == 4 and rows % 8 == 0:
        blocks = devices

        def offsets(position, j):
            return jnp.bitwise_xor(position, j) * rows

        def collect(x, *after):
            return [x, swap(x, "member", 1), swap(tie(x, *after), "member", 2)]

        def complete(held, *after):
            return [*held, swap(lax.optimization_barrier((held[2], *after))[0], "member", 1)]
    else:
        blocks = 1

        def offsets(position, j):
            return 0

        def collect(x, *after):
            return [lax.all_gather(x, "member", axis=2, tiled=True)]

        def complete(held, *after):
            return held

    def across(held):
        return held[min(2, blocks - 1)]

    whole = (nx, nz, rows, ny)
    coefficients = (diffusivity, binding, source)
    cells = nx * nz * rows * ny
    ends = [
        jnp.transpose(ensemble[:, :3, part], (1, 2, 3, 0, 4))
        for part in (slice(0, 2), slice(nx - 2, nx))
    ]
    edges = forecast_call(
        first_edges_kernel,
        "first_edges",
        [*ends, *coefficients],
        [(nz, 2 * rows + 8, ny)] * 2,
        2 * cells // nx,
    )
    fields = [jnp.transpose(ensemble[:, k], (1, 2, 0, 3)) for k in range(species)]
    conserved = fields[1] + fields[2] + fields[3]
    omega, eta = voxel_weights(
        owner, obs_index, observed, obs_var, batches // 2, nx * nz, ny
    )
    around = origin = halos(*edges)
    conserved = collect(conserved, *around, *fields)
    payload = (nz, 2 * rows, ny)
    for step in range(SUBSTEPS // 2 - 2):
        inputs = [*fields, *around, *origin, *coefficients]
        around = halos(
            *forecast_call(
                next_edges_kernel, "next_edges", inputs, [payload] * 2, cells, scratch=[whole] * 8
            )
        )
        fields = forecast_call(
            two_substeps_kernel, "two_substeps", inputs, [whole] * 4, 2 * cells, scratch=[whole] * 4
        )
    inner, end = (nx - 2, nz, rows, ny), (2, nz, rows, ny)
    before, first, last, free, tracer, internal, add, ends = forecast_call(
        last_steps_kernel,
        "last_steps",
        [*fields, *around, *origin, *coefficients],
        [whole, payload, payload, whole, inner, whole, inner, (3, *end)],
        4 * cells,
        scratch=[whole] * 7,
        ready=(omega, eta, *conserved[1:]),
    )
    tracer = collect(tracer)
    around = halos(first, last)
    tracer_ends, free_ends, add_ends = forecast_call(
        last_ends_kernel,
        "last_ends",
        [free, ends, *around, *coefficients],
        [end] * 3,
        cells // nx,
    )
    tracer = complete(tracer, tracer_ends)
    tracer_ends = collect(tracer_ends)
    conserved = complete(conserved, tracer_ends[0])
    begun = gram(owner, omega, eta, None, tracer, offsets, (1, 1))
    tracer_ends = complete(tracer_ends, begun)
    (free,) = forecast_call(
        last_free_kernel,
        "last_free",
        [before, free, free_ends, add, add_ends, *around, *origin, diffusivity],
        [whole],
        cells,
    )
    internal = collect(internal, across(tracer_ends))
    half = gram(owner, omega, eta, begun, tracer_ends, offsets, (0, nx - 1))
    half = half + swap(half, "space", 1)
    free = collect(free, half)
    half = total_over(half, "space", 2)
    other = swap(half, "member", 1)
    internal = complete(internal, half)
    square = (members, LANES)
    total, extended = transform_call(
        early_kernel,
        "transforms_early",
        [square, square],
        [(batches, members, LANES)],
        [half, other],
    )
    free = complete(free, total)
    (weights,) = transform_call(
        functools.partial(late_kernel, offsets=offsets, blocks=blocks, rows=rows),
        "transforms_late",
        [(LANES, LANES) if blocks == 1 else (rows, LANES)],
        [(LANES, LANES)],
        [total, extended],
    )
    if blocks == 1:
        weights = lax.dynamic_slice(weights, (member * rows, 0), (rows, LANES))
    held = free + conserved + internal + tracer + tracer_ends
    return mix(weights, held, blocks, ensemble.shape)


def solution(mesh):
    in_specs = (
        P("member", None, "space", None, None),
        P("space", None, None),
        P("space", None, None),
        P("space", None, None),
        P(),
        P(),
        P(),
        P(),
    )
    out_specs = P("member", None, "space", None, None)
    return jax.shard_map(local, mesh=mesh, in_specs=in_specs, out_specs=out_specs, check_vma=False)
```

```python
import functools

import jax
import jax.numpy as jnp
from jax import lax
from jax.experimental import pallas as pl
from jax.experimental.pallas import tpu as pltpu
from jax.sharding import PartitionSpec as P

SUBSTEPS = 6
NEWTON = 16
UNROLL = 5
LANES = 128
SCOPED = 10 * 2**20

unbind_rate = 0.05
uptake_rate = 0.1
recycle_rate = 0.02

VMEM = pl.BlockSpec(memory_space=pltpu.VMEM)
SMEM = pl.BlockSpec(memory_space=pltpu.SMEM)
bf16 = jnp.bfloat16
f32 = jnp.float32


def split(x):
    high = x.astype(bf16)
    return high, (x - high.astype(f32)).astype(bf16)


def dot_parts(a, b, dims):
    a_high, a_low = a
    b_high, b_low = b
    mul = functools.partial(
        lax.dot_general, dimension_numbers=(dims, ((), ())), preferred_element_type=f32
    )
    return mul(a_high, b_high) + (mul(a_high, b_low) + mul(a_low, b_high))


def wide_left(x):
    return jnp.concatenate(split(x), axis=1)


def wide_right(x):
    both = jnp.concatenate(split(x), axis=1)
    rows, lanes = both.shape
    if rows < lanes // 2:
        both = jnp.concatenate([both, jnp.zeros((lanes // 2 - rows, lanes), bf16)], axis=0)
    return jnp.concatenate([both, both], axis=0)


def wide_dot(left, right):
    out = jnp.dot(left, right, preferred_element_type=f32)
    side = out.shape[1] // 2
    return out[:, :side] + out[:, side:]


NN = ((1,), (0,))
NT = ((1,), (1,))


def position():
    member = lax.axis_index("member")
    return member & 1, lax.axis_index("space"), member


def react(free, receptor, complexed, internal, binding):
    flux = binding * free * receptor
    back = unbind_rate * complexed - flux
    return (
        back,
        receptor + back + recycle_rate * internal,
        complexed + flux - (unbind_rate + uptake_rate) * complexed,
        internal + uptake_rate * complexed - recycle_rate * internal,
    )


def spread_free(free, planes, neighbours, diffusivity):
    lane = lax.broadcasted_iota(jnp.int32, free.shape, 1)
    last = free.shape[1] - 1
    for plane in planes:
        neighbours = plane if neighbours is None else neighbours + plane
    neighbours += jnp.where(lane == last, 0.0, pltpu.roll(free, last, 1))
    neighbours += jnp.where(lane == 0, 0.0, pltpu.roll(free, 1, 1))
    return free + diffusivity * (neighbours - 6.0 * free)


def beside(read, x, z, nx, nz, low, high):
    around = [low if x == 0 else read(x - 1, z), high if x == nx - 1 else read(x + 1, z)]
    around += [read(x, other) for other in (z + 1, z - 1) if 0 <= other < nz]
    return [value for value in around if value is not None]


def edge_free(read, rest, x, nz, nx, z, diffusivity):
    return spread_free(read(x, z), beside(read, x, z, nx, nz, None, None), None, diffusivity) + rest


def first_edges_kernel(below, above, diffusivity, binding, source, first, last):
    _, _, nz, members, _ = below.shape
    nx = diffusivity.shape[0]
    for x, ends, out in ((0, below, first), (nx - 1, above, last)):
        shift = 0 if x == 0 else nx - 2

        def read(at, z, ends=ends, shift=shift):
            return ends[0, at - shift, z]

        for z in range(nz):
            row = pl.ds(z, 1)
            free = read(x, z)
            flux = binding[x, row, :] * free * ends[1, x - shift, z]
            rest = unbind_rate * ends[2, x - shift, z] - flux + source[x, row, :]
            spread = diffusivity[x, row, :]
            out[z, :members, :] = free
            out[z, members : 2 * members, :] = edge_free(read, rest, x, nz, nx, z, spread)
            out[z, 2 * members :, :] = jnp.broadcast_to(spread, (8, spread.shape[1]))


def step_planes(planes, a, r, c, i, outside, diffusivity, binding, source, out_a, outs, keep):
    nx, nz, _, _ = a.shape
    for x in planes:
        for z in range(nz):
            row = pl.ds(z, 1)
            back, *others = react(a[x, z], r[x, z], c[x, z], i[x, z], binding[x, row, :])
            around = beside(lambda x, z: a[x, z], x, z, nx, nz, *outside(x, z))
            out_a[x, z] = (
                spread_free(a[x, z], around, None, diffusivity[x, row, :])
                + back
                + source[x, row, :]
            )
            if x in keep:
                for out, value in zip(outs, others):
                    out[x, z] = value


def before_last(a, low, high):
    nx, _, members, _ = a.shape

    def outside(x, z):
        return (
            low[z, :members, :] if x == 0 else None,
            high[z, :members, :] if x == nx - 1 else None,
        )

    return outside


def after_first(a, low, high, low_first, high_first):
    nx, _, members, _ = a.shape

    def completed(halo, origin, x, z):
        later = halo[z, members : 2 * members, :]
        return later + origin[z, 2 * members : 2 * members + 1, :] * a[x, z]

    def outside(x, z):
        return (
            completed(low, low_first, x, z) if x == 0 else None,
            completed(high, high_first, x, z) if x == nx - 1 else None,
        )

    return outside


def next_edges_kernel(
    a, r, c, i, low, high, low_first, high_first, diffusivity, binding, source, *refs
):
    first, last, *kept = refs
    middle, later = kept[:4], kept[4:]
    nx, nz, members, _ = a.shape
    coefficients = (diffusivity, binding, source)

    def near(depth):
        return [x for x in range(nx) if min(x, nx - 1 - x) < depth]

    step_planes(
        near(3), a, r, c, i, before_last(a, low, high), *coefficients, middle[0], middle[1:], near(2)
    )
    step_planes(
        near(2),
        *middle,
        after_first(a, low, high, low_first, high_first),
        *coefficients,
        later[0],
        later[1:],
        near(1),
    )
    free, receptor, complexed = later[:3]
    for x, out in ((0, first), (nx - 1, last)):
        for z in range(nz):
            row = pl.ds(z, 1)
            flux = binding[x, row, :] * free[x, z] * receptor[x, z]
            rest = unbind_rate * complexed[x, z] - flux + source[x, row, :]
            out[z, :members, :] = free[x, z]
            out[z, members:, :] = edge_free(
                lambda x, z: free[x, z], rest, x, nz, nx, z, diffusivity[x, row, :]
            )


def two_substeps_kernel(
    a, r, c, i, low, high, low_first, high_first, diffusivity, binding, source, *refs
):
    outs, middle = refs[:4], refs[4:]
    everywhere = range(a.shape[0])
    coefficients = (diffusivity, binding, source)
    step_planes(
        everywhere,
        a,
        r,
        c,
        i,
        before_last(a, low, high),
        *coefficients,
        middle[0],
        middle[1:],
        everywhere,
    )
    step_planes(
        everywhere,
        *middle,
        after_first(a, low, high, low_first, high_first),
        *coefficients,
        outs[0],
        outs[1:],
        everywhere,
    )


def last_steps_kernel(
    a, r, c, i, low, high, low_first, high_first, diffusivity, binding, source, *refs
):
    *outs, m0, m1, m2, m3, later_r, later_c, later_i = refs
    before, first, last, free, tracer, inside, add, ends = outs
    nx, nz, members, _ = a.shape
    coefficients = (diffusivity, binding, source)
    two_substeps_kernel(
        a,
        r,
        c,
        i,
        low,
        high,
        low_first,
        high_first,
        *coefficients,
        before,
        later_r,
        later_c,
        later_i,
        m0,
        m1,
        m2,
        m3,
    )
    step_planes(
        range(nx),
        before,
        later_r,
        later_c,
        later_i,
        lambda x, z: (None, None),
        *coefficients,
        free,
        (m1, m2, m3),
        range(nx),
    )
    for x in range(nx):
        for z in range(nz):
            row = pl.ds(z, 1)
            back, _, complexed, internal = react(
                free[x, z], m1[x, z], m2[x, z], m3[x, z], binding[x, row, :]
            )
            inside[x, z] = internal
            if 0 < x < nx - 1:
                tracer[x - 1, z] = complexed + internal
                add[x - 1, z] = back + source[x, row, :]
                continue
            ends[0, x // (nx - 1), z] = m1[x, z]
            ends[1, x // (nx - 1), z] = m2[x, z]
            ends[2, x // (nx - 1), z] = m3[x, z]
    for x, out in ((0, first), (nx - 1, last)):
        for z in range(nz):
            out[z, :members, :] = before[x, z]
            out[z, members:, :] = free[x, z]


def last_ends_kernel(
    free, ends, low, high, diffusivity, binding, source, tracer, out_free, add
):
    nx, nz, members, _ = free.shape
    for end, (x, halo) in enumerate(((0, low), (nx - 1, high))):
        for z in range(nz):
            row = pl.ds(z, 1)
            value = free[x, z] + diffusivity[x, row, :] * halo[z, :members, :]
            back, _, complexed, internal = react(
                value, ends[0, end, z], ends[1, end, z], ends[2, end, z], binding[x, row, :]
            )
            tracer[end, z] = complexed + internal
            out_free[end, z] = value
            add[end, z] = back + source[x, row, :]


def last_free_kernel(
    before, free, free_ends, add, add_ends, low, high, low_first, high_first, diffusivity, out
):
    nx, nz, _, _ = free.shape
    outside = after_first(before, low, high, low_first, high_first)

    def read(x, z):
        return free[x, z] if 0 < x < nx - 1 else free_ends[x // (nx - 1), z]

    for x in range(nx):
        for z in range(nz):
            around = beside(read, x, z, nx, nz, *outside(x, z))
            rest = add[x - 1, z] if 0 < x < nx - 1 else add_ends[x // (nx - 1), z]
            out[x, z] = (
                spread_free(read(x, z), around, None, diffusivity[x, pl.ds(z, 1), :]) + rest
            )


def forecast_call(kernel, name, inputs, outputs, cells, scratch=(), ready=()):
    def body(*refs):
        kernel(*refs[: len(inputs)], *refs[len(inputs) + len(ready) :])

    return pl.pallas_call(
        body,
        out_shape=[jax.ShapeDtypeStruct(shape, f32) for shape in outputs],
        in_specs=[VMEM] * len(inputs) + [pl.BlockSpec(memory_space=pl.ANY)] * len(ready),
        out_specs=[VMEM] * len(outputs),
        scratch_shapes=[pltpu.VMEM(shape, f32) for shape in scratch],
        compiler_params=pltpu.CompilerParams(vmem_limit_bytes=SCOPED),
        cost_estimate=pl.CostEstimate(
            flops=30 * cells, bytes_accessed=32 * cells, transcendentals=0
        ),
        name=name,
    )(*inputs, *ready)


def weights_kernel(owner, obs_index, observed, obs_var, omega, eta):
    place = position()
    count, rows, ny = omega.shape
    batch_size = obs_index.shape[1]
    for k in range(count):
        batch = place[0] * count + k
        mine = owner[batch] == place[1]
        line = pl.ds(batch, 1)
        voxel = obs_index[line, :]
        scale = jnp.where(mine, 1.0, 0.0) / obs_var[line, :]
        shift = ny.bit_length() - 1
        row = lax.shift_right_logical(voxel, shift)
        column = jnp.bitwise_and(voxel, ny - 1)
        at_row = lax.broadcasted_iota(jnp.int32, (rows, batch_size), 0) == row
        at_column = lax.broadcasted_iota(jnp.int32, (ny, batch_size), 0) == column
        both = jnp.concatenate(
            [jnp.where(at_row, scale, 0.0), jnp.where(at_row, scale * observed[line, :], 0.0)],
            axis=0,
        )
        one = both.astype(bf16)
        rest = both - one.astype(f32)
        two = rest.astype(bf16)
        three = (rest - two.astype(f32)).astype(bf16)
        columns = jnp.where(at_column, 1.0, 0.0).astype(bf16)
        sums = lax.dot_general(
            jnp.concatenate([one, two, three], axis=0),
            columns,
            (NT, ((), ())),
            preferred_element_type=f32,
        )
        sums = sums[: 2 * rows] + sums[2 * rows : 4 * rows] + sums[4 * rows :]
        omega[k] = sums[:rows]
        eta[k] = sums[rows:]


def voxel_weights(owner, obs_index, observed, obs_var, count, rows, ny):
    out = jax.ShapeDtypeStruct((count, rows, ny), f32)
    return pl.pallas_call(
        weights_kernel,
        out_shape=[out, out],
        in_specs=[SMEM, VMEM, VMEM, VMEM],
        out_specs=[VMEM, VMEM],
        compiler_params=pltpu.CompilerParams(vmem_limit_bytes=SCOPED),
        name="voxel_weights",
    )(owner, obs_index, observed, obs_var)


def gram_kernel(owner, omega, eta, *refs, offsets, planes, first):
    place = position()
    if first:
        *sources, out, members_at = refs
    else:
        begun, *sources, packed, out, members_at = refs
    count = out.shape[0]
    span, nz, rows, ny = sources[0].shape
    members = members_at.shape[0]
    for k in range(count):
        out[k] = jnp.zeros(out.shape[1:], f32) if first else begun[k]

        @pl.when(owner[place[0] * count + k] == place[1])
        def _(k=k):
            def tile(t, total):
                x, z = t // nz, t % nz
                voxels = pl.ds((planes[0] + x * planes[1]) * nz + z, 1)
                for j, source in enumerate(sources):
                    start = pl.multiple_of(offsets(place[2], j), 8)
                    members_at[pl.ds(start, rows), :] = source[x, z]
                values = members_at[...]
                mean = jnp.sum(values, axis=0, keepdims=True) * (1.0 / members)
                spread = values - mean
                weight = omega[k, voxels, :]
                shift = eta[k, voxels, :] - weight * mean
                tail = lax.broadcasted_iota(jnp.int32, (LANES - members, ny), 0)
                weighted = jnp.concatenate(
                    [spread * weight, jnp.where(tail == 0, shift, 0.0)], axis=0
                )
                return total + dot_parts(split(spread), split(weighted), NT)

            out[k] = lax.fori_loop(0, span * nz, tile, out[k], unroll=4)

    if first:
        return
    row = lax.broadcasted_iota(jnp.int32, (members, LANES), 0)
    column = lax.broadcasted_iota(jnp.int32, (members, LANES), 1)
    above, below = out[0], out[1]

    def pick(where, x):
        return jnp.sum(jnp.where(where, x, 0.0), axis=1, keepdims=True)

    both = jnp.where(column >= row, above, below)
    both = jnp.where(column == members, pick(column == row, below), both)
    both = jnp.where(column == members + 1, pick(column == members, above), both)
    packed[...] = jnp.where(column == members + 2, pick(column == members, below), both)


def gram(owner, omega, eta, begun, sources, offsets, planes):
    _, _, rows, ny = sources[0].shape
    members = rows * len(sources)
    whole = (omega.shape[0], members, LANES)
    work = pltpu.VMEM((members, ny), f32)
    first = begun is None
    return pl.pallas_call(
        functools.partial(gram_kernel, offsets=offsets, planes=planes, first=first),
        out_shape=jax.ShapeDtypeStruct(whole if first else whole[1:], f32),
        in_specs=[SMEM] + [VMEM] * (2 + len(sources) + (not first)),
        out_specs=VMEM,
        scratch_shapes=[work] if first else [pltpu.VMEM(whole, f32), work],
        compiler_params=pltpu.CompilerParams(vmem_limit_bytes=SCOPED),
        name="gram",
    )(owner, omega, eta, *([] if first else [begun]), *sources)


def turned(x):
    rows = x.shape[0]
    whole = jnp.concatenate([x, jnp.zeros((LANES - rows, LANES), f32)], axis=0)
    return whole.T[:rows]


def batch_transform(extended, total, members):
    row = lax.broadcasted_iota(jnp.int32, extended.shape, 0)
    column = lax.broadcasted_iota(jnp.int32, extended.shape, 1)
    inside = column < members
    last = column == members
    identity = jnp.where(row == column, 1.0, 0.0)
    matrix = jnp.where(inside, extended, 0.0)

    mean = jnp.sum(total, axis=1, keepdims=True) * (1.0 / members)
    centred = jnp.where(inside, total - mean, 0.0)
    product = wide_dot(wide_left(matrix), wide_right(jnp.where(last, mean, centred)))
    product = jnp.where(last, extended - product, product)
    product = wide_dot(wide_left(turned(centred)), wide_right(product)) * (1.0 / (members - 1))
    innovation = jnp.sum(jnp.where(last, product, 0.0), axis=1, keepdims=True)
    system = identity + jnp.where(inside, product, 0.0)
    frobenius = jnp.sqrt(jnp.sum(jnp.sum(system * system, axis=1, keepdims=True), axis=0, keepdims=True))

    scaled_root = system / frobenius
    factor = 1.5 * identity - 0.5 * scaled_root
    scaled_root = wide_dot(wide_left(scaled_root), wide_right(factor))
    inverse_root = factor

    def newton(iteration, iterates):
        scaled_root, inverse_root = iterates
        factor = 1.5 * identity - 0.5 * wide_dot(
            wide_left(inverse_root), wide_right(scaled_root)
        )
        return (
            wide_dot(wide_left(scaled_root), wide_right(factor)),
            wide_dot(wide_left(factor), wide_right(inverse_root)),
        )

    scaled_root, inverse_root = lax.fori_loop(1, NEWTON, newton, (scaled_root, inverse_root), unroll=UNROLL)
    root_inv = inverse_root / jnp.sqrt(frobenius)
    mean_weight = jnp.sum(root_inv * innovation, axis=0, keepdims=True)
    mean_weight = jnp.sum(root_inv * mean_weight, axis=1, keepdims=True)
    mixing = jnp.where(inside, root_inv + mean_weight, 0.0)
    mixing = mixing - jnp.sum(mixing, axis=0, keepdims=True) * (1.0 / members)
    mixing = jnp.where(inside, mixing + 1.0 / members, 0.0)
    return wide_dot(wide_left(total), wide_right(mixing))


def early_kernel(mine, other, total, last, ordered):
    place = position()
    members = mine.shape[0]
    row = lax.broadcasted_iota(jnp.int32, (members, LANES), 0)
    column = lax.broadcasted_iota(jnp.int32, (members, LANES), 1)
    inside = column < members

    def pick(where, x):
        return jnp.sum(jnp.where(where, x, 0.0), axis=1, keepdims=True)

    for half, shared in ((place[0], mine), (1 - place[0], other)):
        packed = shared[...]
        above = jnp.where(inside & (column > row), packed, 0.0)
        below = jnp.where(inside & (column < row), packed, 0.0)
        middle = jnp.where(column == row, packed, 0.0)
        side = jnp.where(column == members, pick(column == members + 1, packed), 0.0)
        ordered[2 * half] = above + turned(above) + (middle + side)
        middle = jnp.where(column == row, pick(column == members, packed), 0.0)
        side = jnp.where(column == members, pick(column == members + 2, packed), 0.0)
        ordered[2 * half + 1] = below + turned(below) + (middle + side)
    batches = ordered.shape[0]
    product = jnp.where(row == column, 1.0, 0.0)
    for batch in range(batches - 1):
        product = batch_transform(ordered[batch], product, members)
    total[...] = product
    last[...] = ordered[batches - 1]


def late_kernel(total, last, out, work, *, offsets, blocks, rows):
    place = position()
    members = total.shape[0]
    product = batch_transform(last[...], total[...], members)
    rest = jnp.zeros((LANES - members, LANES), f32)
    work[...] = jnp.concatenate([product, rest], axis=0)
    if blocks == 1:
        out[...] = work[...].T
        return
    parts = [
        work[pl.ds(pl.multiple_of(offsets(place[2], j), 8), rows), :] for j in range(blocks)
    ]
    work[...] = jnp.concatenate([*parts, rest], axis=0).T
    out[...] = work[pl.ds(pl.multiple_of(offsets(place[2], 0), 8), rows), :]


def transform_call(kernel, name, outputs, scratch, inputs):
    return pl.pallas_call(
        kernel,
        out_shape=[jax.ShapeDtypeStruct(shape, f32) for shape in outputs],
        in_specs=[VMEM] * len(inputs),
        out_specs=[VMEM] * len(outputs),
        scratch_shapes=[pltpu.VMEM(shape, f32) for shape in scratch],
        compiler_params=pltpu.CompilerParams(vmem_limit_bytes=SCOPED),
        cost_estimate=pl.CostEstimate(
            flops=10**8, bytes_accessed=10**6, transcendentals=0
        ),
        name=name,
    )(*inputs)


def mix_kernel(weights, *refs, blocks):
    *sources, out = refs
    rows, _, _, nz, _ = out.shape
    x, nx = pl.program_id(0), pl.num_programs(0)
    free, conserved, internal, tracer, tracer_ends = [
        sources[k : k + blocks] for k in range(0, len(sources), blocks)
    ]
    members = blocks * free[0].shape[2]
    high, low = split(weights[:, :members])
    both = jnp.concatenate([high.astype(f32), low.astype(f32)], axis=0).astype(bf16)
    mul = functools.partial(jnp.dot, preferred_element_type=f32)

    def mixed(held, x, z):
        parts = [array[x, z] for array in held]
        values = parts[0] if blocks == 1 else jnp.concatenate(parts, axis=0)
        value_high, value_low = split(values)
        upper = mul(both, value_high)
        return upper[:rows] + (upper[rows:] + mul(high, value_low))

    def plane(tracer, at):
        for z in range(nz):
            bound = mixed(tracer, at, z)
            inside = mixed(internal, x, z)
            out[:, 0, 0, z, :] = mixed(free, x, z)
            out[:, 1, 0, z, :] = mixed(conserved, x, z) - bound
            out[:, 2, 0, z, :] = bound - inside
            out[:, 3, 0, z, :] = inside

    at_end = (x == 0) | (x == nx - 1)

    @pl.when(at_end)
    def _():
        plane(tracer_ends, x // (nx - 1))

    @pl.when(jnp.logical_not(at_end))
    def _():
        plane(tracer, x - 1)


def mix(weights, sources, blocks, shape):
    rows, species, nx, nz, ny = shape
    return pl.pallas_call(
        functools.partial(mix_kernel, blocks=blocks),
        grid=(nx,),
        in_specs=[VMEM] * (1 + len(sources)),
        out_specs=pl.BlockSpec((rows, species, 1, nz, ny), lambda x: (0, 0, x, 0, 0)),
        out_shape=jax.ShapeDtypeStruct(shape, f32),
        compiler_params=pltpu.CompilerParams(vmem_limit_bytes=SCOPED),
        name="mix",
    )(weights, *sources)


def swap(x, axis, bit):
    count = lax.axis_size(axis)
    return lax.ppermute(x, axis, [(k, k ^ bit) for k in range(count)])


def total_over(x, axis, bit):
    while bit < lax.axis_size(axis):
        x = x + swap(x, axis, bit)
        bit *= 2
    return x


def local(ensemble, diffusivity, binding, source, obs_index, owner, observed, obs_var):
    rows, species, nx, nz, ny = ensemble.shape
    devices = lax.axis_size("member")
    spaces = lax.axis_size("space")
    members = rows * devices
    batches = owner.shape[0]
    member = lax.axis_index("member")

    forward = [(k, k + 1) for k in range(spaces - 1)]
    backward = [(k + 1, k) for k in range(spaces - 1)]

    def halos(first, last):
        return lax.ppermute(last, "space", forward), lax.ppermute(first, "space", backward)

    def tie(x, *after):
        return lax.optimization_barrier((x, *after))[0]

    if devices == 4 and rows % 8 == 0:
        blocks = devices

        def offsets(position, j):
            return jnp.bitwise_xor(position, j) * rows

        def collect(x, *after):
            return [x, swap(x, "member", 1), swap(tie(x, *after), "member", 2)]

        def complete(held, *after):
            return [*held, swap(lax.optimization_barrier((held[2], *after))[0], "member", 1)]
    else:
        blocks = 1

        def offsets(position, j):
            return 0

        def collect(x, *after):
            return [lax.all_gather(x, "member", axis=2, tiled=True)]

        def complete(held, *after):
            return held

    def across(held):
        return held[min(2, blocks - 1)]

    whole = (nx, nz, rows, ny)
    coefficients = (diffusivity, binding, source)
    cells = nx * nz * rows * ny
    ends = [
        jnp.transpose(ensemble[:, :3, part], (1, 2, 3, 0, 4))
        for part in (slice(0, 2), slice(nx - 2, nx))
    ]
    edges = forecast_call(
        first_edges_kernel,
        "first_edges",
        [*ends, *coefficients],
        [(nz, 2 * rows + 8, ny)] * 2,
        2 * cells // nx,
    )
    fields = [jnp.transpose(ensemble[:, k], (1, 2, 0, 3)) for k in range(species)]
    conserved = fields[1] + fields[2] + fields[3]
    omega, eta = voxel_weights(
        owner, obs_index, observed, obs_var, batches // 2, nx * nz, ny
    )
    around = origin = halos(*edges)
    conserved = collect(conserved, *around, *fields)
    payload = (nz, 2 * rows, ny)
    for step in range(SUBSTEPS // 2 - 2):
        inputs = [*fields, *around, *origin, *coefficients]
        around = halos(
            *forecast_call(
                next_edges_kernel, "next_edges", inputs, [payload] * 2, cells, scratch=[whole] * 8
            )
        )
        fields = forecast_call(
            two_substeps_kernel, "two_substeps", inputs, [whole] * 4, 2 * cells, scratch=[whole] * 4
        )
    inner, end = (nx - 2, nz, rows, ny), (2, nz, rows, ny)
    before, first, last, free, tracer, internal, add, ends = forecast_call(
        last_steps_kernel,
        "last_steps",
        [*fields, *around, *origin, *coefficients],
        [whole, payload, payload, whole, inner, whole, inner, (3, *end)],
        4 * cells,
        scratch=[whole] * 7,
        ready=(omega, eta),
    )
    tracer = collect(tracer)
    around = halos(first, last)
    tracer_ends, free_ends, add_ends = forecast_call(
        last_ends_kernel,
        "last_ends",
        [free, ends, *around, *coefficients],
        [end] * 3,
        cells // nx,
        ready=conserved[1:],
    )
    tracer = complete(tracer, tracer_ends)
    tracer_ends = collect(tracer_ends)
    conserved = complete(conserved, tracer_ends[0])
    begun = gram(owner, omega, eta, None, tracer, offsets, (1, 1))
    tracer_ends = complete(tracer_ends, begun)
    (free,) = forecast_call(
        last_free_kernel,
        "last_free",
        [before, free, free_ends, add, add_ends, *around, *origin, diffusivity],
        [whole],
        cells,
    )
    internal = collect(internal, across(tracer_ends))
    half = gram(owner, omega, eta, begun, tracer_ends, offsets, (0, nx - 1))
    half = half + swap(half, "space", 1)
    free = collect(free, half)
    half = total_over(half, "space", 2)
    other = swap(half, "member", 1)
    square = (members, LANES)
    total, extended = transform_call(
        early_kernel,
        "transforms_early",
        [square, square],
        [(batches, members, LANES)],
        [half, other],
    )
    internal = complete(internal, total)
    free = complete(free, total)
    (weights,) = transform_call(
        functools.partial(late_kernel, offsets=offsets, blocks=blocks, rows=rows),
        "transforms_late",
        [(LANES, LANES) if blocks == 1 else (rows, LANES)],
        [(LANES, LANES)],
        [total, extended],
    )
    if blocks == 1:
        weights = lax.dynamic_slice(weights, (member * rows, 0), (rows, LANES))
    held = free + conserved + internal + tracer + tracer_ends
    return mix(weights, held, blocks, ensemble.shape)


def solution(mesh):
    in_specs = (
        P("member", None, "space", None, None),
        P("space", None, None),
        P("space", None, None),
        P("space", None, None),
        P(),
        P(),
        P(),
        P(),
    )
    out_specs = P("member", None, "space", None, None)
    return jax.shard_map(local, mesh=mesh, in_specs=in_specs, out_specs=out_specs, check_vma=False)
```

```python
import functools

import jax
import jax.numpy as jnp
from jax import lax
from jax.experimental import pallas as pl
from jax.experimental.pallas import tpu as pltpu
from jax.sharding import PartitionSpec as P

SUBSTEPS = 6
NEWTON = 16
UNROLL = 5
LANES = 128
SCOPED = 10 * 2**20

unbind_rate = 0.05
uptake_rate = 0.1
recycle_rate = 0.02

VMEM = pl.BlockSpec(memory_space=pltpu.VMEM)
SMEM = pl.BlockSpec(memory_space=pltpu.SMEM)
bf16 = jnp.bfloat16
f32 = jnp.float32


def split(x):
    high = x.astype(bf16)
    return high, (x - high.astype(f32)).astype(bf16)


def dot_parts(a, b, dims):
    a_high, a_low = a
    b_high, b_low = b
    mul = functools.partial(
        lax.dot_general, dimension_numbers=(dims, ((), ())), preferred_element_type=f32
    )
    return mul(a_high, b_high) + (mul(a_high, b_low) + mul(a_low, b_high))


def wide_left(x):
    return jnp.concatenate(split(x), axis=1)


def wide_right(x):
    both = jnp.concatenate(split(x), axis=1)
    rows, lanes = both.shape
    if rows < lanes // 2:
        both = jnp.concatenate([both, jnp.zeros((lanes // 2 - rows, lanes), bf16)], axis=0)
    return jnp.concatenate([both, both], axis=0)


def wide_dot(left, right):
    out = jnp.dot(left, right, preferred_element_type=f32)
    side = out.shape[1] // 2
    return out[:, :side] + out[:, side:]


NN = ((1,), (0,))
NT = ((1,), (1,))


def position():
    member = lax.axis_index("member")
    return member & 1, lax.axis_index("space"), member


def react(free, receptor, complexed, internal, binding):
    flux = binding * free * receptor
    back = unbind_rate * complexed - flux
    return (
        back,
        receptor + back + recycle_rate * internal,
        complexed + flux - (unbind_rate + uptake_rate) * complexed,
        internal + uptake_rate * complexed - recycle_rate * internal,
    )


def spread_free(free, planes, neighbours, diffusivity):
    lane = lax.broadcasted_iota(jnp.int32, free.shape, 1)
    last = free.shape[1] - 1
    for plane in planes:
        neighbours = plane if neighbours is None else neighbours + plane
    neighbours += jnp.where(lane == last, 0.0, pltpu.roll(free, last, 1))
    neighbours += jnp.where(lane == 0, 0.0, pltpu.roll(free, 1, 1))
    return free + diffusivity * (neighbours - 6.0 * free)


def beside(read, x, z, nx, nz, low, high):
    around = [low if x == 0 else read(x - 1, z), high if x == nx - 1 else read(x + 1, z)]
    around += [read(x, other) for other in (z + 1, z - 1) if 0 <= other < nz]
    return [value for value in around if value is not None]


def edge_free(read, rest, x, nz, nx, z, diffusivity):
    return spread_free(read(x, z), beside(read, x, z, nx, nz, None, None), None, diffusivity) + rest


def first_edges_kernel(below, above, diffusivity, binding, source, first, last):
    _, _, nz, members, _ = below.shape
    nx = diffusivity.shape[0]
    for x, ends, out in ((0, below, first), (nx - 1, above, last)):
        shift = 0 if x == 0 else nx - 2

        def read(at, z, ends=ends, shift=shift):
            return ends[0, at - shift, z]

        for z in range(nz):
            row = pl.ds(z, 1)
            free = read(x, z)
            flux = binding[x, row, :] * free * ends[1, x - shift, z]
            rest = unbind_rate * ends[2, x - shift, z] - flux + source[x, row, :]
            spread = diffusivity[x, row, :]
            out[z, :members, :] = free
            out[z, members : 2 * members, :] = edge_free(read, rest, x, nz, nx, z, spread)
            out[z, 2 * members :, :] = jnp.broadcast_to(spread, (8, spread.shape[1]))


def step_planes(planes, a, r, c, i, outside, diffusivity, binding, source, out_a, outs, keep):
    nx, nz, _, _ = a.shape
    for x in planes:
        for z in range(nz):
            row = pl.ds(z, 1)
            back, *others = react(a[x, z], r[x, z], c[x, z], i[x, z], binding[x, row, :])
            around = beside(lambda x, z: a[x, z], x, z, nx, nz, *outside(x, z))
            out_a[x, z] = (
                spread_free(a[x, z], around, None, diffusivity[x, row, :])
                + back
                + source[x, row, :]
            )
            if x in keep:
                for out, value in zip(outs, others):
                    out[x, z] = value


def before_last(a, low, high):
    nx, _, members, _ = a.shape

    def outside(x, z):
        return (
            low[z, :members, :] if x == 0 else None,
            high[z, :members, :] if x == nx - 1 else None,
        )

    return outside


def after_first(a, low, high, low_first, high_first):
    nx, _, members, _ = a.shape

    def completed(halo, origin, x, z):
        later = halo[z, members : 2 * members, :]
        return later + origin[z, 2 * members : 2 * members + 1, :] * a[x, z]

    def outside(x, z):
        return (
            completed(low, low_first, x, z) if x == 0 else None,
            completed(high, high_first, x, z) if x == nx - 1 else None,
        )

    return outside


def next_edges_kernel(
    a, r, c, i, low, high, low_first, high_first, diffusivity, binding, source, *refs
):
    first, last, *kept = refs
    middle, later = kept[:4], kept[4:]
    nx, nz, members, _ = a.shape
    coefficients = (diffusivity, binding, source)

    def near(depth):
        return [x for x in range(nx) if min(x, nx - 1 - x) < depth]

    step_planes(
        near(3), a, r, c, i, before_last(a, low, high), *coefficients, middle[0], middle[1:], near(2)
    )
    step_planes(
        near(2),
        *middle,
        after_first(a, low, high, low_first, high_first),
        *coefficients,
        later[0],
        later[1:],
        near(1),
    )
    free, receptor, complexed = later[:3]
    for x, out in ((0, first), (nx - 1, last)):
        for z in range(nz):
            row = pl.ds(z, 1)
            flux = binding[x, row, :] * free[x, z] * receptor[x, z]
            rest = unbind_rate * complexed[x, z] - flux + source[x, row, :]
            out[z, :members, :] = free[x, z]
            out[z, members:, :] = edge_free(
                lambda x, z: free[x, z], rest, x, nz, nx, z, diffusivity[x, row, :]
            )


def two_substeps_kernel(
    a, r, c, i, low, high, low_first, high_first, diffusivity, binding, source, *refs
):
    outs, middle = refs[:4], refs[4:]
    everywhere = range(a.shape[0])
    coefficients = (diffusivity, binding, source)
    step_planes(
        everywhere,
        a,
        r,
        c,
        i,
        before_last(a, low, high),
        *coefficients,
        middle[0],
        middle[1:],
        everywhere,
    )
    step_planes(
        everywhere,
        *middle,
        after_first(a, low, high, low_first, high_first),
        *coefficients,
        outs[0],
        outs[1:],
        everywhere,
    )


def nz_part(a):
    return a.shape[1] // 2


def last_steps_kernel(
    a, r, c, i, low, high, low_first, high_first, diffusivity, binding, source, *refs
):
    *outs, m0, m1, m2, m3, later_r, later_c, later_i = refs
    before, first, last, free, tracer, inside_low, inside_high, add, ends = outs
    part = nz_part(a)
    nx, nz, members, _ = a.shape
    coefficients = (diffusivity, binding, source)
    two_substeps_kernel(
        a,
        r,
        c,
        i,
        low,
        high,
        low_first,
        high_first,
        *coefficients,
        before,
        later_r,
        later_c,
        later_i,
        m0,
        m1,
        m2,
        m3,
    )
    step_planes(
        range(nx),
        before,
        later_r,
        later_c,
        later_i,
        lambda x, z: (None, None),
        *coefficients,
        free,
        (m1, m2, m3),
        range(nx),
    )
    for x in range(nx):
        for z in range(nz):
            row = pl.ds(z, 1)
            back, _, complexed, internal = react(
                free[x, z], m1[x, z], m2[x, z], m3[x, z], binding[x, row, :]
            )
            (inside_low if z < part else inside_high)[x, z % part] = internal
            if 0 < x < nx - 1:
                tracer[x - 1, z] = complexed + internal
                add[x - 1, z] = back + source[x, row, :]
                continue
            ends[0, x // (nx - 1), z] = m1[x, z]
            ends[1, x // (nx - 1), z] = m2[x, z]
            ends[2, x // (nx - 1), z] = m3[x, z]
    for x, out in ((0, first), (nx - 1, last)):
        for z in range(nz):
            out[z, :members, :] = before[x, z]
            out[z, members:, :] = free[x, z]


def last_ends_kernel(
    free, ends, low, high, diffusivity, binding, source, tracer, out_free, add
):
    nx, nz, members, _ = free.shape
    for end, (x, halo) in enumerate(((0, low), (nx - 1, high))):
        for z in range(nz):
            row = pl.ds(z, 1)
            value = free[x, z] + diffusivity[x, row, :] * halo[z, :members, :]
            back, _, complexed, internal = react(
                value, ends[0, end, z], ends[1, end, z], ends[2, end, z], binding[x, row, :]
            )
            tracer[end, z] = complexed + internal
            out_free[end, z] = value
            add[end, z] = back + source[x, row, :]


def last_free_kernel(
    before, free, free_ends, add, add_ends, low, high, low_first, high_first, diffusivity, out
):
    nx, nz, _, _ = free.shape
    outside = after_first(before, low, high, low_first, high_first)

    def read(x, z):
        return free[x, z] if 0 < x < nx - 1 else free_ends[x // (nx - 1), z]

    for x in range(nx):
        for z in range(nz):
            around = beside(read, x, z, nx, nz, *outside(x, z))
            rest = add[x - 1, z] if 0 < x < nx - 1 else add_ends[x // (nx - 1), z]
            out[x, z] = (
                spread_free(read(x, z), around, None, diffusivity[x, pl.ds(z, 1), :]) + rest
            )


def forecast_call(kernel, name, inputs, outputs, cells, scratch=(), ready=()):
    def body(*refs):
        kernel(*refs[: len(inputs)], *refs[len(inputs) + len(ready) :])

    return pl.pallas_call(
        body,
        out_shape=[jax.ShapeDtypeStruct(shape, f32) for shape in outputs],
        in_specs=[VMEM] * len(inputs) + [pl.BlockSpec(memory_space=pl.ANY)] * len(ready),
        out_specs=[VMEM] * len(outputs),
        scratch_shapes=[pltpu.VMEM(shape, f32) for shape in scratch],
        compiler_params=pltpu.CompilerParams(vmem_limit_bytes=SCOPED),
        cost_estimate=pl.CostEstimate(
            flops=30 * cells, bytes_accessed=32 * cells, transcendentals=0
        ),
        name=name,
    )(*inputs, *ready)


def weights_kernel(owner, obs_index, observed, obs_var, omega, eta):
    place = position()
    count, rows, ny = omega.shape
    batch_size = obs_index.shape[1]
    for k in range(count):
        batch = place[0] * count + k
        mine = owner[batch] == place[1]
        line = pl.ds(batch, 1)
        voxel = obs_index[line, :]
        scale = jnp.where(mine, 1.0, 0.0) / obs_var[line, :]
        shift = ny.bit_length() - 1
        row = lax.shift_right_logical(voxel, shift)
        column = jnp.bitwise_and(voxel, ny - 1)
        at_row = lax.broadcasted_iota(jnp.int32, (rows, batch_size), 0) == row
        at_column = lax.broadcasted_iota(jnp.int32, (ny, batch_size), 0) == column
        both = jnp.concatenate(
            [jnp.where(at_row, scale, 0.0), jnp.where(at_row, scale * observed[line, :], 0.0)],
            axis=0,
        )
        one = both.astype(bf16)
        rest = both - one.astype(f32)
        two = rest.astype(bf16)
        three = (rest - two.astype(f32)).astype(bf16)
        columns = jnp.where(at_column, 1.0, 0.0).astype(bf16)
        sums = lax.dot_general(
            jnp.concatenate([one, two, three], axis=0),
            columns,
            (NT, ((), ())),
            preferred_element_type=f32,
        )
        sums = sums[: 2 * rows] + sums[2 * rows : 4 * rows] + sums[4 * rows :]
        omega[k] = sums[:rows]
        eta[k] = sums[rows:]


def voxel_weights(owner, obs_index, observed, obs_var, count, rows, ny):
    out = jax.ShapeDtypeStruct((count, rows, ny), f32)
    return pl.pallas_call(
        weights_kernel,
        out_shape=[out, out],
        in_specs=[SMEM, VMEM, VMEM, VMEM],
        out_specs=[VMEM, VMEM],
        compiler_params=pltpu.CompilerParams(vmem_limit_bytes=SCOPED),
        name="voxel_weights",
    )(owner, obs_index, observed, obs_var)


def gram_kernel(owner, omega, eta, *refs, offsets, planes, first):
    place = position()
    if first:
        *sources, out, members_at = refs
    else:
        begun, *sources, packed, out, members_at = refs
    count = out.shape[0]
    span, nz, rows, ny = sources[0].shape
    members = members_at.shape[0]
    for k in range(count):
        out[k] = jnp.zeros(out.shape[1:], f32) if first else begun[k]

        @pl.when(owner[place[0] * count + k] == place[1])
        def _(k=k):
            def tile(t, total):
                x, z = t // nz, t % nz
                voxels = pl.ds((planes[0] + x * planes[1]) * nz + z, 1)
                for j, source in enumerate(sources):
                    start = pl.multiple_of(offsets(place[2], j), 8)
                    members_at[pl.ds(start, rows), :] = source[x, z]
                values = members_at[...]
                mean = jnp.sum(values, axis=0, keepdims=True) * (1.0 / members)
                spread = values - mean
                weight = omega[k, voxels, :]
                shift = eta[k, voxels, :] - weight * mean
                tail = lax.broadcasted_iota(jnp.int32, (LANES - members, ny), 0)
                weighted = jnp.concatenate(
                    [spread * weight, jnp.where(tail == 0, shift, 0.0)], axis=0
                )
                return total + dot_parts(split(spread), split(weighted), NT)

            out[k] = lax.fori_loop(0, span * nz, tile, out[k], unroll=4)

    if first:
        return
    row = lax.broadcasted_iota(jnp.int32, (members, LANES), 0)
    column = lax.broadcasted_iota(jnp.int32, (members, LANES), 1)
    above, below = out[0], out[1]

    def pick(where, x):
        return jnp.sum(jnp.where(where, x, 0.0), axis=1, keepdims=True)

    both = jnp.where(column >= row, above, below)
    both = jnp.where(column == members, pick(column == row, below), both)
    both = jnp.where(column == members + 1, pick(column == members, above), both)
    packed[...] = jnp.where(column == members + 2, pick(column == members, below), both)


def gram(owner, omega, eta, begun, sources, offsets, planes):
    _, _, rows, ny = sources[0].shape
    members = rows * len(sources)
    whole = (omega.shape[0], members, LANES)
    work = pltpu.VMEM((members, ny), f32)
    first = begun is None
    return pl.pallas_call(
        functools.partial(gram_kernel, offsets=offsets, planes=planes, first=first),
        out_shape=jax.ShapeDtypeStruct(whole if first else whole[1:], f32),
        in_specs=[SMEM] + [VMEM] * (2 + len(sources) + (not first)),
        out_specs=VMEM,
        scratch_shapes=[work] if first else [pltpu.VMEM(whole, f32), work],
        compiler_params=pltpu.CompilerParams(vmem_limit_bytes=SCOPED),
        name="gram",
    )(owner, omega, eta, *([] if first else [begun]), *sources)


def turned(x):
    rows = x.shape[0]
    whole = jnp.concatenate([x, jnp.zeros((LANES - rows, LANES), f32)], axis=0)
    return whole.T[:rows]


def batch_transform(extended, total, members):
    row = lax.broadcasted_iota(jnp.int32, extended.shape, 0)
    column = lax.broadcasted_iota(jnp.int32, extended.shape, 1)
    inside = column < members
    last = column == members
    identity = jnp.where(row == column, 1.0, 0.0)
    matrix = jnp.where(inside, extended, 0.0)

    mean = jnp.sum(total, axis=1, keepdims=True) * (1.0 / members)
    centred = jnp.where(inside, total - mean, 0.0)
    product = wide_dot(wide_left(matrix), wide_right(jnp.where(last, mean, centred)))
    product = jnp.where(last, extended - product, product)
    product = wide_dot(wide_left(turned(centred)), wide_right(product)) * (1.0 / (members - 1))
    innovation = jnp.sum(jnp.where(last, product, 0.0), axis=1, keepdims=True)
    system = identity + jnp.where(inside, product, 0.0)
    frobenius = jnp.sqrt(jnp.sum(jnp.sum(system * system, axis=1, keepdims=True), axis=0, keepdims=True))

    scaled_root = system / frobenius
    factor = 1.5 * identity - 0.5 * scaled_root
    scaled_root = wide_dot(wide_left(scaled_root), wide_right(factor))
    inverse_root = factor

    def newton(iteration, iterates):
        scaled_root, inverse_root = iterates
        factor = 1.5 * identity - 0.5 * wide_dot(
            wide_left(inverse_root), wide_right(scaled_root)
        )
        return (
            wide_dot(wide_left(scaled_root), wide_right(factor)),
            wide_dot(wide_left(factor), wide_right(inverse_root)),
        )

    scaled_root, inverse_root = lax.fori_loop(1, NEWTON, newton, (scaled_root, inverse_root), unroll=UNROLL)
    root_inv = inverse_root / jnp.sqrt(frobenius)
    mean_weight = jnp.sum(root_inv * innovation, axis=0, keepdims=True)
    mean_weight = jnp.sum(root_inv * mean_weight, axis=1, keepdims=True)
    mixing = jnp.where(inside, root_inv + mean_weight, 0.0)
    mixing = mixing - jnp.sum(mixing, axis=0, keepdims=True) * (1.0 / members)
    mixing = jnp.where(inside, mixing + 1.0 / members, 0.0)
    return wide_dot(wide_left(total), wide_right(mixing))


def early_kernel(mine, other, total, last, ordered):
    place = position()
    members = mine.shape[0]
    row = lax.broadcasted_iota(jnp.int32, (members, LANES), 0)
    column = lax.broadcasted_iota(jnp.int32, (members, LANES), 1)
    inside = column < members

    def pick(where, x):
        return jnp.sum(jnp.where(where, x, 0.0), axis=1, keepdims=True)

    for half, shared in ((place[0], mine), (1 - place[0], other)):
        packed = shared[...]
        above = jnp.where(inside & (column > row), packed, 0.0)
        below = jnp.where(inside & (column < row), packed, 0.0)
        middle = jnp.where(column == row, packed, 0.0)
        side = jnp.where(column == members, pick(column == members + 1, packed), 0.0)
        ordered[2 * half] = above + turned(above) + (middle + side)
        middle = jnp.where(column == row, pick(column == members, packed), 0.0)
        side = jnp.where(column == members, pick(column == members + 2, packed), 0.0)
        ordered[2 * half + 1] = below + turned(below) + (middle + side)
    batches = ordered.shape[0]
    product = jnp.where(row == column, 1.0, 0.0)
    for batch in range(batches - 1):
        product = batch_transform(ordered[batch], product, members)
    total[...] = product
    last[...] = ordered[batches - 1]


def late_kernel(total, last, out, work, *, offsets, blocks, rows):
    place = position()
    members = total.shape[0]
    product = batch_transform(last[...], total[...], members)
    rest = jnp.zeros((LANES - members, LANES), f32)
    work[...] = jnp.concatenate([product, rest], axis=0)
    if blocks == 1:
        out[...] = work[...].T
        return
    parts = [
        work[pl.ds(pl.multiple_of(offsets(place[2], j), 8), rows), :] for j in range(blocks)
    ]
    work[...] = jnp.concatenate([*parts, rest], axis=0).T
    out[...] = work[pl.ds(pl.multiple_of(offsets(place[2], 0), 8), rows), :]


def transform_call(kernel, name, outputs, scratch, inputs):
    return pl.pallas_call(
        kernel,
        out_shape=[jax.ShapeDtypeStruct(shape, f32) for shape in outputs],
        in_specs=[VMEM] * len(inputs),
        out_specs=[VMEM] * len(outputs),
        scratch_shapes=[pltpu.VMEM(shape, f32) for shape in scratch],
        compiler_params=pltpu.CompilerParams(vmem_limit_bytes=SCOPED),
        cost_estimate=pl.CostEstimate(
            flops=10**8, bytes_accessed=10**6, transcendentals=0
        ),
        name=name,
    )(*inputs)


def mix_kernel(weights, *refs, blocks):
    *sources, out = refs
    rows, _, _, nz, _ = out.shape
    x, nx = pl.program_id(0), pl.num_programs(0)
    free, conserved, inside_low, inside_high, tracer, tracer_ends = [
        sources[k : k + blocks] for k in range(0, len(sources), blocks)
    ]
    part = nz_part(free[0])
    members = blocks * free[0].shape[2]
    high, low = split(weights[:, :members])
    both = jnp.concatenate([high.astype(f32), low.astype(f32)], axis=0).astype(bf16)
    mul = functools.partial(jnp.dot, preferred_element_type=f32)

    def mixed(held, x, z):
        parts = [array[x, z] for array in held]
        values = parts[0] if blocks == 1 else jnp.concatenate(parts, axis=0)
        value_high, value_low = split(values)
        upper = mul(both, value_high)
        return upper[:rows] + (upper[rows:] + mul(high, value_low))

    def plane(tracer, at):
        for z in range(nz):
            bound = mixed(tracer, at, z)
            inside = mixed(inside_low if z < part else inside_high, x, z % part)
            out[:, 0, 0, z, :] = mixed(free, x, z)
            out[:, 1, 0, z, :] = mixed(conserved, x, z) - bound
            out[:, 2, 0, z, :] = bound - inside
            out[:, 3, 0, z, :] = inside

    at_end = (x == 0) | (x == nx - 1)

    @pl.when(at_end)
    def _():
        plane(tracer_ends, x // (nx - 1))

    @pl.when(jnp.logical_not(at_end))
    def _():
        plane(tracer, x - 1)


def mix(weights, sources, blocks, shape):
    rows, species, nx, nz, ny = shape
    return pl.pallas_call(
        functools.partial(mix_kernel, blocks=blocks),
        grid=(nx,),
        in_specs=[VMEM] * (1 + len(sources)),
        out_specs=pl.BlockSpec((rows, species, 1, nz, ny), lambda x: (0, 0, x, 0, 0)),
        out_shape=jax.ShapeDtypeStruct(shape, f32),
        compiler_params=pltpu.CompilerParams(vmem_limit_bytes=SCOPED),
        name="mix",
    )(weights, *sources)


def swap(x, axis, bit):
    count = lax.axis_size(axis)
    return lax.ppermute(x, axis, [(k, k ^ bit) for k in range(count)])


def total_over(x, axis, bit):
    while bit < lax.axis_size(axis):
        x = x + swap(x, axis, bit)
        bit *= 2
    return x


def local(ensemble, diffusivity, binding, source, obs_index, owner, observed, obs_var):
    rows, species, nx, nz, ny = ensemble.shape
    devices = lax.axis_size("member")
    spaces = lax.axis_size("space")
    members = rows * devices
    batches = owner.shape[0]
    member = lax.axis_index("member")

    forward = [(k, k + 1) for k in range(spaces - 1)]
    backward = [(k + 1, k) for k in range(spaces - 1)]

    def halos(first, last):
        return lax.ppermute(last, "space", forward), lax.ppermute(first, "space", backward)

    def tie(x, *after):
        return lax.optimization_barrier((x, *after))[0]

    if devices == 4 and rows % 8 == 0:
        blocks = devices

        def offsets(position, j):
            return jnp.bitwise_xor(position, j) * rows

        def collect(x, *after):
            return [x, swap(x, "member", 1), swap(tie(x, *after), "member", 2)]

        def complete(held, *after):
            return [*held, swap(lax.optimization_barrier((held[2], *after))[0], "member", 1)]
    else:
        blocks = 1

        def offsets(position, j):
            return 0

        def collect(x, *after):
            return [lax.all_gather(x, "member", axis=2, tiled=True)]

        def complete(held, *after):
            return held

    def across(held):
        return held[min(2, blocks - 1)]

    whole = (nx, nz, rows, ny)
    coefficients = (diffusivity, binding, source)
    cells = nx * nz * rows * ny
    ends = [
        jnp.transpose(ensemble[:, :3, part], (1, 2, 3, 0, 4))
        for part in (slice(0, 2), slice(nx - 2, nx))
    ]
    edges = forecast_call(
        first_edges_kernel,
        "first_edges",
        [*ends, *coefficients],
        [(nz, 2 * rows + 8, ny)] * 2,
        2 * cells // nx,
    )
    fields = [jnp.transpose(ensemble[:, k], (1, 2, 0, 3)) for k in range(species)]
    conserved = fields[1] + fields[2] + fields[3]
    omega, eta = voxel_weights(
        owner, obs_index, observed, obs_var, batches // 2, nx * nz, ny
    )
    around = origin = halos(*edges)
    conserved = collect(conserved)
    payload = (nz, 2 * rows, ny)
    for step in range(SUBSTEPS // 2 - 2):
        inputs = [*fields, *around, *origin, *coefficients]
        around = halos(
            *forecast_call(
                next_edges_kernel, "next_edges", inputs, [payload] * 2, cells, scratch=[whole] * 8
            )
        )
        fields = forecast_call(
            two_substeps_kernel, "two_substeps", inputs, [whole] * 4, 2 * cells, scratch=[whole] * 4
        )
    inner, end, part = (nx - 2, nz, rows, ny), (2, nz, rows, ny), (nx, nz // 2, rows, ny)
    before, first, last, free, tracer, inside_low, inside_high, add, ends = forecast_call(
        last_steps_kernel,
        "last_steps",
        [*fields, *around, *origin, *coefficients],
        [whole, payload, payload, whole, inner, part, part, inner, (3, *end)],
        4 * cells,
        scratch=[whole] * 7,
        ready=(omega, eta, *conserved[1:]),
    )
    tracer = collect(tracer)
    around = halos(first, last)
    tracer_ends, free_ends, add_ends = forecast_call(
        last_ends_kernel,
        "last_ends",
        [free, ends, *around, *coefficients],
        [end] * 3,
        cells // nx,
    )
    tracer = complete(tracer, tracer_ends)
    tracer_ends = collect(tracer_ends)
    conserved = complete(conserved, tracer_ends[0])
    begun = gram(owner, omega, eta, None, tracer, offsets, (1, 1))
    tracer_ends = complete(tracer_ends, begun)
    (free,) = forecast_call(
        last_free_kernel,
        "last_free",
        [before, free, free_ends, add, add_ends, *around, *origin, diffusivity],
        [whole],
        cells,
    )
    inside_low = collect(inside_low, across(tracer_ends), begun)
    half = gram(owner, omega, eta, begun, tracer_ends, offsets, (0, nx - 1))
    half = half + swap(half, "space", 1)
    half = half + swap(half, "space", 2)
    half = tie(half, across(inside_low))
    inside_high = collect(inside_high, half)
    free = collect(free, half)
    half = total_over(half, "space", 4)
    other = swap(half, "member", 1)
    square = (members, LANES)
    total, extended = transform_call(
        early_kernel,
        "transforms_early",
        [square, square],
        [(batches, members, LANES)],
        [half, other],
    )
    inside_low = complete(inside_low, total)
    inside_high = complete(inside_high, total)
    free = complete(free, total)
    (weights,) = transform_call(
        functools.partial(late_kernel, offsets=offsets, blocks=blocks, rows=rows),
        "transforms_late",
        [(LANES, LANES) if blocks == 1 else (rows, LANES)],
        [(LANES, LANES)],
        [total, extended],
    )
    if blocks == 1:
        weights = lax.dynamic_slice(weights, (member * rows, 0), (rows, LANES))
    held = free + conserved + inside_low + inside_high + tracer + tracer_ends
    return mix(weights, held, blocks, ensemble.shape)


def solution(mesh):
    in_specs = (
        P("member", None, "space", None, None),
        P("space", None, None),
        P("space", None, None),
        P("space", None, None),
        P(),
        P(),
        P(),
        P(),
    )
    out_specs = P("member", None, "space", None, None)
    return jax.shard_map(local, mesh=mesh, in_specs=in_specs, out_specs=out_specs, check_vma=False)
```

```python
import functools

import jax
import jax.numpy as jnp
from jax import lax
from jax.experimental import pallas as pl
from jax.experimental.pallas import tpu as pltpu
from jax.sharding import PartitionSpec as P

SUBSTEPS = 6
NEWTON = 16
UNROLL = 5
LANES = 128
SCOPED = 10 * 2**20

unbind_rate = 0.05
uptake_rate = 0.1
recycle_rate = 0.02

VMEM = pl.BlockSpec(memory_space=pltpu.VMEM)
SMEM = pl.BlockSpec(memory_space=pltpu.SMEM)
bf16 = jnp.bfloat16
f32 = jnp.float32


def split(x):
    high = x.astype(bf16)
    return high, (x - high.astype(f32)).astype(bf16)


def dot_parts(a, b, dims):
    a_high, a_low = a
    b_high, b_low = b
    mul = functools.partial(
        lax.dot_general, dimension_numbers=(dims, ((), ())), preferred_element_type=f32
    )
    return mul(a_high, b_high) + (mul(a_high, b_low) + mul(a_low, b_high))


def wide_left(x):
    return jnp.concatenate(split(x), axis=1)


def wide_right(x):
    both = jnp.concatenate(split(x), axis=1)
    rows, lanes = both.shape
    if rows < lanes // 2:
        both = jnp.concatenate([both, jnp.zeros((lanes // 2 - rows, lanes), bf16)], axis=0)
    return jnp.concatenate([both, both], axis=0)


def wide_dot(left, right):
    out = jnp.dot(left, right, preferred_element_type=f32)
    side = out.shape[1] // 2
    return out[:, :side] + out[:, side:]


NN = ((1,), (0,))
NT = ((1,), (1,))


def position():
    member = lax.axis_index("member")
    return member & 1, lax.axis_index("space"), member


def react(free, receptor, complexed, internal, binding):
    flux = binding * free * receptor
    back = unbind_rate * complexed - flux
    return (
        back,
        receptor + back + recycle_rate * internal,
        complexed + flux - (unbind_rate + uptake_rate) * complexed,
        internal + uptake_rate * complexed - recycle_rate * internal,
    )


def spread_free(free, planes, neighbours, diffusivity):
    lane = lax.broadcasted_iota(jnp.int32, free.shape, 1)
    last = free.shape[1] - 1
    for plane in planes:
        neighbours = plane if neighbours is None else neighbours + plane
    neighbours += jnp.where(lane == last, 0.0, pltpu.roll(free, last, 1))
    neighbours += jnp.where(lane == 0, 0.0, pltpu.roll(free, 1, 1))
    return free + diffusivity * (neighbours - 6.0 * free)


def beside(read, x, z, nx, nz, low, high):
    around = [low if x == 0 else read(x - 1, z), high if x == nx - 1 else read(x + 1, z)]
    around += [read(x, other) for other in (z + 1, z - 1) if 0 <= other < nz]
    return [value for value in around if value is not None]


def edge_free(read, rest, x, nz, nx, z, diffusivity):
    return spread_free(read(x, z), beside(read, x, z, nx, nz, None, None), None, diffusivity) + rest


def first_edges_kernel(below, above, diffusivity, binding, source, first, last):
    _, _, nz, members, _ = below.shape
    nx = diffusivity.shape[0]
    for x, ends, out in ((0, below, first), (nx - 1, above, last)):
        shift = 0 if x == 0 else nx - 2

        def read(at, z, ends=ends, shift=shift):
            return ends[0, at - shift, z]

        for z in range(nz):
            row = pl.ds(z, 1)
            free = read(x, z)
            flux = binding[x, row, :] * free * ends[1, x - shift, z]
            rest = unbind_rate * ends[2, x - shift, z] - flux + source[x, row, :]
            spread = diffusivity[x, row, :]
            out[z, :members, :] = free
            out[z, members : 2 * members, :] = edge_free(read, rest, x, nz, nx, z, spread)
            out[z, 2 * members :, :] = jnp.broadcast_to(spread, (8, spread.shape[1]))


def step_planes(planes, a, r, c, i, outside, diffusivity, binding, source, out_a, outs, keep):
    nx, nz, _, _ = a.shape
    for x in planes:
        for z in range(nz):
            row = pl.ds(z, 1)
            back, *others = react(a[x, z], r[x, z], c[x, z], i[x, z], binding[x, row, :])
            around = beside(lambda x, z: a[x, z], x, z, nx, nz, *outside(x, z))
            out_a[x, z] = (
                spread_free(a[x, z], around, None, diffusivity[x, row, :])
                + back
                + source[x, row, :]
            )
            if x in keep:
                for out, value in zip(outs, others):
                    out[x, z] = value


def before_last(a, low, high):
    nx, _, members, _ = a.shape

    def outside(x, z):
        return (
            low[z, :members, :] if x == 0 else None,
            high[z, :members, :] if x == nx - 1 else None,
        )

    return outside


def after_first(a, low, high, low_first, high_first):
    nx, _, members, _ = a.shape

    def completed(halo, origin, x, z):
        later = halo[z, members : 2 * members, :]
        return later + origin[z, 2 * members : 2 * members + 1, :] * a[x, z]

    def outside(x, z):
        return (
            completed(low, low_first, x, z) if x == 0 else None,
            completed(high, high_first, x, z) if x == nx - 1 else None,
        )

    return outside


def next_edges_kernel(
    a, r, c, i, low, high, low_first, high_first, diffusivity, binding, source, *refs
):
    first, last, *kept = refs
    middle, later = kept[:4], kept[4:]
    nx, nz, members, _ = a.shape
    coefficients = (diffusivity, binding, source)

    def near(depth):
        return [x for x in range(nx) if min(x, nx - 1 - x) < depth]

    step_planes(
        near(3), a, r, c, i, before_last(a, low, high), *coefficients, middle[0], middle[1:], near(2)
    )
    step_planes(
        near(2),
        *middle,
        after_first(a, low, high, low_first, high_first),
        *coefficients,
        later[0],
        later[1:],
        near(1),
    )
    free, receptor, complexed = later[:3]
    for x, out in ((0, first), (nx - 1, last)):
        for z in range(nz):
            row = pl.ds(z, 1)
            flux = binding[x, row, :] * free[x, z] * receptor[x, z]
            rest = unbind_rate * complexed[x, z] - flux + source[x, row, :]
            out[z, :members, :] = free[x, z]
            out[z, members:, :] = edge_free(
                lambda x, z: free[x, z], rest, x, nz, nx, z, diffusivity[x, row, :]
            )


def two_substeps_kernel(
    a, r, c, i, low, high, low_first, high_first, diffusivity, binding, source, *refs
):
    outs, middle = refs[:4], refs[4:]
    everywhere = range(a.shape[0])
    coefficients = (diffusivity, binding, source)
    step_planes(
        everywhere,
        a,
        r,
        c,
        i,
        before_last(a, low, high),
        *coefficients,
        middle[0],
        middle[1:],
        everywhere,
    )
    step_planes(
        everywhere,
        *middle,
        after_first(a, low, high, low_first, high_first),
        *coefficients,
        outs[0],
        outs[1:],
        everywhere,
    )


def last_steps_kernel(
    a, r, c, i, low, high, low_first, high_first, diffusivity, binding, source, *refs
):
    *outs, m0, m1, m2, m3, later_r, later_c, later_i = refs
    before, first, last, free, tracer, inside, add, ends = outs
    nx, nz, members, _ = a.shape
    coefficients = (diffusivity, binding, source)
    two_substeps_kernel(
        a,
        r,
        c,
        i,
        low,
        high,
        low_first,
        high_first,
        *coefficients,
        before,
        later_r,
        later_c,
        later_i,
        m0,
        m1,
        m2,
        m3,
    )
    step_planes(
        range(nx),
        before,
        later_r,
        later_c,
        later_i,
        lambda x, z: (None, None),
        *coefficients,
        free,
        (m1, m2, m3),
        range(nx),
    )
    for x in range(nx):
        for z in range(nz):
            row = pl.ds(z, 1)
            back, _, complexed, internal = react(
                free[x, z], m1[x, z], m2[x, z], m3[x, z], binding[x, row, :]
            )
            inside[x, z] = internal
            if 0 < x < nx - 1:
                tracer[x - 1, z] = complexed + internal
                add[x - 1, z] = back + source[x, row, :]
                continue
            ends[0, x // (nx - 1), z] = m1[x, z]
            ends[1, x // (nx - 1), z] = m2[x, z]
            ends[2, x // (nx - 1), z] = m3[x, z]
    for x, out in ((0, first), (nx - 1, last)):
        for z in range(nz):
            out[z, :members, :] = before[x, z]
            out[z, members:, :] = free[x, z]


def last_ends_kernel(
    free, ends, low, high, diffusivity, binding, source, tracer, out_free, add
):
    nx, nz, members, _ = free.shape
    for end, (x, halo) in enumerate(((0, low), (nx - 1, high))):
        for z in range(nz):
            row = pl.ds(z, 1)
            value = free[x, z] + diffusivity[x, row, :] * halo[z, :members, :]
            back, _, complexed, internal = react(
                value, ends[0, end, z], ends[1, end, z], ends[2, end, z], binding[x, row, :]
            )
            tracer[end, z] = complexed + internal
            out_free[end, z] = value
            add[end, z] = back + source[x, row, :]


def last_free_kernel(
    before, free, free_ends, add, add_ends, low, high, low_first, high_first, diffusivity, out
):
    nx, nz, _, _ = free.shape
    outside = after_first(before, low, high, low_first, high_first)

    def read(x, z):
        return free[x, z] if 0 < x < nx - 1 else free_ends[x // (nx - 1), z]

    for x in range(nx):
        for z in range(nz):
            around = beside(read, x, z, nx, nz, *outside(x, z))
            rest = add[x - 1, z] if 0 < x < nx - 1 else add_ends[x // (nx - 1), z]
            out[x, z] = (
                spread_free(read(x, z), around, None, diffusivity[x, pl.ds(z, 1), :]) + rest
            )


def forecast_call(kernel, name, inputs, outputs, cells, scratch=(), ready=()):
    def body(*refs):
        kernel(*refs[: len(inputs)], *refs[len(inputs) + len(ready) :])

    return pl.pallas_call(
        body,
        out_shape=[jax.ShapeDtypeStruct(shape, f32) for shape in outputs],
        in_specs=[VMEM] * len(inputs) + [pl.BlockSpec(memory_space=pl.ANY)] * len(ready),
        out_specs=[VMEM] * len(outputs),
        scratch_shapes=[pltpu.VMEM(shape, f32) for shape in scratch],
        compiler_params=pltpu.CompilerParams(vmem_limit_bytes=SCOPED),
        cost_estimate=pl.CostEstimate(
            flops=30 * cells, bytes_accessed=32 * cells, transcendentals=0
        ),
        name=name,
    )(*inputs, *ready)


def weights_kernel(owner, obs_index, observed, obs_var, omega, eta):
    place = position()
    count, rows, ny = omega.shape
    batch_size = obs_index.shape[1]
    for k in range(count):
        batch = place[0] * count + k
        mine = owner[batch] == place[1]
        line = pl.ds(batch, 1)
        voxel = obs_index[line, :]
        scale = jnp.where(mine, 1.0, 0.0) / obs_var[line, :]
        shift = ny.bit_length() - 1
        row = lax.shift_right_logical(voxel, shift)
        column = jnp.bitwise_and(voxel, ny - 1)
        at_row = lax.broadcasted_iota(jnp.int32, (rows, batch_size), 0) == row
        at_column = lax.broadcasted_iota(jnp.int32, (ny, batch_size), 0) == column
        both = jnp.concatenate(
            [jnp.where(at_row, scale, 0.0), jnp.where(at_row, scale * observed[line, :], 0.0)],
            axis=0,
        )
        one = both.astype(bf16)
        rest = both - one.astype(f32)
        two = rest.astype(bf16)
        three = (rest - two.astype(f32)).astype(bf16)
        columns = jnp.where(at_column, 1.0, 0.0).astype(bf16)
        sums = lax.dot_general(
            jnp.concatenate([one, two, three], axis=0),
            columns,
            (NT, ((), ())),
            preferred_element_type=f32,
        )
        sums = sums[: 2 * rows] + sums[2 * rows : 4 * rows] + sums[4 * rows :]
        omega[k] = sums[:rows]
        eta[k] = sums[rows:]


def voxel_weights(owner, obs_index, observed, obs_var, count, rows, ny):
    out = jax.ShapeDtypeStruct((count, rows, ny), f32)
    return pl.pallas_call(
        weights_kernel,
        out_shape=[out, out],
        in_specs=[SMEM, VMEM, VMEM, VMEM],
        out_specs=[VMEM, VMEM],
        compiler_params=pltpu.CompilerParams(vmem_limit_bytes=SCOPED),
        name="voxel_weights",
    )(owner, obs_index, observed, obs_var)


def gram_kernel(owner, omega, eta, *refs, offsets, planes, first):
    place = position()
    if first:
        *sources, out, members_at = refs
    else:
        begun, *sources, packed, out, members_at = refs
    count = out.shape[0]
    span, nz, rows, ny = sources[0].shape
    members = members_at.shape[0]
    for k in range(count):
        out[k] = jnp.zeros(out.shape[1:], f32) if first else begun[k]

        @pl.when(owner[place[0] * count + k] == place[1])
        def _(k=k):
            def tile(t, total):
                x, z = t // nz, t % nz
                voxels = pl.ds((planes[0] + x * planes[1]) * nz + z, 1)
                for j, source in enumerate(sources):
                    start = pl.multiple_of(offsets(place[2], j), 8)
                    members_at[pl.ds(start, rows), :] = source[x, z]
                values = members_at[...]
                mean = jnp.sum(values, axis=0, keepdims=True) * (1.0 / members)
                spread = values - mean
                weight = omega[k, voxels, :]
                shift = eta[k, voxels, :] - weight * mean
                tail = lax.broadcasted_iota(jnp.int32, (LANES - members, ny), 0)
                weighted = jnp.concatenate(
                    [spread * weight, jnp.where(tail == 0, shift, 0.0)], axis=0
                )
                return total + dot_parts(split(spread), split(weighted), NT)

            out[k] = lax.fori_loop(0, span * nz, tile, out[k], unroll=4)

    if first:
        return
    row = lax.broadcasted_iota(jnp.int32, (members, LANES), 0)
    column = lax.broadcasted_iota(jnp.int32, (members, LANES), 1)
    above, below = out[0], out[1]

    def pick(where, x):
        return jnp.sum(jnp.where(where, x, 0.0), axis=1, keepdims=True)

    both = jnp.where(column >= row, above, below)
    both = jnp.where(column == members, pick(column == row, below), both)
    both = jnp.where(column == members + 1, pick(column == members, above), both)
    packed[...] = jnp.where(column == members + 2, pick(column == members, below), both)


def gram(owner, omega, eta, begun, sources, offsets, planes):
    _, _, rows, ny = sources[0].shape
    members = rows * len(sources)
    whole = (omega.shape[0], members, LANES)
    work = pltpu.VMEM((members, ny), f32)
    first = begun is None
    return pl.pallas_call(
        functools.partial(gram_kernel, offsets=offsets, planes=planes, first=first),
        out_shape=jax.ShapeDtypeStruct(whole if first else whole[1:], f32),
        in_specs=[SMEM] + [VMEM] * (2 + len(sources) + (not first)),
        out_specs=VMEM,
        scratch_shapes=[work] if first else [pltpu.VMEM(whole, f32), work],
        compiler_params=pltpu.CompilerParams(vmem_limit_bytes=SCOPED),
        name="gram",
    )(owner, omega, eta, *([] if first else [begun]), *sources)


def turned(x):
    rows = x.shape[0]
    whole = jnp.concatenate([x, jnp.zeros((LANES - rows, LANES), f32)], axis=0)
    return whole.T[:rows]


def batch_transform(extended, total, members):
    row = lax.broadcasted_iota(jnp.int32, extended.shape, 0)
    column = lax.broadcasted_iota(jnp.int32, extended.shape, 1)
    inside = column < members
    last = column == members
    identity = jnp.where(row == column, 1.0, 0.0)
    matrix = jnp.where(inside, extended, 0.0)

    mean = jnp.sum(total, axis=1, keepdims=True) * (1.0 / members)
    centred = jnp.where(inside, total - mean, 0.0)
    product = wide_dot(wide_left(matrix), wide_right(jnp.where(last, mean, centred)))
    product = jnp.where(last, extended - product, product)
    product = wide_dot(wide_left(turned(centred)), wide_right(product)) * (1.0 / (members - 1))
    innovation = jnp.sum(jnp.where(last, product, 0.0), axis=1, keepdims=True)
    system = identity + jnp.where(inside, product, 0.0)
    frobenius = jnp.sqrt(jnp.sum(jnp.sum(system * system, axis=1, keepdims=True), axis=0, keepdims=True))

    scaled_root = system / frobenius
    factor = 1.5 * identity - 0.5 * scaled_root
    scaled_root = wide_dot(wide_left(scaled_root), wide_right(factor))
    inverse_root = factor

    def newton(iteration, iterates):
        scaled_root, inverse_root = iterates
        factor = 1.5 * identity - 0.5 * wide_dot(
            wide_left(inverse_root), wide_right(scaled_root)
        )
        return (
            wide_dot(wide_left(scaled_root), wide_right(factor)),
            wide_dot(wide_left(factor), wide_right(inverse_root)),
        )

    scaled_root, inverse_root = lax.fori_loop(1, NEWTON, newton, (scaled_root, inverse_root), unroll=UNROLL)
    root_inv = inverse_root / jnp.sqrt(frobenius)
    mean_weight = jnp.sum(root_inv * innovation, axis=0, keepdims=True)
    mean_weight = jnp.sum(root_inv * mean_weight, axis=1, keepdims=True)
    mixing = jnp.where(inside, root_inv + mean_weight, 0.0)
    mixing = mixing - jnp.sum(mixing, axis=0, keepdims=True) * (1.0 / members)
    mixing = jnp.where(inside, mixing + 1.0 / members, 0.0)
    return wide_dot(wide_left(total), wide_right(mixing))


def early_kernel(mine, other, total, last, ordered):
    place = position()
    members = mine.shape[0]
    row = lax.broadcasted_iota(jnp.int32, (members, LANES), 0)
    column = lax.broadcasted_iota(jnp.int32, (members, LANES), 1)
    inside = column < members

    def pick(where, x):
        return jnp.sum(jnp.where(where, x, 0.0), axis=1, keepdims=True)

    for half, shared in ((place[0], mine), (1 - place[0], other)):
        packed = shared[...]
        above = jnp.where(inside & (column > row), packed, 0.0)
        below = jnp.where(inside & (column < row), packed, 0.0)
        middle = jnp.where(column == row, packed, 0.0)
        side = jnp.where(column == members, pick(column == members + 1, packed), 0.0)
        ordered[2 * half] = above + turned(above) + (middle + side)
        middle = jnp.where(column == row, pick(column == members, packed), 0.0)
        side = jnp.where(column == members, pick(column == members + 2, packed), 0.0)
        ordered[2 * half + 1] = below + turned(below) + (middle + side)
    batches = ordered.shape[0]
    product = jnp.where(row == column, 1.0, 0.0)
    for batch in range(batches - 1):
        product = batch_transform(ordered[batch], product, members)
    total[...] = product
    last[...] = ordered[batches - 1]


def late_kernel(total, last, out, work, *, offsets, blocks, rows):
    place = position()
    members = total.shape[0]
    product = batch_transform(last[...], total[...], members)
    rest = jnp.zeros((LANES - members, LANES), f32)
    work[...] = jnp.concatenate([product, rest], axis=0)
    if blocks == 1:
        out[...] = work[...].T
        return
    parts = [
        work[pl.ds(pl.multiple_of(offsets(place[2], j), 8), rows), :] for j in range(blocks)
    ]
    work[...] = jnp.concatenate([*parts, rest], axis=0).T
    out[...] = work[pl.ds(pl.multiple_of(offsets(place[2], 0), 8), rows), :]


def transform_call(kernel, name, outputs, scratch, inputs):
    return pl.pallas_call(
        kernel,
        out_shape=[jax.ShapeDtypeStruct(shape, f32) for shape in outputs],
        in_specs=[VMEM] * len(inputs),
        out_specs=[VMEM] * len(outputs),
        scratch_shapes=[pltpu.VMEM(shape, f32) for shape in scratch],
        compiler_params=pltpu.CompilerParams(vmem_limit_bytes=SCOPED),
        cost_estimate=pl.CostEstimate(
            flops=10**8, bytes_accessed=10**6, transcendentals=0
        ),
        name=name,
    )(*inputs)


def mix_kernel(weights, *refs, blocks):
    *sources, out = refs
    rows, _, _, nz, _ = out.shape
    x, nx = pl.program_id(0), pl.num_programs(0)
    free, conserved, internal, tracer, tracer_ends = [
        sources[k : k + blocks] for k in range(0, len(sources), blocks)
    ]
    members = blocks * free[0].shape[2]
    high, low = split(weights[:, :members])
    both = jnp.concatenate([high.astype(f32), low.astype(f32)], axis=0).astype(bf16)
    mul = functools.partial(jnp.dot, preferred_element_type=f32)

    def mixed(held, x, z):
        parts = [array[x, z] for array in held]
        values = parts[0] if blocks == 1 else jnp.concatenate(parts, axis=0)
        value_high, value_low = split(values)
        upper = mul(both, value_high)
        return upper[:rows] + (upper[rows:] + mul(high, value_low))

    def plane(tracer, at):
        for z in range(nz):
            bound = mixed(tracer, at, z)
            inside = mixed(internal, x, z)
            out[:, 0, 0, z, :] = mixed(free, x, z)
            out[:, 1, 0, z, :] = mixed(conserved, x, z) - bound
            out[:, 2, 0, z, :] = bound - inside
            out[:, 3, 0, z, :] = inside

    at_end = (x == 0) | (x == nx - 1)

    @pl.when(at_end)
    def _():
        plane(tracer_ends, x // (nx - 1))

    @pl.when(jnp.logical_not(at_end))
    def _():
        plane(tracer, x - 1)


def mix(weights, sources, blocks, shape):
    rows, species, nx, nz, ny = shape
    return pl.pallas_call(
        functools.partial(mix_kernel, blocks=blocks),
        grid=(nx,),
        in_specs=[VMEM] * (1 + len(sources)),
        out_specs=pl.BlockSpec((rows, species, 1, nz, ny), lambda x: (0, 0, x, 0, 0)),
        out_shape=jax.ShapeDtypeStruct(shape, f32),
        compiler_params=pltpu.CompilerParams(vmem_limit_bytes=SCOPED),
        name="mix",
    )(weights, *sources)


def swap(x, axis, bit):
    count = lax.axis_size(axis)
    return lax.ppermute(x, axis, [(k, k ^ bit) for k in range(count)])


def total_over(x, axis):
    bit = 1
    while bit < lax.axis_size(axis):
        x = x + swap(x, axis, bit)
        bit *= 2
    return x


def local(ensemble, diffusivity, binding, source, obs_index, owner, observed, obs_var):
    rows, species, nx, nz, ny = ensemble.shape
    devices = lax.axis_size("member")
    spaces = lax.axis_size("space")
    members = rows * devices
    batches = owner.shape[0]
    member = lax.axis_index("member")

    forward = [(k, k + 1) for k in range(spaces - 1)]
    backward = [(k + 1, k) for k in range(spaces - 1)]

    def halos(first, last):
        return lax.ppermute(last, "space", forward), lax.ppermute(first, "space", backward)

    def tie(x, *after):
        return lax.optimization_barrier((x, *after))[0]

    if devices == 4 and rows % 8 == 0:
        blocks = devices

        def offsets(position, j):
            return jnp.bitwise_xor(position, j) * rows

        def collect(x, *after):
            return [x, swap(x, "member", 1), swap(tie(x, *after), "member", 2)]

        def complete(held, *after):
            return [*held, swap(lax.optimization_barrier((held[2], *after))[0], "member", 1)]
    else:
        blocks = 1

        def offsets(position, j):
            return 0

        def collect(x, *after):
            return [lax.all_gather(x, "member", axis=2, tiled=True)]

        def complete(held, *after):
            return held

    def across(held):
        return held[min(2, blocks - 1)]

    whole = (nx, nz, rows, ny)
    coefficients = (diffusivity, binding, source)
    cells = nx * nz * rows * ny
    ends = [
        jnp.transpose(ensemble[:, :3, part], (1, 2, 3, 0, 4))
        for part in (slice(0, 2), slice(nx - 2, nx))
    ]
    edges = forecast_call(
        first_edges_kernel,
        "first_edges",
        [*ends, *coefficients],
        [(nz, 2 * rows + 8, ny)] * 2,
        2 * cells // nx,
    )
    fields = [jnp.transpose(ensemble[:, k], (1, 2, 0, 3)) for k in range(species)]
    conserved = fields[1] + fields[2] + fields[3]
    omega, eta = voxel_weights(
        owner, obs_index, observed, obs_var, batches // 2, nx * nz, ny
    )
    around = origin = halos(*edges)
    conserved = collect(conserved)
    payload = (nz, 2 * rows, ny)
    for step in range(SUBSTEPS // 2 - 2):
        inputs = [*fields, *around, *origin, *coefficients]
        around = halos(
            *forecast_call(
                next_edges_kernel, "next_edges", inputs, [payload] * 2, cells, scratch=[whole] * 8
            )
        )
        fields = forecast_call(
            two_substeps_kernel, "two_substeps", inputs, [whole] * 4, 2 * cells, scratch=[whole] * 4
        )
    inner, end = (nx - 2, nz, rows, ny), (2, nz, rows, ny)
    before, first, last, free, tracer, internal, add, ends = forecast_call(
        last_steps_kernel,
        "last_steps",
        [*fields, *around, *origin, *coefficients],
        [whole, payload, payload, whole, inner, whole, inner, (3, *end)],
        4 * cells,
        scratch=[whole] * 7,
        ready=(omega, eta, *conserved[1:]),
    )
    tracer = collect(tracer)
    around = halos(first, last)
    tracer_ends, free_ends, add_ends = forecast_call(
        last_ends_kernel,
        "last_ends",
        [free, ends, *around, *coefficients],
        [end] * 3,
        cells // nx,
    )
    tracer = complete(tracer, tracer_ends)
    tracer_ends = collect(tracer_ends)
    conserved = complete(conserved, tracer_ends[0])
    begun = gram(owner, omega, eta, None, tracer, offsets, (1, 1))
    tracer_ends = complete(tracer_ends, begun)
    (free,) = forecast_call(
        last_free_kernel,
        "last_free",
        [before, free, free_ends, add, add_ends, *around, *origin, diffusivity],
        [whole],
        cells,
    )
    internal = collect(internal, across(tracer_ends), begun)
    half = gram(owner, omega, eta, begun, tracer_ends, offsets, (0, nx - 1))
    half = tie(total_over(half, "space"), across(internal))
    free = collect(free, half)
    other = swap(half, "member", 1)
    internal = complete(internal, half)
    square = (members, LANES)
    total, extended = transform_call(
        early_kernel,
        "transforms_early",
        [square, square],
        [(batches, members, LANES)],
        [half, other],
    )
    free = complete(free, total)
    (weights,) = transform_call(
        functools.partial(late_kernel, offsets=offsets, blocks=blocks, rows=rows),
        "transforms_late",
        [(LANES, LANES) if blocks == 1 else (rows, LANES)],
        [(LANES, LANES)],
        [total, extended],
    )
    if blocks == 1:
        weights = lax.dynamic_slice(weights, (member * rows, 0), (rows, LANES))
    held = free + conserved + internal + tracer + tracer_ends
    return mix(weights, held, blocks, ensemble.shape)


def solution(mesh):
    in_specs = (
        P("member", None, "space", None, None),
        P("space", None, None),
        P("space", None, None),
        P("space", None, None),
        P(),
        P(),
        P(),
        P(),
    )
    out_specs = P("member", None, "space", None, None)
    return jax.shard_map(local, mesh=mesh, in_specs=in_specs, out_specs=out_specs, check_vma=False)
```

```python
import functools

import jax
import jax.numpy as jnp
from jax import lax
from jax.experimental import pallas as pl
from jax.experimental.pallas import tpu as pltpu
from jax.sharding import PartitionSpec as P

SUBSTEPS = 6
NEWTON = 16
UNROLL = 5
LANES = 128
SCOPED = 10 * 2**20

unbind_rate = 0.05
uptake_rate = 0.1
recycle_rate = 0.02

VMEM = pl.BlockSpec(memory_space=pltpu.VMEM)
SMEM = pl.BlockSpec(memory_space=pltpu.SMEM)
bf16 = jnp.bfloat16
f32 = jnp.float32


def split(x):
    high = x.astype(bf16)
    return high, (x - high.astype(f32)).astype(bf16)


def dot_parts(a, b, dims):
    a_high, a_low = a
    b_high, b_low = b
    mul = functools.partial(
        lax.dot_general, dimension_numbers=(dims, ((), ())), preferred_element_type=f32
    )
    return mul(a_high, b_high) + (mul(a_high, b_low) + mul(a_low, b_high))


def wide_left(x):
    return jnp.concatenate(split(x), axis=1)


def wide_right(x):
    both = jnp.concatenate(split(x), axis=1)
    rows, lanes = both.shape
    if rows < lanes // 2:
        both = jnp.concatenate([both, jnp.zeros((lanes // 2 - rows, lanes), bf16)], axis=0)
    return jnp.concatenate([both, both], axis=0)


def wide_dot(left, right):
    out = jnp.dot(left, right, preferred_element_type=f32)
    side = out.shape[1] // 2
    return out[:, :side] + out[:, side:]


NN = ((1,), (0,))
NT = ((1,), (1,))


def position():
    member = lax.axis_index("member")
    return member & 1, lax.axis_index("space"), member


def react(free, receptor, complexed, internal, binding):
    flux = binding * free * receptor
    back = unbind_rate * complexed - flux
    return (
        back,
        receptor + back + recycle_rate * internal,
        complexed + flux - (unbind_rate + uptake_rate) * complexed,
        internal + uptake_rate * complexed - recycle_rate * internal,
    )


def spread_free(free, planes, neighbours, diffusivity):
    lane = lax.broadcasted_iota(jnp.int32, free.shape, 1)
    last = free.shape[1] - 1
    for plane in planes:
        neighbours = plane if neighbours is None else neighbours + plane
    neighbours += jnp.where(lane == last, 0.0, pltpu.roll(free, last, 1))
    neighbours += jnp.where(lane == 0, 0.0, pltpu.roll(free, 1, 1))
    return free + diffusivity * (neighbours - 6.0 * free)


def beside(read, x, z, nx, nz, low, high):
    around = [low if x == 0 else read(x - 1, z), high if x == nx - 1 else read(x + 1, z)]
    around += [read(x, other) for other in (z + 1, z - 1) if 0 <= other < nz]
    return [value for value in around if value is not None]


def edge_free(read, rest, x, nz, nx, z, diffusivity):
    return spread_free(read(x, z), beside(read, x, z, nx, nz, None, None), None, diffusivity) + rest


def first_edges_kernel(below, above, diffusivity, binding, source, first, last):
    _, _, nz, members, _ = below.shape
    nx = diffusivity.shape[0]
    for x, ends, out in ((0, below, first), (nx - 1, above, last)):
        shift = 0 if x == 0 else nx - 2

        def read(at, z, ends=ends, shift=shift):
            return ends[0, at - shift, z]

        for z in range(nz):
            row = pl.ds(z, 1)
            free = read(x, z)
            flux = binding[x, row, :] * free * ends[1, x - shift, z]
            rest = unbind_rate * ends[2, x - shift, z] - flux + source[x, row, :]
            spread = diffusivity[x, row, :]
            out[z, :members, :] = free
            out[z, members : 2 * members, :] = edge_free(read, rest, x, nz, nx, z, spread)
            out[z, 2 * members :, :] = jnp.broadcast_to(spread, (8, spread.shape[1]))


def step_planes(planes, a, r, c, i, outside, diffusivity, binding, source, out_a, outs, keep):
    nx, nz, _, _ = a.shape
    for x in planes:
        for z in range(nz):
            row = pl.ds(z, 1)
            back, *others = react(a[x, z], r[x, z], c[x, z], i[x, z], binding[x, row, :])
            around = beside(lambda x, z: a[x, z], x, z, nx, nz, *outside(x, z))
            out_a[x, z] = (
                spread_free(a[x, z], around, None, diffusivity[x, row, :])
                + back
                + source[x, row, :]
            )
            if x in keep:
                for out, value in zip(outs, others):
                    out[x, z] = value


def before_last(a, low, high):
    nx, _, members, _ = a.shape

    def outside(x, z):
        return (
            low[z, :members, :] if x == 0 else None,
            high[z, :members, :] if x == nx - 1 else None,
        )

    return outside


def after_first(a, low, high, low_first, high_first):
    nx, _, members, _ = a.shape

    def completed(halo, origin, x, z):
        later = halo[z, members : 2 * members, :]
        return later + origin[z, 2 * members : 2 * members + 1, :] * a[x, z]

    def outside(x, z):
        return (
            completed(low, low_first, x, z) if x == 0 else None,
            completed(high, high_first, x, z) if x == nx - 1 else None,
        )

    return outside


def next_edges_kernel(
    a, r, c, i, low, high, low_first, high_first, diffusivity, binding, source, *refs
):
    first, last, *kept = refs
    middle, later = kept[:4], kept[4:]
    nx, nz, members, _ = a.shape
    coefficients = (diffusivity, binding, source)

    def near(depth):
        return [x for x in range(nx) if min(x, nx - 1 - x) < depth]

    step_planes(
        near(3), a, r, c, i, before_last(a, low, high), *coefficients, middle[0], middle[1:], near(2)
    )
    step_planes(
        near(2),
        *middle,
        after_first(a, low, high, low_first, high_first),
        *coefficients,
        later[0],
        later[1:],
        near(1),
    )
    free, receptor, complexed = later[:3]
    for x, out in ((0, first), (nx - 1, last)):
        for z in range(nz):
            row = pl.ds(z, 1)
            flux = binding[x, row, :] * free[x, z] * receptor[x, z]
            rest = unbind_rate * complexed[x, z] - flux + source[x, row, :]
            out[z, :members, :] = free[x, z]
            out[z, members:, :] = edge_free(
                lambda x, z: free[x, z], rest, x, nz, nx, z, diffusivity[x, row, :]
            )


def two_substeps_kernel(
    a, r, c, i, low, high, low_first, high_first, diffusivity, binding, source, *refs
):
    outs, middle = refs[:4], refs[4:]
    everywhere = range(a.shape[0])
    coefficients = (diffusivity, binding, source)
    step_planes(
        everywhere,
        a,
        r,
        c,
        i,
        before_last(a, low, high),
        *coefficients,
        middle[0],
        middle[1:],
        everywhere,
    )
    step_planes(
        everywhere,
        *middle,
        after_first(a, low, high, low_first, high_first),
        *coefficients,
        outs[0],
        outs[1:],
        everywhere,
    )


def last_steps_kernel(
    a, r, c, i, low, high, low_first, high_first, diffusivity, binding, source, *refs
):
    *outs, m0, m1, m2, m3, later_r, later_c, later_i = refs
    before, first, last, free, tracer, inside, add, ends = outs
    nx, nz, members, _ = a.shape
    coefficients = (diffusivity, binding, source)
    two_substeps_kernel(
        a,
        r,
        c,
        i,
        low,
        high,
        low_first,
        high_first,
        *coefficients,
        before,
        later_r,
        later_c,
        later_i,
        m0,
        m1,
        m2,
        m3,
    )
    step_planes(
        range(nx),
        before,
        later_r,
        later_c,
        later_i,
        lambda x, z: (None, None),
        *coefficients,
        free,
        (m1, m2, m3),
        range(nx),
    )
    for x in range(nx):
        for z in range(nz):
            row = pl.ds(z, 1)
            back, _, complexed, internal = react(
                free[x, z], m1[x, z], m2[x, z], m3[x, z], binding[x, row, :]
            )
            inside[x, z] = internal
            if 0 < x < nx - 1:
                tracer[x - 1, z] = complexed + internal
                add[x - 1, z] = back + source[x, row, :]
                continue
            ends[0, x // (nx - 1), z] = m1[x, z]
            ends[1, x // (nx - 1), z] = m2[x, z]
            ends[2, x // (nx - 1), z] = m3[x, z]
    for x, out in ((0, first), (nx - 1, last)):
        for z in range(nz):
            out[z, :members, :] = before[x, z]
            out[z, members:, :] = free[x, z]


def last_ends_kernel(
    free, ends, low, high, diffusivity, binding, source, tracer, out_free, add
):
    nx, nz, members, _ = free.shape
    for end, (x, halo) in enumerate(((0, low), (nx - 1, high))):
        for z in range(nz):
            row = pl.ds(z, 1)
            value = free[x, z] + diffusivity[x, row, :] * halo[z, :members, :]
            back, _, complexed, internal = react(
                value, ends[0, end, z], ends[1, end, z], ends[2, end, z], binding[x, row, :]
            )
            tracer[end, z] = complexed + internal
            out_free[end, z] = value
            add[end, z] = back + source[x, row, :]


def last_free_kernel(
    before, free, free_ends, add, add_ends, low, high, low_first, high_first, diffusivity, out
):
    nx, nz, _, _ = free.shape
    outside = after_first(before, low, high, low_first, high_first)

    def read(x, z):
        return free[x, z] if 0 < x < nx - 1 else free_ends[x // (nx - 1), z]

    for x in range(nx):
        for z in range(nz):
            around = beside(read, x, z, nx, nz, *outside(x, z))
            rest = add[x - 1, z] if 0 < x < nx - 1 else add_ends[x // (nx - 1), z]
            out[x, z] = (
                spread_free(read(x, z), around, None, diffusivity[x, pl.ds(z, 1), :]) + rest
            )


def forecast_call(kernel, name, inputs, outputs, cells, scratch=(), ready=()):
    def body(*refs):
        kernel(*refs[: len(inputs)], *refs[len(inputs) + len(ready) :])

    return pl.pallas_call(
        body,
        out_shape=[jax.ShapeDtypeStruct(shape, f32) for shape in outputs],
        in_specs=[VMEM] * len(inputs) + [pl.BlockSpec(memory_space=pl.ANY)] * len(ready),
        out_specs=[VMEM] * len(outputs),
        scratch_shapes=[pltpu.VMEM(shape, f32) for shape in scratch],
        compiler_params=pltpu.CompilerParams(vmem_limit_bytes=SCOPED),
        cost_estimate=pl.CostEstimate(
            flops=30 * cells, bytes_accessed=32 * cells, transcendentals=0
        ),
        name=name,
    )(*inputs, *ready)


def weights_kernel(owner, obs_index, observed, obs_var, omega, eta):
    place = position()
    count, rows, ny = omega.shape
    batch_size = obs_index.shape[1]
    for k in range(count):
        batch = place[0] * count + k
        mine = owner[batch] == place[1]
        line = pl.ds(batch, 1)
        voxel = obs_index[line, :]
        scale = jnp.where(mine, 1.0, 0.0) / obs_var[line, :]
        shift = ny.bit_length() - 1
        row = lax.shift_right_logical(voxel, shift)
        column = jnp.bitwise_and(voxel, ny - 1)
        at_row = lax.broadcasted_iota(jnp.int32, (rows, batch_size), 0) == row
        at_column = lax.broadcasted_iota(jnp.int32, (ny, batch_size), 0) == column
        both = jnp.concatenate(
            [jnp.where(at_row, scale, 0.0), jnp.where(at_row, scale * observed[line, :], 0.0)],
            axis=0,
        )
        one = both.astype(bf16)
        rest = both - one.astype(f32)
        two = rest.astype(bf16)
        three = (rest - two.astype(f32)).astype(bf16)
        columns = jnp.where(at_column, 1.0, 0.0).astype(bf16)
        sums = lax.dot_general(
            jnp.concatenate([one, two, three], axis=0),
            columns,
            (NT, ((), ())),
            preferred_element_type=f32,
        )
        sums = sums[: 2 * rows] + sums[2 * rows : 4 * rows] + sums[4 * rows :]
        omega[k] = sums[:rows]
        eta[k] = sums[rows:]


def voxel_weights(owner, obs_index, observed, obs_var, count, rows, ny):
    out = jax.ShapeDtypeStruct((count, rows, ny), f32)
    return pl.pallas_call(
        weights_kernel,
        out_shape=[out, out],
        in_specs=[SMEM, VMEM, VMEM, VMEM],
        out_specs=[VMEM, VMEM],
        compiler_params=pltpu.CompilerParams(vmem_limit_bytes=SCOPED),
        name="voxel_weights",
    )(owner, obs_index, observed, obs_var)


def gram_kernel(owner, omega, eta, *refs, offsets, planes, first):
    place = position()
    if first:
        *sources, out, members_at = refs
    else:
        begun, *sources, packed, out, members_at = refs
    count = out.shape[0]
    span, nz, rows, ny = sources[0].shape
    members = members_at.shape[0]
    for k in range(count):
        out[k] = jnp.zeros(out.shape[1:], f32) if first else begun[k]

        @pl.when(owner[place[0] * count + k] == place[1])
        def _(k=k):
            def tile(t, total):
                x, z = t // nz, t % nz
                voxels = pl.ds((planes[0] + x * planes[1]) * nz + z, 1)
                for j, source in enumerate(sources):
                    start = pl.multiple_of(offsets(place[2], j), 8)
                    members_at[pl.ds(start, rows), :] = source[x, z]
                values = members_at[...]
                mean = jnp.sum(values, axis=0, keepdims=True) * (1.0 / members)
                spread = values - mean
                weight = omega[k, voxels, :]
                shift = eta[k, voxels, :] - weight * mean
                tail = lax.broadcasted_iota(jnp.int32, (LANES - members, ny), 0)
                weighted = jnp.concatenate(
                    [spread * weight, jnp.where(tail == 0, shift, 0.0)], axis=0
                )
                return total + dot_parts(split(spread), split(weighted), NT)

            out[k] = lax.fori_loop(0, span * nz, tile, out[k], unroll=4)

    if first:
        return
    row = lax.broadcasted_iota(jnp.int32, (members, LANES), 0)
    column = lax.broadcasted_iota(jnp.int32, (members, LANES), 1)
    above, below = out[0], out[1]

    def pick(where, x):
        return jnp.sum(jnp.where(where, x, 0.0), axis=1, keepdims=True)

    both = jnp.where(column >= row, above, below)
    both = jnp.where(column == members, pick(column == row, below), both)
    both = jnp.where(column == members + 1, pick(column == members, above), both)
    packed[...] = jnp.where(column == members + 2, pick(column == members, below), both)


def gram(owner, omega, eta, begun, sources, offsets, planes):
    _, _, rows, ny = sources[0].shape
    members = rows * len(sources)
    whole = (omega.shape[0], members, LANES)
    work = pltpu.VMEM((members, ny), f32)
    first = begun is None
    return pl.pallas_call(
        functools.partial(gram_kernel, offsets=offsets, planes=planes, first=first),
        out_shape=jax.ShapeDtypeStruct(whole if first else whole[1:], f32),
        in_specs=[SMEM] + [VMEM] * (2 + len(sources) + (not first)),
        out_specs=VMEM,
        scratch_shapes=[work] if first else [pltpu.VMEM(whole, f32), work],
        compiler_params=pltpu.CompilerParams(vmem_limit_bytes=SCOPED),
        name="gram",
    )(owner, omega, eta, *([] if first else [begun]), *sources)


def turned(x):
    rows = x.shape[0]
    whole = jnp.concatenate([x, jnp.zeros((LANES - rows, LANES), f32)], axis=0)
    return whole.T[:rows]


def batch_transform(extended, total, members):
    row = lax.broadcasted_iota(jnp.int32, extended.shape, 0)
    column = lax.broadcasted_iota(jnp.int32, extended.shape, 1)
    inside = column < members
    last = column == members
    identity = jnp.where(row == column, 1.0, 0.0)
    matrix = jnp.where(inside, extended, 0.0)

    mean = jnp.sum(total, axis=1, keepdims=True) * (1.0 / members)
    centred = jnp.where(inside, total - mean, 0.0)
    product = wide_dot(wide_left(matrix), wide_right(jnp.where(last, mean, centred)))
    product = jnp.where(last, extended - product, product)
    product = wide_dot(wide_left(turned(centred)), wide_right(product)) * (1.0 / (members - 1))
    innovation = jnp.sum(jnp.where(last, product, 0.0), axis=1, keepdims=True)
    system = identity + jnp.where(inside, product, 0.0)
    frobenius = jnp.sqrt(jnp.sum(jnp.sum(system * system, axis=1, keepdims=True), axis=0, keepdims=True))

    scaled_root = system / frobenius
    factor = 1.5 * identity - 0.5 * scaled_root
    scaled_root = wide_dot(wide_left(scaled_root), wide_right(factor))
    inverse_root = factor

    def newton(iteration, iterates):
        scaled_root, inverse_root = iterates
        factor = 1.5 * identity - 0.5 * wide_dot(
            wide_left(inverse_root), wide_right(scaled_root)
        )
        return (
            wide_dot(wide_left(scaled_root), wide_right(factor)),
            wide_dot(wide_left(factor), wide_right(inverse_root)),
        )

    scaled_root, inverse_root = lax.fori_loop(1, NEWTON, newton, (scaled_root, inverse_root), unroll=UNROLL)
    root_inv = inverse_root / jnp.sqrt(frobenius)
    mean_weight = jnp.sum(root_inv * innovation, axis=0, keepdims=True)
    mean_weight = jnp.sum(root_inv * mean_weight, axis=1, keepdims=True)
    mixing = jnp.where(inside, root_inv + mean_weight, 0.0)
    mixing = mixing - jnp.sum(mixing, axis=0, keepdims=True) * (1.0 / members)
    mixing = jnp.where(inside, mixing + 1.0 / members, 0.0)
    return wide_dot(wide_left(total), wide_right(mixing))


def early_kernel(mine, other, total, last, ordered):
    place = position()
    members = mine.shape[0]
    row = lax.broadcasted_iota(jnp.int32, (members, LANES), 0)
    column = lax.broadcasted_iota(jnp.int32, (members, LANES), 1)
    inside = column < members

    def pick(where, x):
        return jnp.sum(jnp.where(where, x, 0.0), axis=1, keepdims=True)

    for half, shared in ((place[0], mine), (1 - place[0], other)):
        packed = shared[...]
        above = jnp.where(inside & (column > row), packed, 0.0)
        below = jnp.where(inside & (column < row), packed, 0.0)
        middle = jnp.where(column == row, packed, 0.0)
        side = jnp.where(column == members, pick(column == members + 1, packed), 0.0)
        ordered[2 * half] = above + turned(above) + (middle + side)
        middle = jnp.where(column == row, pick(column == members, packed), 0.0)
        side = jnp.where(column == members, pick(column == members + 2, packed), 0.0)
        ordered[2 * half + 1] = below + turned(below) + (middle + side)
    batches = ordered.shape[0]
    product = jnp.where(row == column, 1.0, 0.0)
    for batch in range(batches - 1):
        product = batch_transform(ordered[batch], product, members)
    total[...] = product
    last[...] = ordered[batches - 1]


def late_kernel(total, last, out, work, *, offsets, blocks, rows):
    place = position()
    members = total.shape[0]
    product = batch_transform(last[...], total[...], members)
    rest = jnp.zeros((LANES - members, LANES), f32)
    work[...] = jnp.concatenate([product, rest], axis=0)
    if blocks == 1:
        out[...] = work[...].T
        return
    parts = [
        work[pl.ds(pl.multiple_of(offsets(place[2], j), 8), rows), :] for j in range(blocks)
    ]
    work[...] = jnp.concatenate([*parts, rest], axis=0).T
    out[...] = work[pl.ds(pl.multiple_of(offsets(place[2], 0), 8), rows), :]


def transform_call(kernel, name, outputs, scratch, inputs):
    return pl.pallas_call(
        kernel,
        out_shape=[jax.ShapeDtypeStruct(shape, f32) for shape in outputs],
        in_specs=[VMEM] * len(inputs),
        out_specs=[VMEM] * len(outputs),
        scratch_shapes=[pltpu.VMEM(shape, f32) for shape in scratch],
        compiler_params=pltpu.CompilerParams(vmem_limit_bytes=SCOPED),
        cost_estimate=pl.CostEstimate(
            flops=10**8, bytes_accessed=10**6, transcendentals=0
        ),
        name=name,
    )(*inputs)


def mix_kernel(weights, *refs, blocks):
    *sources, out = refs
    rows, _, _, nz, _ = out.shape
    x, nx = pl.program_id(0), pl.num_programs(0)
    free, conserved, internal, tracer, tracer_ends = [
        sources[k : k + blocks] for k in range(0, len(sources), blocks)
    ]
    members = blocks * free[0].shape[2]
    high, low = split(weights[:, :members])
    both = jnp.concatenate([high.astype(f32), low.astype(f32)], axis=0).astype(bf16)
    mul = functools.partial(jnp.dot, preferred_element_type=f32)

    def mixed(held, x, z):
        parts = [array[x, z] for array in held]
        values = parts[0] if blocks == 1 else jnp.concatenate(parts, axis=0)
        value_high, value_low = split(values)
        upper = mul(both, value_high)
        return upper[:rows] + (upper[rows:] + mul(high, value_low))

    def plane(tracer, at):
        for z in range(nz):
            bound = mixed(tracer, at, z)
            inside = mixed(internal, x, z)
            out[:, 0, 0, z, :] = mixed(free, x, z)
            out[:, 1, 0, z, :] = mixed(conserved, x, z) - bound
            out[:, 2, 0, z, :] = bound - inside
            out[:, 3, 0, z, :] = inside

    at_end = (x == 0) | (x == nx - 1)

    @pl.when(at_end)
    def _():
        plane(tracer_ends, x // (nx - 1))

    @pl.when(jnp.logical_not(at_end))
    def _():
        plane(tracer, x - 1)


def mix(weights, sources, blocks, shape):
    rows, species, nx, nz, ny = shape
    return pl.pallas_call(
        functools.partial(mix_kernel, blocks=blocks),
        grid=(nx,),
        in_specs=[VMEM] * (1 + len(sources)),
        out_specs=pl.BlockSpec((rows, species, 1, nz, ny), lambda x: (0, 0, x, 0, 0)),
        out_shape=jax.ShapeDtypeStruct(shape, f32),
        compiler_params=pltpu.CompilerParams(vmem_limit_bytes=SCOPED),
        name="mix",
    )(weights, *sources)


def swap(x, axis, bit):
    count = lax.axis_size(axis)
    return lax.ppermute(x, axis, [(k, k ^ bit) for k in range(count)])


def total_over(x, axis):
    bit = 1
    while bit < lax.axis_size(axis):
        x = x + swap(x, axis, bit)
        bit *= 2
    return x


def local(ensemble, diffusivity, binding, source, obs_index, owner, observed, obs_var):
    rows, species, nx, nz, ny = ensemble.shape
    devices = lax.axis_size("member")
    spaces = lax.axis_size("space")
    members = rows * devices
    batches = owner.shape[0]
    member = lax.axis_index("member")

    forward = [(k, k + 1) for k in range(spaces - 1)]
    backward = [(k + 1, k) for k in range(spaces - 1)]

    def halos(first, last):
        return lax.ppermute(last, "space", forward), lax.ppermute(first, "space", backward)

    def tie(x, *after):
        return lax.optimization_barrier((x, *after))[0]

    if devices == 4 and rows % 8 == 0:
        blocks = devices

        def offsets(position, j):
            return jnp.bitwise_xor(position, j) * rows

        def collect(x, *after):
            return [x, swap(x, "member", 1), swap(tie(x, *after), "member", 2)]

        def complete(held, *after):
            return [*held, swap(lax.optimization_barrier((held[2], *after))[0], "member", 1)]
    else:
        blocks = 1

        def offsets(position, j):
            return 0

        def collect(x, *after):
            return [lax.all_gather(x, "member", axis=2, tiled=True)]

        def complete(held, *after):
            return held

    def across(held):
        return held[min(2, blocks - 1)]

    whole = (nx, nz, rows, ny)
    coefficients = (diffusivity, binding, source)
    cells = nx * nz * rows * ny
    ends = [
        jnp.transpose(ensemble[:, :3, part], (1, 2, 3, 0, 4))
        for part in (slice(0, 2), slice(nx - 2, nx))
    ]
    edges = forecast_call(
        first_edges_kernel,
        "first_edges",
        [*ends, *coefficients],
        [(nz, 2 * rows + 8, ny)] * 2,
        2 * cells // nx,
    )
    fields = [jnp.transpose(ensemble[:, k], (1, 2, 0, 3)) for k in range(species)]
    conserved = fields[1] + fields[2] + fields[3]
    omega, eta = voxel_weights(
        owner, obs_index, observed, obs_var, batches // 2, nx * nz, ny
    )
    around = origin = halos(*edges)
    conserved = collect(conserved)
    payload = (nz, 2 * rows, ny)
    for step in range(SUBSTEPS // 2 - 2):
        inputs = [*fields, *around, *origin, *coefficients]
        around = halos(
            *forecast_call(
                next_edges_kernel, "next_edges", inputs, [payload] * 2, cells, scratch=[whole] * 8
            )
        )
        fields = forecast_call(
            two_substeps_kernel, "two_substeps", inputs, [whole] * 4, 2 * cells, scratch=[whole] * 4
        )
    inner, end = (nx - 2, nz, rows, ny), (2, nz, rows, ny)
    before, first, last, free, tracer, internal, add, ends = forecast_call(
        last_steps_kernel,
        "last_steps",
        [*fields, *around, *origin, *coefficients],
        [whole, payload, payload, whole, inner, whole, inner, (3, *end)],
        4 * cells,
        scratch=[whole] * 7,
        ready=(omega, eta, *conserved[1:]),
    )
    tracer = collect(tracer)
    around = halos(first, last)
    tracer_ends, free_ends, add_ends = forecast_call(
        last_ends_kernel,
        "last_ends",
        [free, ends, *around, *coefficients],
        [end] * 3,
        cells // nx,
    )
    tracer = complete(tracer, tracer_ends)
    tracer_ends = collect(tracer_ends)
    conserved = complete(conserved, tracer_ends[0])
    begun = gram(owner, omega, eta, None, tracer, offsets, (1, 1))
    tracer_ends = complete(tracer_ends, begun)
    internal = collect(internal, across(tracer_ends), begun)
    (free,) = forecast_call(
        last_free_kernel,
        "last_free",
        [before, free, free_ends, add, add_ends, *around, *origin, diffusivity],
        [whole],
        cells,
        ready=[*conserved[3:], *internal[1:2]] if blocks > 1 else (),
    )
    half = gram(owner, omega, eta, begun, tracer_ends, offsets, (0, nx - 1))
    half = total_over(half, "space")
    other = swap(half, "member", 1)
    half = tie(half, other, across(internal))
    free = collect(free, half)
    internal = complete(internal, half)
    square = (members, LANES)
    total, extended = transform_call(
        early_kernel,
        "transforms_early",
        [square, square],
        [(batches, members, LANES)],
        [half, other],
    )
    free = complete(free, total)
    (weights,) = transform_call(
        functools.partial(late_kernel, offsets=offsets, blocks=blocks, rows=rows),
        "transforms_late",
        [(LANES, LANES) if blocks == 1 else (rows, LANES)],
        [(LANES, LANES)],
        [total, extended],
    )
    if blocks == 1:
        weights = lax.dynamic_slice(weights, (member * rows, 0), (rows, LANES))
    held = free + conserved + internal + tracer + tracer_ends
    return mix(weights, held, blocks, ensemble.shape)


def solution(mesh):
    in_specs = (
        P("member", None, "space", None, None),
        P("space", None, None),
        P("space", None, None),
        P("space", None, None),
        P(),
        P(),
        P(),
        P(),
    )
    out_specs = P("member", None, "space", None, None)
    return jax.shard_map(local, mesh=mesh, in_specs=in_specs, out_specs=out_specs, check_vma=False)
```

```python
import functools

import jax
import jax.numpy as jnp
from jax import lax
from jax.experimental import pallas as pl
from jax.experimental.pallas import tpu as pltpu
from jax.sharding import PartitionSpec as P

SUBSTEPS = 6
NEWTON = 16
UNROLL = 5
LANES = 128
SCOPED = 10 * 2**20

unbind_rate = 0.05
uptake_rate = 0.1
recycle_rate = 0.02

VMEM = pl.BlockSpec(memory_space=pltpu.VMEM)
SMEM = pl.BlockSpec(memory_space=pltpu.SMEM)
bf16 = jnp.bfloat16
f32 = jnp.float32


def split(x):
    high = x.astype(bf16)
    return high, (x - high.astype(f32)).astype(bf16)


def dot_parts(a, b, dims):
    a_high, a_low = a
    b_high, b_low = b
    mul = functools.partial(
        lax.dot_general, dimension_numbers=(dims, ((), ())), preferred_element_type=f32
    )
    return mul(a_high, b_high) + (mul(a_high, b_low) + mul(a_low, b_high))


def wide_left(x):
    return jnp.concatenate(split(x), axis=1)


def wide_right(x):
    both = jnp.concatenate(split(x), axis=1)
    rows, lanes = both.shape
    if rows < lanes // 2:
        both = jnp.concatenate([both, jnp.zeros((lanes // 2 - rows, lanes), bf16)], axis=0)
    return jnp.concatenate([both, both], axis=0)


def wide_dot(left, right):
    out = jnp.dot(left, right, preferred_element_type=f32)
    side = out.shape[1] // 2
    return out[:, :side] + out[:, side:]


NN = ((1,), (0,))
NT = ((1,), (1,))


def position():
    member = lax.axis_index("member")
    return member & 1, lax.axis_index("space"), member


def react(free, receptor, complexed, internal, binding):
    flux = binding * free * receptor
    back = unbind_rate * complexed - flux
    return (
        back,
        receptor + back + recycle_rate * internal,
        complexed + flux - (unbind_rate + uptake_rate) * complexed,
        internal + uptake_rate * complexed - recycle_rate * internal,
    )


def spread_free(free, planes, neighbours, diffusivity):
    lane = lax.broadcasted_iota(jnp.int32, free.shape, 1)
    last = free.shape[1] - 1
    for plane in planes:
        neighbours = plane if neighbours is None else neighbours + plane
    neighbours += jnp.where(lane == last, 0.0, pltpu.roll(free, last, 1))
    neighbours += jnp.where(lane == 0, 0.0, pltpu.roll(free, 1, 1))
    return free + diffusivity * (neighbours - 6.0 * free)


def beside(read, x, z, nx, nz, low, high):
    around = [low if x == 0 else read(x - 1, z), high if x == nx - 1 else read(x + 1, z)]
    around += [read(x, other) for other in (z + 1, z - 1) if 0 <= other < nz]
    return [value for value in around if value is not None]


def edge_free(read, rest, x, nz, nx, z, diffusivity):
    return spread_free(read(x, z), beside(read, x, z, nx, nz, None, None), None, diffusivity) + rest


def first_edges_kernel(below, above, diffusivity, binding, source, first, last):
    _, _, nz, members, _ = below.shape
    nx = diffusivity.shape[0]
    for x, ends, out in ((0, below, first), (nx - 1, above, last)):
        shift = 0 if x == 0 else nx - 2

        def read(at, z, ends=ends, shift=shift):
            return ends[0, at - shift, z]

        for z in range(nz):
            row = pl.ds(z, 1)
            free = read(x, z)
            flux = binding[x, row, :] * free * ends[1, x - shift, z]
            rest = unbind_rate * ends[2, x - shift, z] - flux + source[x, row, :]
            spread = diffusivity[x, row, :]
            out[z, :members, :] = free
            out[z, members : 2 * members, :] = edge_free(read, rest, x, nz, nx, z, spread)
            out[z, 2 * members :, :] = jnp.broadcast_to(spread, (8, spread.shape[1]))


def step_planes(planes, a, r, c, i, outside, diffusivity, binding, source, out_a, outs, keep):
    nx, nz, _, _ = a.shape
    for x in planes:
        for z in range(nz):
            row = pl.ds(z, 1)
            back, *others = react(a[x, z], r[x, z], c[x, z], i[x, z], binding[x, row, :])
            around = beside(lambda x, z: a[x, z], x, z, nx, nz, *outside(x, z))
            out_a[x, z] = (
                spread_free(a[x, z], around, None, diffusivity[x, row, :])
                + back
                + source[x, row, :]
            )
            if x in keep:
                for out, value in zip(outs, others):
                    out[x, z] = value


def before_last(a, low, high):
    nx, _, members, _ = a.shape

    def outside(x, z):
        return (
            low[z, :members, :] if x == 0 else None,
            high[z, :members, :] if x == nx - 1 else None,
        )

    return outside


def after_first(a, low, high, low_first, high_first):
    nx, _, members, _ = a.shape

    def completed(halo, origin, x, z):
        later = halo[z, members : 2 * members, :]
        return later + origin[z, 2 * members : 2 * members + 1, :] * a[x, z]

    def outside(x, z):
        return (
            completed(low, low_first, x, z) if x == 0 else None,
            completed(high, high_first, x, z) if x == nx - 1 else None,
        )

    return outside


def next_edges_kernel(
    a, r, c, i, low, high, low_first, high_first, diffusivity, binding, source, *refs
):
    first, last, *kept = refs
    middle, later = kept[:4], kept[4:]
    nx, nz, members, _ = a.shape
    coefficients = (diffusivity, binding, source)

    def near(depth):
        return [x for x in range(nx) if min(x, nx - 1 - x) < depth]

    step_planes(
        near(3), a, r, c, i, before_last(a, low, high), *coefficients, middle[0], middle[1:], near(2)
    )
    step_planes(
        near(2),
        *middle,
        after_first(a, low, high, low_first, high_first),
        *coefficients,
        later[0],
        later[1:],
        near(1),
    )
    free, receptor, complexed = later[:3]
    for x, out in ((0, first), (nx - 1, last)):
        for z in range(nz):
            row = pl.ds(z, 1)
            flux = binding[x, row, :] * free[x, z] * receptor[x, z]
            rest = unbind_rate * complexed[x, z] - flux + source[x, row, :]
            out[z, :members, :] = free[x, z]
            out[z, members:, :] = edge_free(
                lambda x, z: free[x, z], rest, x, nz, nx, z, diffusivity[x, row, :]
            )


def two_substeps_kernel(
    a, r, c, i, low, high, low_first, high_first, diffusivity, binding, source, *refs
):
    outs, middle = refs[:4], refs[4:]
    everywhere = range(a.shape[0])
    coefficients = (diffusivity, binding, source)
    step_planes(
        everywhere,
        a,
        r,
        c,
        i,
        before_last(a, low, high),
        *coefficients,
        middle[0],
        middle[1:],
        everywhere,
    )
    step_planes(
        everywhere,
        *middle,
        after_first(a, low, high, low_first, high_first),
        *coefficients,
        outs[0],
        outs[1:],
        everywhere,
    )


def last_steps_kernel(
    a, r, c, i, low, high, low_first, high_first, diffusivity, binding, source, *refs
):
    *outs, m0, m1, m2, m3, later_r, later_c, later_i = refs
    before, first, last, free, tracer, inside, add, ends = outs
    nx, nz, members, _ = a.shape
    coefficients = (diffusivity, binding, source)
    two_substeps_kernel(
        a,
        r,
        c,
        i,
        low,
        high,
        low_first,
        high_first,
        *coefficients,
        before,
        later_r,
        later_c,
        later_i,
        m0,
        m1,
        m2,
        m3,
    )
    step_planes(
        range(nx),
        before,
        later_r,
        later_c,
        later_i,
        lambda x, z: (None, None),
        *coefficients,
        free,
        (m1, m2, m3),
        range(nx),
    )
    for x in range(nx):
        for z in range(nz):
            row = pl.ds(z, 1)
            back, _, complexed, internal = react(
                free[x, z], m1[x, z], m2[x, z], m3[x, z], binding[x, row, :]
            )
            inside[x, z] = internal
            if 0 < x < nx - 1:
                tracer[x - 1, z] = complexed + internal
                add[x - 1, z] = back + source[x, row, :]
                continue
            ends[0, x // (nx - 1), z] = m1[x, z]
            ends[1, x // (nx - 1), z] = m2[x, z]
            ends[2, x // (nx - 1), z] = m3[x, z]
    for x, out in ((0, first), (nx - 1, last)):
        for z in range(nz):
            out[z, :members, :] = before[x, z]
            out[z, members:, :] = free[x, z]


def last_ends_kernel(
    free, ends, low, high, diffusivity, binding, source, tracer, out_free, add
):
    nx, nz, members, _ = free.shape
    for end, (x, halo) in enumerate(((0, low), (nx - 1, high))):
        for z in range(nz):
            row = pl.ds(z, 1)
            value = free[x, z] + diffusivity[x, row, :] * halo[z, :members, :]
            back, _, complexed, internal = react(
                value, ends[0, end, z], ends[1, end, z], ends[2, end, z], binding[x, row, :]
            )
            tracer[end, z] = complexed + internal
            out_free[end, z] = value
            add[end, z] = back + source[x, row, :]


def last_free_kernel(
    before, free, free_ends, add, add_ends, low, high, low_first, high_first, diffusivity, out
):
    nx, nz, _, _ = free.shape
    outside = after_first(before, low, high, low_first, high_first)

    def read(x, z):
        return free[x, z] if 0 < x < nx - 1 else free_ends[x // (nx - 1), z]

    for x in range(nx):
        for z in range(nz):
            around = beside(read, x, z, nx, nz, *outside(x, z))
            rest = add[x - 1, z] if 0 < x < nx - 1 else add_ends[x // (nx - 1), z]
            out[x, z] = (
                spread_free(read(x, z), around, None, diffusivity[x, pl.ds(z, 1), :]) + rest
            )


def forecast_call(kernel, name, inputs, outputs, cells, scratch=(), ready=()):
    def body(*refs):
        kernel(*refs[: len(inputs)], *refs[len(inputs) + len(ready) :])

    return pl.pallas_call(
        body,
        out_shape=[jax.ShapeDtypeStruct(shape, f32) for shape in outputs],
        in_specs=[VMEM] * len(inputs) + [pl.BlockSpec(memory_space=pl.ANY)] * len(ready),
        out_specs=[VMEM] * len(outputs),
        scratch_shapes=[pltpu.VMEM(shape, f32) for shape in scratch],
        compiler_params=pltpu.CompilerParams(vmem_limit_bytes=SCOPED),
        cost_estimate=pl.CostEstimate(
            flops=30 * cells, bytes_accessed=32 * cells, transcendentals=0
        ),
        name=name,
    )(*inputs, *ready)


def weights_kernel(owner, obs_index, observed, obs_var, omega, eta):
    place = position()
    count, rows, ny = omega.shape
    batch_size = obs_index.shape[1]
    for k in range(count):
        batch = place[0] * count + k
        mine = owner[batch] == place[1]
        line = pl.ds(batch, 1)
        voxel = obs_index[line, :]
        scale = jnp.where(mine, 1.0, 0.0) / obs_var[line, :]
        shift = ny.bit_length() - 1
        row = lax.shift_right_logical(voxel, shift)
        column = jnp.bitwise_and(voxel, ny - 1)
        at_row = lax.broadcasted_iota(jnp.int32, (rows, batch_size), 0) == row
        at_column = lax.broadcasted_iota(jnp.int32, (ny, batch_size), 0) == column
        both = jnp.concatenate(
            [jnp.where(at_row, scale, 0.0), jnp.where(at_row, scale * observed[line, :], 0.0)],
            axis=0,
        )
        one = both.astype(bf16)
        rest = both - one.astype(f32)
        two = rest.astype(bf16)
        three = (rest - two.astype(f32)).astype(bf16)
        columns = jnp.where(at_column, 1.0, 0.0).astype(bf16)
        sums = lax.dot_general(
            jnp.concatenate([one, two, three], axis=0),
            columns,
            (NT, ((), ())),
            preferred_element_type=f32,
        )
        sums = sums[: 2 * rows] + sums[2 * rows : 4 * rows] + sums[4 * rows :]
        omega[k] = sums[:rows]
        eta[k] = sums[rows:]


def voxel_weights(owner, obs_index, observed, obs_var, count, rows, ny):
    out = jax.ShapeDtypeStruct((count, rows, ny), f32)
    return pl.pallas_call(
        weights_kernel,
        out_shape=[out, out],
        in_specs=[SMEM, VMEM, VMEM, VMEM],
        out_specs=[VMEM, VMEM],
        compiler_params=pltpu.CompilerParams(vmem_limit_bytes=SCOPED),
        name="voxel_weights",
    )(owner, obs_index, observed, obs_var)


def gram_kernel(owner, omega, eta, *refs, offsets, planes, first):
    place = position()
    if first:
        *sources, out, members_at = refs
    else:
        begun, *sources, packed, out, members_at = refs
    count = out.shape[0]
    span, nz, rows, ny = sources[0].shape
    members = members_at.shape[0]
    for k in range(count):
        out[k] = jnp.zeros(out.shape[1:], f32) if first else begun[k]

        @pl.when(owner[place[0] * count + k] == place[1])
        def _(k=k):
            def tile(t, total):
                x, z = t // nz, t % nz
                voxels = pl.ds((planes[0] + x * planes[1]) * nz + z, 1)
                for j, source in enumerate(sources):
                    start = pl.multiple_of(offsets(place[2], j), 8)
                    members_at[pl.ds(start, rows), :] = source[x, z]
                values = members_at[...]
                mean = jnp.sum(values, axis=0, keepdims=True) * (1.0 / members)
                spread = values - mean
                weight = omega[k, voxels, :]
                shift = eta[k, voxels, :] - weight * mean
                tail = lax.broadcasted_iota(jnp.int32, (LANES - members, ny), 0)
                weighted = jnp.concatenate(
                    [spread * weight, jnp.where(tail == 0, shift, 0.0)], axis=0
                )
                return total + dot_parts(split(spread), split(weighted), NT)

            out[k] = lax.fori_loop(0, span * nz, tile, out[k], unroll=4)

    if first:
        return
    row = lax.broadcasted_iota(jnp.int32, (members, LANES), 0)
    column = lax.broadcasted_iota(jnp.int32, (members, LANES), 1)
    above, below = out[0], out[1]

    def pick(where, x):
        return jnp.sum(jnp.where(where, x, 0.0), axis=1, keepdims=True)

    both = jnp.where(column >= row, above, below)
    both = jnp.where(column == members, pick(column == row, below), both)
    both = jnp.where(column == members + 1, pick(column == members, above), both)
    packed[...] = jnp.where(column == members + 2, pick(column == members, below), both)


def gram(owner, omega, eta, begun, sources, offsets, planes):
    _, _, rows, ny = sources[0].shape
    members = rows * len(sources)
    whole = (omega.shape[0], members, LANES)
    work = pltpu.VMEM((members, ny), f32)
    first = begun is None
    return pl.pallas_call(
        functools.partial(gram_kernel, offsets=offsets, planes=planes, first=first),
        out_shape=jax.ShapeDtypeStruct(whole if first else whole[1:], f32),
        in_specs=[SMEM] + [VMEM] * (2 + len(sources) + (not first)),
        out_specs=VMEM,
        scratch_shapes=[work] if first else [pltpu.VMEM(whole, f32), work],
        compiler_params=pltpu.CompilerParams(vmem_limit_bytes=SCOPED),
        name="gram",
    )(owner, omega, eta, *([] if first else [begun]), *sources)


def turned(x):
    rows = x.shape[0]
    whole = jnp.concatenate([x, jnp.zeros((LANES - rows, LANES), f32)], axis=0)
    return whole.T[:rows]


def batch_transform(extended, total, members):
    row = lax.broadcasted_iota(jnp.int32, extended.shape, 0)
    column = lax.broadcasted_iota(jnp.int32, extended.shape, 1)
    inside = column < members
    last = column == members
    identity = jnp.where(row == column, 1.0, 0.0)
    matrix = jnp.where(inside, extended, 0.0)

    mean = jnp.sum(total, axis=1, keepdims=True) * (1.0 / members)
    centred = jnp.where(inside, total - mean, 0.0)
    product = wide_dot(wide_left(matrix), wide_right(jnp.where(last, mean, centred)))
    product = jnp.where(last, extended - product, product)
    product = wide_dot(wide_left(turned(centred)), wide_right(product)) * (1.0 / (members - 1))
    innovation = jnp.sum(jnp.where(last, product, 0.0), axis=1, keepdims=True)
    system = identity + jnp.where(inside, product, 0.0)
    frobenius = jnp.sqrt(jnp.sum(jnp.sum(system * system, axis=1, keepdims=True), axis=0, keepdims=True))

    scaled_root = system / frobenius
    factor = 1.5 * identity - 0.5 * scaled_root
    scaled_root = wide_dot(wide_left(scaled_root), wide_right(factor))
    inverse_root = factor

    def newton(iteration, iterates):
        scaled_root, inverse_root = iterates
        factor = 1.5 * identity - 0.5 * wide_dot(
            wide_left(inverse_root), wide_right(scaled_root)
        )
        return (
            wide_dot(wide_left(scaled_root), wide_right(factor)),
            wide_dot(wide_left(factor), wide_right(inverse_root)),
        )

    scaled_root, inverse_root = lax.fori_loop(1, NEWTON, newton, (scaled_root, inverse_root), unroll=UNROLL)
    root_inv = inverse_root / jnp.sqrt(frobenius)
    mean_weight = jnp.sum(root_inv * innovation, axis=0, keepdims=True)
    mean_weight = jnp.sum(root_inv * mean_weight, axis=1, keepdims=True)
    mixing = jnp.where(inside, root_inv + mean_weight, 0.0)
    mixing = mixing - jnp.sum(mixing, axis=0, keepdims=True) * (1.0 / members)
    mixing = jnp.where(inside, mixing + 1.0 / members, 0.0)
    return wide_dot(wide_left(total), wide_right(mixing))


def early_kernel(mine, other, total, last, ordered):
    place = position()
    members = mine.shape[0]
    row = lax.broadcasted_iota(jnp.int32, (members, LANES), 0)
    column = lax.broadcasted_iota(jnp.int32, (members, LANES), 1)
    inside = column < members

    def pick(where, x):
        return jnp.sum(jnp.where(where, x, 0.0), axis=1, keepdims=True)

    for half, shared in ((place[0], mine), (1 - place[0], other)):
        packed = shared[...]
        above = jnp.where(inside & (column > row), packed, 0.0)
        below = jnp.where(inside & (column < row), packed, 0.0)
        middle = jnp.where(column == row, packed, 0.0)
        side = jnp.where(column == members, pick(column == members + 1, packed), 0.0)
        ordered[2 * half] = above + turned(above) + (middle + side)
        middle = jnp.where(column == row, pick(column == members, packed), 0.0)
        side = jnp.where(column == members, pick(column == members + 2, packed), 0.0)
        ordered[2 * half + 1] = below + turned(below) + (middle + side)
    batches = ordered.shape[0]
    product = jnp.where(row == column, 1.0, 0.0)
    for batch in range(batches - 1):
        product = batch_transform(ordered[batch], product, members)
    total[...] = product
    last[...] = ordered[batches - 1]


def late_kernel(total, last, out, work, *, offsets, blocks, rows):
    place = position()
    members = total.shape[0]
    product = batch_transform(last[...], total[...], members)
    rest = jnp.zeros((LANES - members, LANES), f32)
    work[...] = jnp.concatenate([product, rest], axis=0)
    if blocks == 1:
        out[...] = work[...].T
        return
    parts = [
        work[pl.ds(pl.multiple_of(offsets(place[2], j), 8), rows), :] for j in range(blocks)
    ]
    work[...] = jnp.concatenate([*parts, rest], axis=0).T
    out[...] = work[pl.ds(pl.multiple_of(offsets(place[2], 0), 8), rows), :]


def transform_call(kernel, name, outputs, scratch, inputs):
    return pl.pallas_call(
        kernel,
        out_shape=[jax.ShapeDtypeStruct(shape, f32) for shape in outputs],
        in_specs=[VMEM] * len(inputs),
        out_specs=[VMEM] * len(outputs),
        scratch_shapes=[pltpu.VMEM(shape, f32) for shape in scratch],
        compiler_params=pltpu.CompilerParams(vmem_limit_bytes=SCOPED),
        cost_estimate=pl.CostEstimate(
            flops=10**8, bytes_accessed=10**6, transcendentals=0
        ),
        name=name,
    )(*inputs)


def mix_kernel(weights, *refs, blocks):
    *sources, out = refs
    rows, _, _, nz, _ = out.shape
    step, steps = pl.program_id(0), pl.num_programs(0)
    planes = out.shape[2]
    nx = steps * planes
    free, conserved, internal, tracer, tracer_ends = [
        sources[k : k + blocks] for k in range(0, len(sources), blocks)
    ]
    members = blocks * free[0].shape[2]
    high, low = split(weights[:, :members])
    both = jnp.concatenate([high.astype(f32), low.astype(f32)], axis=0).astype(bf16)
    mul = functools.partial(jnp.dot, preferred_element_type=f32)

    def mixed(held, x, z):
        parts = [array[x, z] for array in held]
        values = parts[0] if blocks == 1 else jnp.concatenate(parts, axis=0)
        value_high, value_low = split(values)
        upper = mul(both, value_high)
        return upper[:rows] + (upper[rows:] + mul(high, value_low))

    def plane(tracer, at, x, k):
        for z in range(nz):
            bound = mixed(tracer, at, z)
            inside = mixed(internal, x, z)
            out[:, 0, k, z, :] = mixed(free, x, z)
            out[:, 1, k, z, :] = mixed(conserved, x, z) - bound
            out[:, 2, k, z, :] = bound - inside
            out[:, 3, k, z, :] = inside

    for k in range(planes):
        x = step * planes + k
        at_end = (x == 0) | (x == nx - 1)

        @pl.when(at_end)
        def _(x=x, k=k):
            plane(tracer_ends, x // (nx - 1), x, k)

        @pl.when(jnp.logical_not(at_end))
        def _(x=x, k=k):
            plane(tracer, x - 1, x, k)


def mix(weights, sources, blocks, shape):
    rows, species, nx, nz, ny = shape
    planes = 2 if nx % 2 == 0 else 1
    return pl.pallas_call(
        functools.partial(mix_kernel, blocks=blocks),
        grid=(nx // planes,),
        in_specs=[VMEM] * (1 + len(sources)),
        out_specs=pl.BlockSpec((rows, species, planes, nz, ny), lambda x: (0, 0, x, 0, 0)),
        out_shape=jax.ShapeDtypeStruct(shape, f32),
        compiler_params=pltpu.CompilerParams(vmem_limit_bytes=SCOPED),
        name="mix",
    )(weights, *sources)


def swap(x, axis, bit):
    count = lax.axis_size(axis)
    return lax.ppermute(x, axis, [(k, k ^ bit) for k in range(count)])


def total_over(x, axis, before_last):
    bit = 1
    while bit < lax.axis_size(axis):
        if 2 * bit >= lax.axis_size(axis):
            x = lax.optimization_barrier((x, *before_last))[0]
        x = x + swap(x, axis, bit)
        bit *= 2
    return x


def local(ensemble, diffusivity, binding, source, obs_index, owner, observed, obs_var):
    rows, species, nx, nz, ny = ensemble.shape
    devices = lax.axis_size("member")
    spaces = lax.axis_size("space")
    members = rows * devices
    batches = owner.shape[0]
    member = lax.axis_index("member")

    forward = [(k, k + 1) for k in range(spaces - 1)]
    backward = [(k + 1, k) for k in range(spaces - 1)]

    def halos(first, last):
        return lax.ppermute(last, "space", forward), lax.ppermute(first, "space", backward)

    def tie(x, *after):
        return lax.optimization_barrier((x, *after))[0]

    if devices == 4 and rows % 8 == 0:
        blocks = devices

        def offsets(position, j):
            return jnp.bitwise_xor(position, j) * rows

        def beside_core(x):
            return [x, swap(x, "member", 1)]

        def collect(x, *after):
            return [*beside_core(x), swap(tie(x, *after), "member", 2)]

        def complete(held, *after):
            return [*held, swap(lax.optimization_barrier((held[2], *after))[0], "member", 1)]
    else:
        blocks = 1

        def offsets(position, j):
            return 0

        def beside_core(x):
            return [x]

        def collect(x, *after):
            return [lax.all_gather(x, "member", axis=2, tiled=True)]

        def complete(held, *after):
            return held

    def across(held):
        return held[min(2, blocks - 1)]

    whole = (nx, nz, rows, ny)
    coefficients = (diffusivity, binding, source)
    cells = nx * nz * rows * ny
    ends = [
        jnp.transpose(ensemble[:, :3, part], (1, 2, 3, 0, 4))
        for part in (slice(0, 2), slice(nx - 2, nx))
    ]
    edges = forecast_call(
        first_edges_kernel,
        "first_edges",
        [*ends, *coefficients],
        [(nz, 2 * rows + 8, ny)] * 2,
        2 * cells // nx,
    )
    fields = [jnp.transpose(ensemble[:, k], (1, 2, 0, 3)) for k in range(species)]
    conserved = fields[1] + fields[2] + fields[3]
    omega, eta = voxel_weights(
        owner, obs_index, observed, obs_var, batches // 2, nx * nz, ny
    )
    around = origin = halos(*edges)
    conserved = collect(conserved)
    payload = (nz, 2 * rows, ny)
    for step in range(SUBSTEPS // 2 - 2):
        inputs = [*fields, *around, *origin, *coefficients]
        around = halos(
            *forecast_call(
                next_edges_kernel, "next_edges", inputs, [payload] * 2, cells, scratch=[whole] * 8
            )
        )
        fields = forecast_call(
            two_substeps_kernel, "two_substeps", inputs, [whole] * 4, 2 * cells, scratch=[whole] * 4
        )
    inner, end = (nx - 2, nz, rows, ny), (2, nz, rows, ny)
    before, first, last, free, tracer, internal, add, ends = forecast_call(
        last_steps_kernel,
        "last_steps",
        [*fields, *around, *origin, *coefficients],
        [whole, payload, payload, whole, inner, whole, inner, (3, *end)],
        4 * cells,
        scratch=[whole] * 7,
        ready=(omega, eta, *conserved[1:]),
    )
    tracer = collect(tracer)
    around = halos(first, last)
    tracer_ends, free_ends, add_ends = forecast_call(
        last_ends_kernel,
        "last_ends",
        [free, ends, *around, *coefficients],
        [end] * 3,
        cells // nx,
    )
    tracer = complete(tracer, tracer_ends)
    tracer_ends = collect(tracer_ends)
    conserved = complete(conserved, tracer_ends[0])
    begun = gram(owner, omega, eta, None, tracer, offsets, (1, 1))
    tracer_ends = complete(tracer_ends, begun)
    internal = collect(internal, across(tracer_ends), begun)
    (free,) = forecast_call(
        last_free_kernel,
        "last_free",
        [before, free, free_ends, add, add_ends, *around, *origin, diffusivity],
        [whole],
        cells,
        ready=[*conserved[3:], *internal[1:2]] if blocks > 1 else (),
    )
    half = gram(owner, omega, eta, begun, tracer_ends, offsets, (0, nx - 1))
    held = beside_core(free)
    half = total_over(half, "space", held)
    other = swap(half, "member", 1)
    half = tie(half, other, across(internal))
    free = [*held, swap(tie(free, half), "member", 2)] if blocks > 1 else collect(free)
    internal = complete(internal, half)
    square = (members, LANES)
    total, extended = transform_call(
        early_kernel,
        "transforms_early",
        [square, square],
        [(batches, members, LANES)],
        [half, other],
    )
    free = complete(free, total)
    (weights,) = transform_call(
        functools.partial(late_kernel, offsets=offsets, blocks=blocks, rows=rows),
        "transforms_late",
        [(LANES, LANES) if blocks == 1 else (rows, LANES)],
        [(LANES, LANES)],
        [total, extended],
    )
    if blocks == 1:
        weights = lax.dynamic_slice(weights, (member * rows, 0), (rows, LANES))
    held = free + conserved + internal + tracer + tracer_ends
    return mix(weights, held, blocks, ensemble.shape)


def solution(mesh):
    in_specs = (
        P("member", None, "space", None, None),
        P("space", None, None),
        P("space", None, None),
        P("space", None, None),
        P(),
        P(),
        P(),
        P(),
    )
    out_specs = P("member", None, "space", None, None)
    return jax.shard_map(local, mesh=mesh, in_specs=in_specs, out_specs=out_specs, check_vma=False)
```

```python
import functools

import jax
import jax.numpy as jnp
from jax import lax
from jax.experimental import pallas as pl
from jax.experimental.pallas import tpu as pltpu
from jax.sharding import PartitionSpec as P

SUBSTEPS = 6
NEWTON = 16
UNROLL = 5
LANES = 128
SCOPED = 10 * 2**20

unbind_rate = 0.05
uptake_rate = 0.1
recycle_rate = 0.02

VMEM = pl.BlockSpec(memory_space=pltpu.VMEM)
SMEM = pl.BlockSpec(memory_space=pltpu.SMEM)
bf16 = jnp.bfloat16
f32 = jnp.float32


def split(x):
    high = x.astype(bf16)
    return high, (x - high.astype(f32)).astype(bf16)


def dot_parts(a, b, dims):
    a_high, a_low = a
    b_high, b_low = b
    mul = functools.partial(
        lax.dot_general, dimension_numbers=(dims, ((), ())), preferred_element_type=f32
    )
    return mul(a_high, b_high) + (mul(a_high, b_low) + mul(a_low, b_high))


def wide_left(x):
    return jnp.concatenate(split(x), axis=1)


def wide_right(x):
    both = jnp.concatenate(split(x), axis=1)
    rows, lanes = both.shape
    if rows < lanes // 2:
        both = jnp.concatenate([both, jnp.zeros((lanes // 2 - rows, lanes), bf16)], axis=0)
    return jnp.concatenate([both, both], axis=0)


def wide_dot(left, right):
    out = jnp.dot(left, right, preferred_element_type=f32)
    side = out.shape[1] // 2
    return out[:, :side] + out[:, side:]


NN = ((1,), (0,))
NT = ((1,), (1,))


def position():
    member = lax.axis_index("member")
    return member & 1, lax.axis_index("space"), member


def react(free, receptor, complexed, internal, binding):
    flux = binding * free * receptor
    back = unbind_rate * complexed - flux
    return (
        back,
        receptor + back + recycle_rate * internal,
        complexed + flux - (unbind_rate + uptake_rate) * complexed,
        internal + uptake_rate * complexed - recycle_rate * internal,
    )


def spread_free(free, planes, neighbours, diffusivity):
    lane = lax.broadcasted_iota(jnp.int32, free.shape, 1)
    last = free.shape[1] - 1
    for plane in planes:
        neighbours = plane if neighbours is None else neighbours + plane
    neighbours += jnp.where(lane == last, 0.0, pltpu.roll(free, last, 1))
    neighbours += jnp.where(lane == 0, 0.0, pltpu.roll(free, 1, 1))
    return free + diffusivity * (neighbours - 6.0 * free)


def beside(read, x, z, nx, nz, low, high):
    around = [low if x == 0 else read(x - 1, z), high if x == nx - 1 else read(x + 1, z)]
    around += [read(x, other) for other in (z + 1, z - 1) if 0 <= other < nz]
    return [value for value in around if value is not None]


def edge_free(read, rest, x, nz, nx, z, diffusivity):
    return spread_free(read(x, z), beside(read, x, z, nx, nz, None, None), None, diffusivity) + rest


def first_edges_kernel(below, above, diffusivity, binding, source, first, last):
    _, _, nz, members, _ = below.shape
    nx = diffusivity.shape[0]
    for x, ends, out in ((0, below, first), (nx - 1, above, last)):
        shift = 0 if x == 0 else nx - 2

        def read(at, z, ends=ends, shift=shift):
            return ends[0, at - shift, z]

        for z in range(nz):
            row = pl.ds(z, 1)
            free = read(x, z)
            flux = binding[x, row, :] * free * ends[1, x - shift, z]
            rest = unbind_rate * ends[2, x - shift, z] - flux + source[x, row, :]
            spread = diffusivity[x, row, :]
            out[z, :members, :] = free
            out[z, members : 2 * members, :] = edge_free(read, rest, x, nz, nx, z, spread)
            out[z, 2 * members :, :] = jnp.broadcast_to(spread, (8, spread.shape[1]))


def step_planes(planes, a, r, c, i, outside, diffusivity, binding, source, out_a, outs, keep):
    nx, nz, _, _ = a.shape
    for x in planes:
        for z in range(nz):
            row = pl.ds(z, 1)
            back, *others = react(a[x, z], r[x, z], c[x, z], i[x, z], binding[x, row, :])
            around = beside(lambda x, z: a[x, z], x, z, nx, nz, *outside(x, z))
            out_a[x, z] = (
                spread_free(a[x, z], around, None, diffusivity[x, row, :])
                + back
                + source[x, row, :]
            )
            if x in keep:
                for out, value in zip(outs, others):
                    out[x, z] = value


def before_last(a, low, high):
    nx, _, members, _ = a.shape

    def outside(x, z):
        return (
            low[z, :members, :] if x == 0 else None,
            high[z, :members, :] if x == nx - 1 else None,
        )

    return outside


def after_first(a, low, high, low_first, high_first):
    nx, _, members, _ = a.shape

    def completed(halo, origin, x, z):
        later = halo[z, members : 2 * members, :]
        return later + origin[z, 2 * members : 2 * members + 1, :] * a[x, z]

    def outside(x, z):
        return (
            completed(low, low_first, x, z) if x == 0 else None,
            completed(high, high_first, x, z) if x == nx - 1 else None,
        )

    return outside


def next_edges_kernel(
    a, r, c, i, low, high, low_first, high_first, diffusivity, binding, source, *refs
):
    first, last, *kept = refs
    middle, later = kept[:4], kept[4:]
    nx, nz, members, _ = a.shape
    coefficients = (diffusivity, binding, source)

    def near(depth):
        return [x for x in range(nx) if min(x, nx - 1 - x) < depth]

    step_planes(
        near(3), a, r, c, i, before_last(a, low, high), *coefficients, middle[0], middle[1:], near(2)
    )
    step_planes(
        near(2),
        *middle,
        after_first(a, low, high, low_first, high_first),
        *coefficients,
        later[0],
        later[1:],
        near(1),
    )
    free, receptor, complexed = later[:3]
    for x, out in ((0, first), (nx - 1, last)):
        for z in range(nz):
            row = pl.ds(z, 1)
            flux = binding[x, row, :] * free[x, z] * receptor[x, z]
            rest = unbind_rate * complexed[x, z] - flux + source[x, row, :]
            out[z, :members, :] = free[x, z]
            out[z, members:, :] = edge_free(
                lambda x, z: free[x, z], rest, x, nz, nx, z, diffusivity[x, row, :]
            )


def two_substeps_kernel(
    a, r, c, i, low, high, low_first, high_first, diffusivity, binding, source, *refs
):
    outs, middle = refs[:4], refs[4:]
    everywhere = range(a.shape[0])
    coefficients = (diffusivity, binding, source)
    step_planes(
        everywhere,
        a,
        r,
        c,
        i,
        before_last(a, low, high),
        *coefficients,
        middle[0],
        middle[1:],
        everywhere,
    )
    step_planes(
        everywhere,
        *middle,
        after_first(a, low, high, low_first, high_first),
        *coefficients,
        outs[0],
        outs[1:],
        everywhere,
    )


def last_steps_kernel(
    a, r, c, i, low, high, low_first, high_first, diffusivity, binding, source, *refs
):
    *outs, m0, m1, m2, m3, later_r, later_c, later_i = refs
    before, first, last, free, tracer, inside, add, ends = outs
    nx, nz, members, _ = a.shape
    coefficients = (diffusivity, binding, source)
    two_substeps_kernel(
        a,
        r,
        c,
        i,
        low,
        high,
        low_first,
        high_first,
        *coefficients,
        before,
        later_r,
        later_c,
        later_i,
        m0,
        m1,
        m2,
        m3,
    )
    step_planes(
        range(nx),
        before,
        later_r,
        later_c,
        later_i,
        lambda x, z: (None, None),
        *coefficients,
        free,
        (m1, m2, m3),
        range(nx),
    )
    for x in range(nx):
        for z in range(nz):
            row = pl.ds(z, 1)
            back, _, complexed, internal = react(
                free[x, z], m1[x, z], m2[x, z], m3[x, z], binding[x, row, :]
            )
            inside[x, z] = internal
            if 0 < x < nx - 1:
                tracer[x - 1, z] = complexed + internal
                add[x - 1, z] = back + source[x, row, :]
                continue
            ends[0, x // (nx - 1), z] = m1[x, z]
            ends[1, x // (nx - 1), z] = m2[x, z]
            ends[2, x // (nx - 1), z] = m3[x, z]
    for x, out in ((0, first), (nx - 1, last)):
        for z in range(nz):
            out[z, :members, :] = before[x, z]
            out[z, members:, :] = free[x, z]


def last_ends_kernel(
    free, ends, low, high, diffusivity, binding, source, tracer, out_free, add
):
    nx, nz, members, _ = free.shape
    for end, (x, halo) in enumerate(((0, low), (nx - 1, high))):
        for z in range(nz):
            row = pl.ds(z, 1)
            value = free[x, z] + diffusivity[x, row, :] * halo[z, :members, :]
            back, _, complexed, internal = react(
                value, ends[0, end, z], ends[1, end, z], ends[2, end, z], binding[x, row, :]
            )
            tracer[end, z] = complexed + internal
            out_free[end, z] = value
            add[end, z] = back + source[x, row, :]


def last_free_kernel(
    before, free, free_ends, add, add_ends, low, high, low_first, high_first, diffusivity, out
):
    nx, nz, _, _ = free.shape
    outside = after_first(before, low, high, low_first, high_first)

    def read(x, z):
        return free[x, z] if 0 < x < nx - 1 else free_ends[x // (nx - 1), z]

    for x in range(nx):
        for z in range(nz):
            around = beside(read, x, z, nx, nz, *outside(x, z))
            rest = add[x - 1, z] if 0 < x < nx - 1 else add_ends[x // (nx - 1), z]
            out[x, z] = (
                spread_free(read(x, z), around, None, diffusivity[x, pl.ds(z, 1), :]) + rest
            )


def forecast_call(kernel, name, inputs, outputs, cells, scratch=(), ready=()):
    def body(*refs):
        kernel(*refs[: len(inputs)], *refs[len(inputs) + len(ready) :])

    return pl.pallas_call(
        body,
        out_shape=[jax.ShapeDtypeStruct(shape, f32) for shape in outputs],
        in_specs=[VMEM] * len(inputs) + [pl.BlockSpec(memory_space=pl.ANY)] * len(ready),
        out_specs=[VMEM] * len(outputs),
        scratch_shapes=[pltpu.VMEM(shape, f32) for shape in scratch],
        compiler_params=pltpu.CompilerParams(vmem_limit_bytes=SCOPED),
        cost_estimate=pl.CostEstimate(
            flops=30 * cells, bytes_accessed=32 * cells, transcendentals=0
        ),
        name=name,
    )(*inputs, *ready)


def weights_kernel(owner, obs_index, observed, obs_var, omega, eta):
    place = position()
    count, rows, ny = omega.shape
    batch_size = obs_index.shape[1]
    for k in range(count):
        batch = place[0] * count + k
        mine = owner[batch] == place[1]
        line = pl.ds(batch, 1)
        voxel = obs_index[line, :]
        scale = jnp.where(mine, 1.0, 0.0) / obs_var[line, :]
        shift = ny.bit_length() - 1
        row = lax.shift_right_logical(voxel, shift)
        column = jnp.bitwise_and(voxel, ny - 1)
        at_row = lax.broadcasted_iota(jnp.int32, (rows, batch_size), 0) == row
        at_column = lax.broadcasted_iota(jnp.int32, (ny, batch_size), 0) == column
        both = jnp.concatenate(
            [jnp.where(at_row, scale, 0.0), jnp.where(at_row, scale * observed[line, :], 0.0)],
            axis=0,
        )
        one = both.astype(bf16)
        rest = both - one.astype(f32)
        two = rest.astype(bf16)
        three = (rest - two.astype(f32)).astype(bf16)
        columns = jnp.where(at_column, 1.0, 0.0).astype(bf16)
        sums = lax.dot_general(
            jnp.concatenate([one, two, three], axis=0),
            columns,
            (NT, ((), ())),
            preferred_element_type=f32,
        )
        sums = sums[: 2 * rows] + sums[2 * rows : 4 * rows] + sums[4 * rows :]
        omega[k] = sums[:rows]
        eta[k] = sums[rows:]


def voxel_weights(owner, obs_index, observed, obs_var, count, rows, ny):
    out = jax.ShapeDtypeStruct((count, rows, ny), f32)
    return pl.pallas_call(
        weights_kernel,
        out_shape=[out, out],
        in_specs=[SMEM, VMEM, VMEM, VMEM],
        out_specs=[VMEM, VMEM],
        compiler_params=pltpu.CompilerParams(vmem_limit_bytes=SCOPED),
        name="voxel_weights",
    )(owner, obs_index, observed, obs_var)


def gram_kernel(owner, omega, eta, *refs, offsets, planes, first):
    place = position()
    if first:
        *sources, out, members_at = refs
    else:
        begun, *sources, packed, out, members_at = refs
    count = out.shape[0]
    span, nz, rows, ny = sources[0].shape
    members = members_at.shape[0]
    for k in range(count):
        out[k] = jnp.zeros(out.shape[1:], f32) if first else begun[k]

        @pl.when(owner[place[0] * count + k] == place[1])
        def _(k=k):
            def tile(t, total):
                x, z = t // nz, t % nz
                voxels = pl.ds((planes[0] + x * planes[1]) * nz + z, 1)
                for j, source in enumerate(sources):
                    start = pl.multiple_of(offsets(place[2], j), 8)
                    members_at[pl.ds(start, rows), :] = source[x, z]
                values = members_at[...]
                mean = jnp.sum(values, axis=0, keepdims=True) * (1.0 / members)
                spread = values - mean
                weight = omega[k, voxels, :]
                shift = eta[k, voxels, :] - weight * mean
                tail = lax.broadcasted_iota(jnp.int32, (LANES - members, ny), 0)
                weighted = jnp.concatenate(
                    [spread * weight, jnp.where(tail == 0, shift, 0.0)], axis=0
                )
                return total + dot_parts(split(spread), split(weighted), NT)

            out[k] = lax.fori_loop(0, span * nz, tile, out[k], unroll=4)

    if first:
        return
    row = lax.broadcasted_iota(jnp.int32, (members, LANES), 0)
    column = lax.broadcasted_iota(jnp.int32, (members, LANES), 1)
    above, below = out[0], out[1]

    def pick(where, x):
        return jnp.sum(jnp.where(where, x, 0.0), axis=1, keepdims=True)

    both = jnp.where(column >= row, above, below)
    both = jnp.where(column == members, pick(column == row, below), both)
    both = jnp.where(column == members + 1, pick(column == members, above), both)
    packed[...] = jnp.where(column == members + 2, pick(column == members, below), both)


def gram(owner, omega, eta, begun, sources, offsets, planes):
    _, _, rows, ny = sources[0].shape
    members = rows * len(sources)
    whole = (omega.shape[0], members, LANES)
    work = pltpu.VMEM((members, ny), f32)
    first = begun is None
    return pl.pallas_call(
        functools.partial(gram_kernel, offsets=offsets, planes=planes, first=first),
        out_shape=jax.ShapeDtypeStruct(whole if first else whole[1:], f32),
        in_specs=[SMEM] + [VMEM] * (2 + len(sources) + (not first)),
        out_specs=VMEM,
        scratch_shapes=[work] if first else [pltpu.VMEM(whole, f32), work],
        compiler_params=pltpu.CompilerParams(vmem_limit_bytes=SCOPED),
        name="gram",
    )(owner, omega, eta, *([] if first else [begun]), *sources)


def turned(x):
    rows = x.shape[0]
    whole = jnp.concatenate([x, jnp.zeros((LANES - rows, LANES), f32)], axis=0)
    return whole.T[:rows]


def batch_transform(extended, total, members):
    row = lax.broadcasted_iota(jnp.int32, extended.shape, 0)
    column = lax.broadcasted_iota(jnp.int32, extended.shape, 1)
    inside = column < members
    last = column == members
    identity = jnp.where(row == column, 1.0, 0.0)
    matrix = jnp.where(inside, extended, 0.0)

    mean = jnp.sum(total, axis=1, keepdims=True) * (1.0 / members)
    centred = jnp.where(inside, total - mean, 0.0)
    product = wide_dot(wide_left(matrix), wide_right(jnp.where(last, mean, centred)))
    product = jnp.where(last, extended - product, product)
    product = wide_dot(wide_left(turned(centred)), wide_right(product)) * (1.0 / (members - 1))
    innovation = jnp.sum(jnp.where(last, product, 0.0), axis=1, keepdims=True)
    system = identity + jnp.where(inside, product, 0.0)
    frobenius = jnp.sqrt(jnp.sum(jnp.sum(system * system, axis=1, keepdims=True), axis=0, keepdims=True))

    scaled_root = system / frobenius
    factor = 1.5 * identity - 0.5 * scaled_root
    scaled_root = wide_dot(wide_left(scaled_root), wide_right(factor))
    inverse_root = factor

    def newton(iteration, iterates):
        scaled_root, inverse_root = iterates
        factor = 1.5 * identity - 0.5 * wide_dot(
            wide_left(inverse_root), wide_right(scaled_root)
        )
        return (
            wide_dot(wide_left(scaled_root), wide_right(factor)),
            wide_dot(wide_left(factor), wide_right(inverse_root)),
        )

    scaled_root, inverse_root = lax.fori_loop(1, NEWTON, newton, (scaled_root, inverse_root), unroll=UNROLL)
    root_inv = inverse_root / jnp.sqrt(frobenius)
    mean_weight = jnp.sum(root_inv * innovation, axis=0, keepdims=True)
    mean_weight = jnp.sum(root_inv * mean_weight, axis=1, keepdims=True)
    mixing = jnp.where(inside, root_inv + mean_weight, 0.0)
    mixing = mixing - jnp.sum(mixing, axis=0, keepdims=True) * (1.0 / members)
    mixing = jnp.where(inside, mixing + 1.0 / members, 0.0)
    return wide_dot(wide_left(total), wide_right(mixing))


def early_kernel(mine, other, total, last, ordered):
    place = position()
    members = mine.shape[0]
    row = lax.broadcasted_iota(jnp.int32, (members, LANES), 0)
    column = lax.broadcasted_iota(jnp.int32, (members, LANES), 1)
    inside = column < members

    def pick(where, x):
        return jnp.sum(jnp.where(where, x, 0.0), axis=1, keepdims=True)

    for half, shared in ((place[0], mine), (1 - place[0], other)):
        packed = shared[...]
        above = jnp.where(inside & (column > row), packed, 0.0)
        below = jnp.where(inside & (column < row), packed, 0.0)
        middle = jnp.where(column == row, packed, 0.0)
        side = jnp.where(column == members, pick(column == members + 1, packed), 0.0)
        ordered[2 * half] = above + turned(above) + (middle + side)
        middle = jnp.where(column == row, pick(column == members, packed), 0.0)
        side = jnp.where(column == members, pick(column == members + 2, packed), 0.0)
        ordered[2 * half + 1] = below + turned(below) + (middle + side)
    batches = ordered.shape[0]
    product = jnp.where(row == column, 1.0, 0.0)
    for batch in range(batches - 1):
        product = batch_transform(ordered[batch], product, members)
    total[...] = product
    last[...] = ordered[batches - 1]


def late_kernel(total, last, out, work, *, offsets, blocks, rows):
    place = position()
    members = total.shape[0]
    product = batch_transform(last[...], total[...], members)
    rest = jnp.zeros((LANES - members, LANES), f32)
    work[...] = jnp.concatenate([product, rest], axis=0)
    if blocks == 1:
        out[...] = work[...].T
        return
    parts = [
        work[pl.ds(pl.multiple_of(offsets(place[2], j), 8), rows), :] for j in range(blocks)
    ]
    work[...] = jnp.concatenate([*parts, rest], axis=0).T
    out[...] = work[pl.ds(pl.multiple_of(offsets(place[2], 0), 8), rows), :]


def transform_call(kernel, name, outputs, scratch, inputs):
    return pl.pallas_call(
        kernel,
        out_shape=[jax.ShapeDtypeStruct(shape, f32) for shape in outputs],
        in_specs=[VMEM] * len(inputs),
        out_specs=[VMEM] * len(outputs),
        scratch_shapes=[pltpu.VMEM(shape, f32) for shape in scratch],
        compiler_params=pltpu.CompilerParams(vmem_limit_bytes=SCOPED),
        cost_estimate=pl.CostEstimate(
            flops=10**8, bytes_accessed=10**6, transcendentals=0
        ),
        name=name,
    )(*inputs)


def mix_kernel(weights, *refs, blocks):
    *sources, out = refs
    rows, _, _, nz, _ = out.shape
    step, steps = pl.program_id(0), pl.num_programs(0)
    planes = out.shape[2]
    nx = steps * planes
    free, conserved, internal, tracer, tracer_ends = [
        sources[k : k + blocks] for k in range(0, len(sources), blocks)
    ]
    members = blocks * free[0].shape[2]
    high, low = split(weights[:, :members])
    both = jnp.concatenate([high.astype(f32), low.astype(f32)], axis=0).astype(bf16)
    mul = functools.partial(jnp.dot, preferred_element_type=f32)

    def mixed(held, x, z):
        parts = [array[x, z] for array in held]
        values = parts[0] if blocks == 1 else jnp.concatenate(parts, axis=0)
        value_high, value_low = split(values)
        upper = mul(both, value_high)
        return upper[:rows] + (upper[rows:] + mul(high, value_low))

    def plane(tracer, at, x, k):
        for z in range(nz):
            bound = mixed(tracer, at, z)
            inside = mixed(internal, x, z)
            out[:, 0, k, z, :] = mixed(free, x, z)
            out[:, 1, k, z, :] = mixed(conserved, x, z) - bound
            out[:, 2, k, z, :] = bound - inside
            out[:, 3, k, z, :] = inside

    for k in range(planes):
        x = step * planes + k
        at_end = (x == 0) | (x == nx - 1)

        @pl.when(at_end)
        def _(x=x, k=k):
            plane(tracer_ends, x // (nx - 1), x, k)

        @pl.when(jnp.logical_not(at_end))
        def _(x=x, k=k):
            plane(tracer, x - 1, x, k)


def mix(weights, sources, blocks, shape):
    rows, species, nx, nz, ny = shape
    planes = next(count for count in (4, 2, 1) if nx % count == 0)
    return pl.pallas_call(
        functools.partial(mix_kernel, blocks=blocks),
        grid=(nx // planes,),
        in_specs=[VMEM] * (1 + len(sources)),
        out_specs=pl.BlockSpec((rows, species, planes, nz, ny), lambda x: (0, 0, x, 0, 0)),
        out_shape=jax.ShapeDtypeStruct(shape, f32),
        compiler_params=pltpu.CompilerParams(vmem_limit_bytes=SCOPED),
        name="mix",
    )(weights, *sources)


def swap(x, axis, bit):
    count = lax.axis_size(axis)
    return lax.ppermute(x, axis, [(k, k ^ bit) for k in range(count)])


def total_over(x, axis, before_last):
    bit = 1
    while bit < lax.axis_size(axis):
        if 2 * bit >= lax.axis_size(axis):
            x = lax.optimization_barrier((x, *before_last))[0]
        x = x + swap(x, axis, bit)
        bit *= 2
    return x


def local(ensemble, diffusivity, binding, source, obs_index, owner, observed, obs_var):
    rows, species, nx, nz, ny = ensemble.shape
    devices = lax.axis_size("member")
    spaces = lax.axis_size("space")
    members = rows * devices
    batches = owner.shape[0]
    member = lax.axis_index("member")

    forward = [(k, k + 1) for k in range(spaces - 1)]
    backward = [(k + 1, k) for k in range(spaces - 1)]

    def halos(first, last):
        return lax.ppermute(last, "space", forward), lax.ppermute(first, "space", backward)

    def tie(x, *after):
        return lax.optimization_barrier((x, *after))[0]

    if devices == 4 and rows % 8 == 0:
        blocks = devices

        def offsets(position, j):
            return jnp.bitwise_xor(position, j) * rows

        def beside_core(x):
            return [x, swap(x, "member", 1)]

        def collect(x, *after):
            return [*beside_core(x), swap(tie(x, *after), "member", 2)]

        def complete(held, *after):
            return [*held, swap(lax.optimization_barrier((held[2], *after))[0], "member", 1)]
    else:
        blocks = 1

        def offsets(position, j):
            return 0

        def beside_core(x):
            return [x]

        def collect(x, *after):
            return [lax.all_gather(x, "member", axis=2, tiled=True)]

        def complete(held, *after):
            return held

    def across(held):
        return held[min(2, blocks - 1)]

    whole = (nx, nz, rows, ny)
    coefficients = (diffusivity, binding, source)
    cells = nx * nz * rows * ny
    ends = [
        jnp.transpose(ensemble[:, :3, part], (1, 2, 3, 0, 4))
        for part in (slice(0, 2), slice(nx - 2, nx))
    ]
    edges = forecast_call(
        first_edges_kernel,
        "first_edges",
        [*ends, *coefficients],
        [(nz, 2 * rows + 8, ny)] * 2,
        2 * cells // nx,
    )
    fields = [jnp.transpose(ensemble[:, k], (1, 2, 0, 3)) for k in range(species)]
    conserved = fields[1] + fields[2] + fields[3]
    omega, eta = voxel_weights(
        owner, obs_index, observed, obs_var, batches // 2, nx * nz, ny
    )
    around = origin = halos(*edges)
    conserved = collect(conserved)
    payload = (nz, 2 * rows, ny)
    for step in range(SUBSTEPS // 2 - 2):
        inputs = [*fields, *around, *origin, *coefficients]
        around = halos(
            *forecast_call(
                next_edges_kernel, "next_edges", inputs, [payload] * 2, cells, scratch=[whole] * 8
            )
        )
        fields = forecast_call(
            two_substeps_kernel, "two_substeps", inputs, [whole] * 4, 2 * cells, scratch=[whole] * 4
        )
    inner, end = (nx - 2, nz, rows, ny), (2, nz, rows, ny)
    before, first, last, free, tracer, internal, add, ends = forecast_call(
        last_steps_kernel,
        "last_steps",
        [*fields, *around, *origin, *coefficients],
        [whole, payload, payload, whole, inner, whole, inner, (3, *end)],
        4 * cells,
        scratch=[whole] * 7,
        ready=(omega, eta, *conserved[1:]),
    )
    tracer = collect(tracer)
    around = halos(first, last)
    tracer_ends, free_ends, add_ends = forecast_call(
        last_ends_kernel,
        "last_ends",
        [free, ends, *around, *coefficients],
        [end] * 3,
        cells // nx,
    )
    tracer = complete(tracer, tracer_ends)
    tracer_ends = collect(tracer_ends)
    conserved = complete(conserved, tracer_ends[0])
    begun = gram(owner, omega, eta, None, tracer, offsets, (1, 1))
    tracer_ends = complete(tracer_ends, begun)
    internal = collect(internal, across(tracer_ends), begun)
    (free,) = forecast_call(
        last_free_kernel,
        "last_free",
        [before, free, free_ends, add, add_ends, *around, *origin, diffusivity],
        [whole],
        cells,
        ready=[*conserved[3:], *internal[1:2]] if blocks > 1 else (),
    )
    half = gram(owner, omega, eta, begun, tracer_ends, offsets, (0, nx - 1))
    held = beside_core(free)
    half = total_over(half, "space", held)
    other = swap(half, "member", 1)
    half = tie(half, other, across(internal))
    free = [*held, swap(tie(free, half), "member", 2)] if blocks > 1 else collect(free)
    internal = complete(internal, half)
    square = (members, LANES)
    total, extended = transform_call(
        early_kernel,
        "transforms_early",
        [square, square],
        [(batches, members, LANES)],
        [half, other],
    )
    free = complete(free, total)
    (weights,) = transform_call(
        functools.partial(late_kernel, offsets=offsets, blocks=blocks, rows=rows),
        "transforms_late",
        [(LANES, LANES) if blocks == 1 else (rows, LANES)],
        [(LANES, LANES)],
        [total, extended],
    )
    if blocks == 1:
        weights = lax.dynamic_slice(weights, (member * rows, 0), (rows, LANES))
    held = free + conserved + internal + tracer + tracer_ends
    return mix(weights, held, blocks, ensemble.shape)


def solution(mesh):
    in_specs = (
        P("member", None, "space", None, None),
        P("space", None, None),
        P("space", None, None),
        P("space", None, None),
        P(),
        P(),
        P(),
        P(),
    )
    out_specs = P("member", None, "space", None, None)
    return jax.shard_map(local, mesh=mesh, in_specs=in_specs, out_specs=out_specs, check_vma=False)
```
